32 devices in a mesh: rep: 4 (over y, core), grp: 8 (over z, x).
Axes of the slice: x: 2, y: 2, z: 4, core: 2. Of those that a mesh axis runs over, the one named last changes fastest.
Arguments:
- tokens: bfloat16 [4096, 1536], P(('rep', 'grp')), may hold values from -6 to 6
- attn_gain: bfloat16 [1536], P('grp'), may hold values from 0.5 to 1.5
- w_qkv: bfloat16 [1536, 2560], P('grp'), may hold values from -0.15625 to 0.15625
- q_gain: bfloat16 [64], replicated, may hold values from 0.5 to 1.5
- k_gain: bfloat16 [64], replicated, may hold values from 0.5 to 1.5
- w_out: bfloat16 [1536, 1536], P('grp'), may hold values from -0.875 to 0.875
- ffn_gain: bfloat16 [1536], P('grp'), may hold values from 0.5 to 1.5
- w_gate_up: bfloat16 [1536, 9216], P('grp'), may hold values from -0.15625 to 0.15625
- w_down: bfloat16 [4608, 1536], P('grp'), may hold values from -0.09375 to 0.09375
- cotangent: bfloat16 [4096, 1536], P(('rep', 'grp')), may hold values from -6 to 6
- segment_ids: int32 [4096], P(('rep', 'grp')), may hold values from 0 to 7, as said below
Outputs:
- mixed: bfloat16 [4096, 1536], P(('rep', 'grp'))
- input_grad: float32 [4096, 1536], P(('rep', 'grp'))
- attn_gain_grad: float32 [1536], P('grp')
- w_qkv_grad: float32 [1536, 2560], P('grp')
- q_gain_grad: float32 [64], replicated
- k_gain_grad: float32 [64], replicated
- w_out_grad: float32 [1536, 1536], P('grp')
- ffn_gain_grad: float32 [1536], P('grp')
- w_gate_up_grad: float32 [1536, 9216], P('grp')
- w_down_grad: float32 [4608, 1536], P('grp')
The draws below stay inside these ranges and needn't reach their ends.
Inputs may be any that keep to these rules, and one draw needn't show every extreme that they name: `segment_ids`: Non-decreasing within each sequence of 1024 tokens and 0 at its first token; every document number appears in every sequence.
All inputs are finite; a program needn't handle non-finite values.
Results may differ from the reference program's by a relative error of at most 0.02.
Values may be sent and summed in bfloat16 or wider, within the bound.
A program may use at most 320 MiB of HBM per device.

```python
import jax
import jax.numpy as jnp
from jax import lax

D = 1536
HEADS = 24
KV_HEADS = 8
HEAD_DIM = 64
FF = 4608
TOK_DEV = 128
DOCS = 8
TOKENS = 4096
N_REP = 4
N_GRP = 8


def layout(key):
    length = TOK_DEV * N_GRP
    cuts = DOCS - 1

    def one(sub):
        key_a, key_b, key_c = jax.random.split(sub, 3)
        early = jax.random.randint(key_a, (), 0, DOCS)
        front = jax.random.permutation(key_b, TOK_DEV - 1)[:cuts] + 1
        back = jax.random.permutation(key_c, TOK_DEV - 1)[:cuts] + (length - TOK_DEV + 1)
        slot = jnp.arange(cuts, dtype=jnp.int32)
        front = jnp.where(slot < early, front, length)
        back = jnp.where(slot < cuts - early, back, length)
        chosen = jnp.sort(jnp.concatenate([front, back]))[:cuts]
        return jnp.concatenate([jnp.zeros((1,), jnp.int32), chosen.astype(jnp.int32)])
    return jax.vmap(one)(jax.random.split(key, N_REP))


def draw_segment_ids(key, part):
    starts = layout(key)
    length = TOK_DEV * N_GRP
    place = jnp.arange(length, dtype=jnp.int32)
    counted = jnp.sum((starts[:, 1:, None] <= place[None, None, :]).astype(jnp.int32), axis=1)
    return counted.reshape(N_REP * length).astype(jnp.int32)


def block_scale(rng, dims, shards, smallest, largest):
    level = 1.0
    for axis_at, blocks in shards:
        draws = jax.random.uniform(jax.random.fold_in(jax.random.fold_in(rng, 6), axis_at), (blocks,), jnp.float32, smallest / len(shards), largest / len(shards))
        level = level * jnp.repeat(jnp.exp(draws), dims[axis_at] // blocks).reshape((-1,) + (1,) * (len(dims) - 1 - axis_at))
    return level


def scatter_about(rng, shape, deviation, limit, shards=(), held_as=jnp.bfloat16):
    factor_of = block_scale(rng, shape, shards, -0.22, 0.18) if shards else 1.0
    entries = jax.random.normal(rng, shape, jnp.float32) * deviation * factor_of
    return jnp.minimum(jnp.maximum(entries, -limit), limit).astype(held_as)


def setup_inputs(seed: int = 0) -> dict:
    splits = jax.random.split(jax.random.key(seed), 12)
    return {
        "tokens": scatter_about(splits[0], (TOKENS, D), 1.0, 6.0, ((0, 32),)),
        "attn_gain": jnp.clip(1.0 + 0.1 * jax.random.normal(splits[1], (D,), jnp.float32), 0.5, 1.5).astype(jnp.bfloat16),
        "w_qkv": scatter_about(splits[2], (D, (HEADS + 2 * KV_HEADS) * HEAD_DIM), D ** -0.5, 0.15625, ((0, 8),)),
        "q_gain": jnp.clip(1.0 + 0.1 * jax.random.normal(splits[3], (HEAD_DIM,), jnp.float32), 0.5, 1.5).astype(jnp.bfloat16),
        "k_gain": jnp.clip(1.0 + 0.1 * jax.random.normal(splits[4], (HEAD_DIM,), jnp.float32), 0.5, 1.5).astype(jnp.bfloat16),
        "w_out": scatter_about(splits[5], (HEADS * HEAD_DIM, D), (HEADS * HEAD_DIM // 32) ** -0.5, 0.875, ((0, 8),)),
        "ffn_gain": jnp.clip(1.0 + 0.1 * jax.random.normal(splits[6], (D,), jnp.float32), 0.5, 1.5).astype(jnp.bfloat16),
        "w_gate_up": scatter_about(splits[7], (D, 2 * FF), D ** -0.5, 0.15625, ((0, 8),)),
        "w_down": scatter_about(splits[8], (FF, D), FF ** -0.5, 0.09375, ((0, 8),)),
        "cotangent": scatter_about(splits[9], (TOKENS, D), 1.0, 6.0, ((0, 32),)),
        "segment_ids": draw_segment_ids(jax.random.fold_in(splits[11], 71), 0),
    }


@jax.custom_vjp
def low(v):
    return lax.optimization_barrier(v.astype(jnp.bfloat16)).astype(jnp.float32)

@jax.custom_vjp
def low_back(v):
    return v

def low_keep(v):
    return (low(v), None)

def low_pass(kept, grad):
    return (grad,)

def back_keep(v):
    return (v, None)

def back_low(kept, grad):
    return (low(grad),)
low.defvjp(low_keep, low_pass)
low_back.defvjp(back_keep, back_low)
EPS = 1e-05
THETA = 1000000.0
HIGH = lax.Precision.HIGHEST

def matmul(left, right):
    return jnp.dot(left, right, precision=HIGH)

def rms(values, gain):
    return values * lax.rsqrt(lax.optimization_barrier(jnp.mean(values * values, axis=-1, keepdims=True)) + EPS) * gain

def rope_tables(positions):
    half = HEAD_DIM // 2
    freq = jnp.exp(-jnp.log(THETA) * jnp.arange(half, dtype=jnp.float32) * 2.0 / HEAD_DIM)
    angle = positions.astype(jnp.float32)[:, None] * freq[None, :]
    return (jnp.cos(angle), jnp.sin(angle))

def rotate(values, cosine, sine):
    half = values.shape[-1] // 2
    first = values[..., :half]
    second = values[..., half:]
    cos_b = cosine[:, None, :]
    sin_b = sine[:, None, :]
    return jnp.concatenate([first * cos_b - second * sin_b, second * cos_b + first * sin_b], axis=-1)

def layer(xs, attn_gain, w_qkv, q_gain, k_gain, w_out, ffn_gain, w_gate_up, w_down, cosine, sine, allowed):
    length = xs.shape[0]
    q_width = HEADS * HEAD_DIM
    kv_width = KV_HEADS * HEAD_DIM
    group = HEADS // KV_HEADS
    normed = low(rms(xs, attn_gain))
    qkv = low_back(matmul(normed, w_qkv))
    q_raw = qkv[:, :q_width].reshape(length, HEADS, HEAD_DIM)
    k_raw = qkv[:, q_width:q_width + kv_width].reshape(length, KV_HEADS, HEAD_DIM)
    values = low(qkv[:, q_width + kv_width:]).reshape(length, KV_HEADS, HEAD_DIM)
    queries = low(rotate(rms(q_raw, q_gain), cosine, sine))
    keys = low(rotate(rms(k_raw, k_gain), cosine, sine))
    queries = queries.reshape(length, KV_HEADS, group, HEAD_DIM)
    scores = jnp.einsum('qhgd,khd->hgqk', queries, keys, precision=HIGH) * HEAD_DIM ** (-0.5)
    scores = low_back(scores)
    scores = jnp.where(allowed[None, None, :, :], scores, -1e+30)
    probs = low(jax.nn.softmax(scores, axis=-1))
    attended = jnp.einsum('hgqk,khd->qhgd', probs, values, precision=HIGH).reshape(length, q_width)
    attended = low(low_back(attended))
    mid = xs + low_back(matmul(attended, w_out))
    normed_two = low(rms(mid, ffn_gain))
    gate_up = low_back(matmul(normed_two, w_gate_up))
    hidden = low(jax.nn.silu(gate_up[:, :FF]) * gate_up[:, FF:])
    return mid + low_back(matmul(hidden, w_down))

def reference(tokens, attn_gain, w_qkv, q_gain, k_gain, w_out, ffn_gain, w_gate_up, w_down, cotangent, segment_ids):
    length = TOK_DEV * N_GRP
    weights = tuple((a.astype(jnp.float32) for a in (attn_gain, w_qkv, q_gain, k_gain, w_out, ffn_gain, w_gate_up, w_down)))
    inputs = tokens.astype(jnp.float32).reshape(N_REP, length, D)
    grads_out = cotangent.astype(jnp.float32).reshape(N_REP, length, D)
    segments = segment_ids.reshape(N_REP, length)

    def step(totals, item):
        xs, grad_y, seg = item
        index = jnp.arange(length, dtype=jnp.int32)
        cosine, sine = rope_tables(index)
        allowed = (seg[:, None] == seg[None, :]) & (index[None, :] <= index[:, None])

        def forward(xx, *ws):
            return layer(xx, *ws, cosine, sine, allowed)
        out, pull = jax.vjp(forward, xs, *weights)
        grads = pull(grad_y)
        totals = tuple((a + b for a, b in zip(totals, grads[1:])))
        return (totals, (out.astype(jnp.bfloat16), grads[0]))
    start = tuple((jnp.zeros(w.shape, jnp.float32) for w in weights))
    totals, (outs, input_grads) = lax.scan(step, start, (inputs, grads_out, segments))
    return (outs.reshape(N_REP * length, D), input_grads.reshape(N_REP * length, D), totals[0], totals[1], totals[2], totals[3], totals[4], totals[5], totals[6], totals[7])
```

```python
import functools

import jax
import jax.numpy as jnp
from jax import lax
from jax.experimental import pallas as pl
from jax.experimental.pallas import tpu as pltpu
from jax.sharding import PartitionSpec as P

HEADS = 24
KV_HEADS = 8
HEAD_DIM = 64
GROUP = HEADS // KV_HEADS
Q_COLS = GROUP * HEAD_DIM
HEAD_COLS = Q_COLS + 2 * HEAD_DIM

EPS = 1e-05
THETA = 1000000.0
MESH = pl.DeviceIdType.MESH
F32 = jnp.float32
BF16 = jnp.bfloat16

VMEM = pl.BlockSpec(memory_space=pltpu.VMEM)
ANY = pl.BlockSpec(memory_space=pl.ANY)


def here():
    rep = lax.axis_index("rep")
    grp = lax.axis_index("grp")
    r = rep % 4
    return rep - r, r // 2, r % 2, grp // 2, grp % 2


def device(base, y, c, z, x):
    return {"rep": base + 2 * y + c, "grp": 2 * z + x}


def remote(src, dst, send, recv, to):
    return pltpu.make_async_remote_copy(
        src_ref=src, dst_ref=dst, send_sem=send, recv_sem=recv, device_id=to, device_id_type=MESH
    )


def greet(targets):
    barrier = pltpu.get_barrier_semaphore()
    for to in targets:
        pl.semaphore_signal(barrier, inc=1, device_id=to, device_id_type=MESH)
    pl.semaphore_wait(barrier, len(targets))


def neighbours():
    base, y, c, z, x = here()
    to_c = device(base, y, 1 - c, z, x)
    to_x = device(base, y, c, z, 1 - x)
    to_y = device(base, 1 - y, c, z, x)
    return to_c, to_x, to_y


GATHER_SEMS = 8


class Gather:
    def __init__(self, src, out, send, recv, local):
        self.src, self.out, self.send, self.recv, self.local = src, out, send, recv, local
        _, y, c, _, x = here()
        self.to_c, self.to_x, self.to_y = neighbours()
        slot = lambda a, b, d: 4 * a + 2 * b + d
        self.own = slot(y, c, x)
        self.at_c, self.at_x, self.at_y = slot(y, 1 - c, x), slot(y, c, 1 - x), slot(1 - y, c, x)
        self.at_xc, self.at_yc = slot(y, 1 - c, 1 - x), slot(1 - y, 1 - c, x)
        self.at_xy, self.at_xyc = slot(1 - y, c, 1 - x), slot(1 - y, 1 - c, 1 - x)
        self.half = src.shape[0] // 2

    def part(self, ref, k):
        return ref.at[pl.ds(k * self.half, self.half)]

    def copy(self, k, src, dst, to):
        return remote(src, dst, self.send.at[k], self.recv.at[k], to)

    def start(self):
        out, src = self.out, self.src
        self.keep = pltpu.make_async_copy(src, out.at[self.own], self.local)
        self.keep.start()
        self.sent = [
            self.copy(0, src, out.at[self.own], self.to_x),
            self.copy(1, src, out.at[self.own], self.to_y),
            self.copy(2, src, out.at[self.own], self.to_c),
        ]
        for copy in self.sent:
            copy.start()

    def forward(self):
        out = self.out
        self.copy(0, self.src, out.at[self.at_x], self.to_x).wait_recv()
        first = self.part(out.at[self.at_x], 0)
        self.go(3, first, first, self.to_y)
        self.go(4, out.at[self.at_x], out.at[self.at_x], self.to_c)
        self.copy(1, self.src, out.at[self.at_y], self.to_y).wait_recv()
        second = self.part(out.at[self.at_y], 1)
        self.go(5, second, second, self.to_x)
        self.go(6, out.at[self.at_y], out.at[self.at_y], self.to_c)

    def go(self, k, src, dst, to):
        copy = self.copy(k, src, dst, to)
        copy.start()
        self.sent.append(copy)

    def finish(self):
        out = self.out
        first = self.part(out.at[self.at_xy], 0)
        second = self.part(out.at[self.at_xy], 1)
        self.copy(3, first, first, self.to_y).wait_recv()
        self.copy(5, second, second, self.to_x).wait_recv()
        self.go(7, out.at[self.at_xy], out.at[self.at_xy], self.to_c)
        for k, at in ((2, self.at_c), (4, self.at_xc), (6, self.at_yc), (7, self.at_xyc)):
            self.copy(k, out.at[at], out.at[at], self.to_c).wait_recv()
        for copy in self.sent:
            copy.wait_send()
        self.keep.wait()


SUM_SEMS = 10


def sum_scratch(width):
    return [
        pltpu.VMEM((4, 128, width), BF16),
        pltpu.VMEM((4, 128, width), BF16),
        pltpu.VMEM((2, 64, width), BF16),
        pltpu.VMEM((2, 64, width), BF16),
        pltpu.VMEM((2, 64, width), BF16),
        pltpu.VMEM((2, 64, width), BF16),
        pltpu.VMEM((128, width), F32),
        pltpu.SemaphoreType.DMA((SUM_SEMS,)),
        pltpu.SemaphoreType.DMA((SUM_SEMS,)),
    ]


class Summed:
    def __init__(self, part, scratch):
        self.part = part
        (self.r1, self.chip, self.rx, self.ry, self.mine, self.late, self.out,
         self.send, self.recv) = scratch
        _, self.y, self.c, _, self.x = here()
        self.to_c, self.to_x, self.to_y = neighbours()
        y, x = self.y, self.x
        self.order = ((1 - y, 1 - x), (y, 1 - x), (1 - y, x), (y, x))
        self.sent = []

    def copy(self, k, src, dst, to):
        return remote(src, dst, self.send.at[k], self.recv.at[k], to)

    def go(self, k, src, dst, to):
        copy = self.copy(k, src, dst, to)
        copy.start()
        self.sent.append(copy)

    def start(self):
        for k, (y, x) in enumerate(self.order):
            self.go(k, self.part.at[4 * y + 2 * (1 - self.c) + x], self.r1.at[2 * y + x], self.to_c)

    def middle(self):
        x, y, c = self.x, self.y, self.c
        top, low = pl.ds(0, 64), pl.ds(64, 64)
        for k, (b, a) in enumerate(self.order):
            at = 2 * b + a
            self.copy(k, self.r1.at[at], self.r1.at[at], self.to_c).wait_recv()
            total = self.part[4 * b + 2 * c + a].astype(F32) + self.r1[at].astype(F32)
            if k == 3:
                self.out[...] = total
                continue
            self.chip[at] = total.astype(BF16)
            if k in (0, 1):
                self.go(4 + k, self.chip.at[at, top], self.rx.at[b], self.to_x)
            if k in (0, 2):
                self.go(6 + k // 2, self.chip.at[at, low], self.ry.at[a], self.to_y)
        self.copy(4, self.rx.at[1 - y], self.rx.at[1 - y], self.to_x).wait_recv()
        self.mine[0] = (
            self.chip[2 * (1 - y) + x, 0:64].astype(F32) + self.rx[1 - y].astype(F32)
        ).astype(BF16)
        self.go(8, self.mine.at[0], self.late.at[0], self.to_y)
        self.copy(6, self.ry.at[1 - x], self.ry.at[1 - x], self.to_y).wait_recv()
        self.mine[1] = (
            self.chip[2 * y + 1 - x, 64:128].astype(F32) + self.ry[1 - x].astype(F32)
        ).astype(BF16)
        self.go(9, self.mine.at[1], self.late.at[1], self.to_x)

    def finish(self):
        x, y = self.x, self.y
        self.copy(5, self.rx.at[y], self.rx.at[y], self.to_x).wait_recv()
        self.copy(7, self.ry.at[x], self.ry.at[x], self.to_y).wait_recv()
        self.copy(8, self.late.at[0], self.late.at[0], self.to_y).wait_recv()
        self.copy(9, self.late.at[1], self.late.at[1], self.to_x).wait_recv()
        self.out[0:64] += self.rx[y].astype(F32) + self.late[0].astype(F32)
        self.out[64:128] += self.ry[x].astype(F32) + self.late[1].astype(F32)
        for copy in self.sent:
            copy.wait_send()


def dma(n):
    return pltpu.SemaphoreType.DMA((n,))


def params(cid, limit=60):
    return pltpu.CompilerParams(
        collective_id=cid, has_side_effects=True, vmem_limit_bytes=limit * 2**20
    )


def local_params(limit=60):
    return pltpu.CompilerParams(vmem_limit_bytes=limit * 2**20)


def gather_kernel(zs, tok, cot, seg, wq, gains, tok_o, cot_o, seg_o, wq_o, gains_o,
                  sa, ra, sb, rb, sc, rc, sw, rw, sg, rg, keep):
    base, y, c, z, x = here()
    to_c, to_x, to_y = neighbours()
    far = []
    for k in range(1, 2 * zs):
        zk, xk = (z + k // 2) % zs, (x + k % 2) % 2
        far.append((device(base, y, c, zk, xk), xk))
    greet([to_c, to_y] + [d for d, _ in far])
    a = Gather(tok, tok_o, sa, ra, keep.at[0])
    b = Gather(cot, cot_o, sb, rb, keep.at[1])
    s = Gather(seg, seg_o, sc, rc, keep.at[2])
    own = 2 * z + x
    s.start()
    a.start()
    sent = []
    for k, (to, xk) in enumerate(far):
        sent.append(remote(wq.at[xk], wq_o.at[own], sw.at[k], rw.at[k], to))
        sent.append(remote(gains, gains_o.at[own], sg.at[k], rg.at[k], to))
    for copy in sent:
        copy.start()
    mine = [
        pltpu.make_async_copy(wq.at[x], wq_o.at[own], keep.at[3]),
        pltpu.make_async_copy(gains, gains_o.at[own], keep.at[4]),
    ]
    for copy in mine:
        copy.start()
    b.start()
    s.forward()
    a.forward()
    s.finish()
    a.finish()
    b.forward()
    b.finish()
    for copy in sent:
        copy.wait_send()
    for k in range(1, 2 * zs):
        zk, xk = (z + zs - k // 2) % zs, (x + k % 2) % 2
        at = 2 * zk + xk
        remote(wq.at[0], wq_o.at[at], sw.at[k - 1], rw.at[k - 1], to_c).wait_recv()
        remote(gains, gains_o.at[at], sg.at[k - 1], rg.at[k - 1], to_c).wait_recv()
    for copy in mine:
        copy.wait()


def first_gather(zs, tok, cot, seg, wq, gains):
    shape = jax.ShapeDtypeStruct
    n = 2 * zs - 1
    return pl.pallas_call(
        functools.partial(gather_kernel, zs),
        name="gather_first",
        out_shape=(
            shape((8,) + tok.shape, BF16),
            shape((8,) + cot.shape, BF16),
            shape((8,) + seg.shape, seg.dtype),
            shape((2 * zs,) + wq.shape[1:], BF16),
            shape((2 * zs,) + gains.shape, BF16),
        ),
        in_specs=[ANY] * 5,
        out_specs=(ANY,) * 5,
        scratch_shapes=[dma(8)] * 6 + [dma(n)] * 4 + [dma(5)],
        compiler_params=params(0),
    )(tok, cot, seg, wq, gains)


def up_kernel(zs, kv, seg, kv_o, seg_o, sk, rk, ss, rs, keep):
    base, y, c, z, x = here()
    others = [device(base, y, c, (z + k) % zs, x) for k in range(1, zs)]
    greet(others)
    mine = [
        pltpu.make_async_copy(kv, kv_o.at[z], keep.at[0]),
        pltpu.make_async_copy(seg, seg_o.at[z], keep.at[1]),
    ]
    for copy in mine:
        copy.start()
    for k in range(1, zs):
        @pl.when(z + k < zs)
        def _():
            to = device(base, y, c, (z + k) % zs, x)
            remote(seg, seg_o.at[z], ss.at[k - 1], rs.at[k - 1], to).start()
            remote(kv, kv_o.at[z], sk.at[k - 1], rk.at[k - 1], to).start()
    for k in range(1, zs):
        @pl.when(z - k >= 0)
        def _():
            at = (z + zs - k) % zs
            to = device(base, y, c, at, x)
            remote(seg, seg_o.at[at], ss.at[k - 1], rs.at[k - 1], to).wait_recv()
            remote(kv, kv_o.at[at], sk.at[k - 1], rk.at[k - 1], to).wait_recv()
    for k in range(1, zs):
        @pl.when(z + k < zs)
        def _():
            to = device(base, y, c, (z + k) % zs, x)
            remote(seg, seg_o.at[z], ss.at[k - 1], rs.at[k - 1], to).wait_send()
            remote(kv, kv_o.at[z], sk.at[k - 1], rk.at[k - 1], to).wait_send()
    for copy in mine:
        copy.wait()


def send_up(zs, kv, seg):
    shape = jax.ShapeDtypeStruct
    n = zs - 1
    return pl.pallas_call(
        functools.partial(up_kernel, zs),
        name="send_up",
        out_shape=(shape((zs,) + kv.shape, BF16), shape((zs,) + seg.shape, seg.dtype)),
        in_specs=[ANY] * 2,
        out_specs=(ANY,) * 2,
        scratch_shapes=[dma(n)] * 4 + [dma(2)],
        compiler_params=params(1),
    )(kv, seg)


def scores_of(q, k, q_seg, k_seg, diagonal, span):
    s = lax.dot_general(q, k, (((1,), (1,)), ((), ())), preferred_element_type=F32)
    allowed = q_seg == k_seg
    if diagonal:
        row = lax.broadcasted_iota(jnp.int32, s.shape, 0) % span
        col = lax.broadcasted_iota(jnp.int32, s.shape, 1)
        allowed = allowed & (col <= row)
    return jnp.where(allowed, jnp.exp(s), 0.0)


def attend_kernel(q_ref, kv_ref, qseg_ref, kseg_ref, o_ref, inv_ref, acc, tot):
    _, _, _, z, _ = here()
    span = kv_ref.shape[2]

    def sequence(s, carry):
        q = q_ref[s]
        q_seg = qseg_ref[s]

        def block(at, diagonal):
            kv = kv_ref[at, s]
            p = scores_of(q, kv[:, :HEAD_DIM], q_seg, kseg_ref[at, s], diagonal, span)
            tot[...] += jnp.sum(p, axis=1, keepdims=True)
            acc[...] += jnp.dot(p.astype(BF16), kv[:, HEAD_DIM:], preferred_element_type=F32)

        acc[...] = jnp.zeros_like(acc)
        tot[...] = jnp.zeros_like(tot)

        def step(at, inner):
            block(at, False)
            return inner

        lax.fori_loop(0, z, step, 0)
        block(z, True)
        inv = 1.0 / tot[...]
        inv_ref[s] = inv
        o_ref[s] = acc[...] * inv
        return carry

    lax.fori_loop(0, q_ref.shape[0], sequence, 0)


def attend(q, kv, q_seg, k_seg):
    shape = jax.ShapeDtypeStruct
    seqs, rows, _ = q.shape
    return pl.pallas_call(
        attend_kernel,
        name="attend",
        out_shape=(shape(q.shape, F32), shape((seqs, rows, 1), F32)),
        in_specs=[VMEM] * 4,
        out_specs=(VMEM,) * 2,
        scratch_shapes=[pltpu.VMEM((rows, HEAD_DIM), F32), pltpu.VMEM((rows, 1), F32)],
        compiler_params=local_params(),
        cost_estimate=pl.CostEstimate(
            flops=4 * seqs * rows * 1024 * HEAD_DIM, bytes_accessed=8 * 2**20,
            transcendentals=seqs * rows * 1024),
    )(q, kv, q_seg, k_seg)


def attend_back_kernel(q_ref, kv_ref, qseg_ref, kseg_ref, inv_ref, o_ref, do_ref,
                       dq_ref, dkv_ref, acc):
    _, _, _, z, _ = here()
    span = kv_ref.shape[2]
    first = (((0,), (0,)), ((), ()))
    last = (((1,), (1,)), ((), ()))

    def sequence(s, carry):
        q = q_ref[s]
        q_seg = qseg_ref[s]
        inv = inv_ref[s]
        do = do_ref[s]
        delta = jnp.sum(do.astype(F32) * o_ref[s], axis=1, keepdims=True)
        acc[...] = jnp.zeros_like(acc)

        def block(at, diagonal):
            kv = kv_ref[at, s]
            key = kv[:, :HEAD_DIM]
            p = scores_of(q, key, q_seg, kseg_ref[at, s], diagonal, span) * inv
            dp = lax.dot_general(do, kv[:, HEAD_DIM:], last, preferred_element_type=F32)
            ds = (p * (dp - delta)).astype(BF16)
            acc[...] += jnp.dot(ds, key, preferred_element_type=F32)
            dk = lax.dot_general(ds, q, first, preferred_element_type=F32)
            dv = lax.dot_general(p.astype(BF16), do, first, preferred_element_type=F32)
            dkv_ref[at, s] = jnp.concatenate([dk, dv], axis=1).astype(BF16)

        def step(at, inner):
            block(at, False)
            return inner

        lax.fori_loop(0, z, step, 0)
        block(z, True)
        dq_ref[s] = acc[...] * HEAD_DIM ** (-0.5)
        return carry

    lax.fori_loop(0, q_ref.shape[0], sequence, 0)


def attend_back(q, kv, q_seg, k_seg, inv, o, do):
    shape = jax.ShapeDtypeStruct
    seqs, rows, _ = q.shape
    return pl.pallas_call(
        attend_back_kernel,
        name="attend_back",
        out_shape=(shape(q.shape, F32), shape(kv.shape, BF16)),
        in_specs=[VMEM] * 7,
        out_specs=(VMEM,) * 2,
        scratch_shapes=[pltpu.VMEM((rows, HEAD_DIM), F32)],
        compiler_params=local_params(),
        cost_estimate=pl.CostEstimate(
            flops=10 * seqs * rows * 1024 * HEAD_DIM, bytes_accessed=12 * 2**20,
            transcendentals=seqs * rows * 1024),
    )(q, kv, q_seg, k_seg, inv, o, do)


def down_kernel(zs, dkv, total, got, sk, rk):
    base, y, c, z, x = here()
    others = [device(base, y, c, (z + k) % zs, x) for k in range(1, zs)]
    greet(others)
    for k in range(1, zs):
        @pl.when(z - k >= 0)
        def _():
            at = (z + zs - k) % zs
            remote(dkv.at[at], got.at[k - 1], sk.at[k - 1], rk.at[k - 1],
                   device(base, y, c, at, x)).start()
    total[...] = dkv[z].astype(F32)
    for k in range(1, zs):
        @pl.when(z + k < zs)
        def _():
            remote(dkv.at[0], got.at[k - 1], sk.at[k - 1], rk.at[k - 1], others[0]).wait_recv()
            total[...] += got[k - 1].astype(F32)
    for k in range(1, zs):
        @pl.when(z - k >= 0)
        def _():
            at = (z + zs - k) % zs
            remote(dkv.at[at], got.at[k - 1], sk.at[k - 1], rk.at[k - 1], others[0]).wait_send()


def send_down(zs, dkv):
    n = zs - 1
    return pl.pallas_call(
        functools.partial(down_kernel, zs),
        name="send_down",
        out_shape=jax.ShapeDtypeStruct(dkv.shape[1:], F32),
        in_specs=[VMEM],
        out_specs=VMEM,
        scratch_shapes=[pltpu.VMEM((n,) + dkv.shape[1:], BF16), dma(n), dma(n)],
        compiler_params=params(2),
    )(dkv)


def inverse_rms(v):
    return lax.rsqrt(jnp.mean(v * v, axis=-1, keepdims=True) + EPS)


def norm_back(dy, v, inv, gain):
    scaled = dy * gain
    gain_grad = jnp.sum(dy * v * inv, axis=0, keepdims=True)
    inner = jnp.mean(scaled * v, axis=-1, keepdims=True)
    return inv * scaled - v * inv * inv * inv * inner, gain_grad


def mid_kernel(part, tok, gain, mid_o, all_o, *rest):
    scratch, (low, sg, rg, keep) = rest[:9], rest[9:]
    greet(neighbours())
    summed = Summed(part, scratch)
    summed.start()
    summed.middle()
    summed.finish()
    mid = tok[...].astype(F32) + summed.out[...]
    mid_o[...] = mid
    low[...] = (mid * inverse_rms(mid) * gain[...]).astype(BF16)
    gather = Gather(low, all_o, sg, rg, keep.at[0])
    gather.start()
    gather.forward()
    gather.finish()


def mid_call(part, tok, gain):
    shape = jax.ShapeDtypeStruct
    return pl.pallas_call(
        mid_kernel,
        name="sum_mid",
        out_shape=(shape(tok.shape, F32), shape((8,) + tok.shape, BF16)),
        in_specs=[VMEM] * 3,
        out_specs=(VMEM, ANY),
        scratch_shapes=sum_scratch(tok.shape[1])
        + [pltpu.VMEM(tok.shape, BF16), dma(8), dma(8), dma(1)],
        compiler_params=params(3),
    )(part, tok, gain)


def dmid_kernel(part, part_mixed, mid, cot, gain, dmid_o, gain_o, mixed_o, all_o, *rest):
    sa, sb, (low, sg, rg, keep) = rest[:9], rest[9:18], rest[18:]
    greet(neighbours())
    first = Summed(part, sa)
    second = Summed(part_mixed, sb)
    first.start()
    first.middle()
    second.start()
    first.finish()
    v = mid[...]
    dv, gain_grad = norm_back(first.out[...], v, inverse_rms(v), gain[...])
    gain_o[...] = gain_grad
    dmid = cot[...].astype(F32) + dv
    dmid_o[...] = dmid
    low[...] = dmid.astype(BF16)
    gather = Gather(low, all_o, sg, rg, keep.at[0])
    gather.start()
    second.middle()
    gather.forward()
    gather.finish()
    second.finish()
    mixed_o[...] = (v + second.out[...]).astype(BF16)


def dmid_call(part, part_mixed, mid, cot, gain):
    shape = jax.ShapeDtypeStruct
    width = mid.shape[1]
    return pl.pallas_call(
        dmid_kernel,
        name="sum_dmid",
        out_shape=(shape(mid.shape, F32), shape((1, width), F32), shape(mid.shape, BF16),
                   shape((8,) + mid.shape, BF16)),
        in_specs=[VMEM] * 5,
        out_specs=(VMEM, VMEM, VMEM, ANY),
        scratch_shapes=sum_scratch(width) + sum_scratch(width)
        + [pltpu.VMEM(mid.shape, BF16), dma(8), dma(8), dma(1)],
        compiler_params=params(4),
    )(part, part_mixed, mid, cot, gain)


def input_kernel(part, tok, dmid, gain, out_o, gain_o, *scratch):
    greet(neighbours())
    summed = Summed(part, scratch)
    summed.start()
    summed.middle()
    summed.finish()
    v = tok[...].astype(F32)
    dv, gain_grad = norm_back(summed.out[...], v, inverse_rms(v), gain[...])
    gain_o[...] = gain_grad
    out_o[...] = dmid[...] + dv


def input_call(part, tok, dmid, gain):
    shape = jax.ShapeDtypeStruct
    return pl.pallas_call(
        input_kernel,
        name="sum_input",
        out_shape=(shape(dmid.shape, F32), shape((1, dmid.shape[1]), F32)),
        in_specs=[VMEM] * 4,
        out_specs=(VMEM, VMEM),
        scratch_shapes=sum_scratch(dmid.shape[1]),
        compiler_params=params(5),
    )(part, tok, dmid, gain)


def z_turn(array, k, zs):
    pairs = [(2 * z + x, 2 * ((z + k) % zs) + x) for z in range(zs) for x in range(2)]
    return lax.ppermute(array, "grp", pairs)


def x_swap(array, zs):
    pairs = [(2 * z + x, 2 * z + 1 - x) for z in range(zs) for x in range(2)]
    return lax.ppermute(array, "grp", pairs)


def r_swap(array, k):
    reps = lax.axis_size("rep")
    return lax.ppermute(array, "rep", [(i, i ^ k) for i in range(reps)])


def pick(stack, at):
    return lax.dynamic_index_in_dim(stack, at, 0, keepdims=False)


def z_gather(own, z, zs):
    turned = jnp.stack([own] + [z_turn(own, k, zs) for k in range(1, zs)])
    return turned[(z - jnp.arange(zs)) % zs]


def z_sum(blocks, z, zs):
    total = pick(blocks, z).astype(F32)
    for k in range(1, zs):
        total = total + z_turn(pick(blocks, (z + k) % zs), k, zs).astype(F32)
    return total.astype(BF16)


def over_quads(array):
    reps = lax.axis_size("rep")
    if reps == 4:
        return array
    rows = [[j + 4 * q for q in range(reps // 4)] for j in range(4)]
    return lax.psum(array, "rep", axis_index_groups=rows)


def r_gather(own, r):
    core = r_swap(own, 1)
    other = r_swap(own, 2)
    both = r_swap(other, 1)
    turned = jnp.stack([own, core, other, both])
    return turned[r ^ jnp.arange(4)]


def scatter_rows(grad, z, x, r, zs):
    rows = grad.shape[0] // (2 * zs)
    cols = grad.shape[1]
    mine = over_quads(z_sum(grad.reshape(zs, 2, rows, cols), z, zs))
    keep, give = pick(mine, x), pick(mine, 1 - x)
    got = x_swap(give, zs)
    pair = jnp.where(x == 0, jnp.stack([keep, got], 1), jnp.stack([got, keep], 1))
    whole = r_gather(pair, r)
    return whole.transpose(1, 0, 2, 3).reshape(rows, 8, cols).astype(F32)


def scatter_head(grad, z, r, zs):
    rows, cols = grad.shape
    quarter = grad.reshape(4, rows // 4, cols)
    got = [pick(quarter, r)] + [r_swap(pick(quarter, r ^ k), k) for k in range(1, 4)]
    heads = jnp.stack(got)[r ^ jnp.arange(4)]
    mine = over_quads(z_sum(heads, z, zs))
    return r_gather(mine, r).reshape(rows, cols).astype(F32)


def rope_tables(positions):
    half = HEAD_DIM // 2
    freq = jnp.exp(-jnp.log(THETA) * jnp.arange(half, dtype=F32) * 2.0 / HEAD_DIM)
    angle = positions.astype(F32)[:, None] * freq[None, :]
    return jnp.cos(angle), jnp.sin(angle)


def rotate(values, cosine, sine):
    half = HEAD_DIM // 2
    first, second = values[..., :half], values[..., half:]
    return jnp.concatenate(
        [first * cosine - second * sine, second * cosine + first * sine], axis=-1
    )


def head_norm_back(dy, v, inv, gain):
    scaled = dy * gain
    gain_grad = jnp.sum((dy * v * inv).reshape(-1, HEAD_DIM), axis=0)
    inner = jnp.mean(scaled * v, axis=-1, keepdims=True)
    return inv * scaled - v * inv * inv * inv * inner, gain_grad


def dot_last(left, right):
    return lax.dot_general(left, right, (((1,), (1,)), ((), ())), preferred_element_type=F32)


def dot_first(left, right):
    return lax.dot_general(left, right, (((0,), (0,)), ((), ())), preferred_element_type=F32)


def dot(left, right):
    return jnp.dot(left, right, preferred_element_type=F32)


def local(tokens, attn_gain, w_qkv, q_gain, k_gain, w_out, ffn_gain, w_gate_up, w_down,
          cotangent, segment_ids):
    rows, width = tokens.shape
    zs = lax.axis_size("grp") // 2
    _, y, c, z, x = here()
    r = 2 * y + c
    q_width, kv_width = HEADS * HEAD_DIM, KV_HEADS * HEAD_DIM
    ff = w_gate_up.shape[1] // 2
    part = ff // 8
    own_rows = w_qkv.shape[0]
    span = 2 * rows
    cut = lax.dynamic_slice_in_dim

    q_pair = cut(w_qkv, 2 * Q_COLS * r, 2 * Q_COLS, 1)
    k_pair = cut(w_qkv, q_width + 2 * HEAD_DIM * r, 2 * HEAD_DIM, 1)
    v_pair = cut(w_qkv, q_width + kv_width + 2 * HEAD_DIM * r, 2 * HEAD_DIM, 1)
    wq = jnp.stack([
        jnp.concatenate([
            q_pair[:, i * Q_COLS:(i + 1) * Q_COLS],
            k_pair[:, i * HEAD_DIM:(i + 1) * HEAD_DIM],
            v_pair[:, i * HEAD_DIM:(i + 1) * HEAD_DIM]], 1)
        for i in range(2)])
    gains = jnp.zeros((16, 256), BF16)
    gains = gains.at[0, :own_rows].set(attn_gain).at[1, :own_rows].set(ffn_gain)
    seg = jnp.broadcast_to(segment_ids[None, :], (16, rows))

    tok_all, cot_all, seg_all, wq_all, gains_all = first_gather(
        zs, tokens, cotangent, seg, wq, gains)
    w_qkv_t = wq_all.reshape(width, HEAD_COLS)
    gain_one = gains_all[:, 0, :own_rows].reshape(1, width).astype(F32)
    gain_two = gains_all[:, 1, :own_rows].reshape(1, width).astype(F32)

    quarter = jnp.concatenate([
        cut(w_down, r * (part // 4), part // 4, 0), cut(w_out, r * (own_rows // 4), own_rows // 4, 0)], 0)
    heads = z_gather(quarter, z, zs)
    got = [pick(heads, r)] + [r_swap(pick(heads, r ^ k), k) for k in range(1, 4)]
    whole = jnp.stack(got)[r ^ jnp.arange(4)]
    w_down_t = whole[:, :part // 4].reshape(part, width)
    w_out_t = whole[:, part // 4:].reshape(own_rows, width)
    pair = cut(w_gate_up.reshape(own_rows, 2, ff), 2 * part * r, 2 * part, 2)
    pair = jnp.stack([pair[:, :, :part], pair[:, :, part:]]).reshape(2, own_rows, 2 * part)
    keep, give = pick(pair, x), pick(pair, 1 - x)
    got = x_swap(give, zs)
    unit = jnp.where(x == 0, jnp.stack([keep, got]), jnp.stack([got, keep]))
    w_gu_t = z_gather(unit, z, zs).reshape(width, 2 * part)

    xs = tok_all.reshape(8 * rows, width).astype(F32)
    normed = (xs * inverse_rms(xs) * gain_one).astype(BF16)
    qkv = dot(normed, w_qkv_t)
    q_raw = qkv[:, :Q_COLS].reshape(4, span, GROUP, HEAD_DIM).transpose(0, 2, 1, 3)
    k_raw = qkv[:, Q_COLS:Q_COLS + HEAD_DIM].reshape(4, span, HEAD_DIM)
    values = qkv[:, Q_COLS + HEAD_DIM:].astype(BF16)
    q_scale, k_scale = q_gain.astype(F32), k_gain.astype(F32)
    q_inv, k_inv = inverse_rms(q_raw), inverse_rms(k_raw)
    cosine, sine = rope_tables(span * z + jnp.arange(span, dtype=jnp.int32))
    queries = rotate(q_raw * q_inv * q_scale, cosine, sine) * HEAD_DIM ** (-0.5)
    queries = queries.astype(BF16).reshape(4, GROUP * span, HEAD_DIM)
    keys = rotate(k_raw * k_inv * k_scale, cosine, sine).astype(BF16)
    kv = jnp.concatenate([keys.reshape(4 * span, HEAD_DIM), values], 1)
    kv_all, segs = send_up(zs, kv, seg_all[:, 0].reshape(8, rows))
    kv_all = kv_all.reshape(zs, 4, span, 2 * HEAD_DIM)
    k_seg = segs.reshape(zs, 4, 1, span)
    q_seg = jnp.tile(seg_all[:, 0].reshape(4, span), (1, GROUP))[:, :, None]
    attended_full, inv_total = attend(queries, kv_all, q_seg, k_seg)
    attended = (
        attended_full.reshape(4, GROUP, span, HEAD_DIM).transpose(0, 2, 1, 3)
        .reshape(8 * rows, Q_COLS).astype(BF16))
    out_part = dot(attended, w_out_t).astype(BF16).reshape(8, rows, width)
    mid, normed_two = mid_call(out_part, tokens, gain_two)

    n2 = normed_two.reshape(8 * rows, width)
    cot = cot_all.reshape(8 * rows, width)
    gate_up = dot(n2, w_gu_t)
    gate, up = gate_up[:, :part], gate_up[:, part:]
    sigma = jax.nn.sigmoid(gate)
    active = gate * sigma
    hidden = (active * up).astype(BF16)
    mixed_part = dot(hidden, w_down_t).astype(BF16).reshape(8, rows, width)
    dh = dot_last(cot, w_down_t)
    dgu = jnp.concatenate(
        [dh * up * sigma * (1.0 + gate * (1.0 - sigma)), dh * active], axis=1).astype(BF16)
    dn2_part = dot_last(dgu, w_gu_t).astype(BF16).reshape(8, rows, width)
    down_grad = scatter_head(dot_first(hidden, cot).astype(BF16), z, r, zs)
    gu_grad = scatter_rows(dot_first(n2, dgu).astype(BF16), z, x, r, zs)
    gu_grad = gu_grad.reshape(own_rows, 8, 2, part).transpose(0, 2, 1, 3).reshape(own_rows, 2 * ff)

    dmid, gain_two_grad, mixed, dbranch = dmid_call(dn2_part, mixed_part, mid, cotangent, gain_two)
    dbranch = dbranch.reshape(8 * rows, width)
    dattended = dot_last(dbranch, w_out_t).astype(BF16)
    dattended = (
        dattended.reshape(4, span, GROUP, HEAD_DIM).transpose(0, 2, 1, 3)
        .reshape(4, GROUP * span, HEAD_DIM))
    out_grad = scatter_head(dot_first(attended, dbranch).astype(BF16), z, r, zs)
    dq, dkv = attend_back(queries, kv_all, q_seg, k_seg, inv_total, attended_full, dattended)
    dkv = send_down(zs, dkv.reshape(zs, 4 * span, 2 * HEAD_DIM))
    dq = rotate(dq.reshape(4, GROUP, span, HEAD_DIM), cosine, -sine)
    dk = rotate(dkv[:, :HEAD_DIM].reshape(4, span, HEAD_DIM), cosine, -sine)
    dq_raw, q_gain_part = head_norm_back(dq, q_raw, q_inv, q_scale)
    dk_raw, k_gain_part = head_norm_back(dk, k_raw, k_inv, k_scale)
    dqkv = jnp.concatenate([
        dq_raw.transpose(0, 2, 1, 3).reshape(8 * rows, Q_COLS),
        dk_raw.reshape(8 * rows, HEAD_DIM), dkv[:, HEAD_DIM:]], 1).astype(BF16)
    in_part = dot_last(dqkv, w_qkv_t).astype(BF16).reshape(8, rows, width)
    qkv_grad = scatter_rows(dot_first(normed, dqkv).astype(BF16), z, x, r, zs)
    qkv_grad = jnp.concatenate([
        qkv_grad[:, :, :Q_COLS].reshape(own_rows, q_width),
        qkv_grad[:, :, Q_COLS:Q_COLS + HEAD_DIM].reshape(own_rows, kv_width),
        qkv_grad[:, :, Q_COLS + HEAD_DIM:].reshape(own_rows, kv_width)], 1)
    input_grad, gain_one_grad = input_call(in_part, tokens, dmid, gain_one)

    head_gains = jnp.concatenate([q_gain_part, k_gain_part])
    pad = jnp.zeros((1, width), F32).at[0, :2 * HEAD_DIM].set(head_gains)
    gains_sum = lax.psum(jnp.concatenate([gain_one_grad, gain_two_grad, pad], 0), ("rep", "grp"))
    place = 2 * z + x
    gain_one_out = cut(gains_sum[0], place * own_rows, own_rows, 0)
    gain_two_out = cut(gains_sum[1], place * own_rows, own_rows, 0)
    return (mixed, input_grad, gain_one_out, qkv_grad, gains_sum[2, :HEAD_DIM],
            gains_sum[2, HEAD_DIM:2 * HEAD_DIM], out_grad, gain_two_out, gu_grad, down_grad)


def solution(mesh):
    rows, split = P(("rep", "grp"), None), P("grp", None)
    return jax.shard_map(
        local,
        mesh=mesh,
        in_specs=(rows, P("grp"), split, P(), P(), split, P("grp"), split, split, rows,
                  P(("rep", "grp"))),
        out_specs=(rows, rows, P("grp"), split, P(), P(), split, P("grp"), split, split),
        check_vma=False,
    )
```

```python
import functools

import jax
import jax.numpy as jnp
from jax import lax
from jax.experimental import pallas as pl
from jax.experimental.pallas import tpu as pltpu
from jax.sharding import PartitionSpec as P

HEADS = 24
KV_HEADS = 8
HEAD_DIM = 64
GROUP = HEADS // KV_HEADS
Q_COLS = GROUP * HEAD_DIM
HEAD_COLS = Q_COLS + 2 * HEAD_DIM

EPS = 1e-05
THETA = 1000000.0
MESH = pl.DeviceIdType.MESH
F32 = jnp.float32
BF16 = jnp.bfloat16

VMEM = pl.BlockSpec(memory_space=pltpu.VMEM)
ANY = pl.BlockSpec(memory_space=pl.ANY)


def here():
    rep = lax.axis_index("rep")
    grp = lax.axis_index("grp")
    r = rep % 4
    return rep - r, r // 2, r % 2, grp // 2, grp % 2


def device(base, y, c, z, x):
    return {"rep": base + 2 * y + c, "grp": 2 * z + x}


def remote(src, dst, send, recv, to):
    return pltpu.make_async_remote_copy(
        src_ref=src, dst_ref=dst, send_sem=send, recv_sem=recv, device_id=to, device_id_type=MESH
    )


def greet(targets):
    barrier = pltpu.get_barrier_semaphore()
    for to in targets:
        pl.semaphore_signal(barrier, inc=1, device_id=to, device_id_type=MESH)
    pl.semaphore_wait(barrier, len(targets))


def neighbours():
    base, y, c, z, x = here()
    to_c = device(base, y, 1 - c, z, x)
    to_x = device(base, y, c, z, 1 - x)
    to_y = device(base, 1 - y, c, z, x)
    return to_c, to_x, to_y


GATHER_SEMS = 8


class Gather:
    def __init__(self, src, out, send, recv, local):
        self.src, self.out, self.send, self.recv, self.local = src, out, send, recv, local
        _, y, c, _, x = here()
        self.to_c, self.to_x, self.to_y = neighbours()
        slot = lambda a, b, d: 4 * a + 2 * b + d
        self.own = slot(y, c, x)
        self.at_c, self.at_x, self.at_y = slot(y, 1 - c, x), slot(y, c, 1 - x), slot(1 - y, c, x)
        self.at_xc, self.at_yc = slot(y, 1 - c, 1 - x), slot(1 - y, 1 - c, x)
        self.at_xy, self.at_xyc = slot(1 - y, c, 1 - x), slot(1 - y, 1 - c, 1 - x)
        self.half = src.shape[0] // 2

    def part(self, ref, k):
        return ref.at[pl.ds(k * self.half, self.half)]

    def copy(self, k, src, dst, to):
        return remote(src, dst, self.send.at[k], self.recv.at[k], to)

    def start(self):
        out, src = self.out, self.src
        self.keep = pltpu.make_async_copy(src, out.at[self.own], self.local)
        self.keep.start()
        self.sent = [
            self.copy(0, src, out.at[self.own], self.to_x),
            self.copy(1, src, out.at[self.own], self.to_y),
            self.copy(2, src, out.at[self.own], self.to_c),
        ]
        for copy in self.sent:
            copy.start()

    def forward(self):
        out = self.out
        self.copy(0, self.src, out.at[self.at_x], self.to_x).wait_recv()
        first = self.part(out.at[self.at_x], 0)
        self.go(3, first, first, self.to_y)
        self.go(4, out.at[self.at_x], out.at[self.at_x], self.to_c)
        self.copy(1, self.src, out.at[self.at_y], self.to_y).wait_recv()
        second = self.part(out.at[self.at_y], 1)
        self.go(5, second, second, self.to_x)
        self.go(6, out.at[self.at_y], out.at[self.at_y], self.to_c)

    def go(self, k, src, dst, to):
        copy = self.copy(k, src, dst, to)
        copy.start()
        self.sent.append(copy)

    def finish(self):
        out = self.out
        first = self.part(out.at[self.at_xy], 0)
        second = self.part(out.at[self.at_xy], 1)
        self.copy(3, first, first, self.to_y).wait_recv()
        self.copy(5, second, second, self.to_x).wait_recv()
        self.go(7, out.at[self.at_xy], out.at[self.at_xy], self.to_c)
        for k, at in ((2, self.at_c), (4, self.at_xc), (6, self.at_yc), (7, self.at_xyc)):
            self.copy(k, out.at[at], out.at[at], self.to_c).wait_recv()
        for copy in self.sent:
            copy.wait_send()
        self.keep.wait()


def dma(n):
    return pltpu.SemaphoreType.DMA((n,))


def params(cid, limit=60):
    return pltpu.CompilerParams(
        collective_id=cid, has_side_effects=True, vmem_limit_bytes=limit * 2**20
    )


def inverse_rms(v):
    return lax.rsqrt(jnp.mean(v * v, axis=-1, keepdims=True) + EPS)


def norm_back(dy, v, inv, gain):
    scaled = dy * gain
    gain_grad = jnp.sum(dy * v * inv, axis=0, keepdims=True)
    inner = jnp.mean(scaled * v, axis=-1, keepdims=True)
    return inv * scaled - v * inv * inv * inv * inner, gain_grad


def when(cond):
    return pl.when(cond)


def lanes(shape):
    return lax.broadcasted_iota(jnp.int32, shape, len(shape) - 1)


def roll(v, by):
    return pltpu.roll(v, by % v.shape[-1], v.ndim - 1)


class Along:
    def __init__(self, src, slot, send, recv, flip=False, mate=None):
        self.src, self.slot, self.send, self.recv = src, slot, send, recv
        self.base, self.y, self.c, self.z, self.x = here()
        self.to = (1 - self.x) if flip else self.x
        self.got = mate if flip else slot
        self.flip = flip

    def at(self, zk, x):
        return device(self.base, self.y, self.c, zk, x)

    def copy(self, d):
        zk = (self.z + d + 4) % 4
        return remote(self.src, self.slot(self.z), self.send.at[d + 2], self.recv.at[self.z],
                      self.at(zk, self.to))

    def fits(self, d):
        return (self.z + d >= 0) & (self.z + d < 4)

    def start(self):
        if self.flip:
            self.copy(0).start()
        for d in (2, -2, 1, -1):
            pl.when(self.fits(d))(lambda d=d: self.copy(d).start())

    def arrival(self, zk):
        ref = self.got(zk)
        return remote(ref, ref, self.send.at[0], self.recv.at[zk], self.at(self.z, 1 - self.x))

    def passed(self, zk, to):
        ref = self.got(zk)
        return remote(ref, ref, self.send.at[5], self.recv.at[zk], self.at(to, self.x))

    def forward(self):
        @pl.when(self.z == 2)
        def _():
            self.arrival(0).wait_recv()
            self.passed(0, 3).start()

        @pl.when(self.z == 1)
        def _():
            self.arrival(3).wait_recv()
            self.passed(3, 0).start()

    def wait(self, zk):
        early = ((self.z == 2) & (zk == 0)) | ((self.z == 1) & (zk == 3))
        due = jnp.logical_not(early)
        if not self.flip:
            due = due & (self.z != zk)
        pl.when(due)(lambda: self.arrival(zk).wait_recv())

    def finish(self):
        for zk in range(4):
            self.wait(zk)

    def sent(self):
        if self.flip:
            self.copy(0).wait_send()
        for d in (2, -2, 1, -1):
            pl.when(self.fits(d))(lambda d=d: self.copy(d).wait_send())
        pl.when(self.z == 2)(lambda: self.passed(0, 3).wait_send())
        pl.when(self.z == 1)(lambda: self.passed(3, 0).wait_send())


def layer_mates():
    base, y, c, z, x = here()
    return [
        device(base, (y + k // 4) % 2, (c + k // 2) % 2, z, (x + k) % 2) for k in range(1, 8)
    ]


def z_mates():
    base, y, c, z, x = here()
    return [device(base, y, c, (z + k // 2) % 4, (x + k) % 2) for k in range(2, 8)]


def rotated(u, cos, sin):
    lane = lanes(u.shape)
    return u * cos + jnp.where(lane < 32, roll(u, -32), roll(u, 32)) * sin


def low_half(v):
    return jnp.where(lanes(v.shape) < HEAD_DIM, v, 0.0)


def high_half(v):
    return jnp.where(lanes(v.shape) >= HEAD_DIM, v, 0.0)


def split_heads(tile_a, tile_b):
    return [low_half(tile_a), low_half(roll(tile_a, 64)), low_half(tile_b),
            low_half(roll(tile_b, 64))]


def head_inverse(u):
    return lax.rsqrt(jnp.sum(u * u, axis=-1, keepdims=True) * (1.0 / HEAD_DIM) + EPS)


def exp_scores(q, kv, q_seg, k_seg, diagonal):
    s = lax.dot_general(q, kv, (((1,), (1,)), ((), ())), preferred_element_type=F32)
    allowed = q_seg == k_seg
    if diagonal:
        row = lax.broadcasted_iota(jnp.int32, allowed.shape, 0)
        col = lax.broadcasted_iota(jnp.int32, allowed.shape, 1)
        allowed = allowed & (col <= row)
    n = allowed.shape[0]
    return jnp.concatenate([
        jnp.where(allowed, jnp.exp(s[n * j:n * (j + 1)]), 0.0) for j in range(GROUP)], axis=0)


def segment_row(segs, zk, s):
    return jnp.concatenate([segs[zk, 2 * s, 0:1], segs[zk, 2 * s + 1, 0:1]], axis=1)


def segment_columns(segs, zk, s):
    parts = []
    for i in range(2):
        row = jnp.broadcast_to(segs[zk, 2 * s + i, 0:1], (128, 128))
        parts.append(jnp.transpose(row))
    col = jnp.concatenate(parts, axis=0)
    return jnp.concatenate([col, col], axis=1)


class SeqSum:
    def __init__(self, part, scratch):
        self.part = part
        (self.r1, self.chip, self.rx, self.ry, self.mine, self.late, self.out,
         self.send, self.recv) = scratch
        _, self.y, self.c, _, self.x = here()
        self.to_c, self.to_x, self.to_y = neighbours()

    def copy(self, k, src, dst, to):
        return remote(src, dst, self.send.at[k], self.recv.at[k], to)

    def swap(self, b, a):
        at = 2 * b + a
        return self.copy(at, self.part.at[4 * b + 2 * (1 - self.c) + a], self.r1.at[at], self.to_c)

    def give(self, b):
        for a in range(2):
            self.swap(b, a).start()

    def along_x(self, b):
        at = 2 * b + 1 - self.x
        return self.copy(4 + b, self.chip.at[at, pl.ds(0, 64)], self.rx.at[b], self.to_x)

    def along_y(self, a):
        at = 2 * (1 - self.y) + a
        return self.copy(6 + a, self.chip.at[at, pl.ds(64, 64)], self.ry.at[a], self.to_y)

    def last_y(self):
        return self.copy(8, self.mine.at[0], self.late.at[0], self.to_y)

    def last_x(self):
        return self.copy(9, self.mine.at[1], self.late.at[1], self.to_x)

    def total(self, b, a):
        self.swap(b, a).wait_recv()
        at = 2 * b + a
        return self.part[4 * b + 2 * self.c + a].astype(F32) + self.r1[at].astype(F32)

    def take_far(self):
        b = 1 - self.y
        for a in (1 - self.x, self.x):
            self.chip[2 * b + a] = self.total(b, a).astype(BF16)
            self.along_y(a).start()
            if a is not self.x:
                self.along_x(b).start()

    def take_near(self):
        b, x = self.y, self.x
        self.chip[2 * b + 1 - x] = self.total(b, 1 - x).astype(BF16)
        self.along_x(b).start()
        self.out[...] = self.total(b, x)

    def middle(self):
        x, y = self.x, self.y
        self.along_x(1 - y).wait_recv()
        self.mine[0] = (
            self.chip[2 * (1 - y) + x, 0:64].astype(F32) + self.rx[1 - y].astype(F32)
        ).astype(BF16)
        self.last_y().start()
        self.along_y(1 - x).wait_recv()
        self.mine[1] = (
            self.chip[2 * y + 1 - x, 64:128].astype(F32) + self.ry[1 - x].astype(F32)
        ).astype(BF16)
        self.last_x().start()

    def finish(self):
        x, y = self.x, self.y
        self.along_x(y).wait_recv()
        self.along_y(x).wait_recv()
        self.last_y().wait_recv()
        self.last_x().wait_recv()
        self.out[0:64] += self.rx[y].astype(F32) + self.late[0].astype(F32)
        self.out[64:128] += self.ry[x].astype(F32) + self.late[1].astype(F32)

    def sent(self):
        for b in range(2):
            for a in range(2):
                self.swap(b, a).wait_send()
            self.along_x(b).wait_send()
            self.along_y(b).wait_send()
        self.last_y().wait_send()
        self.last_x().wait_send()


def seq_scratch(width):
    return [
        pltpu.VMEM((4, 128, width), BF16),
        pltpu.VMEM((4, 128, width), BF16),
        pltpu.VMEM((2, 64, width), BF16),
        pltpu.VMEM((2, 64, width), BF16),
        pltpu.VMEM((2, 64, width), BF16),
        pltpu.VMEM((2, 64, width), BF16),
        pltpu.VMEM((128, width), F32),
        dma(10),
        dma(10),
    ]


FWD_IN = ("tok", "cot", "seg", "wq", "gains", "wgu", "wd", "wo", "qg", "kg", "cos", "sin")
FWD_OUT = ("normed", "cot_all", "n2_all", "wq_all", "wo_all", "wd_all", "wgu_all", "qkv", "q",
           "kv", "segs", "o", "att", "mid", "g_one", "g_two",
           "gains_all")


def forward_kernel(names, *refs):
    m = dict(zip(names, refs))
    base, y, c, z, x = here()
    r = 2 * y + c
    to_c, to_x, to_y = neighbours()
    greet(layer_mates() + z_mates())
    rows, width = m["tok"].shape
    quarter_d, quarter_o = m["wd"].shape[0] // 4, m["wo"].shape[0] // 4
    own_rows = m["wq"].shape[1]
    half_cols = m["wgu"].shape[1] // 2
    piece = m["raw"].shape[2]
    part = piece // 2
    keep = m["keep"]
    own = 2 * z + x
    t_own = 2 * r + x

    def local_copy(k, src, dst):
        return pltpu.make_async_copy(src, dst, keep.at[k])

    tok = Gather(m["tok"], m["tok_all"], m["ga_s"], m["ga_r"], keep.at[0])
    cot = Gather(m["cot"], m["cot_all"], m["gb_s"], m["gb_r"], keep.at[1])
    tok.start()
    segs = m["segs_v"]
    mates = layer_mates()

    def seg_copy(k):
        return remote(m["seg"], segs.at[z, t_own], m["sg_s"].at[k - 1], m["sg_r"].at[k - 1],
                      mates[k - 1])

    def gain_target(k):
        return device(base, y, c, (z + k // 2) % 4, (x + k) % 2)

    def gain_copy(k):
        return remote(m["gains"], m["gains_all"].at[own], m["gn_s"].at[k - 1],
                      m["gn_r"].at[k - 1], gain_target(k))

    for k in range(1, 8):
        seg_copy(k).start()
    wq = m["wq_v"]

    def wq_slot(zk, a):
        return wq.at[pl.ds((2 * zk + a) * own_rows, own_rows)]

    near = Along(m["wq"].at[x], lambda zk: wq_slot(zk, x), m["wa_s"], m["wa_r"])
    flip = Along(m["wq"].at[1 - x], lambda zk: wq_slot(zk, x), m["wb_s"], m["wb_r"],
                 flip=True, mate=lambda zk: wq_slot(zk, 1 - x))
    near.start()
    flip.start()
    for k in range(1, 8):
        gain_copy(k).start()
    local = [
        local_copy(2, m["wq"].at[x], wq_slot(z, x)),
        local_copy(3, m["gains"], m["gains_all"].at[own]),
        local_copy(4, m["seg"], segs.at[z, t_own]),
        local_copy(5, m["wgu"].at[:, pl.ds(piece * r, piece)], m["raw"].at[0]),
        local_copy(6, m["wgu"].at[:, pl.ds(half_cols + piece * r, piece)], m["raw"].at[1]),
    ]
    for copy in local:
        copy.start()
    out_q = Along(m["wo"].at[pl.ds(quarter_o * r, quarter_o)], lambda zk: m["zo"].at[zk],
                  m["wo_s"], m["wo_r"])
    down_q = Along(m["wd"].at[pl.ds(quarter_d * r, quarter_d)], lambda zk: m["zd"].at[zk],
                   m["wd_s"], m["wd_r"])
    out_q.start()
    quarters = [
        local_copy(7, m["wo"].at[pl.ds(quarter_o * r, quarter_o)], m["zo"].at[z]),
        local_copy(8, m["wd"].at[pl.ds(quarter_d * r, quarter_d)], m["zd"].at[z]),
    ]
    for copy in quarters:
        copy.start()

    local[3].wait()
    local[4].wait()
    gate, up = m["raw"].at[0], m["raw"].at[1]
    pair = m["pair"]
    main = (part // 128) * 128
    for a in range(2):
        at = a * (piece - main)
        pair[a, :, 0:main] = gate[:, at:at + main]
        pair[a, :, main:2 * main] = up[:, at:at + main]
    g_tile = gate[:, main:main + 128].astype(F32)
    u_tile = up[:, main:main + 128].astype(F32)
    low = lanes(g_tile.shape) < HEAD_DIM
    pair[0, :, 2 * main:] = jnp.where(low, g_tile, roll(u_tile, 64)).astype(BF16)
    pair[1, :, 2 * main:] = jnp.where(low, roll(g_tile, 64), u_tile).astype(BF16)
    wgu = m["wgu_all"]

    def gu_rows(zk, a):
        return wgu.at[pl.ds((2 * zk + a) * own_rows, own_rows)]

    def gu_unit(zk):
        return wgu.at[pl.ds(2 * zk * own_rows, 2 * own_rows)]

    cross = remote(pair.at[1 - x], gu_rows(z, x), m["xc_s"], m["xc_r"], to_x)
    cross_in = remote(pair.at[x], gu_rows(z, 1 - x), m["xc_s"], m["xc_r"], to_x)
    cross.start()
    mine = local_copy(5, pair.at[x], gu_rows(z, x))
    mine.start()

    tok.forward()
    near.forward()
    flip.forward()
    tok.finish()
    cot.start()
    near.finish()
    flip.finish()
    down_q.start()
    out_q.forward()
    for k in range(1, 8):
        at = 2 * ((z + 4 - k // 2) % 4) + (x + k) % 2
        remote(m["gains"], m["gains_all"].at[at], m["gn_s"].at[k - 1], m["gn_r"].at[k - 1],
               to_c).wait_recv()
        seg_copy(k).wait_recv()
    for k in (0, 1, 2):
        local[k].wait()
    gather_gains = pltpu.make_async_copy(m["gains_all"], m["gains_v"], keep.at[3])
    gather_gains.start()
    gather_gains.wait()
    gain_rows = []
    for i in range(2):
        gain_rows.append(jnp.concatenate(
            [m["gains_v"][k, 0:16].astype(F32)[i:i + 1, :own_rows] for k in range(8)], axis=1))
    m["g_one"][...], m["g_two"][...] = gain_rows
    kv = m["kv_v"]
    q_all, qkv_all = m["q_v"], m["qkv_v"]
    qg, kg, cos, sin = m["qg"][...], m["kg"][...], m["cos"][...], m["sin"][...]
    span = 2 * rows

    def order(k):
        return (y + 1 + k) % 2, (c + 1 + k // 2) % 2

    def kv_copy(d, s):
        return remote(kv.at[z, s], kv.at[z, s], m["kv_s"].at[d - 1, s], m["kv_r"].at[z, s],
                      device(base, y, c, (z + d) % 4, x))

    def kv_pass(s):
        return remote(kv.at[0, s], kv.at[0, s], m["kv_s"].at[2, s], m["kv_r"].at[0, s],
                      device(base, y, c, 3, x))

    def kv_arrival(zk, s):
        return remote(kv.at[zk, s], kv.at[zk, s], m["kv_s"].at[0, s], m["kv_r"].at[zk, s], to_x)

    def seg_up(k):
        return remote(segs.at[z], segs.at[z], m["su_s"].at[k - 1], m["su_r"].at[z],
                      device(base, y, c, (z + k) % 4, x))

    for k in range(1, 4):
        pl.when(z + k < 4)(lambda k=k: seg_up(k).start())

    def project(k, carry):
        b, e = order(k)
        s = 2 * b + e
        tokens = m["tok_all"][pl.ds(2 * s, 2)].reshape(span, width).astype(F32)
        normed = (tokens * inverse_rms(tokens) * m["g_one"][...]).astype(BF16)
        m["tok_all"][pl.ds(2 * s, 2)] = normed.reshape(2, rows, width)
        qkv = jnp.dot(normed, wq[...], preferred_element_type=F32)
        qkv_all[s] = qkv
        heads = split_heads(qkv[:, 0:128], qkv[:, 128:256])
        for j in range(GROUP):
            u = heads[j]
            u = rotated(u * head_inverse(u) * qg[0:1], cos, sin) * HEAD_DIM ** (-0.5)
            q_all[s, pl.ds(j * span, span)] = u.astype(BF16)
        u = heads[GROUP]
        u = rotated(u * head_inverse(u) * kg[0:1], cos, sin)
        v = jnp.concatenate([jnp.zeros((span, HEAD_DIM), F32), qkv[:, 256:320]], axis=1)
        kv[z, s] = (u + v).astype(BF16)
        for d in (2, 1):
            pl.when(z + d < 4)(lambda d=d: kv_copy(d, s).start())
        return carry

    lax.fori_loop(0, 4, project, 0)
    exports = [local_copy(9, m["tok_all"], m["normed"]), local_copy(10, wq, m["wq_all"]),
               local_copy(11, qkv_all, m["qkv"]), local_copy(12, q_all, m["q"])]
    for copy in exports:
        copy.start()

    mine.wait()
    cross_in.wait_recv()
    gu = Along(gu_unit(z), gu_unit, m["wg_s"], m["wg_r"])
    gu.start()
    cot.forward()

    def hand(k, zk, src, dst, sems, n):
        ss, rs = sems
        to = device(base, zk // 2, zk % 2, z, x)
        pl.when(r != zk)(lambda: remote(src.at[zk], dst.at[pl.ds(n * r, n)], ss.at[zk],
                                        rs.at[r], to).start())

        @pl.when(r == zk)
        def _():
            copy = local_copy(k, src.at[zk], dst.at[pl.ds(n * r, n)])
            copy.start()
            copy.wait()

    def handed(src, dst, sems, n):
        ss, rs = sems
        for rk in range(4):
            ref = dst.at[pl.ds(n * rk, n)]
            pl.when(r != rk)(lambda ref=ref, rk=rk: remote(
                src.at[0], ref, ss.at[0], rs.at[rk], to_x).wait_recv())

    def hand_sent(src, dst, sems, n):
        ss, rs = sems
        for zk in range(4):
            pl.when(r != zk)(lambda zk=zk: remote(
                src.at[zk], dst.at[pl.ds(0, n)], ss.at[zk], rs.at[0], to_x).wait_send())

    quarters[0].wait()
    out_q.finish()
    out_sems = (m["ho_s"], m["ho_r"])
    down_sems = (m["hd_s"], m["hd_r"])
    for zk in range(4):
        hand(13, zk, m["zo"], m["wo_v"], out_sems, quarter_o)

    for k in range(1, 4):
        pl.when(z - k >= 0)(lambda k=k: remote(
            segs.at[0], segs.at[(z + 4 - k) % 4], m["su_s"].at[k - 1],
            m["su_r"].at[(z + 4 - k) % 4], to_x).wait_recv())

    summed = SeqSum(m["part"], [m[n] for n in SUM_NAMES])
    o_all, att = m["o_v"], m["att_v"]
    acc, q_seg = m["acc"], m["q_seg"]

    def attend_one(k, carry):
        b, e = order(k)
        s = 2 * b + e
        q_seg[...] = segment_columns(segs, z, s)

        def block(zk, diagonal):
            tile = kv[zk, s]
            p = exp_scores(q_all[s], tile, q_seg[...], segment_row(segs, zk, s), diagonal)
            ones = jnp.where(lanes(tile.shape) < HEAD_DIM, 1.0, tile.astype(F32)).astype(BF16)
            add = jnp.dot(p.astype(BF16), ones, preferred_element_type=F32)
            if diagonal:
                acc[...] = add
            else:
                acc[...] += add

        block(z, True)

        @pl.when(z == 2)
        def _():
            kv_arrival(0, s).wait_recv()
            kv_pass(s).start()

        def step(i, inner):
            zk = z - 1 - i
            pl.when(jnp.logical_not((z == 2) & (zk == 0)))(
                lambda: kv_arrival(zk, s).wait_recv())
            block(zk, False)
            return inner

        lax.fori_loop(0, z, step, 0)
        total = acc[...]
        inv = 1.0 / jnp.where(lanes(total.shape) < HEAD_DIM, total, 1.0)
        inv = jnp.where(lanes(total.shape) < HEAD_DIM, inv, roll(inv, 64))
        o = total * inv
        o_all[s] = jnp.where(lanes(o.shape) < HEAD_DIM, inv, o)
        o = high_half(o)
        first, second, third = o[0:span], o[span:2 * span], o[2 * span:]
        att[s, :, 0:128] = (roll(first, 64) + second).astype(BF16)
        att[s, :, 128:192] = roll(third, 64)[:, 0:HEAD_DIM].astype(BF16)
        pl.when(k == 0)(lambda: handed(m["zo"], m["wo_v"], out_sems, quarter_o))
        out = jnp.dot(att[s], m["wo_v"][...], preferred_element_type=F32).astype(BF16)
        m["part"][pl.ds(2 * s, 2)] = out.reshape(2, rows, width)
        pl.when(k < 2)(lambda: summed.give(b))
        pl.when(k == 2)(summed.take_far)
        pl.when(k == 3)(summed.take_near)
        return carry

    lax.fori_loop(0, 4, attend_one, 0)
    more = [local_copy(14, o_all, m["o"]),
            local_copy(16, att, m["att"]), local_copy(17, kv, m["kv"]),
            local_copy(18, segs, m["segs"]), local_copy(19, m["wo_v"], m["wo_all"])]
    for copy in more:
        copy.start()
    down_q.forward()
    summed.middle()
    gu.forward()
    summed.finish()
    mid = m["tok"][...].astype(F32) + summed.out[...]
    m["mid"][...] = mid
    m["low"][...] = (mid * inverse_rms(mid) * m["g_two"][...]).astype(BF16)
    n2 = Gather(m["low"], m["n2_all"], m["gc_s"], m["gc_r"], keep.at[20])
    n2.start()
    quarters[1].wait()
    down_q.finish()
    for zk in range(4):
        hand(13, zk, m["zd"], m["wd_all"], down_sems, quarter_d)
    cot.finish()
    n2.forward()
    n2.finish()
    handed(m["zd"], m["wd_all"], down_sems, quarter_d)
    gu.finish()

    for along in (near, flip, out_q, down_q, gu):
        along.sent()
    summed.sent()
    cross.wait_send()
    for k in range(1, 8):
        seg_copy(k).wait_send()
        gain_copy(k).wait_send()
    for k in range(1, 4):
        pl.when(z + k < 4)(lambda k=k: seg_up(k).wait_send())

    def kv_sent(s, carry):
        for d in (1, 2):
            pl.when(z + d < 4)(lambda d=d: kv_copy(d, s).wait_send())
        pl.when(z == 2)(lambda: kv_pass(s).wait_send())
        return carry

    lax.fori_loop(0, 4, kv_sent, 0)
    hand_sent(m["zo"], m["wo_v"], out_sems, quarter_o)
    hand_sent(m["zd"], m["wd_all"], down_sems, quarter_d)
    for copy in exports + more:
        copy.wait()


SUM_NAMES = ("r1", "chip", "rx", "ry", "mine", "late", "sum_out", "sum_s", "sum_r")


def forward_call(tok, cot, seg, wq, gains, wgu, wd, wo, qg, kg, cos, sin):
    shape = jax.ShapeDtypeStruct
    rows, width = tok.shape
    span = 2 * rows
    own_rows = wq.shape[1]
    part = wgu.shape[1] // 16
    outs = {
        "normed": shape((8, rows, width), BF16),
        "cot_all": shape((8, rows, width), BF16),
        "n2_all": shape((8, rows, width), BF16),
        "wq_all": shape((width, HEAD_COLS), BF16),
        "wo_all": shape((Q_COLS, width), BF16),
        "wd_all": shape((part, width), BF16),
        "wgu_all": shape((width, 2 * part), BF16),
        "qkv": shape((4, span, HEAD_COLS), F32),
        "q": shape((4, GROUP * span, 128), BF16),
        "kv": shape((4, 4, span, 128), BF16),
        "segs": shape((4, 8) + seg.shape, seg.dtype),
        "o": shape((4, GROUP * span, 128), F32),
        "att": shape((4, span, Q_COLS), BF16),
        "mid": shape((rows, width), F32),
        "g_one": shape((1, width), F32),
        "g_two": shape((1, width), F32),
        "gains_all": shape((8,) + gains.shape, BF16),
    }
    sems = {
        "ga_s": dma(8), "ga_r": dma(8), "gb_s": dma(8), "gb_r": dma(8), "gc_s": dma(8),
        "gc_r": dma(8), "sg_s": dma(7), "sg_r": dma(7), "gn_s": dma(7), "gn_r": dma(7),
        "wa_s": dma(6), "wa_r": dma(4), "wb_s": dma(6), "wb_r": dma(4), "wo_s": dma(6),
        "wo_r": dma(4), "wd_s": dma(6), "wd_r": dma(4), "wg_s": dma(6), "wg_r": dma(4),
        "xc_s": pltpu.SemaphoreType.DMA, "xc_r": pltpu.SemaphoreType.DMA,
        "kv_s": pltpu.SemaphoreType.DMA((3, 4)), "kv_r": pltpu.SemaphoreType.DMA((4, 4)),
        "su_s": dma(3), "su_r": dma(4), "ho_s": dma(4), "ho_r": dma(4), "hd_s": dma(4),
        "hd_r": dma(4), "keep": dma(21),
    }
    buffers = {
        "tok_all": pltpu.VMEM((8, rows, width), BF16),
        "segs_v": pltpu.VMEM((4, 8) + seg.shape, seg.dtype),
        "wq_v": pltpu.VMEM((width, HEAD_COLS), BF16),
        "gains_v": pltpu.VMEM((8,) + gains.shape, BF16),
        "raw": pltpu.VMEM((2, own_rows, 2 * part), BF16),
        "pair": pltpu.VMEM((2, own_rows, 2 * part), BF16),
        "zo": pltpu.VMEM((4, wo.shape[0] // 4, width), BF16),
        "zd": pltpu.VMEM((4, wd.shape[0] // 4, width), BF16),
        "wo_v": pltpu.VMEM((Q_COLS, width), BF16),
        "qkv_v": pltpu.VMEM((4, span, HEAD_COLS), F32),
        "q_v": pltpu.VMEM((4, GROUP * span, 128), BF16),
        "kv_v": pltpu.VMEM((4, 4, span, 128), BF16),
        "o_v": pltpu.VMEM((4, GROUP * span, 128), F32),
        "att_v": pltpu.VMEM((4, span, Q_COLS), BF16),
        "acc": pltpu.VMEM((GROUP * span, 128), F32),
        "q_seg": pltpu.VMEM((span, span), jnp.int32),
        "part": pltpu.VMEM((8, rows, width), BF16),
        "low": pltpu.VMEM((rows, width), BF16),
    }
    buffers.update(zip(SUM_NAMES, seq_scratch(width)))
    names = FWD_IN + FWD_OUT + tuple(buffers) + tuple(sems)
    specs = {n: VMEM for n in ("tok", "seg", "gains", "wq", "qg", "kg", "cos", "sin")}
    outs_list = pl.pallas_call(
        functools.partial(forward_kernel, names),
        name="forward",
        out_shape=tuple(outs[n] for n in FWD_OUT),
        in_specs=[specs.get(n, ANY) for n in FWD_IN],
        out_specs=tuple(VMEM if n in ("mid", "g_one", "g_two") else ANY for n in FWD_OUT),
        scratch_shapes=list(buffers.values()) + list(sems.values()),
        compiler_params=params(0),
    )(tok, cot, seg, wq, gains, wgu, wd, wo, qg, kg, cos, sin)
    return dict(zip(FWD_OUT, outs_list))


class ZSum:
    def __init__(self, block, slot, send, recv):
        self.block, self.slot, self.send, self.recv = block, slot, send, recv
        self.base, self.y, self.c, self.z, self.x = here()

    def to(self, zk):
        return device(self.base, self.y, self.c, zk, self.x)

    def direct(self, zk):
        return remote(self.block(zk), self.slot(self.z), self.send.at[zk], self.recv.at[self.z],
                      self.to(zk))

    def far(self, zk, by):
        return remote(self.block(zk), self.slot(by), self.send.at[zk], self.recv.at[4],
                      self.to(by))

    def first(self, i):
        up = (self.z // 2)
        return up * i + (1 - up) * (3 - i)

    def start(self, zk):
        z = self.z
        late = ((z == 1) & (zk == 3)) | ((z == 2) & (zk == 0))
        end = ((z == 0) & (zk == 3)) | ((z == 3) & (zk == 0))
        pl.when((zk != z) & jnp.logical_not(late) & jnp.logical_not(end))(
            lambda: self.direct(zk).start())
        pl.when((z == 0) & (zk == 3))(lambda: self.far(3, 1).start())
        pl.when((z == 3) & (zk == 0))(lambda: self.far(0, 2).start())

    def merge(self, add):
        @pl.when(self.z == 1)
        def _():
            self.far(3, 1).wait_recv()
            add(self.block(3), self.slot(1))
            self.direct(3).start()

        @pl.when(self.z == 2)
        def _():
            self.far(0, 2).wait_recv()
            add(self.block(0), self.slot(2))
            self.direct(0).start()

    def arrive(self, zk):
        ref = self.slot(zk)
        remote(ref, ref, self.send.at[0], self.recv.at[zk], self.to(zk)).wait_recv()

    def middle(self):
        return (self.z == 1) | (self.z == 2)

    def wait(self):
        z = self.z

        @pl.when(self.middle())
        def _():
            for zk in (z - 1, z + 1, (z + 2) % 4):
                self.arrive(zk)

        @pl.when(jnp.logical_not(self.middle()))
        def _():
            for zk in (1, 2):
                self.arrive(zk)

    def collect(self, total):
        z = self.z
        pl.when(self.middle())(
            lambda: total([self.slot(zk) for zk in (z - 1, z + 1, (z + 2) % 4)]))
        pl.when(jnp.logical_not(self.middle()))(
            lambda: total([self.slot(zk) for zk in (1, 2)]))

    def sent(self):
        for zk in range(4):
            pl.when(self.z != zk)(lambda zk=zk: self.direct(zk).wait_send())


class RepShare:
    def __init__(self, at, send, recv):
        self.at, self.send, self.recv = at, send, recv
        _, self.y, self.c, _, _ = here()
        self.to_c, _, self.to_y = neighbours()
        self.r = 2 * self.y + self.c

    def copy(self, k, r, to):
        return remote(self.at(r), self.at(r), self.send.at[k], self.recv.at[k], to)

    def start(self):
        self.copy(0, self.r, self.to_y).start()
        self.copy(1, self.r, self.to_c).start()

    def forward(self):
        other = 2 * (1 - self.y) + self.c
        self.copy(0, other, self.to_y).wait_recv()
        self.copy(2, other, self.to_c).start()

    def finish(self):
        self.copy(1, 2 * self.y + 1 - self.c, self.to_c).wait_recv()
        self.copy(2, 2 * (1 - self.y) + 1 - self.c, self.to_c).wait_recv()

    def sent(self):
        self.copy(0, self.r, self.to_y).wait_send()
        self.copy(1, self.r, self.to_c).wait_send()
        self.copy(2, self.r, self.to_c).wait_send()


def first_dims(left, right):
    return lax.dot_general(left, right, (((0,), (0,)), ((), ())), preferred_element_type=F32)


def last_dims(left, right):
    return lax.dot_general(left, right, (((1,), (1,)), ((), ())), preferred_element_type=F32)


def head_back(dy, u, gain):
    inv = head_inverse(u)
    scaled = dy * gain
    gain_grad = jnp.sum(dy * u * inv, axis=0, keepdims=True)
    inner = jnp.sum(scaled * u, axis=-1, keepdims=True) * (1.0 / HEAD_DIM)
    return inv * scaled - u * (inv * inv * inv * inner), gain_grad


BWD_IN = ("n2", "cot_all", "wgu", "wd", "wo", "wq", "normed", "qkv", "q", "kv", "segs", "o", "att",
          "mid", "tok", "cot", "g_one", "g_two", "qg", "kg", "cos", "sin")
BWD_SMALL = ("mid", "tok", "cot", "g_one", "g_two", "qg", "kg", "cos", "sin")
BWD_OUT = ("mixed", "input_grad", "gu_g", "do_g", "qkv_g", "gains_g", "gu_slot",
           "do_slot")
SUM_B = tuple("input_grad" if n == "sum_out" else n + "_b" for n in SUM_NAMES)


def backward_kernel(names, *refs):
    m = dict(zip(names, refs))
    base, y, c, z, x = here()
    r = 2 * y + c
    to_c, to_x, to_y = neighbours()
    z_same = [device(base, y, c, (z + k) % 4, x) for k in range(1, 4)]
    mates = layer_mates()
    greet(mates + z_same)
    rows, width = m["tok"].shape
    span = 2 * rows
    keep = m["keep"]
    part = m["wd"].shape[0]
    main = (part // 128) * 128
    own_rows = m["wo"].shape[0]
    rest = part - main
    quarter_d, quarter_o = part // 4, own_rows // 4

    def order(k):
        return (y + 1 + k) % 2, (c + 1 + k // 2) % 2

    def load(k, src, dst):
        copy = pltpu.make_async_copy(src, dst, keep.at[k])
        copy.start()
        return copy

    n2, cot, wgu, wd = m["n2_v"], m["cot_v"], m["wgu_v"], m["wd_v"]
    first_loads = [
        load(0, m["wgu"], wgu), load(1, m["n2"], n2), load(2, m["cot_all"], cot),
        load(3, m["wd"].at[pl.ds(rest * x, main)], wd.at[pl.ds(0, main)]),
        load(4, m["wd"].at[pl.ds(main * (1 - x), rest)], wd.at[pl.ds(main, rest)]),
    ]
    later = [load(5 + i, m[n], m[n + "_v"]) for i, n in enumerate(
        ("wo", "wq", "qkv", "q", "kv", "segs", "o", "att"))]
    wd[pl.ds(main + rest, 128 - rest)] = jnp.zeros((128 - rest, width), BF16)
    for copy in first_loads:
        copy.wait()

    hidden, dgu, parts = m["hidden"], m["dgu"], m["part"]
    summed = SeqSum(parts, [m[n] for n in SUM_NAMES])

    def feed(k, carry):
        b, e = order(k)
        s = 2 * b + e
        at = pl.ds(s * span, span)
        gu = jnp.dot(n2[pl.ds(2 * s, 2)].reshape(span, width), wgu[...],
                     preferred_element_type=F32)
        dh = last_dims(cot[pl.ds(2 * s, 2)].reshape(span, width), wd[...])
        for lo, hi in ((0, main), (main, main + 128)):
            if lo == 0:
                gate, up = gu[:, :main], gu[:, main:2 * main]
            else:
                tile = gu[:, 2 * main:]
                gate, up = low_half(tile), low_half(roll(tile, 64))
            grad = dh[:, lo:hi]
            sigma = 1.0 / (1.0 + jnp.exp(-gate))
            active = gate * sigma
            hidden[at, lo:hi] = (active * up).astype(BF16)
            d_gate = grad * up * sigma * (1.0 + gate * (1.0 - sigma))
            d_up = grad * active
            if lo == 0:
                dgu[at, 0:main] = d_gate.astype(BF16)
                dgu[at, main:2 * main] = d_up.astype(BF16)
            else:
                dgu[at, 2 * main:] = (d_gate + roll(low_half(d_up), 64)).astype(BF16)
        out = last_dims(dgu[at], wgu[...]).astype(BF16)
        parts[pl.ds(2 * s, 2)] = out.reshape(2, rows, width)
        pl.when(k < 2)(lambda: summed.give(b))
        pl.when(k == 2)(summed.take_far)
        pl.when(k == 3)(summed.take_near)
        return carry

    lax.fori_loop(0, 4, feed, 0)

    ggu = m["ggu"]
    block_rows = 2 * own_rows
    gu_sum = ZSum(lambda zk: ggu.at[zk], lambda zk: m["gu_slot"].at[zk], m["zg_s"], m["zg_r"])

    def grad_gu(i, carry):
        zk = gu_sum.first(i)
        cols = pl.ds(pl.multiple_of(zk * block_rows, 128), block_rows)
        left = n2[:, :, cols].reshape(8 * rows, block_rows)
        ggu[zk] = first_dims(left, dgu[...]).astype(BF16)
        gu_sum.start(zk)
        return carry

    lax.fori_loop(0, 2, grad_gu, 0)
    summed.middle()
    lax.fori_loop(2, 4, grad_gu, 0)
    summed.finish()

    v = m["mid"][...]
    dv, gain_grad = norm_back(summed.out[...], v, inverse_rms(v), m["g_two"][...])
    m["row_two"][...] = gain_grad
    dmid = m["cot"][...].astype(F32) + dv
    m["dmid"][...] = dmid
    m["low"][...] = dmid.astype(BF16)
    branch = Gather(m["low"], m["db"], m["ga_s"], m["ga_r"], keep.at[13])
    branch.start()
    normed = n2
    copy_normed = load(1, m["normed"], normed)

    gdo, got = m["gdo"], m["got"]
    summed.sent()
    units = part // rest
    for j in range(0, main + 128, 128):
        grad = first_dims(hidden[:, j:j + 128], cot[...].reshape(8 * rows, width)).astype(BF16)
        for h in range(2):
            u = 2 * (j // 128) + h
            if u < units:
                to = (u + x) % units
                parts[to // 2, pl.ds(rest * (to % 2), rest)] = grad[rest * h:rest * (h + 1)]
    for i in range(4):
        lo = quarter_d * i
        first, last = lo // rows, (lo + quarter_d - 1) // rows + 1
        span_rows = parts[first:last].reshape((last - first) * rows, width)
        gdo[i, 0:quarter_d] = span_rows[lo - first * rows:lo - first * rows + quarter_d]
    branch.forward()

    mixed = SeqSum(parts, [m[n] for n in SUM_B])

    def down(k, carry):
        b, e = order(k)
        s = 2 * b + e
        out = jnp.dot(hidden[pl.ds(s * span, span)], wd[...], preferred_element_type=F32)
        parts[pl.ds(2 * s, 2)] = out.astype(BF16).reshape(2, rows, width)
        pl.when(k < 2)(lambda: mixed.give(b))
        pl.when(k == 2)(mixed.take_far)
        pl.when(k == 3)(mixed.take_near)
        return carry

    lax.fori_loop(0, 4, down, 0)
    branch.finish()

    def add_far(block, slot):
        copy = pltpu.make_async_copy(slot, dgu.at[pl.ds(0, block_rows)], keep.at[0])
        copy.start()
        copy.wait()
        block[...] = (block[...].astype(F32) + dgu[0:block_rows].astype(F32)).astype(BF16)

    gu_sum.merge(add_far)

    def hand(i, lo, n, ss, rs):
        return remote(gdo.at[i, pl.ds(lo, n)], got.at[r, pl.ds(lo, n)], ss.at[i], rs.at[r],
                      device(base, i // 2, i % 2, z, x))

    def hand_all(lo, n, ss, rs):
        for i in range(4):
            pl.when(r != i)(lambda i=i: hand(i, lo, n, ss, rs).start())
        got[r, lo:lo + n] = gdo[r, lo:lo + n]

    def handed(lo, n, ss, rs):
        for i in range(4):
            pl.when(r != i)(lambda i=i: remote(
                gdo.at[i, pl.ds(lo, n)], got.at[i, pl.ds(lo, n)], ss.at[i], rs.at[i],
                to_c).wait_recv())

    def hand_sent(lo, n, ss, rs):
        for i in range(4):
            pl.when(r != i)(lambda i=i: hand(i, lo, n, ss, rs).wait_send())

    hand_all(0, quarter_d, m["hd_s"], m["hd_r"])

    for copy in later:
        copy.wait()
    q_all, kv, segs, o_all, att = m["q_v"], m["kv_v"], m["segs_v"], m["o_v"], m["att_v"]
    wo, wq, qkv = m["wo_v"], m["wq_v"], m["qkv_v"]
    db, dkv, dqkv, acc, q_seg, do_v = m["db"], m["kv_v"], m["dqkv"], m["acc"], m["q_seg"], m["do"]
    own_kv = m["own_kv"]
    qg, kg, cos, sin = m["qg"][0:1], m["kg"][0:1], m["cos"][...], m["sin"][...]
    m["row_head"][...] = jnp.zeros((1, 128), F32)

    def kv_sum(s):
        return ZSum(lambda zk: dkv.at[zk, s], lambda zk: m["kv_slot"].at[zk, s],
                    m["zk_s"].at[s], m["zk_r"].at[s])

    def attend_one(k, carry):
        b, e = order(k)
        s = 2 * b + e
        grads = db[pl.ds(2 * s, 2)].reshape(span, width)
        d_att = last_dims(grads, wo[...])
        first = d_att[:, 0:128]
        third = jnp.concatenate([jnp.zeros((span, HEAD_DIM), F32), d_att[:, 128:192]], axis=1)
        d_out = jnp.concatenate([high_half(roll(first, 64)), high_half(first), third], axis=0)
        d_out = d_out.astype(BF16).astype(F32)
        o = o_all[s]
        d_out = (d_out * roll(o, 64)).astype(BF16)
        do_v[...] = d_out
        delta = jnp.sum(d_out.astype(F32) * high_half(o), axis=1, keepdims=True)
        q_seg[...] = segment_columns(segs, z, s)
        acc[...] = jnp.zeros_like(acc)

        def block(zk, diagonal):
            tile = kv[zk, s]
            q = q_all[s]
            d_out = do_v[...]
            p = exp_scores(q, tile, q_seg[...], segment_row(segs, zk, s), diagonal)
            ds = (p * (last_dims(d_out, tile) - delta)).astype(BF16)
            acc[...] += jnp.dot(ds, tile, preferred_element_type=F32)
            return first_dims(ds, q) + first_dims(p.astype(BF16), d_out)

        def step(zk, inner):
            dkv[zk, s] = block(zk, False).astype(BF16)
            pl.when((z == 3) & (zk == 0))(lambda: kv_sum(s).far(0, 2).start())
            pl.when(jnp.logical_not(((z == 3) | (z == 2)) & (zk == 0)))(
                lambda: kv_sum(s).direct(zk).start())
            return inner

        lax.fori_loop(0, z, step, 0)
        own_kv[s] = block(z, True)
        tiles = split_heads(qkv[s, :, 0:128], qkv[s, :, 128:256])
        back = []
        for j in range(GROUP):
            dy = rotated(low_half(acc[pl.ds(j * span, span)]) * HEAD_DIM ** (-0.5), cos, -sin)
            raw, gain_part = head_back(dy, tiles[j], qg)
            m["row_head"][...] += gain_part
            back.append(raw)
        dqkv[s, :, 0:128] = (back[0] + roll(back[1], 64)).astype(BF16)
        dqkv[s, :, 128:256] = back[2].astype(BF16)
        pl.when(k == 1)(mixed.middle)
        return carry

    lax.fori_loop(0, 4, attend_one, 0)

    for j in range(0, width, 512):
        cols = slice(j, j + 512)
        grad = first_dims(att[...].reshape(8 * rows, Q_COLS),
                          db[:, :, cols].reshape(8 * rows, 512)).astype(BF16)
        for i in range(4):
            gdo[i, quarter_d:quarter_d + quarter_o, cols] = grad[quarter_o * i:quarter_o * (i + 1)]
    hand_all(quarter_d, quarter_o, m["ho_s"], m["ho_r"])

    def kv_merge(k, carry):
        b, e = order(k)
        s = 2 * b + e

        @pl.when(z == 2)
        def _():
            one = kv_sum(s)
            one.far(0, 2).wait_recv()
            dkv[0, s] = (dkv[0, s].astype(F32) + m["kv_slot"][2, s].astype(F32)).astype(BF16)
            one.direct(0).start()
        return carry

    lax.fori_loop(0, 4, kv_merge, 0)
    mixed.finish()
    m["mixed"][...] = (m["mid"][...] + mixed.out[...]).astype(BF16)
    mixed.sent()

    handed(0, quarter_d, m["hd_s"], m["hd_r"])
    handed(quarter_d, quarter_o, m["ho_s"], m["ho_r"])
    do_sum = ZSum(lambda zk: got.at[zk], lambda zk: m["do_slot"].at[zk], m["zd_s"], m["zd_r"])

    def start_do(i, carry):
        do_sum.start(do_sum.first(i))
        return carry

    lax.fori_loop(0, 4, start_do, 0)

    inputs = SeqSum(parts, [m[n] for n in SUM_NAMES])

    def finish_one(k, carry):
        b, e = order(k)
        s = 2 * b + e
        for d in (1, 2):
            @pl.when(z + d < 4)
            def _():
                kv_sum(s).arrive(z + d)
                own_kv[s] += m["kv_slot"][z + d, s].astype(F32)
        total = own_kv[s]
        u = split_heads(qkv[s, :, 0:128], qkv[s, :, 128:256])[GROUP]
        dy = rotated(low_half(total), cos, -sin)
        raw, gain_part = head_back(dy, u, kg)
        m["row_head"][...] += roll(gain_part, 64)
        tile = dqkv[s, :, 128:256].astype(F32)
        dqkv[s, :, 128:256] = (low_half(tile) + roll(raw, 64)).astype(BF16)
        dqkv[s, :, 256:320] = roll(total, 64)[:, 0:HEAD_DIM].astype(BF16)
        out = last_dims(dqkv[s], wq[...]).astype(BF16)
        parts[pl.ds(2 * s, 2)] = out.reshape(2, rows, width)
        pl.when(k < 2)(lambda: inputs.give(b))
        pl.when(k == 2)(inputs.take_far)
        pl.when(k == 3)(inputs.take_near)
        return carry

    lax.fori_loop(0, 4, finish_one, 0)
    copy_normed.wait()
    gqkv = m["gqkv"]
    qkv_sum = ZSum(lambda zk: gqkv.at[zk], lambda zk: m["qkv_slot"].at[zk], m["zq_s"], m["zq_r"])

    def grad_qkv(i, carry):
        zk = qkv_sum.first(i)
        cols = pl.ds(pl.multiple_of(zk * block_rows, 128), block_rows)
        left = normed[:, :, cols].reshape(8 * rows, block_rows)
        gqkv[zk] = first_dims(left, dqkv[...].reshape(8 * rows, HEAD_COLS)).astype(BF16)
        qkv_sum.start(zk)
        return carry

    lax.fori_loop(0, 4, grad_qkv, 0)
    inputs.middle()

    def add_vmem(block, slot):
        block[...] = (block[...].astype(F32) + slot[...].astype(F32)).astype(BF16)

    hand_sent(0, quarter_d, m["hd_s"], m["hd_r"])
    hand_sent(quarter_d, quarter_o, m["ho_s"], m["ho_r"])

    def add_do(block, slot):
        copy = pltpu.make_async_copy(slot, gdo.at[0], keep.at[0])
        copy.start()
        copy.wait()
        block[...] = (block[...].astype(F32) + gdo[0].astype(F32)).astype(BF16)

    do_sum.merge(add_do)

    t_own = 2 * r + x
    gu_sum.sent()
    gu_sum.wait()

    def total_gu(slots):
        copies = []
        for i, slot in enumerate(slots):
            copy = pltpu.make_async_copy(slot, dgu.at[pl.ds(0, block_rows)], keep.at[0])
            copy.start()
            copy.wait()
            ggu[z] = (ggu[z].astype(F32) + dgu[0:block_rows].astype(F32)).astype(BF16)

    gu_sum.collect(total_gu)
    gu_out, qkv_out, do_out = m["gu_g"], m["qkv_g"], m["do_g"]

    def swap(src, out, ss, rs):
        return remote(src.at[z, pl.ds(own_rows * (1 - x), own_rows)], out.at[t_own], ss, rs, to_x)

    def keep_own(k, src, out):
        return pltpu.make_async_copy(src.at[z, pl.ds(own_rows * x, own_rows)], out.at[t_own],
                                     keep.at[k])

    def swapped(src, out, ss, rs):
        return remote(src.at[z, pl.ds(own_rows * x, own_rows)], out.at[2 * r + 1 - x], ss, rs,
                      to_x)

    gu_swap = swap(ggu, gu_out, m["xg_s"], m["xg_r"])
    gu_swap.start()
    gu_keep = keep_own(14, ggu, gu_out)
    gu_keep.start()
    gu_keep.wait()
    gu_share = RepShare(lambda i: gu_out.at[pl.ds(2 * i, 2)], m["rg_s"], m["rg_r"])

    inputs.finish()
    v = m["tok"][...].astype(F32)
    dv, gain_grad = norm_back(inputs.out[...], v, inverse_rms(v), m["g_one"][...])
    m["input_grad"][...] = m["dmid"][...] + dv

    rows_v = m["rows_v"]
    rows_v[0, 0:1] = gain_grad
    rows_v[0, 1:2] = m["row_two"][...]
    rows_v[0, 2:3, 0:128] = m["row_head"][...]

    def gain_copy(k):
        return remote(rows_v.at[0], rows_v.at[k], m["gn_s"].at[k - 1], m["gn_r"].at[k - 1],
                      mates[k - 1])

    for k in range(1, 8):
        gain_copy(k).start()

    swapped(ggu, gu_out, m["xg_s"], m["xg_r"]).wait_recv()
    gu_share.start()
    qkv_sum.merge(add_vmem)
    for k in range(1, 8):
        gain_copy(k).wait_recv()
    total = rows_v[0]
    for k in range(1, 8):
        total = total + rows_v[k]
    z_rows = m["z_rows"]
    z_rows[0] = total

    def gain_z(k):
        return remote(z_rows.at[0], z_rows.at[k], m["gz_s"].at[k - 1], m["gz_r"].at[k - 1],
                      z_same[k - 1])

    for k in range(1, 4):
        gain_z(k).start()

    do_sum.wait()

    def total_do(slots):
        copies = [pltpu.make_async_copy(slot, gdo.at[i], keep.at[i])
                  for i, slot in enumerate(slots)]
        for copy in copies:
            copy.start()
        for copy in copies:
            copy.wait()
        total = got[z].astype(F32)
        for i in range(len(slots)):
            total = total + gdo[i].astype(F32)
        m["do_own"][...] = total.astype(BF16)

    do_sum.collect(total_do)
    do_keep = pltpu.make_async_copy(m["do_own"], do_out.at[r], keep.at[15])
    do_keep.start()
    do_keep.wait()
    do_share = RepShare(lambda i: do_out.at[i], m["rd_s"], m["rd_r"])
    do_share.start()
    gu_share.forward()

    qkv_sum.wait()

    def total_qkv(slots):
        total = gqkv[z].astype(F32)
        for slot in slots:
            total = total + slot[...].astype(F32)
        m["qkv_own"][0] = total.astype(BF16)

    qkv_sum.collect(total_qkv)
    own = m["qkv_own"]
    qkv_swap = remote(own.at[0, pl.ds(own_rows * (1 - x), own_rows)], qkv_out.at[t_own],
                      m["xq_s"], m["xq_r"], to_x)
    qkv_swap.start()
    qkv_keep = pltpu.make_async_copy(own.at[0, pl.ds(own_rows * x, own_rows)],
                                     qkv_out.at[t_own], keep.at[16])
    qkv_keep.start()
    qkv_keep.wait()
    qkv_share = RepShare(lambda i: qkv_out.at[pl.ds(2 * i, 2)], m["rq_s"], m["rq_r"])
    remote(own.at[0, pl.ds(0, own_rows)], qkv_out.at[2 * r + 1 - x], m["xq_s"], m["xq_r"],
           to_x).wait_recv()
    qkv_share.start()
    do_share.forward()
    for k in range(1, 4):
        gain_z(k).wait_recv()
    m["gains_g"][...] = z_rows[0] + z_rows[1] + z_rows[2] + z_rows[3]
    qkv_share.forward()
    for share in (gu_share, do_share, qkv_share):
        share.finish()

    for share in (gu_share, do_share, qkv_share):
        share.sent()
    gu_swap.wait_send()
    qkv_swap.wait_send()
    for k in range(1, 8):
        gain_copy(k).wait_send()
    for k in range(1, 4):
        gain_z(k).wait_send()
    do_sum.sent()
    qkv_sum.sent()
    inputs.sent()

    def kv_sent(s, carry):
        for zk in range(3):
            pl.when(z > zk)(lambda zk=zk: kv_sum(s).direct(zk).wait_send())
        return carry

    lax.fori_loop(0, 4, kv_sent, 0)


def backward_call(f, tok, cot, qg, kg, cos, sin):
    shape = jax.ShapeDtypeStruct
    rows, width = tok.shape
    span = 2 * rows
    own_rows, part = f["wo_all"].shape[0], f["wd_all"].shape[0]
    cols = f["wgu_all"].shape[1]
    quarter = (part + own_rows) // 4
    args = {"n2": f["n2_all"], "cot_all": f["cot_all"], "wgu": f["wgu_all"], "wd": f["wd_all"],
            "wo": f["wo_all"], "wq": f["wq_all"], "tok": tok, "cot": cot, "qg": qg, "kg": kg,
            "cos": cos, "sin": sin}
    for n in ("normed", "qkv", "q", "kv", "segs", "o", "att", "mid", "g_one", "g_two"):
        args[n] = f[n]
    outs = {
        "mixed": shape((rows, width), BF16),
        "input_grad": shape((rows, width), F32),
        "gu_g": shape((8, own_rows, cols), BF16),
        "do_g": shape((4, quarter, width), BF16),
        "qkv_g": shape((8, own_rows, HEAD_COLS), BF16),
        "gains_g": shape((8, width), F32),
        "gu_slot": shape((4, 2 * own_rows, cols), BF16),
        "do_slot": shape((4, quarter, width), BF16),
    }
    same = lambda n, dtype=None: pltpu.VMEM(args[n].shape, dtype or args[n].dtype)
    buffers = {
        "n2_v": same("n2"), "cot_v": same("cot_all"), "wgu_v": same("wgu"),
        "wd_v": pltpu.VMEM(((part // 128 + 1) * 128, width), BF16),
        "wo_v": same("wo"), "wq_v": same("wq"), "qkv_v": same("qkv"), "q_v": same("q"),
        "kv_v": same("kv"), "segs_v": same("segs"), "o_v": same("o"), "att_v": same("att"),
        "hidden": pltpu.VMEM((8 * rows, (part // 128 + 1) * 128), BF16),
        "dgu": pltpu.VMEM((8 * rows, cols), BF16),
        "part": pltpu.VMEM((8, rows, width), BF16),
        "ggu": pltpu.VMEM((4, 2 * own_rows, cols), BF16),
        "gdo": pltpu.VMEM((4, quarter, width), BF16),
        "got": pltpu.VMEM((4, quarter, width), BF16),
        "do_own": pltpu.VMEM((quarter, width), BF16),
        "db": pltpu.VMEM((8, rows, width), BF16),
        "dmid": pltpu.VMEM((rows, width), F32),
        "low": pltpu.VMEM((rows, width), BF16),
        "kv_slot": same("kv"),
        "own_kv": pltpu.VMEM((4, span, 128), F32),
        "dqkv": pltpu.VMEM((4, span, HEAD_COLS), BF16),
        "acc": pltpu.VMEM((GROUP * span, 128), F32),
        "do": pltpu.VMEM((GROUP * span, 128), BF16),
        "q_seg": pltpu.VMEM((span, span), jnp.int32),
        "gqkv": pltpu.VMEM((4, 2 * own_rows, HEAD_COLS), BF16),
        "qkv_slot": pltpu.VMEM((4, 2 * own_rows, HEAD_COLS), BF16),
        "qkv_own": pltpu.VMEM((1, 2 * own_rows, HEAD_COLS), BF16),
        "row_two": pltpu.VMEM((1, width), F32),
        "row_head": pltpu.VMEM((1, 128), F32),
        "rows_v": pltpu.VMEM((8, 8, width), F32),
        "z_rows": pltpu.VMEM((4, 8, width), F32),
    }
    buffers.update(zip(SUM_NAMES, seq_scratch(width)))
    buffers.update((n, b) for n, b in zip(SUM_B, seq_scratch(width)) if n != "input_grad")
    two = pltpu.SemaphoreType.DMA
    sems = {
        "ga_s": dma(8), "ga_r": dma(8), "zg_s": dma(4), "zg_r": dma(5), "zd_s": dma(4),
        "zd_r": dma(5), "zq_s": dma(4), "zq_r": dma(5), "zk_s": two((4, 4)), "zk_r": two((4, 5)),
        "hd_s": dma(4), "hd_r": dma(4), "ho_s": dma(4), "ho_r": dma(4), "xg_s": two, "xg_r": two,
        "xq_s": two, "xq_r": two, "rg_s": dma(3), "rg_r": dma(3), "rd_s": dma(3), "rd_r": dma(3),
        "rq_s": dma(3), "rq_r": dma(3), "gn_s": dma(7), "gn_r": dma(7), "gz_s": dma(3),
        "gz_r": dma(3), "keep": dma(17),
    }
    names = BWD_IN + BWD_OUT + tuple(buffers) + tuple(sems)
    outs_list = pl.pallas_call(
        functools.partial(backward_kernel, names),
        name="backward",
        out_shape=tuple(outs[n] for n in BWD_OUT),
        in_specs=[VMEM if n in BWD_SMALL else ANY for n in BWD_IN],
        out_specs=tuple(VMEM if n in ("mixed", "input_grad", "gains_g") else ANY
                        for n in BWD_OUT),
        scratch_shapes=list(buffers.values()) + list(sems.values()),
        compiler_params=params(1, 63),
    )(*[args[n] for n in BWD_IN])
    return dict(zip(BWD_OUT, outs_list))


def order_kernel(gu, do, qkv, gu_o, down_o, out_o, qkv_o):
    which = pl.program_id(1)
    cols = gu.shape[2]
    main = cols // 2 // 128 * 128
    piece = cols
    quarter_d = down_o.shape[0]
    low = lanes((gu.shape[1], 128)) < HEAD_DIM
    first, second = gu[0, :, 2 * main:].astype(F32), gu[1, :, 2 * main:].astype(F32)

    @pl.when(which == 0)
    def _():
        gu_o[:, 0:main] = gu[0, :, 0:main].astype(F32)
        gu_o[:, main:main + 128] = jnp.where(low, first, roll(second, 64))
        gu_o[:, main + 128:] = gu[1, :, 0:main].astype(F32)
        down_o[...] = do[0, 0:quarter_d].astype(F32)

    @pl.when(which == 1)
    def _():
        gu_o[:, 0:main] = gu[0, :, main:2 * main].astype(F32)
        gu_o[:, main:main + 128] = jnp.where(low, roll(first, 64), second)
        gu_o[:, main + 128:] = gu[1, :, main:2 * main].astype(F32)
        out_o[...] = do[0, quarter_d:].astype(F32)

    @pl.when(which == 0)
    def _():
        i = pl.program_id(0)
        a, b = qkv[0].astype(F32), qkv[1].astype(F32)
        at = lambda start, n: pl.ds(pl.multiple_of(start, 128), n)
        q_cols, kv_cols = HEADS * HEAD_DIM, KV_HEADS * HEAD_DIM
        half = lambda v, w: jnp.where(low, v, w)
        a1, a2, b0, b1 = a[:, 128:256], a[:, 256:], b[:, 0:128], b[:, 128:256]
        qkv_o[:, at(i * 2 * Q_COLS, 128)] = a[:, 0:128]
        qkv_o[:, at(i * 2 * Q_COLS + 128, 128)] = half(a1, roll(b0, 64))
        qkv_o[:, at(i * 2 * Q_COLS + 256, 128)] = half(roll(b0, 64), roll(b1, 64))
        qkv_o[:, at(q_cols + i * 128, 128)] = half(roll(a1, 64), b1)
        qkv_o[:, at(q_cols + kv_cols + i * 128, 128)] = jnp.concatenate([a2, b[:, 256:]], axis=1)


def order_call(gu, do, qkv, part):
    shape = jax.ShapeDtypeStruct
    _, own_rows, cols = gu.shape
    width = do.shape[2]
    quarter_d = part // 4
    quarter_o = do.shape[1] - quarter_d
    return pl.pallas_call(
        order_kernel,
        name="final_order",
        grid=(4, 2),
        out_shape=(
            shape((own_rows, 8 * cols), F32), shape((part, width), F32),
            shape((4 * quarter_o, width), F32),
            shape((own_rows, (HEADS + 2 * KV_HEADS) * HEAD_DIM), F32)),
        in_specs=[
            pl.BlockSpec((2, own_rows, cols), lambda i, w: (i, 0, 0)),
            pl.BlockSpec((1, do.shape[1], width), lambda i, w: (i, 0, 0)),
            pl.BlockSpec((2, own_rows, qkv.shape[2]), lambda i, w: (i, 0, 0))],
        out_specs=(
            pl.BlockSpec((own_rows, cols), lambda i, w: (0, 4 * w + i)),
            pl.BlockSpec((quarter_d, width), lambda i, w: (i, 0)),
            pl.BlockSpec((quarter_o, width), lambda i, w: (i, 0)),
            pl.BlockSpec((own_rows, (HEADS + 2 * KV_HEADS) * HEAD_DIM), lambda i, w: (0, 0))),
        compiler_params=pltpu.CompilerParams(
            dimension_semantics=("arbitrary", "arbitrary"), vmem_limit_bytes=48 * 2**20),
    )(gu, do, qkv)


def rope_tables(positions):
    half = HEAD_DIM // 2
    freq = jnp.exp(-jnp.log(THETA) * jnp.arange(half, dtype=F32) * 2.0 / HEAD_DIM)
    angle = positions.astype(F32)[:, None] * freq[None, :]
    cos, sin = jnp.cos(angle), jnp.sin(angle)
    zero = jnp.zeros_like(cos)
    return jnp.concatenate([cos, cos, zero, zero], 1), jnp.concatenate([-sin, sin, zero, zero], 1)


def over_quads(array):
    reps = lax.axis_size("rep")
    if reps == 4:
        return array
    rows = [[j + 4 * q for q in range(reps // 4)] for j in range(4)]
    return lax.psum(array, "rep", axis_index_groups=rows)


def local(tokens, attn_gain, w_qkv, q_gain, k_gain, w_out, ffn_gain, w_gate_up, w_down,
          cotangent, segment_ids):
    rows, width = tokens.shape
    _, y, c, z, x = here()
    r = 2 * y + c
    q_width, kv_width = HEADS * HEAD_DIM, KV_HEADS * HEAD_DIM
    own_rows = w_qkv.shape[0]
    span = 2 * rows
    cut = lax.dynamic_slice_in_dim

    q_pair = cut(w_qkv, 2 * Q_COLS * r, 2 * Q_COLS, 1)
    k_pair = cut(w_qkv, q_width + 2 * HEAD_DIM * r, 2 * HEAD_DIM, 1)
    v_pair = cut(w_qkv, q_width + kv_width + 2 * HEAD_DIM * r, 2 * HEAD_DIM, 1)
    wq = jnp.stack([
        jnp.concatenate([
            q_pair[:, i * Q_COLS:(i + 1) * Q_COLS],
            k_pair[:, i * HEAD_DIM:(i + 1) * HEAD_DIM],
            v_pair[:, i * HEAD_DIM:(i + 1) * HEAD_DIM]], 1)
        for i in range(2)])
    gains = jnp.zeros((16, 256), BF16)
    gains = gains.at[0, :own_rows].set(attn_gain).at[1, :own_rows].set(ffn_gain)
    seg = jnp.broadcast_to(segment_ids[None, :], (8, rows))
    cos, sin = rope_tables(span * z + jnp.arange(span, dtype=jnp.int32))

    def padded(gain):
        return jnp.zeros((8, 128), F32).at[:, :HEAD_DIM].set(gain.astype(F32)[None])

    qg, kg = padded(q_gain), padded(k_gain)
    f = forward_call(tokens, cotangent, seg, wq, gains, w_gate_up, w_down, w_out, qg, kg, cos, sin)
    g = backward_call(f, tokens, cotangent, qg, kg, cos, sin)
    gu, down, out, qkv = order_call(
        over_quads(g["gu_g"]), over_quads(g["do_g"]), over_quads(g["qkv_g"]), w_down.shape[0])
    gains_sum = over_quads(g["gains_g"])
    place = 2 * z + x
    gain_one = cut(gains_sum[0], place * own_rows, own_rows, 0)
    gain_two = cut(gains_sum[1], place * own_rows, own_rows, 0)
    return (g["mixed"], g["input_grad"], gain_one, qkv, gains_sum[2, :HEAD_DIM],
            gains_sum[2, HEAD_DIM:2 * HEAD_DIM], out, gain_two, gu, down)


def solution(mesh):
    rows, split = P(("rep", "grp"), None), P("grp", None)
    return jax.shard_map(
        local,
        mesh=mesh,
        in_specs=(rows, P("grp"), split, P(), P(), split, P("grp"), split, split, rows,
                  P(("rep", "grp"))),
        out_specs=(rows, rows, P("grp"), split, P(), P(), split, P("grp"), split, split),
        check_vma=False,
    )
```

```python
import functools

import jax
import jax.numpy as jnp
from jax import lax
from jax.experimental import pallas as pl
from jax.experimental.pallas import tpu as pltpu
from jax.sharding import PartitionSpec as P

HEADS = 24
KV_HEADS = 8
HEAD_DIM = 64
GROUP = HEADS // KV_HEADS
Q_COLS = GROUP * HEAD_DIM
HEAD_COLS = Q_COLS + 2 * HEAD_DIM

EPS = 1e-05
THETA = 1000000.0
MESH = pl.DeviceIdType.MESH
F32 = jnp.float32
BF16 = jnp.bfloat16

VMEM = pl.BlockSpec(memory_space=pltpu.VMEM)
ANY = pl.BlockSpec(memory_space=pl.ANY)


def here():
    rep = lax.axis_index("rep")
    grp = lax.axis_index("grp")
    r = rep % 4
    return rep - r, r // 2, r % 2, grp // 2, grp % 2


def device(base, y, c, z, x):
    return {"rep": base + 2 * y + c, "grp": 2 * z + x}


def remote(src, dst, send, recv, to):
    return pltpu.make_async_remote_copy(
        src_ref=src, dst_ref=dst, send_sem=send, recv_sem=recv, device_id=to, device_id_type=MESH
    )


def greet(targets):
    barrier = pltpu.get_barrier_semaphore()
    for to in targets:
        pl.semaphore_signal(barrier, inc=1, device_id=to, device_id_type=MESH)
    pl.semaphore_wait(barrier, len(targets))


def neighbours():
    base, y, c, z, x = here()
    to_c = device(base, y, 1 - c, z, x)
    to_x = device(base, y, c, z, 1 - x)
    to_y = device(base, 1 - y, c, z, x)
    return to_c, to_x, to_y


GATHER_SEMS = 8


class Gather:
    def __init__(self, src, out, send, recv, local):
        self.src, self.out, self.send, self.recv, self.local = src, out, send, recv, local
        _, y, c, _, x = here()
        self.to_c, self.to_x, self.to_y = neighbours()
        slot = lambda a, b, d: 4 * a + 2 * b + d
        self.own = slot(y, c, x)
        self.at_c, self.at_x, self.at_y = slot(y, 1 - c, x), slot(y, c, 1 - x), slot(1 - y, c, x)
        self.at_xc, self.at_yc = slot(y, 1 - c, 1 - x), slot(1 - y, 1 - c, x)
        self.at_xy, self.at_xyc = slot(1 - y, c, 1 - x), slot(1 - y, 1 - c, 1 - x)
        self.half = src.shape[0] // 2

    def part(self, ref, k):
        return ref.at[pl.ds(k * self.half, self.half)]

    def copy(self, k, src, dst, to):
        return remote(src, dst, self.send.at[k], self.recv.at[k], to)

    def start(self):
        out, src = self.out, self.src
        self.keep = pltpu.make_async_copy(src, out.at[self.own], self.local)
        self.keep.start()
        self.sent = [
            self.copy(0, src, out.at[self.own], self.to_x),
            self.copy(1, src, out.at[self.own], self.to_y),
            self.copy(2, src, out.at[self.own], self.to_c),
        ]
        for copy in self.sent:
            copy.start()

    def forward(self):
        out = self.out
        self.copy(0, self.src, out.at[self.at_x], self.to_x).wait_recv()
        first = self.part(out.at[self.at_x], 0)
        self.go(3, first, first, self.to_y)
        self.go(4, out.at[self.at_x], out.at[self.at_x], self.to_c)
        self.copy(1, self.src, out.at[self.at_y], self.to_y).wait_recv()
        second = self.part(out.at[self.at_y], 1)
        self.go(5, second, second, self.to_x)
        self.go(6, out.at[self.at_y], out.at[self.at_y], self.to_c)

    def go(self, k, src, dst, to):
        copy = self.copy(k, src, dst, to)
        copy.start()
        self.sent.append(copy)

    def finish(self):
        out = self.out
        first = self.part(out.at[self.at_xy], 0)
        second = self.part(out.at[self.at_xy], 1)
        self.copy(3, first, first, self.to_y).wait_recv()
        self.copy(5, second, second, self.to_x).wait_recv()
        self.go(7, out.at[self.at_xy], out.at[self.at_xy], self.to_c)
        for k, at in ((2, self.at_c), (4, self.at_xc), (6, self.at_yc), (7, self.at_xyc)):
            self.copy(k, out.at[at], out.at[at], self.to_c).wait_recv()
        for copy in self.sent:
            copy.wait_send()
        self.keep.wait()


def dma(n):
    return pltpu.SemaphoreType.DMA((n,))


def params(cid, limit=60):
    return pltpu.CompilerParams(
        collective_id=cid, has_side_effects=True, vmem_limit_bytes=limit * 2**20
    )


def inverse_rms(v):
    return lax.rsqrt(jnp.mean(v * v, axis=-1, keepdims=True) + EPS)


def norm_back(dy, v, inv, gain):
    scaled = dy * gain
    gain_grad = jnp.sum(dy * v * inv, axis=0, keepdims=True)
    inner = jnp.mean(scaled * v, axis=-1, keepdims=True)
    return inv * scaled - v * inv * inv * inv * inner, gain_grad


def when(cond):
    return pl.when(cond)


def lanes(shape):
    return lax.broadcasted_iota(jnp.int32, shape, len(shape) - 1)


def roll(v, by):
    return pltpu.roll(v, by % v.shape[-1], v.ndim - 1)


class Along:
    def __init__(self, src, slot, send, recv):
        self.src, self.slot, self.send, self.recv = src, slot, send, recv
        self.base, self.y, self.c, self.z, self.x = here()

    def at(self, zk, x):
        return device(self.base, self.y, self.c, zk, x)

    def copy(self, d):
        zk = (self.z + d + 4) % 4
        return remote(self.src, self.slot(self.z), self.send.at[d + 2], self.recv.at[self.z],
                      self.at(zk, self.x))

    def fits(self, d):
        return (self.z + d >= 0) & (self.z + d < 4)

    def first(self):
        for d in (2, -2):
            pl.when(self.fits(d))(lambda d=d: self.copy(d).start())
        pl.when(self.z == 2)(lambda: self.copy(1).start())
        pl.when(self.z == 1)(lambda: self.copy(-1).start())

    def second(self):
        pl.when(self.z < 2)(lambda: self.copy(1).start())
        pl.when(self.z >= 2)(lambda: self.copy(-1).start())

    def arrival(self, zk):
        ref = self.slot(zk)
        return remote(ref, ref, self.send.at[0], self.recv.at[zk], self.at(self.z, 1 - self.x))

    def passed(self, zk, to):
        ref = self.slot(zk)
        return remote(ref, ref, self.send.at[5], self.recv.at[zk], self.at(to, self.x))

    def forward(self):
        @pl.when(self.z == 2)
        def _():
            self.arrival(0).wait_recv()
            self.passed(0, 3).start()

        @pl.when(self.z == 1)
        def _():
            self.arrival(3).wait_recv()
            self.passed(3, 0).start()

    def wait(self, zk):
        early = ((self.z == 2) & (zk == 0)) | ((self.z == 1) & (zk == 3))
        due = jnp.logical_not(early) & (self.z != zk)
        pl.when(due)(lambda: self.arrival(zk).wait_recv())

    def finish(self):
        for zk in range(4):
            self.wait(zk)

    def sent(self):
        for d in (2, -2, 1, -1):
            pl.when(self.fits(d))(lambda d=d: self.copy(d).wait_send())
        pl.when(self.z == 2)(lambda: self.passed(0, 3).wait_send())
        pl.when(self.z == 1)(lambda: self.passed(3, 0).wait_send())


def layer_mates():
    base, y, c, z, x = here()
    return [
        device(base, (y + k // 4) % 2, (c + k // 2) % 2, z, (x + k) % 2) for k in range(1, 8)
    ]


def z_mates():
    base, y, c, z, x = here()
    return [device(base, y, c, (z + k // 2) % 4, (x + k) % 2) for k in range(2, 8)]


def rotated(u, cos, sin):
    lane = lanes(u.shape)
    return u * cos + jnp.where(lane < 32, roll(u, -32), roll(u, 32)) * sin


def low_half(v):
    return jnp.where(lanes(v.shape) < HEAD_DIM, v, 0.0)


def high_half(v):
    return jnp.where(lanes(v.shape) >= HEAD_DIM, v, 0.0)


def split_heads(tile_a, tile_b):
    return [low_half(tile_a), low_half(roll(tile_a, 64)), low_half(tile_b),
            low_half(roll(tile_b, 64))]


def head_inverse(u):
    return lax.rsqrt(jnp.sum(u * u, axis=-1, keepdims=True) * (1.0 / HEAD_DIM) + EPS)


def exp_scores(q, kv, q_seg, k_seg, diagonal):
    s = lax.dot_general(q, kv, (((1,), (1,)), ((), ())), preferred_element_type=F32)
    allowed = q_seg == k_seg
    if diagonal:
        row = lax.broadcasted_iota(jnp.int32, allowed.shape, 0)
        col = lax.broadcasted_iota(jnp.int32, allowed.shape, 1)
        allowed = allowed & (col <= row)
    n = allowed.shape[0]
    return jnp.concatenate([
        jnp.where(allowed, jnp.exp(s[n * j:n * (j + 1)]), 0.0) for j in range(GROUP)], axis=0)


def segment_row(segs, zk, s):
    return jnp.concatenate([segs[zk, 2 * s, 0:1], segs[zk, 2 * s + 1, 0:1]], axis=1)


def segment_columns(segs, zk, s):
    parts = []
    for i in range(2):
        row = jnp.broadcast_to(segs[zk, 2 * s + i, 0:1], (128, 128))
        parts.append(jnp.transpose(row))
    col = jnp.concatenate(parts, axis=0)
    return jnp.concatenate([col, col], axis=1)


class SeqSum:
    def __init__(self, part, scratch):
        self.part = part
        (self.r1, self.chip, self.rx, self.ry, self.mine, self.late, self.out,
         self.send, self.recv) = scratch
        _, self.y, self.c, _, self.x = here()
        self.to_c, self.to_x, self.to_y = neighbours()

    def copy(self, k, src, dst, to):
        return remote(src, dst, self.send.at[k], self.recv.at[k], to)

    def swap(self, b, a):
        at = 2 * b + a
        return self.copy(at, self.part.at[4 * b + 2 * (1 - self.c) + a], self.r1.at[at], self.to_c)

    def give(self, b):
        for a in range(2):
            self.swap(b, a).start()

    def along_x(self, b):
        at = 2 * b + 1 - self.x
        return self.copy(4 + b, self.chip.at[at, pl.ds(0, 64)], self.rx.at[b], self.to_x)

    def along_y(self, a):
        at = 2 * (1 - self.y) + a
        return self.copy(6 + a, self.chip.at[at, pl.ds(64, 64)], self.ry.at[a], self.to_y)

    def last_y(self):
        return self.copy(8, self.mine.at[0], self.late.at[0], self.to_y)

    def last_x(self):
        return self.copy(9, self.mine.at[1], self.late.at[1], self.to_x)

    def total(self, b, a):
        self.swap(b, a).wait_recv()
        at = 2 * b + a
        return self.part[4 * b + 2 * self.c + a].astype(F32) + self.r1[at].astype(F32)

    def take_far(self):
        b = 1 - self.y
        for a in (1 - self.x, self.x):
            self.chip[2 * b + a] = self.total(b, a).astype(BF16)
            self.along_y(a).start()
            if a is not self.x:
                self.along_x(b).start()

    def take_near(self):
        b, x = self.y, self.x
        self.chip[2 * b + 1 - x] = self.total(b, 1 - x).astype(BF16)
        self.along_x(b).start()
        self.out[...] = self.total(b, x)

    def middle(self):
        x, y = self.x, self.y
        self.along_x(1 - y).wait_recv()
        self.mine[0] = (
            self.chip[2 * (1 - y) + x, 0:64].astype(F32) + self.rx[1 - y].astype(F32)
        ).astype(BF16)
        self.last_y().start()
        self.along_y(1 - x).wait_recv()
        self.mine[1] = (
            self.chip[2 * y + 1 - x, 64:128].astype(F32) + self.ry[1 - x].astype(F32)
        ).astype(BF16)
        self.last_x().start()

    def finish(self):
        x, y = self.x, self.y
        self.along_x(y).wait_recv()
        self.along_y(x).wait_recv()
        self.last_y().wait_recv()
        self.last_x().wait_recv()
        self.out[0:64] += self.rx[y].astype(F32) + self.late[0].astype(F32)
        self.out[64:128] += self.ry[x].astype(F32) + self.late[1].astype(F32)

    def sent(self):
        for b in range(2):
            for a in range(2):
                self.swap(b, a).wait_send()
            self.along_x(b).wait_send()
            self.along_y(b).wait_send()
        self.last_y().wait_send()
        self.last_x().wait_send()


def seq_scratch(width):
    return [
        pltpu.VMEM((4, 128, width), BF16),
        pltpu.VMEM((4, 128, width), BF16),
        pltpu.VMEM((2, 64, width), BF16),
        pltpu.VMEM((2, 64, width), BF16),
        pltpu.VMEM((2, 64, width), BF16),
        pltpu.VMEM((2, 64, width), BF16),
        pltpu.VMEM((128, width), F32),
        dma(10),
        dma(10),
    ]


FWD_IN = ("tok", "cot", "seg", "wq", "gains", "wgu", "wd", "wo", "qg", "kg", "cos", "sin")
FWD_OUT = ("normed", "cot_all", "n2_all", "wq_all", "wo_all", "wd_all", "wgu_all", "qkv", "q",
           "kv", "segs", "o", "att", "mid", "g_one", "g_two",
           "gains_all")


def forward_kernel(names, *refs):
    m = dict(zip(names, refs))
    base, y, c, z, x = here()
    r = 2 * y + c
    to_c, to_x, to_y = neighbours()
    greet(layer_mates() + z_mates())
    rows, width = m["tok"].shape
    quarter_d, quarter_o = m["wd"].shape[0] // 4, m["wo"].shape[0] // 4
    own_rows = m["wq"].shape[1]
    half_cols = m["wgu"].shape[1] // 2
    piece = m["raw"].shape[2]
    part = piece // 2
    keep = m["keep"]
    own = 2 * z + x
    t_own = 2 * r + x

    def local_copy(k, src, dst):
        return pltpu.make_async_copy(src, dst, keep.at[k])

    tok = Gather(m["tok"], m["tok_all"], m["ga_s"], m["ga_r"], keep.at[0])
    cot = Gather(m["cot"], m["cot_all"], m["gb_s"], m["gb_r"], keep.at[1])
    segs = m["segs_v"]
    mates = layer_mates()

    def seg_copy(k):
        return remote(m["seg"], segs.at[z, t_own], m["sg_s"].at[k - 1], m["sg_r"].at[k - 1],
                      mates[k - 1])

    def gain_target(k):
        return device(base, y, c, (z + k // 2) % 4, (x + k) % 2)

    def gain_copy(k):
        return remote(m["gains"], m["gains_all"].at[own], m["gn_s"].at[k - 1],
                      m["gn_r"].at[k - 1], gain_target(k))

    wq = m["wq_v"]

    def wq_slot(zk, a):
        return wq.at[pl.ds((2 * zk + a) * own_rows, own_rows)]

    near = Along(m["wq"].at[x], lambda zk: wq_slot(zk, x), m["wa_s"], m["wa_r"])
    flip = Along(wq_slot(z, 1 - x), lambda zk: wq_slot(zk, 1 - x), m["wb_s"], m["wb_r"])
    over = remote(m["wq"].at[1 - x], wq_slot(z, x), m["wx_s"], m["wx_r"], to_x)
    over_in = remote(m["wq"].at[x], wq_slot(z, 1 - x), m["wx_s"], m["wx_r"], to_x)
    for k in range(1, 8):
        seg_copy(k).start()
    over.start()
    near.first()
    near.second()
    tok.start()
    local = [
        local_copy(2, m["wq"].at[x], wq_slot(z, x)),
        local_copy(3, m["gains"], m["gains_all"].at[own]),
        local_copy(4, m["seg"], segs.at[z, t_own]),
        local_copy(5, m["wgu"].at[:, pl.ds(piece * r, piece)], m["raw"].at[0]),
        local_copy(6, m["wgu"].at[:, pl.ds(half_cols + piece * r, piece)], m["raw"].at[1]),
    ]
    for copy in local:
        copy.start()
    for k in range(1, 8):
        gain_copy(k).start()
    out_q = Along(m["wo"].at[pl.ds(quarter_o * r, quarter_o)], lambda zk: m["zo"].at[zk],
                  m["wo_s"], m["wo_r"])
    down_q = Along(m["wd"].at[pl.ds(quarter_d * r, quarter_d)], lambda zk: m["zd"].at[zk],
                   m["wd_s"], m["wd_r"])
    quarters = [
        local_copy(7, m["wo"].at[pl.ds(quarter_o * r, quarter_o)], m["zo"].at[z]),
        local_copy(8, m["wd"].at[pl.ds(quarter_d * r, quarter_d)], m["zd"].at[z]),
    ]
    for copy in quarters:
        copy.start()
    over_in.wait_recv()
    flip.first()
    flip.second()
    out_q.first()
    out_q.second()

    def seg_up(k):
        return remote(segs.at[z], segs.at[z], m["su_s"].at[k - 1], m["su_r"].at[z],
                      device(base, y, c, (z + k) % 4, x))

    for k in range(1, 8):
        seg_copy(k).wait_recv()
    local[2].wait()
    for k in range(3, 0, -1):
        pl.when(z + k < 4)(lambda k=k: seg_up(k).start())

    local[3].wait()
    local[4].wait()
    gate, up = m["raw"].at[0], m["raw"].at[1]
    pair = m["pair"]
    main = (part // 128) * 128
    for a in range(2):
        at = a * (piece - main)
        pair[a, :, 0:main] = gate[:, at:at + main]
        pair[a, :, main:2 * main] = up[:, at:at + main]
    g_tile = gate[:, main:main + 128].astype(F32)
    u_tile = up[:, main:main + 128].astype(F32)
    low = lanes(g_tile.shape) < HEAD_DIM
    pair[0, :, 2 * main:] = jnp.where(low, g_tile, roll(u_tile, 64)).astype(BF16)
    pair[1, :, 2 * main:] = jnp.where(low, roll(g_tile, 64), u_tile).astype(BF16)
    wgu = m["wgu_all"]

    def gu_rows(zk, a):
        return wgu.at[pl.ds((2 * zk + a) * own_rows, own_rows)]

    def gu_unit(zk):
        return wgu.at[pl.ds(2 * zk * own_rows, 2 * own_rows)]

    cross = remote(pair.at[1 - x], gu_rows(z, x), m["xc_s"], m["xc_r"], to_x)
    cross_in = remote(pair.at[x], gu_rows(z, 1 - x), m["xc_s"], m["xc_r"], to_x)
    tok.forward()
    cross.start()
    mine = local_copy(5, pair.at[x], gu_rows(z, x))
    mine.start()
    near.forward()
    flip.forward()
    out_q.forward()
    tok.finish()
    cot.start()
    near.finish()
    flip.finish()
    for k in range(1, 8):
        at = 2 * ((z + 4 - k // 2) % 4) + (x + k) % 2
        remote(m["gains"], m["gains_all"].at[at], m["gn_s"].at[k - 1], m["gn_r"].at[k - 1],
               to_c).wait_recv()
    for k in (0, 1):
        local[k].wait()
    gather_gains = pltpu.make_async_copy(m["gains_all"], m["gains_v"], keep.at[3])
    gather_gains.start()
    gather_gains.wait()
    gain_rows = []
    for i in range(2):
        gain_rows.append(jnp.concatenate(
            [m["gains_v"][k, 0:16].astype(F32)[i:i + 1, :own_rows] for k in range(8)], axis=1))
    m["g_one"][...], m["g_two"][...] = gain_rows
    kv = m["kv_v"]
    q_all, qkv_all = m["q_v"], m["qkv_v"]
    qg, kg, cos, sin = m["qg"][...], m["kg"][...], m["cos"][...], m["sin"][...]
    span = 2 * rows

    def order(k):
        return (y + 1 + k) % 2, (c + 1 + k // 2) % 2

    def kv_copy(d, s):
        return remote(kv.at[z, s], kv.at[z, s], m["kv_s"].at[d - 1, s], m["kv_r"].at[z, s],
                      device(base, y, c, (z + d) % 4, x))

    def kv_arrival(zk, s):
        return remote(kv.at[zk, s], kv.at[zk, s], m["kv_s"].at[0, s], m["kv_r"].at[zk, s], to_x)

    def project(k, carry):
        b, e = order(k)
        s = 2 * b + e
        tokens = m["tok_all"][pl.ds(2 * s, 2)].reshape(span, width).astype(F32)
        normed = (tokens * inverse_rms(tokens) * m["g_one"][...]).astype(BF16)
        m["tok_all"][pl.ds(2 * s, 2)] = normed.reshape(2, rows, width)
        qkv = jnp.dot(normed, wq[...], preferred_element_type=F32)
        qkv_all[s] = qkv
        heads = split_heads(qkv[:, 0:128], qkv[:, 128:256])
        for j in range(GROUP):
            u = heads[j]
            u = rotated(u * head_inverse(u) * qg[0:1], cos, sin) * HEAD_DIM ** (-0.5)
            q_all[s, pl.ds(j * span, span)] = u.astype(BF16)
        u = heads[GROUP]
        u = rotated(u * head_inverse(u) * kg[0:1], cos, sin)
        v = jnp.concatenate([jnp.zeros((span, HEAD_DIM), F32), qkv[:, 256:320]], axis=1)
        kv[z, s] = (u + v).astype(BF16)
        for d in (3, 2, 1):
            pl.when(z + d < 4)(lambda d=d: kv_copy(d, s).start())
        return carry

    lax.fori_loop(0, 4, project, 0)
    exports = [local_copy(9, m["tok_all"], m["normed"]), local_copy(10, wq, m["wq_all"]),
               local_copy(11, qkv_all, m["qkv"]), local_copy(12, q_all, m["q"])]
    for copy in exports:
        copy.start()

    mine.wait()
    cross_in.wait_recv()
    gu = Along(gu_unit(z), gu_unit, m["wg_s"], m["wg_r"])
    down_q.first()
    gu.first()
    down_q.second()
    gu.second()
    cot.forward()

    def hand(k, zk, src, dst, sems, n):
        ss, rs = sems
        to = device(base, zk // 2, zk % 2, z, x)
        pl.when(r != zk)(lambda: remote(src.at[zk], dst.at[pl.ds(n * r, n)], ss.at[zk],
                                        rs.at[r], to).start())

        @pl.when(r == zk)
        def _():
            copy = local_copy(k, src.at[zk], dst.at[pl.ds(n * r, n)])
            copy.start()
            copy.wait()

    def handed(src, dst, sems, n):
        ss, rs = sems
        for rk in range(4):
            ref = dst.at[pl.ds(n * rk, n)]
            pl.when(r != rk)(lambda ref=ref, rk=rk: remote(
                src.at[0], ref, ss.at[0], rs.at[rk], to_x).wait_recv())

    def hand_sent(src, dst, sems, n):
        ss, rs = sems
        for zk in range(4):
            pl.when(r != zk)(lambda zk=zk: remote(
                src.at[zk], dst.at[pl.ds(0, n)], ss.at[zk], rs.at[0], to_x).wait_send())

    quarters[0].wait()
    out_q.finish()
    out_sems = (m["ho_s"], m["ho_r"])
    down_sems = (m["hd_s"], m["hd_r"])
    for zk in range(4):
        hand(13, zk, m["zo"], m["wo_v"], out_sems, quarter_o)

    for k in range(1, 4):
        pl.when(z - k >= 0)(lambda k=k: remote(
            segs.at[0], segs.at[(z + 4 - k) % 4], m["su_s"].at[k - 1],
            m["su_r"].at[(z + 4 - k) % 4], to_x).wait_recv())

    summed = SeqSum(m["part"], [m[n] for n in SUM_NAMES])
    o_all, att = m["o_v"], m["att_v"]
    acc, q_seg = m["acc"], m["q_seg"]

    def attend_one(k, carry):
        b, e = order(k)
        s = 2 * b + e
        q_seg[...] = segment_columns(segs, z, s)

        def block(zk, diagonal):
            tile = kv[zk, s]
            p = exp_scores(q_all[s], tile, q_seg[...], segment_row(segs, zk, s), diagonal)
            ones = jnp.where(lanes(tile.shape) < HEAD_DIM, 1.0, tile.astype(F32)).astype(BF16)
            add = jnp.dot(p.astype(BF16), ones, preferred_element_type=F32)
            if diagonal:
                acc[...] = add
            else:
                acc[...] += add

        block(z, True)

        def step(i, inner):
            zk = z - 1 - i
            kv_arrival(zk, s).wait_recv()
            block(zk, False)
            return inner

        lax.fori_loop(0, z, step, 0)
        total = acc[...]
        inv = 1.0 / jnp.where(lanes(total.shape) < HEAD_DIM, total, 1.0)
        inv = jnp.where(lanes(total.shape) < HEAD_DIM, inv, roll(inv, 64))
        o = total * inv
        o_all[s] = jnp.where(lanes(o.shape) < HEAD_DIM, inv, o)
        o = high_half(o)
        first, second, third = o[0:span], o[span:2 * span], o[2 * span:]
        att[s, :, 0:128] = (roll(first, 64) + second).astype(BF16)
        att[s, :, 128:192] = roll(third, 64)[:, 0:HEAD_DIM].astype(BF16)
        pl.when(k == 0)(lambda: handed(m["zo"], m["wo_v"], out_sems, quarter_o))
        out = jnp.dot(att[s], m["wo_v"][...], preferred_element_type=F32).astype(BF16)
        m["part"][pl.ds(2 * s, 2)] = out.reshape(2, rows, width)
        pl.when(k < 2)(lambda: summed.give(b))
        pl.when(k == 2)(summed.take_far)
        pl.when(k == 3)(summed.take_near)
        return carry

    lax.fori_loop(0, 4, attend_one, 0)
    more = [local_copy(14, o_all, m["o"]),
            local_copy(16, att, m["att"]), local_copy(17, kv, m["kv"]),
            local_copy(18, segs, m["segs"]), local_copy(19, m["wo_v"], m["wo_all"])]
    for copy in more:
        copy.start()
    summed.middle()
    down_q.forward()
    summed.finish()
    mid = m["tok"][...].astype(F32) + summed.out[...]
    m["mid"][...] = mid
    m["low"][...] = (mid * inverse_rms(mid) * m["g_two"][...]).astype(BF16)
    n2 = Gather(m["low"], m["n2_all"], m["gc_s"], m["gc_r"], keep.at[20])
    n2.start()
    cot.finish()
    n2.forward()
    gu.forward()
    quarters[1].wait()
    down_q.finish()
    for zk in range(4):
        hand(13, zk, m["zd"], m["wd_all"], down_sems, quarter_d)
    n2.finish()
    handed(m["zd"], m["wd_all"], down_sems, quarter_d)
    gu.finish()

    for along in (near, flip, out_q, down_q, gu):
        along.sent()
    summed.sent()
    cross.wait_send()
    over.wait_send()
    for k in range(1, 8):
        seg_copy(k).wait_send()
        gain_copy(k).wait_send()
    for k in range(1, 4):
        pl.when(z + k < 4)(lambda k=k: seg_up(k).wait_send())

    def kv_sent(s, carry):
        for d in (1, 2, 3):
            pl.when(z + d < 4)(lambda d=d: kv_copy(d, s).wait_send())
        return carry

    lax.fori_loop(0, 4, kv_sent, 0)
    hand_sent(m["zo"], m["wo_v"], out_sems, quarter_o)
    hand_sent(m["zd"], m["wd_all"], down_sems, quarter_d)
    for copy in exports + more:
        copy.wait()


SUM_NAMES = ("r1", "chip", "rx", "ry", "mine", "late", "sum_out", "sum_s", "sum_r")


def forward_call(tok, cot, seg, wq, gains, wgu, wd, wo, qg, kg, cos, sin):
    shape = jax.ShapeDtypeStruct
    rows, width = tok.shape
    span = 2 * rows
    own_rows = wq.shape[1]
    part = wgu.shape[1] // 16
    outs = {
        "normed": shape((8, rows, width), BF16),
        "cot_all": shape((8, rows, width), BF16),
        "n2_all": shape((8, rows, width), BF16),
        "wq_all": shape((width, HEAD_COLS), BF16),
        "wo_all": shape((Q_COLS, width), BF16),
        "wd_all": shape((part, width), BF16),
        "wgu_all": shape((width, 2 * part), BF16),
        "qkv": shape((4, span, HEAD_COLS), F32),
        "q": shape((4, GROUP * span, 128), BF16),
        "kv": shape((4, 4, span, 128), BF16),
        "segs": shape((4, 8) + seg.shape, seg.dtype),
        "o": shape((4, GROUP * span, 128), F32),
        "att": shape((4, span, Q_COLS), BF16),
        "mid": shape((rows, width), F32),
        "g_one": shape((1, width), F32),
        "g_two": shape((1, width), F32),
        "gains_all": shape((8,) + gains.shape, BF16),
    }
    sems = {
        "ga_s": dma(8), "ga_r": dma(8), "gb_s": dma(8), "gb_r": dma(8), "gc_s": dma(8),
        "gc_r": dma(8), "sg_s": dma(7), "sg_r": dma(7), "gn_s": dma(7), "gn_r": dma(7),
        "wa_s": dma(6), "wa_r": dma(4), "wb_s": dma(6), "wb_r": dma(4), "wo_s": dma(6),
        "wo_r": dma(4), "wd_s": dma(6), "wd_r": dma(4), "wg_s": dma(6), "wg_r": dma(4),
        "wx_s": pltpu.SemaphoreType.DMA, "wx_r": pltpu.SemaphoreType.DMA,
        "xc_s": pltpu.SemaphoreType.DMA, "xc_r": pltpu.SemaphoreType.DMA,
        "kv_s": pltpu.SemaphoreType.DMA((3, 4)), "kv_r": pltpu.SemaphoreType.DMA((4, 4)),
        "su_s": dma(3), "su_r": dma(4), "ho_s": dma(4), "ho_r": dma(4), "hd_s": dma(4),
        "hd_r": dma(4), "keep": dma(21),
    }
    buffers = {
        "tok_all": pltpu.VMEM((8, rows, width), BF16),
        "segs_v": pltpu.VMEM((4, 8) + seg.shape, seg.dtype),
        "wq_v": pltpu.VMEM((width, HEAD_COLS), BF16),
        "gains_v": pltpu.VMEM((8,) + gains.shape, BF16),
        "raw": pltpu.VMEM((2, own_rows, 2 * part), BF16),
        "pair": pltpu.VMEM((2, own_rows, 2 * part), BF16),
        "zo": pltpu.VMEM((4, wo.shape[0] // 4, width), BF16),
        "zd": pltpu.VMEM((4, wd.shape[0] // 4, width), BF16),
        "wo_v": pltpu.VMEM((Q_COLS, width), BF16),
        "qkv_v": pltpu.VMEM((4, span, HEAD_COLS), F32),
        "q_v": pltpu.VMEM((4, GROUP * span, 128), BF16),
        "kv_v": pltpu.VMEM((4, 4, span, 128), BF16),
        "o_v": pltpu.VMEM((4, GROUP * span, 128), F32),
        "att_v": pltpu.VMEM((4, span, Q_COLS), BF16),
        "acc": pltpu.VMEM((GROUP * span, 128), F32),
        "q_seg": pltpu.VMEM((span, span), jnp.int32),
        "part": pltpu.VMEM((8, rows, width), BF16),
        "low": pltpu.VMEM((rows, width), BF16),
    }
    buffers.update(zip(SUM_NAMES, seq_scratch(width)))
    names = FWD_IN + FWD_OUT + tuple(buffers) + tuple(sems)
    specs = {n: VMEM for n in ("tok", "seg", "gains", "wq", "qg", "kg", "cos", "sin")}
    outs_list = pl.pallas_call(
        functools.partial(forward_kernel, names),
        name="forward",
        out_shape=tuple(outs[n] for n in FWD_OUT),
        in_specs=[specs.get(n, ANY) for n in FWD_IN],
        out_specs=tuple(VMEM if n in ("mid", "g_one", "g_two") else ANY for n in FWD_OUT),
        scratch_shapes=list(buffers.values()) + list(sems.values()),
        compiler_params=params(0),
    )(tok, cot, seg, wq, gains, wgu, wd, wo, qg, kg, cos, sin)
    return dict(zip(FWD_OUT, outs_list))


class ZSum:
    def __init__(self, block, slot, send, recv):
        self.block, self.slot, self.send, self.recv = block, slot, send, recv
        self.base, self.y, self.c, self.z, self.x = here()

    def to(self, zk):
        return device(self.base, self.y, self.c, zk, self.x)

    def direct(self, zk):
        return remote(self.block(zk), self.slot(self.z), self.send.at[zk], self.recv.at[self.z],
                      self.to(zk))

    def far(self, zk, by):
        return remote(self.block(zk), self.slot(by), self.send.at[zk], self.recv.at[4],
                      self.to(by))

    def first(self, i):
        up = (self.z // 2)
        return up * i + (1 - up) * (3 - i)

    def start(self, zk):
        z = self.z
        late = ((z == 1) & (zk == 3)) | ((z == 2) & (zk == 0))
        end = ((z == 0) & (zk == 3)) | ((z == 3) & (zk == 0))
        pl.when((zk != z) & jnp.logical_not(late) & jnp.logical_not(end))(
            lambda: self.direct(zk).start())
        pl.when((z == 0) & (zk == 3))(lambda: self.far(3, 1).start())
        pl.when((z == 3) & (zk == 0))(lambda: self.far(0, 2).start())

    def merge(self, add):
        @pl.when(self.z == 1)
        def _():
            self.far(3, 1).wait_recv()
            add(self.block(3), self.slot(1))
            self.direct(3).start()

        @pl.when(self.z == 2)
        def _():
            self.far(0, 2).wait_recv()
            add(self.block(0), self.slot(2))
            self.direct(0).start()

    def arrive(self, zk):
        ref = self.slot(zk)
        remote(ref, ref, self.send.at[0], self.recv.at[zk], self.to(zk)).wait_recv()

    def middle(self):
        return (self.z == 1) | (self.z == 2)

    def wait(self):
        z = self.z

        @pl.when(self.middle())
        def _():
            for zk in (z - 1, z + 1, (z + 2) % 4):
                self.arrive(zk)

        @pl.when(jnp.logical_not(self.middle()))
        def _():
            for zk in (1, 2):
                self.arrive(zk)

    def collect(self, total):
        z = self.z
        pl.when(self.middle())(
            lambda: total([self.slot(zk) for zk in (z - 1, z + 1, (z + 2) % 4)]))
        pl.when(jnp.logical_not(self.middle()))(
            lambda: total([self.slot(zk) for zk in (1, 2)]))

    def sent(self):
        for zk in range(4):
            pl.when(self.z != zk)(lambda zk=zk: self.direct(zk).wait_send())


class RepShare:
    def __init__(self, at, send, recv):
        self.at, self.send, self.recv = at, send, recv
        _, self.y, self.c, _, _ = here()
        self.to_c, _, self.to_y = neighbours()
        self.r = 2 * self.y + self.c

    def copy(self, k, r, to):
        return remote(self.at(r), self.at(r), self.send.at[k], self.recv.at[k], to)

    def start(self):
        self.copy(0, self.r, self.to_y).start()
        self.copy(1, self.r, self.to_c).start()

    def forward(self):
        other = 2 * (1 - self.y) + self.c
        self.copy(0, other, self.to_y).wait_recv()
        self.copy(2, other, self.to_c).start()

    def finish(self):
        self.copy(1, 2 * self.y + 1 - self.c, self.to_c).wait_recv()
        self.copy(2, 2 * (1 - self.y) + 1 - self.c, self.to_c).wait_recv()

    def sent(self):
        self.copy(0, self.r, self.to_y).wait_send()
        self.copy(1, self.r, self.to_c).wait_send()
        self.copy(2, self.r, self.to_c).wait_send()


def first_dims(left, right):
    return lax.dot_general(left, right, (((0,), (0,)), ((), ())), preferred_element_type=F32)


def last_dims(left, right):
    return lax.dot_general(left, right, (((1,), (1,)), ((), ())), preferred_element_type=F32)


def head_back(dy, u, gain):
    inv = head_inverse(u)
    scaled = dy * gain
    gain_grad = jnp.sum(dy * u * inv, axis=0, keepdims=True)
    inner = jnp.sum(scaled * u, axis=-1, keepdims=True) * (1.0 / HEAD_DIM)
    return inv * scaled - u * (inv * inv * inv * inner), gain_grad


BWD_IN = ("n2", "cot_all", "wgu", "wd", "wo", "wq", "normed", "qkv", "q", "kv", "segs", "o", "att",
          "mid", "tok", "cot", "g_one", "g_two", "qg", "kg", "cos", "sin")
BWD_SMALL = ("mid", "tok", "cot", "g_one", "g_two", "qg", "kg", "cos", "sin")
BWD_OUT = ("mixed", "input_grad", "gu_g", "do_g", "qkv_g", "gains_g", "gu_slot",
           "do_slot")
SUM_B = tuple("input_grad" if n == "sum_out" else n + "_b" for n in SUM_NAMES)


def backward_kernel(names, *refs):
    m = dict(zip(names, refs))
    base, y, c, z, x = here()
    r = 2 * y + c
    to_c, to_x, to_y = neighbours()
    z_same = [device(base, y, c, (z + k) % 4, x) for k in range(1, 4)]
    mates = layer_mates()
    greet(mates + z_same)
    rows, width = m["tok"].shape
    span = 2 * rows
    keep = m["keep"]
    part = m["wd"].shape[0]
    main = (part // 128) * 128
    own_rows = m["wo"].shape[0]
    rest = part - main
    quarter_d, quarter_o = part // 4, own_rows // 4

    def order(k):
        return (y + 1 + k) % 2, (c + 1 + k // 2) % 2

    def load(k, src, dst):
        copy = pltpu.make_async_copy(src, dst, keep.at[k])
        copy.start()
        return copy

    n2, cot, wgu, wd = m["n2_v"], m["cot_v"], m["wgu_v"], m["wd_v"]
    first_loads = [
        load(0, m["wgu"], wgu), load(1, m["n2"], n2), load(2, m["cot_all"], cot),
        load(3, m["wd"].at[pl.ds(rest * x, main)], wd.at[pl.ds(0, main)]),
        load(4, m["wd"].at[pl.ds(main * (1 - x), rest)], wd.at[pl.ds(main, rest)]),
    ]
    later = [load(5 + i, m[n], m[n + "_v"]) for i, n in enumerate(
        ("wo", "wq", "qkv", "q", "kv", "segs", "o", "att"))]
    wd[pl.ds(main + rest, 128 - rest)] = jnp.zeros((128 - rest, width), BF16)
    for copy in first_loads:
        copy.wait()

    hidden, dgu, parts = m["hidden"], m["dgu"], m["part"]
    summed = SeqSum(parts, [m[n] for n in SUM_NAMES])

    def feed(k, carry):
        b, e = order(k)
        s = 2 * b + e
        at = pl.ds(s * span, span)
        gu = jnp.dot(n2[pl.ds(2 * s, 2)].reshape(span, width), wgu[...],
                     preferred_element_type=F32)
        dh = last_dims(cot[pl.ds(2 * s, 2)].reshape(span, width), wd[...])
        for lo, hi in ((0, main), (main, main + 128)):
            if lo == 0:
                gate, up = gu[:, :main], gu[:, main:2 * main]
            else:
                tile = gu[:, 2 * main:]
                gate, up = low_half(tile), low_half(roll(tile, 64))
            grad = dh[:, lo:hi]
            sigma = 1.0 / (1.0 + jnp.exp(-gate))
            active = gate * sigma
            hidden[at, lo:hi] = (active * up).astype(BF16)
            d_gate = grad * up * sigma * (1.0 + gate * (1.0 - sigma))
            d_up = grad * active
            if lo == 0:
                dgu[at, 0:main] = d_gate.astype(BF16)
                dgu[at, main:2 * main] = d_up.astype(BF16)
            else:
                dgu[at, 2 * main:] = (d_gate + roll(low_half(d_up), 64)).astype(BF16)
        out = last_dims(dgu[at], wgu[...]).astype(BF16)
        parts[pl.ds(2 * s, 2)] = out.reshape(2, rows, width)
        pl.when(k < 2)(lambda: summed.give(b))
        pl.when(k == 2)(summed.take_far)
        pl.when(k == 3)(summed.take_near)
        return carry

    lax.fori_loop(0, 4, feed, 0)

    ggu = m["ggu"]
    block_rows = 2 * own_rows
    gu_sum = ZSum(lambda zk: ggu.at[zk], lambda zk: m["gu_slot"].at[zk], m["zg_s"], m["zg_r"])

    def grad_gu(i, carry):
        zk = gu_sum.first(i)
        cols = pl.ds(pl.multiple_of(zk * block_rows, 128), block_rows)
        left = n2[:, :, cols].reshape(8 * rows, block_rows)
        ggu[zk] = first_dims(left, dgu[...]).astype(BF16)
        gu_sum.start(zk)
        return carry

    lax.fori_loop(0, 2, grad_gu, 0)
    summed.middle()
    lax.fori_loop(2, 4, grad_gu, 0)
    summed.finish()

    v = m["mid"][...]
    dv, gain_grad = norm_back(summed.out[...], v, inverse_rms(v), m["g_two"][...])
    m["row_two"][...] = gain_grad
    dmid = m["cot"][...].astype(F32) + dv
    m["dmid"][...] = dmid
    m["low"][...] = dmid.astype(BF16)
    branch = Gather(m["low"], m["db"], m["ga_s"], m["ga_r"], keep.at[13])
    branch.start()
    normed = n2
    copy_normed = load(1, m["normed"], normed)

    gdo, got = m["gdo"], m["got"]
    summed.sent()
    units = part // rest
    for j in range(0, main + 128, 128):
        grad = first_dims(hidden[:, j:j + 128], cot[...].reshape(8 * rows, width)).astype(BF16)
        for h in range(2):
            u = 2 * (j // 128) + h
            if u < units:
                to = (u + x) % units
                parts[to // 2, pl.ds(rest * (to % 2), rest)] = grad[rest * h:rest * (h + 1)]
    for i in range(4):
        lo = quarter_d * i
        first, last = lo // rows, (lo + quarter_d - 1) // rows + 1
        span_rows = parts[first:last].reshape((last - first) * rows, width)
        gdo[i, 0:quarter_d] = span_rows[lo - first * rows:lo - first * rows + quarter_d]
    branch.forward()

    mixed = SeqSum(parts, [m[n] for n in SUM_B])

    def down(k, carry):
        b, e = order(k)
        s = 2 * b + e
        out = jnp.dot(hidden[pl.ds(s * span, span)], wd[...], preferred_element_type=F32)
        parts[pl.ds(2 * s, 2)] = out.astype(BF16).reshape(2, rows, width)
        pl.when(k < 2)(lambda: mixed.give(b))
        pl.when(k == 2)(mixed.take_far)
        pl.when(k == 3)(mixed.take_near)
        return carry

    lax.fori_loop(0, 4, down, 0)
    branch.finish()

    def add_far(block, slot):
        copy = pltpu.make_async_copy(slot, dgu.at[pl.ds(0, block_rows)], keep.at[0])
        copy.start()
        copy.wait()
        block[...] = (block[...].astype(F32) + dgu[0:block_rows].astype(F32)).astype(BF16)

    gu_sum.merge(add_far)

    def hand(i, lo, n, ss, rs):
        return remote(gdo.at[i, pl.ds(lo, n)], got.at[r, pl.ds(lo, n)], ss.at[i], rs.at[r],
                      device(base, i // 2, i % 2, z, x))

    def hand_all(lo, n, ss, rs):
        for i in range(4):
            pl.when(r != i)(lambda i=i: hand(i, lo, n, ss, rs).start())
        got[r, lo:lo + n] = gdo[r, lo:lo + n]

    def handed(lo, n, ss, rs):
        for i in range(4):
            pl.when(r != i)(lambda i=i: remote(
                gdo.at[i, pl.ds(lo, n)], got.at[i, pl.ds(lo, n)], ss.at[i], rs.at[i],
                to_c).wait_recv())

    def hand_sent(lo, n, ss, rs):
        for i in range(4):
            pl.when(r != i)(lambda i=i: hand(i, lo, n, ss, rs).wait_send())

    hand_all(0, quarter_d, m["hd_s"], m["hd_r"])

    for copy in later:
        copy.wait()
    q_all, kv, segs, o_all, att = m["q_v"], m["kv_v"], m["segs_v"], m["o_v"], m["att_v"]
    wo, wq, qkv = m["wo_v"], m["wq_v"], m["qkv_v"]
    db, dkv, dqkv, acc, q_seg, do_v = m["db"], m["kv_v"], m["dqkv"], m["acc"], m["q_seg"], m["do"]
    own_kv = m["own_kv"]
    qg, kg, cos, sin = m["qg"][0:1], m["kg"][0:1], m["cos"][...], m["sin"][...]
    m["row_head"][...] = jnp.zeros((1, 128), F32)

    def kv_sum(s):
        return ZSum(lambda zk: dkv.at[zk, s], lambda zk: m["kv_slot"].at[zk, s],
                    m["zk_s"].at[s], m["zk_r"].at[s])

    def attend_one(k, carry):
        b, e = order(k)
        s = 2 * b + e
        grads = db[pl.ds(2 * s, 2)].reshape(span, width)
        d_att = last_dims(grads, wo[...])
        first = d_att[:, 0:128]
        third = jnp.concatenate([jnp.zeros((span, HEAD_DIM), F32), d_att[:, 128:192]], axis=1)
        d_out = jnp.concatenate([high_half(roll(first, 64)), high_half(first), third], axis=0)
        d_out = d_out.astype(BF16).astype(F32)
        o = o_all[s]
        d_out = (d_out * roll(o, 64)).astype(BF16)
        do_v[...] = d_out
        delta = jnp.sum(d_out.astype(F32) * high_half(o), axis=1, keepdims=True)
        q_seg[...] = segment_columns(segs, z, s)
        acc[...] = jnp.zeros_like(acc)

        def block(zk, diagonal):
            tile = kv[zk, s]
            q = q_all[s]
            d_out = do_v[...]
            p = exp_scores(q, tile, q_seg[...], segment_row(segs, zk, s), diagonal)
            ds = (p * (last_dims(d_out, tile) - delta)).astype(BF16)
            acc[...] += jnp.dot(ds, tile, preferred_element_type=F32)
            return first_dims(ds, q) + first_dims(p.astype(BF16), d_out)

        def step(zk, inner):
            dkv[zk, s] = block(zk, False).astype(BF16)
            pl.when((z == 3) & (zk == 0))(lambda: kv_sum(s).far(0, 2).start())
            pl.when(jnp.logical_not(((z == 3) | (z == 2)) & (zk == 0)))(
                lambda: kv_sum(s).direct(zk).start())
            return inner

        lax.fori_loop(0, z, step, 0)
        own_kv[s] = block(z, True)
        tiles = split_heads(qkv[s, :, 0:128], qkv[s, :, 128:256])
        back = []
        for j in range(GROUP):
            dy = rotated(low_half(acc[pl.ds(j * span, span)]) * HEAD_DIM ** (-0.5), cos, -sin)
            raw, gain_part = head_back(dy, tiles[j], qg)
            m["row_head"][...] += gain_part
            back.append(raw)
        dqkv[s, :, 0:128] = (back[0] + roll(back[1], 64)).astype(BF16)
        dqkv[s, :, 128:256] = back[2].astype(BF16)
        pl.when(k == 1)(mixed.middle)
        return carry

    lax.fori_loop(0, 4, attend_one, 0)

    for j in range(0, width, 512):
        cols = slice(j, j + 512)
        grad = first_dims(att[...].reshape(8 * rows, Q_COLS),
                          db[:, :, cols].reshape(8 * rows, 512)).astype(BF16)
        for i in range(4):
            gdo[i, quarter_d:quarter_d + quarter_o, cols] = grad[quarter_o * i:quarter_o * (i + 1)]
    hand_all(quarter_d, quarter_o, m["ho_s"], m["ho_r"])

    def kv_merge(k, carry):
        b, e = order(k)
        s = 2 * b + e

        @pl.when(z == 2)
        def _():
            one = kv_sum(s)
            one.far(0, 2).wait_recv()
            dkv[0, s] = (dkv[0, s].astype(F32) + m["kv_slot"][2, s].astype(F32)).astype(BF16)
            one.direct(0).start()
        return carry

    lax.fori_loop(0, 4, kv_merge, 0)
    mixed.finish()
    m["mixed"][...] = (m["mid"][...] + mixed.out[...]).astype(BF16)
    mixed.sent()

    handed(0, quarter_d, m["hd_s"], m["hd_r"])
    handed(quarter_d, quarter_o, m["ho_s"], m["ho_r"])
    do_sum = ZSum(lambda zk: got.at[zk], lambda zk: m["do_slot"].at[zk], m["zd_s"], m["zd_r"])

    def start_do(i, carry):
        do_sum.start(do_sum.first(i))
        return carry

    lax.fori_loop(0, 4, start_do, 0)

    inputs = SeqSum(parts, [m[n] for n in SUM_NAMES])

    def finish_one(k, carry):
        b, e = order(k)
        s = 2 * b + e
        for d in (1, 2):
            @pl.when(z + d < 4)
            def _():
                kv_sum(s).arrive(z + d)
                own_kv[s] += m["kv_slot"][z + d, s].astype(F32)
        total = own_kv[s]
        u = split_heads(qkv[s, :, 0:128], qkv[s, :, 128:256])[GROUP]
        dy = rotated(low_half(total), cos, -sin)
        raw, gain_part = head_back(dy, u, kg)
        m["row_head"][...] += roll(gain_part, 64)
        tile = dqkv[s, :, 128:256].astype(F32)
        dqkv[s, :, 128:256] = (low_half(tile) + roll(raw, 64)).astype(BF16)
        dqkv[s, :, 256:320] = roll(total, 64)[:, 0:HEAD_DIM].astype(BF16)
        out = last_dims(dqkv[s], wq[...]).astype(BF16)
        parts[pl.ds(2 * s, 2)] = out.reshape(2, rows, width)
        pl.when(k < 2)(lambda: inputs.give(b))
        pl.when(k == 2)(inputs.take_far)
        pl.when(k == 3)(inputs.take_near)
        return carry

    lax.fori_loop(0, 4, finish_one, 0)
    copy_normed.wait()
    gqkv = m["gqkv"]
    qkv_sum = ZSum(lambda zk: gqkv.at[zk], lambda zk: m["qkv_slot"].at[zk], m["zq_s"], m["zq_r"])

    def grad_qkv(i, carry):
        zk = qkv_sum.first(i)
        cols = pl.ds(pl.multiple_of(zk * block_rows, 128), block_rows)
        left = normed[:, :, cols].reshape(8 * rows, block_rows)
        gqkv[zk] = first_dims(left, dqkv[...].reshape(8 * rows, HEAD_COLS)).astype(BF16)
        qkv_sum.start(zk)
        return carry

    lax.fori_loop(0, 4, grad_qkv, 0)
    inputs.middle()

    def add_vmem(block, slot):
        block[...] = (block[...].astype(F32) + slot[...].astype(F32)).astype(BF16)

    hand_sent(0, quarter_d, m["hd_s"], m["hd_r"])
    hand_sent(quarter_d, quarter_o, m["ho_s"], m["ho_r"])

    def add_do(block, slot):
        copy = pltpu.make_async_copy(slot, gdo.at[0], keep.at[0])
        copy.start()
        copy.wait()
        block[...] = (block[...].astype(F32) + gdo[0].astype(F32)).astype(BF16)

    do_sum.merge(add_do)

    t_own = 2 * r + x
    gu_sum.sent()
    gu_sum.wait()

    def total_gu(slots):
        copies = []
        for i, slot in enumerate(slots):
            copy = pltpu.make_async_copy(slot, dgu.at[pl.ds(0, block_rows)], keep.at[0])
            copy.start()
            copy.wait()
            ggu[z] = (ggu[z].astype(F32) + dgu[0:block_rows].astype(F32)).astype(BF16)

    gu_sum.collect(total_gu)
    gu_out, qkv_out, do_out = m["gu_g"], m["qkv_g"], m["do_g"]

    def swap(src, out, ss, rs):
        return remote(src.at[z, pl.ds(own_rows * (1 - x), own_rows)], out.at[t_own], ss, rs, to_x)

    def keep_own(k, src, out):
        return pltpu.make_async_copy(src.at[z, pl.ds(own_rows * x, own_rows)], out.at[t_own],
                                     keep.at[k])

    def swapped(src, out, ss, rs):
        return remote(src.at[z, pl.ds(own_rows * x, own_rows)], out.at[2 * r + 1 - x], ss, rs,
                      to_x)

    gu_swap = swap(ggu, gu_out, m["xg_s"], m["xg_r"])
    gu_swap.start()
    gu_keep = keep_own(14, ggu, gu_out)
    gu_keep.start()
    gu_keep.wait()
    gu_share = RepShare(lambda i: gu_out.at[pl.ds(2 * i, 2)], m["rg_s"], m["rg_r"])

    inputs.finish()
    v = m["tok"][...].astype(F32)
    dv, gain_grad = norm_back(inputs.out[...], v, inverse_rms(v), m["g_one"][...])
    m["input_grad"][...] = m["dmid"][...] + dv

    rows_v = m["rows_v"]
    rows_v[0, 0:1] = gain_grad
    rows_v[0, 1:2] = m["row_two"][...]
    rows_v[0, 2:3, 0:128] = m["row_head"][...]

    def gain_copy(k):
        return remote(rows_v.at[0], rows_v.at[k], m["gn_s"].at[k - 1], m["gn_r"].at[k - 1],
                      mates[k - 1])

    for k in range(1, 8):
        gain_copy(k).start()

    swapped(ggu, gu_out, m["xg_s"], m["xg_r"]).wait_recv()
    gu_share.start()
    qkv_sum.merge(add_vmem)
    for k in range(1, 8):
        gain_copy(k).wait_recv()
    total = rows_v[0]
    for k in range(1, 8):
        total = total + rows_v[k]
    z_rows = m["z_rows"]
    z_rows[0] = total

    def gain_z(k):
        return remote(z_rows.at[0], z_rows.at[k], m["gz_s"].at[k - 1], m["gz_r"].at[k - 1],
                      z_same[k - 1])

    for k in range(1, 4):
        gain_z(k).start()

    do_sum.wait()

    def total_do(slots):
        copies = [pltpu.make_async_copy(slot, gdo.at[i], keep.at[i])
                  for i, slot in enumerate(slots)]
        for copy in copies:
            copy.start()
        for copy in copies:
            copy.wait()
        total = got[z].astype(F32)
        for i in range(len(slots)):
            total = total + gdo[i].astype(F32)
        m["do_own"][...] = total.astype(BF16)

    do_sum.collect(total_do)
    do_keep = pltpu.make_async_copy(m["do_own"], do_out.at[r], keep.at[15])
    do_keep.start()
    do_keep.wait()
    do_share = RepShare(lambda i: do_out.at[i], m["rd_s"], m["rd_r"])
    do_share.start()
    gu_share.forward()

    qkv_sum.wait()

    def total_qkv(slots):
        total = gqkv[z].astype(F32)
        for slot in slots:
            total = total + slot[...].astype(F32)
        m["qkv_own"][0] = total.astype(BF16)

    qkv_sum.collect(total_qkv)
    own = m["qkv_own"]
    qkv_swap = remote(own.at[0, pl.ds(own_rows * (1 - x), own_rows)], qkv_out.at[t_own],
                      m["xq_s"], m["xq_r"], to_x)
    qkv_swap.start()
    qkv_keep = pltpu.make_async_copy(own.at[0, pl.ds(own_rows * x, own_rows)],
                                     qkv_out.at[t_own], keep.at[16])
    qkv_keep.start()
    qkv_keep.wait()
    qkv_share = RepShare(lambda i: qkv_out.at[pl.ds(2 * i, 2)], m["rq_s"], m["rq_r"])
    remote(own.at[0, pl.ds(0, own_rows)], qkv_out.at[2 * r + 1 - x], m["xq_s"], m["xq_r"],
           to_x).wait_recv()
    qkv_share.start()
    do_share.forward()
    for k in range(1, 4):
        gain_z(k).wait_recv()
    m["gains_g"][...] = z_rows[0] + z_rows[1] + z_rows[2] + z_rows[3]
    qkv_share.forward()
    for share in (gu_share, do_share, qkv_share):
        share.finish()

    for share in (gu_share, do_share, qkv_share):
        share.sent()
    gu_swap.wait_send()
    qkv_swap.wait_send()
    for k in range(1, 8):
        gain_copy(k).wait_send()
    for k in range(1, 4):
        gain_z(k).wait_send()
    do_sum.sent()
    qkv_sum.sent()
    inputs.sent()

    def kv_sent(s, carry):
        for zk in range(3):
            pl.when(z > zk)(lambda zk=zk: kv_sum(s).direct(zk).wait_send())
        return carry

    lax.fori_loop(0, 4, kv_sent, 0)


def backward_call(f, tok, cot, qg, kg, cos, sin):
    shape = jax.ShapeDtypeStruct
    rows, width = tok.shape
    span = 2 * rows
    own_rows, part = f["wo_all"].shape[0], f["wd_all"].shape[0]
    cols = f["wgu_all"].shape[1]
    quarter = (part + own_rows) // 4
    args = {"n2": f["n2_all"], "cot_all": f["cot_all"], "wgu": f["wgu_all"], "wd": f["wd_all"],
            "wo": f["wo_all"], "wq": f["wq_all"], "tok": tok, "cot": cot, "qg": qg, "kg": kg,
            "cos": cos, "sin": sin}
    for n in ("normed", "qkv", "q", "kv", "segs", "o", "att", "mid", "g_one", "g_two"):
        args[n] = f[n]
    outs = {
        "mixed": shape((rows, width), BF16),
        "input_grad": shape((rows, width), F32),
        "gu_g": shape((8, own_rows, cols), BF16),
        "do_g": shape((4, quarter, width), BF16),
        "qkv_g": shape((8, own_rows, HEAD_COLS), BF16),
        "gains_g": shape((8, width), F32),
        "gu_slot": shape((4, 2 * own_rows, cols), BF16),
        "do_slot": shape((4, quarter, width), BF16),
    }
    same = lambda n, dtype=None: pltpu.VMEM(args[n].shape, dtype or args[n].dtype)
    buffers = {
        "n2_v": same("n2"), "cot_v": same("cot_all"), "wgu_v": same("wgu"),
        "wd_v": pltpu.VMEM(((part // 128 + 1) * 128, width), BF16),
        "wo_v": same("wo"), "wq_v": same("wq"), "qkv_v": same("qkv"), "q_v": same("q"),
        "kv_v": same("kv"), "segs_v": same("segs"), "o_v": same("o"), "att_v": same("att"),
        "hidden": pltpu.VMEM((8 * rows, (part // 128 + 1) * 128), BF16),
        "dgu": pltpu.VMEM((8 * rows, cols), BF16),
        "part": pltpu.VMEM((8, rows, width), BF16),
        "ggu": pltpu.VMEM((4, 2 * own_rows, cols), BF16),
        "gdo": pltpu.VMEM((4, quarter, width), BF16),
        "got": pltpu.VMEM((4, quarter, width), BF16),
        "do_own": pltpu.VMEM((quarter, width), BF16),
        "db": pltpu.VMEM((8, rows, width), BF16),
        "dmid": pltpu.VMEM((rows, width), F32),
        "low": pltpu.VMEM((rows, width), BF16),
        "kv_slot": same("kv"),
        "own_kv": pltpu.VMEM((4, span, 128), F32),
        "dqkv": pltpu.VMEM((4, span, HEAD_COLS), BF16),
        "acc": pltpu.VMEM((GROUP * span, 128), F32),
        "do": pltpu.VMEM((GROUP * span, 128), BF16),
        "q_seg": pltpu.VMEM((span, span), jnp.int32),
        "gqkv": pltpu.VMEM((4, 2 * own_rows, HEAD_COLS), BF16),
        "qkv_slot": pltpu.VMEM((4, 2 * own_rows, HEAD_COLS), BF16),
        "qkv_own": pltpu.VMEM((1, 2 * own_rows, HEAD_COLS), BF16),
        "row_two": pltpu.VMEM((1, width), F32),
        "row_head": pltpu.VMEM((1, 128), F32),
        "rows_v": pltpu.VMEM((8, 8, width), F32),
        "z_rows": pltpu.VMEM((4, 8, width), F32),
    }
    buffers.update(zip(SUM_NAMES, seq_scratch(width)))
    buffers.update((n, b) for n, b in zip(SUM_B, seq_scratch(width)) if n != "input_grad")
    two = pltpu.SemaphoreType.DMA
    sems = {
        "ga_s": dma(8), "ga_r": dma(8), "zg_s": dma(4), "zg_r": dma(5), "zd_s": dma(4),
        "zd_r": dma(5), "zq_s": dma(4), "zq_r": dma(5), "zk_s": two((4, 4)), "zk_r": two((4, 5)),
        "hd_s": dma(4), "hd_r": dma(4), "ho_s": dma(4), "ho_r": dma(4), "xg_s": two, "xg_r": two,
        "xq_s": two, "xq_r": two, "rg_s": dma(3), "rg_r": dma(3), "rd_s": dma(3), "rd_r": dma(3),
        "rq_s": dma(3), "rq_r": dma(3), "gn_s": dma(7), "gn_r": dma(7), "gz_s": dma(3),
        "gz_r": dma(3), "keep": dma(17),
    }
    names = BWD_IN + BWD_OUT + tuple(buffers) + tuple(sems)
    outs_list = pl.pallas_call(
        functools.partial(backward_kernel, names),
        name="backward",
        out_shape=tuple(outs[n] for n in BWD_OUT),
        in_specs=[VMEM if n in BWD_SMALL else ANY for n in BWD_IN],
        out_specs=tuple(VMEM if n in ("mixed", "input_grad", "gains_g") else ANY
                        for n in BWD_OUT),
        scratch_shapes=list(buffers.values()) + list(sems.values()),
        compiler_params=params(1, 63),
    )(*[args[n] for n in BWD_IN])
    return dict(zip(BWD_OUT, outs_list))


def order_kernel(gu, do, qkv, gu_o, down_o, out_o, qkv_o):
    which = pl.program_id(1)
    cols = gu.shape[2]
    main = cols // 2 // 128 * 128
    piece = cols
    quarter_d = down_o.shape[0]
    low = lanes((gu.shape[1], 128)) < HEAD_DIM
    first, second = gu[0, :, 2 * main:].astype(F32), gu[1, :, 2 * main:].astype(F32)

    @pl.when(which == 0)
    def _():
        gu_o[:, 0:main] = gu[0, :, 0:main].astype(F32)
        gu_o[:, main:main + 128] = jnp.where(low, first, roll(second, 64))
        gu_o[:, main + 128:] = gu[1, :, 0:main].astype(F32)
        down_o[...] = do[0, 0:quarter_d].astype(F32)

    @pl.when(which == 1)
    def _():
        gu_o[:, 0:main] = gu[0, :, main:2 * main].astype(F32)
        gu_o[:, main:main + 128] = jnp.where(low, roll(first, 64), second)
        gu_o[:, main + 128:] = gu[1, :, main:2 * main].astype(F32)
        out_o[...] = do[0, quarter_d:].astype(F32)

    @pl.when(which == 0)
    def _():
        i = pl.program_id(0)
        a, b = qkv[0].astype(F32), qkv[1].astype(F32)
        at = lambda start, n: pl.ds(pl.multiple_of(start, 128), n)
        q_cols, kv_cols = HEADS * HEAD_DIM, KV_HEADS * HEAD_DIM
        half = lambda v, w: jnp.where(low, v, w)
        a1, a2, b0, b1 = a[:, 128:256], a[:, 256:], b[:, 0:128], b[:, 128:256]
        qkv_o[:, at(i * 2 * Q_COLS, 128)] = a[:, 0:128]
        qkv_o[:, at(i * 2 * Q_COLS + 128, 128)] = half(a1, roll(b0, 64))
        qkv_o[:, at(i * 2 * Q_COLS + 256, 128)] = half(roll(b0, 64), roll(b1, 64))
        qkv_o[:, at(q_cols + i * 128, 128)] = half(roll(a1, 64), b1)
        qkv_o[:, at(q_cols + kv_cols + i * 128, 128)] = jnp.concatenate([a2, b[:, 256:]], axis=1)


def order_call(gu, do, qkv, part):
    shape = jax.ShapeDtypeStruct
    _, own_rows, cols = gu.shape
    width = do.shape[2]
    quarter_d = part // 4
    quarter_o = do.shape[1] - quarter_d
    return pl.pallas_call(
        order_kernel,
        name="final_order",
        grid=(4, 2),
        out_shape=(
            shape((own_rows, 8 * cols), F32), shape((part, width), F32),
            shape((4 * quarter_o, width), F32),
            shape((own_rows, (HEADS + 2 * KV_HEADS) * HEAD_DIM), F32)),
        in_specs=[
            pl.BlockSpec((2, own_rows, cols), lambda i, w: (i, 0, 0)),
            pl.BlockSpec((1, do.shape[1], width), lambda i, w: (i, 0, 0)),
            pl.BlockSpec((2, own_rows, qkv.shape[2]), lambda i, w: (i, 0, 0))],
        out_specs=(
            pl.BlockSpec((own_rows, cols), lambda i, w: (0, 4 * w + i)),
            pl.BlockSpec((quarter_d, width), lambda i, w: (i, 0)),
            pl.BlockSpec((quarter_o, width), lambda i, w: (i, 0)),
            pl.BlockSpec((own_rows, (HEADS + 2 * KV_HEADS) * HEAD_DIM), lambda i, w: (0, 0))),
        compiler_params=pltpu.CompilerParams(
            dimension_semantics=("arbitrary", "arbitrary"), vmem_limit_bytes=48 * 2**20),
    )(gu, do, qkv)


def rope_tables(positions):
    half = HEAD_DIM // 2
    freq = jnp.exp(-jnp.log(THETA) * jnp.arange(half, dtype=F32) * 2.0 / HEAD_DIM)
    angle = positions.astype(F32)[:, None] * freq[None, :]
    cos, sin = jnp.cos(angle), jnp.sin(angle)
    zero = jnp.zeros_like(cos)
    return jnp.concatenate([cos, cos, zero, zero], 1), jnp.concatenate([-sin, sin, zero, zero], 1)


def over_quads(array):
    reps = lax.axis_size("rep")
    if reps == 4:
        return array
    rows = [[j + 4 * q for q in range(reps // 4)] for j in range(4)]
    return lax.psum(array, "rep", axis_index_groups=rows)


def local(tokens, attn_gain, w_qkv, q_gain, k_gain, w_out, ffn_gain, w_gate_up, w_down,
          cotangent, segment_ids):
    rows, width = tokens.shape
    _, y, c, z, x = here()
    r = 2 * y + c
    q_width, kv_width = HEADS * HEAD_DIM, KV_HEADS * HEAD_DIM
    own_rows = w_qkv.shape[0]
    span = 2 * rows
    cut = lax.dynamic_slice_in_dim

    q_pair = cut(w_qkv, 2 * Q_COLS * r, 2 * Q_COLS, 1)
    k_pair = cut(w_qkv, q_width + 2 * HEAD_DIM * r, 2 * HEAD_DIM, 1)
    v_pair = cut(w_qkv, q_width + kv_width + 2 * HEAD_DIM * r, 2 * HEAD_DIM, 1)
    wq = jnp.stack([
        jnp.concatenate([
            q_pair[:, i * Q_COLS:(i + 1) * Q_COLS],
            k_pair[:, i * HEAD_DIM:(i + 1) * HEAD_DIM],
            v_pair[:, i * HEAD_DIM:(i + 1) * HEAD_DIM]], 1)
        for i in range(2)])
    gains = jnp.zeros((16, 256), BF16)
    gains = gains.at[0, :own_rows].set(attn_gain).at[1, :own_rows].set(ffn_gain)
    seg = jnp.broadcast_to(segment_ids[None, :], (8, rows))
    cos, sin = rope_tables(span * z + jnp.arange(span, dtype=jnp.int32))

    def padded(gain):
        return jnp.zeros((8, 128), F32).at[:, :HEAD_DIM].set(gain.astype(F32)[None])

    qg, kg = padded(q_gain), padded(k_gain)
    f = forward_call(tokens, cotangent, seg, wq, gains, w_gate_up, w_down, w_out, qg, kg, cos, sin)
    g = backward_call(f, tokens, cotangent, qg, kg, cos, sin)
    gu, down, out, qkv = order_call(
        over_quads(g["gu_g"]), over_quads(g["do_g"]), over_quads(g["qkv_g"]), w_down.shape[0])
    gains_sum = over_quads(g["gains_g"])
    place = 2 * z + x
    gain_one = cut(gains_sum[0], place * own_rows, own_rows, 0)
    gain_two = cut(gains_sum[1], place * own_rows, own_rows, 0)
    return (g["mixed"], g["input_grad"], gain_one, qkv, gains_sum[2, :HEAD_DIM],
            gains_sum[2, HEAD_DIM:2 * HEAD_DIM], out, gain_two, gu, down)


def solution(mesh):
    rows, split = P(("rep", "grp"), None), P("grp", None)
    return jax.shard_map(
        local,
        mesh=mesh,
        in_specs=(rows, P("grp"), split, P(), P(), split, P("grp"), split, split, rows,
                  P(("rep", "grp"))),
        out_specs=(rows, rows, P("grp"), split, P(), P(), split, P("grp"), split, split),
        check_vma=False,
    )
```

```python
import functools

import jax
import jax.numpy as jnp
from jax import lax
from jax.experimental import pallas as pl
from jax.experimental.pallas import tpu as pltpu
from jax.sharding import PartitionSpec as P

HEADS = 24
KV_HEADS = 8
HEAD_DIM = 64
GROUP = HEADS // KV_HEADS
Q_COLS = GROUP * HEAD_DIM
HEAD_COLS = Q_COLS + 2 * HEAD_DIM

EPS = 1e-05
THETA = 1000000.0
MESH = pl.DeviceIdType.MESH
F32 = jnp.float32
BF16 = jnp.bfloat16

VMEM = pl.BlockSpec(memory_space=pltpu.VMEM)
ANY = pl.BlockSpec(memory_space=pl.ANY)


def here():
    rep = lax.axis_index("rep")
    grp = lax.axis_index("grp")
    r = rep % 4
    return rep - r, r // 2, r % 2, grp // 2, grp % 2


def device(base, y, c, z, x):
    return {"rep": base + 2 * y + c, "grp": 2 * z + x}


def remote(src, dst, send, recv, to):
    return pltpu.make_async_remote_copy(
        src_ref=src, dst_ref=dst, send_sem=send, recv_sem=recv, device_id=to, device_id_type=MESH
    )


def greet(targets):
    barrier = pltpu.get_barrier_semaphore()
    for to in targets:
        pl.semaphore_signal(barrier, inc=1, device_id=to, device_id_type=MESH)
    pl.semaphore_wait(barrier, len(targets))


def neighbours():
    base, y, c, z, x = here()
    to_c = device(base, y, 1 - c, z, x)
    to_x = device(base, y, c, z, 1 - x)
    to_y = device(base, 1 - y, c, z, x)
    return to_c, to_x, to_y


GATHER_SEMS = 8


class Gather:
    def __init__(self, src, out, send, recv, local):
        self.src, self.out, self.send, self.recv, self.local = src, out, send, recv, local
        _, y, c, _, x = here()
        self.to_c, self.to_x, self.to_y = neighbours()
        slot = lambda a, b, d: 4 * a + 2 * b + d
        self.own = slot(y, c, x)
        self.at_c, self.at_x, self.at_y = slot(y, 1 - c, x), slot(y, c, 1 - x), slot(1 - y, c, x)
        self.at_xc, self.at_yc = slot(y, 1 - c, 1 - x), slot(1 - y, 1 - c, x)
        self.at_xy, self.at_xyc = slot(1 - y, c, 1 - x), slot(1 - y, 1 - c, 1 - x)
        self.half = src.shape[0] // 2

    def part(self, ref, k):
        return ref.at[pl.ds(k * self.half, self.half)]

    def copy(self, k, src, dst, to):
        return remote(src, dst, self.send.at[k], self.recv.at[k], to)

    def start(self):
        out, src = self.out, self.src
        self.keep = pltpu.make_async_copy(src, out.at[self.own], self.local)
        self.keep.start()
        self.sent = [
            self.copy(0, src, out.at[self.own], self.to_x),
            self.copy(1, src, out.at[self.own], self.to_y),
            self.copy(2, src, out.at[self.own], self.to_c),
        ]
        for copy in self.sent:
            copy.start()

    def forward(self):
        out = self.out
        self.copy(0, self.src, out.at[self.at_x], self.to_x).wait_recv()
        first = self.part(out.at[self.at_x], 0)
        self.go(3, first, first, self.to_y)
        self.go(4, out.at[self.at_x], out.at[self.at_x], self.to_c)
        self.copy(1, self.src, out.at[self.at_y], self.to_y).wait_recv()
        second = self.part(out.at[self.at_y], 1)
        self.go(5, second, second, self.to_x)
        self.go(6, out.at[self.at_y], out.at[self.at_y], self.to_c)

    def go(self, k, src, dst, to):
        copy = self.copy(k, src, dst, to)
        copy.start()
        self.sent.append(copy)

    def finish(self):
        out = self.out
        first = self.part(out.at[self.at_xy], 0)
        second = self.part(out.at[self.at_xy], 1)
        self.copy(3, first, first, self.to_y).wait_recv()
        self.copy(5, second, second, self.to_x).wait_recv()
        self.go(7, out.at[self.at_xy], out.at[self.at_xy], self.to_c)
        for k, at in ((2, self.at_c), (4, self.at_xc), (6, self.at_yc), (7, self.at_xyc)):
            self.copy(k, out.at[at], out.at[at], self.to_c).wait_recv()
        for copy in self.sent:
            copy.wait_send()
        self.keep.wait()


def dma(n):
    return pltpu.SemaphoreType.DMA((n,))


def params(cid, limit=60):
    return pltpu.CompilerParams(
        collective_id=cid, has_side_effects=True, vmem_limit_bytes=limit * 2**20
    )


def inverse_rms(v):
    return lax.rsqrt(jnp.mean(v * v, axis=-1, keepdims=True) + EPS)


def norm_back(dy, v, inv, gain):
    scaled = dy * gain
    gain_grad = jnp.sum(dy * v * inv, axis=0, keepdims=True)
    inner = jnp.mean(scaled * v, axis=-1, keepdims=True)
    return inv * scaled - v * inv * inv * inv * inner, gain_grad


def when(cond):
    return pl.when(cond)


def lanes(shape):
    return lax.broadcasted_iota(jnp.int32, shape, len(shape) - 1)


def roll(v, by):
    return pltpu.roll(v, by % v.shape[-1], v.ndim - 1)


class Along:
    def __init__(self, src, slot, send, recv):
        self.src, self.slot, self.send, self.recv = src, slot, send, recv
        self.base, self.y, self.c, self.z, self.x = here()

    def at(self, zk, x):
        return device(self.base, self.y, self.c, zk, x)

    def copy(self, d):
        zk = (self.z + d + 4) % 4
        return remote(self.src, self.slot(self.z), self.send.at[d + 2], self.recv.at[self.z],
                      self.at(zk, self.x))

    def fits(self, d):
        return (self.z + d >= 0) & (self.z + d < 4)

    def first(self):
        for d in (2, -2):
            pl.when(self.fits(d))(lambda d=d: self.copy(d).start())
        pl.when(self.z == 2)(lambda: self.copy(1).start())
        pl.when(self.z == 1)(lambda: self.copy(-1).start())

    def second(self):
        pl.when(self.z < 2)(lambda: self.copy(1).start())
        pl.when(self.z >= 2)(lambda: self.copy(-1).start())

    def arrival(self, zk):
        ref = self.slot(zk)
        return remote(ref, ref, self.send.at[0], self.recv.at[zk], self.at(self.z, 1 - self.x))

    def passed(self, zk, to):
        ref = self.slot(zk)
        return remote(ref, ref, self.send.at[5], self.recv.at[zk], self.at(to, self.x))

    def forward(self):
        @pl.when(self.z == 2)
        def _():
            self.arrival(0).wait_recv()
            self.passed(0, 3).start()

        @pl.when(self.z == 1)
        def _():
            self.arrival(3).wait_recv()
            self.passed(3, 0).start()

    def wait(self, zk):
        early = ((self.z == 2) & (zk == 0)) | ((self.z == 1) & (zk == 3))
        due = jnp.logical_not(early) & (self.z != zk)
        pl.when(due)(lambda: self.arrival(zk).wait_recv())

    def finish(self):
        for zk in range(4):
            self.wait(zk)

    def sent(self):
        for d in (2, -2, 1, -1):
            pl.when(self.fits(d))(lambda d=d: self.copy(d).wait_send())
        pl.when(self.z == 2)(lambda: self.passed(0, 3).wait_send())
        pl.when(self.z == 1)(lambda: self.passed(3, 0).wait_send())


class Chain:
    def __init__(self, slot, send, recv):
        self.slot, self.send, self.recv = slot, send, recv
        self.base, self.y, self.c, self.z, self.x = here()

    def copy(self, k, zk, to):
        return remote(self.slot(zk), self.slot(zk), self.send.at[k], self.recv.at[zk],
                      device(self.base, self.y, self.c, to, self.x))

    def arrive(self, zk):
        self.copy(0, zk, self.z).wait_recv()

    def inner(self):
        return (self.z == 1) | (self.z == 2)

    def start_ends(self):
        pl.when(self.z == 0)(lambda: self.copy(0, 0, 1).start())
        pl.when(self.z == 3)(lambda: self.copy(1, 3, 2).start())

    def start_inner(self):
        z = self.z

        @pl.when(self.inner())
        def _():
            self.copy(0, z, z + 1).start()
            self.copy(1, z, z - 1).start()

    def pass_ends(self):
        @pl.when(self.z == 1)
        def _():
            self.arrive(0)
            self.copy(2, 0, 2).start()

        @pl.when(self.z == 2)
        def _():
            self.arrive(3)
            self.copy(3, 3, 1).start()

    def pass_inner(self):
        @pl.when(self.z == 1)
        def _():
            self.arrive(2)
            self.copy(3, 2, 0).start()

        @pl.when(self.z == 2)
        def _():
            self.arrive(1)
            self.copy(2, 1, 3).start()

    def second(self):
        self.pass_ends()
        self.pass_inner()

    def third(self):
        @pl.when(self.z == 2)
        def _():
            self.arrive(0)
            self.copy(4, 0, 3).start()

        @pl.when(self.z == 1)
        def _():
            self.arrive(3)
            self.copy(4, 3, 0).start()

    def finish(self):
        pl.when(self.z == 0)(lambda: [self.arrive(zk) for zk in (1, 2, 3)] and None)
        pl.when(self.z == 3)(lambda: [self.arrive(zk) for zk in (2, 1, 0)] and None)

    def sent(self):
        z = self.z
        pl.when(z < 3)(lambda: self.copy(0, z, z + 1).wait_send())
        pl.when(z > 0)(lambda: self.copy(1, z, z - 1).wait_send())

        @pl.when(self.inner())
        def _():
            self.copy(2, z - 1, z + 1).wait_send()
            self.copy(3, z + 1, z - 1).wait_send()
            self.copy(4, z, z + 1).wait_send()


class ChainSum:
    def __init__(self, block, slot, send, recv):
        self.block, self.slot, self.send, self.recv = block, slot, send, recv
        self.base, self.y, self.c, self.z, self.x = here()

    def copy(self, zk, to, at):
        return remote(self.block(zk), self.slot(at), self.send.at[zk], self.recv.at[at],
                      device(self.base, self.y, self.c, to, self.x))

    def arrive(self, at):
        self.copy(0, self.z, at).wait_recv()

    def start(self):
        @pl.when(self.z == 0)
        def _():
            for zk, at in ((3, 3), (2, 2), (1, 4)):
                self.copy(zk, 1, at).start()

        @pl.when(self.z == 3)
        def _():
            for zk in (0, 1, 2):
                self.copy(zk, 2, zk).start()

    def start_one(self, zk):
        for to, at in ((3, 3), (2, 2), (1, 4)):
            pl.when((self.z == 0) & (zk == to))(
                lambda to=to, at=at: self.copy(to, 1, at).start())
        for to in (0, 1, 2):
            pl.when((self.z == 3) & (zk == to))(lambda to=to: self.copy(to, 2, to).start())

    def first_hop(self, add):
        @pl.when(self.z == 1)
        def _():
            for zk, at in ((3, 3), (2, 4)):
                self.arrive(zk)
                add(self.block(zk), self.slot(zk))
                self.copy(zk, 2, at).start()

        @pl.when(self.z == 2)
        def _():
            for zk in (0, 1):
                self.arrive(zk)
                add(self.block(zk), self.slot(zk))
                self.copy(zk, 1, zk).start()

    def second_hop(self, add):
        @pl.when(self.z == 1)
        def _():
            self.arrive(0)
            add(self.block(0), self.slot(0))
            self.copy(0, 0, 0).start()

        @pl.when(self.z == 2)
        def _():
            self.arrive(3)
            add(self.block(3), self.slot(3))
            self.copy(3, 3, 4).start()

    def collect(self, total):
        z = self.z

        def take(ats):
            for at in ats:
                self.arrive(at)
            total([self.slot(at) for at in ats])

        pl.when(z == 0)(lambda: take([0]))
        pl.when(z == 3)(lambda: take([4]))
        pl.when((z == 1) | (z == 2))(lambda: take([z, 4]))

    def sent(self):
        for zk in range(4):
            pl.when(self.z != zk)(lambda zk=zk: self.copy(zk, 0, 0).wait_send())


def layer_mates():
    base, y, c, z, x = here()
    return [
        device(base, (y + k // 4) % 2, (c + k // 2) % 2, z, (x + k) % 2) for k in range(1, 8)
    ]


def z_mates():
    base, y, c, z, x = here()
    return [device(base, y, c, (z + k // 2) % 4, (x + k) % 2) for k in range(2, 8)]


def rotated(u, cos, sin):
    lane = lanes(u.shape)
    return u * cos + jnp.where(lane < 32, roll(u, -32), roll(u, 32)) * sin


def low_half(v):
    return jnp.where(lanes(v.shape) < HEAD_DIM, v, 0.0)


def high_half(v):
    return jnp.where(lanes(v.shape) >= HEAD_DIM, v, 0.0)


def split_heads(tile_a, tile_b):
    return [low_half(tile_a), low_half(roll(tile_a, 64)), low_half(tile_b),
            low_half(roll(tile_b, 64))]


def head_inverse(u):
    return lax.rsqrt(jnp.sum(u * u, axis=-1, keepdims=True) * (1.0 / HEAD_DIM) + EPS)


def exp_scores(q, kv, q_seg, k_seg, diagonal):
    s = lax.dot_general(q, kv, (((1,), (1,)), ((), ())), preferred_element_type=F32)
    allowed = q_seg == k_seg
    if diagonal:
        row = lax.broadcasted_iota(jnp.int32, allowed.shape, 0)
        col = lax.broadcasted_iota(jnp.int32, allowed.shape, 1)
        allowed = allowed & (col <= row)
    n = allowed.shape[0]
    return jnp.concatenate([
        jnp.where(allowed, jnp.exp(s[n * j:n * (j + 1)]), 0.0) for j in range(GROUP)], axis=0)


def segment_row(segs, zk, s):
    return jnp.concatenate([segs[zk, 2 * s, 0:1], segs[zk, 2 * s + 1, 0:1]], axis=1)


def segment_columns(segs, zk, s):
    parts = []
    for i in range(2):
        row = jnp.broadcast_to(segs[zk, 2 * s + i, 0:1], (128, 128))
        parts.append(jnp.transpose(row))
    col = jnp.concatenate(parts, axis=0)
    return jnp.concatenate([col, col], axis=1)


class SeqSum:
    def __init__(self, part, scratch):
        self.part = part
        (self.r1, self.chip, self.rx, self.ry, self.mine, self.late, self.out,
         self.send, self.recv) = scratch
        _, self.y, self.c, _, self.x = here()
        self.to_c, self.to_x, self.to_y = neighbours()

    def copy(self, k, src, dst, to):
        return remote(src, dst, self.send.at[k], self.recv.at[k], to)

    def swap(self, b, a):
        at = 2 * b + a
        return self.copy(at, self.part.at[4 * b + 2 * (1 - self.c) + a], self.r1.at[at], self.to_c)

    def give(self, b):
        for a in range(2):
            self.swap(b, a).start()

    def along_x(self, b):
        at = 2 * b + 1 - self.x
        return self.copy(4 + b, self.chip.at[at, pl.ds(0, 64)], self.rx.at[b], self.to_x)

    def along_y(self, a):
        at = 2 * (1 - self.y) + a
        return self.copy(6 + a, self.chip.at[at, pl.ds(64, 64)], self.ry.at[a], self.to_y)

    def last_y(self):
        return self.copy(8, self.mine.at[0], self.late.at[0], self.to_y)

    def last_x(self):
        return self.copy(9, self.mine.at[1], self.late.at[1], self.to_x)

    def total(self, b, a):
        self.swap(b, a).wait_recv()
        at = 2 * b + a
        return self.part[4 * b + 2 * self.c + a].astype(F32) + self.r1[at].astype(F32)

    def take_far(self):
        b = 1 - self.y
        for a in (1 - self.x, self.x):
            self.chip[2 * b + a] = self.total(b, a).astype(BF16)
            self.along_y(a).start()
            if a is not self.x:
                self.along_x(b).start()

    def take_near(self):
        b, x = self.y, self.x
        self.chip[2 * b + 1 - x] = self.total(b, 1 - x).astype(BF16)
        self.along_x(b).start()
        self.out[...] = self.total(b, x)

    def middle(self):
        x, y = self.x, self.y
        self.along_x(1 - y).wait_recv()
        self.mine[0] = (
            self.chip[2 * (1 - y) + x, 0:64].astype(F32) + self.rx[1 - y].astype(F32)
        ).astype(BF16)
        self.last_y().start()
        self.along_y(1 - x).wait_recv()
        self.mine[1] = (
            self.chip[2 * y + 1 - x, 64:128].astype(F32) + self.ry[1 - x].astype(F32)
        ).astype(BF16)
        self.last_x().start()

    def finish(self):
        x, y = self.x, self.y
        self.along_x(y).wait_recv()
        self.along_y(x).wait_recv()
        self.last_y().wait_recv()
        self.last_x().wait_recv()
        self.out[0:64] += self.rx[y].astype(F32) + self.late[0].astype(F32)
        self.out[64:128] += self.ry[x].astype(F32) + self.late[1].astype(F32)

    def given(self):
        for b in range(2):
            for a in range(2):
                self.swap(b, a).wait_send()

    def passed(self):
        for b in range(2):
            self.along_x(b).wait_send()
            self.along_y(b).wait_send()
        self.last_y().wait_send()
        self.last_x().wait_send()

    def sent(self):
        self.given()
        self.passed()


def seq_scratch(width):
    return [
        pltpu.VMEM((4, 128, width), BF16),
        pltpu.VMEM((4, 128, width), BF16),
        pltpu.VMEM((2, 64, width), BF16),
        pltpu.VMEM((2, 64, width), BF16),
        pltpu.VMEM((2, 64, width), BF16),
        pltpu.VMEM((2, 64, width), BF16),
        pltpu.VMEM((128, width), F32),
        dma(10),
        dma(10),
    ]


def first_dims(left, right):
    return lax.dot_general(left, right, (((0,), (0,)), ((), ())), preferred_element_type=F32)


def last_dims(left, right):
    return lax.dot_general(left, right, (((1,), (1,)), ((), ())), preferred_element_type=F32)


def swiglu(gate, up, grad):
    sigma = 1.0 / (1.0 + jnp.exp(-gate))
    active = gate * sigma
    d_gate = grad * up * sigma * (1.0 + gate * (1.0 - sigma))
    return ((active * up).astype(BF16), d_gate.astype(BF16), (grad * active).astype(BF16))


class DirectBoth:
    def __init__(self, half, slot, send, recv):
        self.half, self.slot, self.send, self.recv = half, slot, send, recv
        self.base, self.y, self.c, self.z, self.x = here()

    def copy(self, zk, a):
        return remote(self.half(zk, a), self.slot(self.z, self.x), self.send.at[zk, a],
                      self.recv.at[self.z, self.x], device(self.base, self.y, self.c, zk, a))

    def start(self, zk):
        self.copy(zk, 1 - self.x).start()
        pl.when(zk != self.z)(lambda: self.copy(zk, self.x).start())

    def arrive(self, zk, a):
        ref = self.slot(zk, a)
        remote(ref, ref, self.send.at[0, 0], self.recv.at[zk, a],
               device(self.base, self.y, self.c, self.z, 1 - self.x)).wait_recv()

    def sent(self):
        for k in range(1, 8):
            self.copy((self.z + k // 2) % 4, (self.x + k) % 2).wait_send()


class RepShare:
    def __init__(self, at, send, recv):
        self.at, self.send, self.recv = at, send, recv
        _, self.y, self.c, _, _ = here()
        self.to_c, _, self.to_y = neighbours()
        self.r = 2 * self.y + self.c

    def copy(self, k, r, to):
        return remote(self.at(r), self.at(r), self.send.at[k], self.recv.at[k], to)

    def start(self):
        self.copy(0, self.r, self.to_y).start()
        self.copy(1, self.r, self.to_c).start()

    def forward(self):
        other = 2 * (1 - self.y) + self.c
        self.copy(0, other, self.to_y).wait_recv()
        self.copy(2, other, self.to_c).start()

    def finish(self):
        self.copy(1, 2 * self.y + 1 - self.c, self.to_c).wait_recv()
        self.copy(2, 2 * (1 - self.y) + 1 - self.c, self.to_c).wait_recv()

    def sent(self):
        self.copy(0, self.r, self.to_y).wait_send()
        self.copy(1, self.r, self.to_c).wait_send()
        self.copy(2, self.r, self.to_c).wait_send()


def head_back(dy, u, gain):
    inv = head_inverse(u)
    scaled = dy * gain
    gain_grad = jnp.sum(dy * u * inv, axis=0, keepdims=True)
    inner = jnp.sum(scaled * u, axis=-1, keepdims=True) * (1.0 / HEAD_DIM)
    return inv * scaled - u * (inv * inv * inv * inner), gain_grad


def block_kernel(names, *refs):
    m = dict(zip(names, refs))
    base, y, c, z, x = here()
    r = 2 * y + c
    to_c, to_x, to_y = neighbours()
    greet(layer_mates() + z_mates())
    rows, width = m["tok"].shape
    quarter_o = m["wo"].shape[0] // 4
    own_rows = m["wq"].shape[1]
    half_cols = m["wgu"].shape[1] // 2
    piece = half_cols // 4
    part = piece // 2
    main = part // 128 * 128
    half_a = main // 2
    rows_a, rows_b, rest = half_a // 4, (part - half_a) // 4, part - main
    keep = m["keep"]
    own = 2 * z + x
    t_own = 2 * r + x

    def local_copy(k, src, dst):
        return pltpu.make_async_copy(src, dst, keep.at[k])

    hidden, dgu, wgu, wd_v = m["hidden"], m["dgu"], m["wgu_v"], m["wd_v"]
    cols_a = 2 * half_a
    cols_b = dgu.shape[1] - cols_a

    def raw(i):
        return dgu.at[pl.ds(i * own_rows, own_rows)]

    def pair(a, first, n):
        return dgu.at[pl.ds((2 + a) * own_rows, own_rows), pl.ds(first, n)]

    def loaded(k, src, dst):
        copy = local_copy(k, src, dst)
        copy.start()
        return copy

    tok = Gather(m["tok"], m["tok_all"], m["ga_s"], m["ga_r"], keep.at[0])
    cot = Gather(m["cot"], m["cot_v"], m["gb_s"], m["gb_r"], keep.at[1])
    segs = m["segs_v"]
    mates = layer_mates()

    def seg_copy(k):
        return remote(m["seg"], segs.at[z, t_own], m["sg_s"].at[k - 1], m["sg_r"].at[k - 1],
                      mates[k - 1])

    def gain_target(k):
        return device(base, y, c, (z + k // 2) % 4, (x + k) % 2)

    def gain_copy(k):
        return remote(m["gains"], m["gains_all"].at[own], m["gn_s"].at[k - 1],
                      m["gn_r"].at[k - 1], gain_target(k))

    wq = m["wq_v"]

    def wq_slot(zk, a):
        return wq.at[pl.ds((2 * zk + a) * own_rows, own_rows)]

    near = Along(m["wq"].at[x], lambda zk: wq_slot(zk, x), m["wa_s"], m["wa_r"])
    flip = Along(wq_slot(z, 1 - x), lambda zk: wq_slot(zk, 1 - x), m["wb_s"], m["wb_r"])
    over = remote(m["wq"].at[1 - x], wq_slot(z, x), m["wx_s"], m["wx_r"], to_x)
    over_in = remote(m["wq"].at[x], wq_slot(z, 1 - x), m["wx_s"], m["wx_r"], to_x)
    for k in range(1, 8):
        seg_copy(k).start()
    over.start()
    near.first()
    near.second()
    tok.start()
    local = [
        local_copy(2, m["wq"].at[x], wq_slot(z, x)),
        local_copy(3, m["gains"], m["gains_all"].at[own]),
        local_copy(4, m["seg"], segs.at[z, t_own]),
        local_copy(5, m["wgu"].at[:, pl.ds(piece * r, piece)], raw(0)),
        local_copy(6, m["wgu"].at[:, pl.ds(half_cols + piece * r, piece)], raw(1)),
    ]
    for copy in local:
        copy.start()
    for k in range(1, 8):
        gain_copy(k).start()
    out_q = Along(m["wo"].at[pl.ds(quarter_o * r, quarter_o)], lambda zk: m["zo"].at[zk],
                  m["wo_s"], m["wo_r"])
    last = r // 3
    tail_at = rest * x + half_a + rows_b * r + 16 - last * x * part
    quarters = [
        local_copy(7, m["wo"].at[pl.ds(quarter_o * r, quarter_o)], m["zo"].at[z]),
        local_copy(8, m["wd"].at[pl.ds(rest * x + rows_a * r, rows_a)], m["za"].at[z]),
        local_copy(13, m["wd"].at[pl.ds(rest * x + half_a + rows_b * r, 16)],
                   m["zb"].at[z, pl.ds(0, 16)]),
        local_copy(14, m["wd"].at[pl.ds(tail_at, rows_b - 16)],
                   m["zb"].at[z, pl.ds(16, rows_b - 16)]),
    ]
    for copy in quarters:
        copy.start()
    over_in.wait_recv()
    flip.first()
    flip.second()
    out_q.first()
    out_q.second()

    def seg_up(k):
        return remote(segs.at[z], segs.at[z], m["su_s"].at[k - 1], m["su_r"].at[z],
                      device(base, y, c, (z + k) % 4, x))

    for k in range(1, 8):
        seg_copy(k).wait_recv()
    local[2].wait()
    for k in range(3, 0, -1):
        pl.when(z + k < 4)(lambda k=k: seg_up(k).start())

    local[3].wait()
    local[4].wait()
    gate, up = raw(0), raw(1)
    for a in range(2):
        at = a * (piece - main)
        for i, src in enumerate((gate, up)):
            pair(a, i * half_a, half_a)[...] = src[:, at:at + half_a]
            pair(a, cols_a + i * half_a, half_a)[...] = src[:, at + half_a:at + main]
    g_tile = gate[:, main:main + 128].astype(F32)
    u_tile = up[:, main:main + 128].astype(F32)
    low = lanes(g_tile.shape) < HEAD_DIM
    pair(0, 2 * main, 128)[...] = jnp.where(low, g_tile, roll(u_tile, 64)).astype(BF16)
    pair(1, 2 * main, 128)[...] = jnp.where(low, roll(g_tile, 64), u_tile).astype(BF16)

    def unit(first, n):
        return lambda zk: wgu.at[pl.ds(2 * zk * own_rows, 2 * own_rows), pl.ds(first, n)]

    def crossing(first, n, ss, rs, k):
        cols = pl.ds(first, n)
        mine = wgu.at[pl.ds((2 * z + x) * own_rows, own_rows), cols]
        other = wgu.at[pl.ds((2 * z + 1 - x) * own_rows, own_rows), cols]
        return (remote(pair(1 - x, first, n), mine, ss, rs, to_x),
                remote(pair(x, first, n), other, ss, rs, to_x),
                local_copy(k, pair(x, first, n), mine))

    cross_a, cross_a_in, mine_a = crossing(0, cols_a, m["xa_s"], m["xa_r"], 5)
    cross_b, cross_b_in, mine_b = crossing(cols_a, cols_b, m["xb_s"], m["xb_r"], 6)
    gate_a = Chain(unit(0, cols_a), m["ca_s"], m["ca_r"])
    gate_b = Chain(unit(cols_a, cols_b), m["cb_s"], m["cb_r"])
    down_a = Chain(lambda zk: m["za"].at[zk], m["da_s"], m["da_r"])
    down_b = Chain(lambda zk: m["zb"].at[zk], m["db_s"], m["db_r"])
    tok.forward()
    for copy in (cross_a, mine_a, cross_b, mine_b):
        copy.start()
    near.forward()
    flip.forward()
    out_q.forward()
    tok.finish()
    cot.start()
    near.finish()
    flip.finish()
    for k in range(1, 8):
        at = 2 * ((z + 4 - k // 2) % 4) + (x + k) % 2
        remote(m["gains"], m["gains_all"].at[at], m["gn_s"].at[k - 1], m["gn_r"].at[k - 1],
               to_c).wait_recv()
    for k in (0, 1):
        local[k].wait()
    gather_gains = pltpu.make_async_copy(m["gains_all"], m["gains_v"], keep.at[3])
    gather_gains.start()
    gather_gains.wait()
    gain_rows = []
    for i in range(2):
        gain_rows.append(jnp.concatenate(
            [m["gains_v"][k, 0:16].astype(F32)[i:i + 1, :own_rows] for k in range(8)], axis=1))
    m["g_one"][...], m["g_two"][...] = gain_rows
    kv = m["kv_v"]
    q_all, qkv_all = m["q_v"], m["qkv_v"]
    qg, kg, cos, sin = m["qg"][...], m["kg"][...], m["cos"][...], m["sin"][...]
    span = 2 * rows

    def order(k):
        return (y + 1 + k) % 2, (c + 1 + k // 2) % 2

    def kv_copy(d, s):
        return remote(kv.at[z, s], kv.at[z, s], m["kv_s"].at[d - 1, s], m["kv_r"].at[z, s],
                      device(base, y, c, (z + d) % 4, x))

    def kv_arrival(zk, s):
        return remote(kv.at[zk, s], kv.at[zk, s], m["kv_s"].at[0, s], m["kv_r"].at[zk, s], to_x)

    def project(k, carry):
        b, e = order(k)
        s = 2 * b + e
        tokens = m["tok_all"][pl.ds(2 * s, 2)].reshape(span, width).astype(F32)
        normed = (tokens * inverse_rms(tokens) * m["g_one"][...]).astype(BF16)
        m["tok_all"][pl.ds(2 * s, 2)] = normed.reshape(2, rows, width)
        qkv = jnp.dot(normed, wq[...], preferred_element_type=F32)
        qkv_all[s] = qkv[:, 0:256]
        heads = split_heads(qkv[:, 0:128], qkv[:, 128:256])
        for j in range(GROUP):
            u = heads[j]
            u = rotated(u * head_inverse(u) * qg[0:1], cos, sin) * HEAD_DIM ** (-0.5)
            q_all[s, pl.ds(j * span, span)] = u.astype(BF16)
        u = heads[GROUP]
        u = rotated(u * head_inverse(u) * kg[0:1], cos, sin)
        v = jnp.concatenate([jnp.zeros((span, HEAD_DIM), F32), qkv[:, 256:320]], axis=1)
        kv[z, s] = (u + v).astype(BF16)
        for d in (3, 2, 1):
            pl.when(z + d < 4)(lambda d=d: kv_copy(d, s).start())
        return carry

    lax.fori_loop(0, 4, project, 0)
    for copy in quarters[1:]:
        copy.wait()
    down_a.start_ends()
    down_a.start_inner()
    for copy in (mine_a, mine_b):
        copy.wait()
    cross_a_in.wait_recv()
    gate_a.start_ends()
    gate_a.start_inner()
    cross_b_in.wait_recv()
    down_b.start_ends()
    gate_b.start_ends()
    cot.forward()

    def hand(k, zk, src, dst, sems, n):
        ss, rs = sems
        to = device(base, zk // 2, zk % 2, z, x)
        pl.when(r != zk)(lambda: remote(src.at[zk], dst.at[pl.ds(n * r, n)], ss.at[zk],
                                        rs.at[r], to).start())

        @pl.when(r == zk)
        def _():
            copy = local_copy(k, src.at[zk], dst.at[pl.ds(n * r, n)])
            copy.start()
            copy.wait()

    def handed(src, dst, sems, n):
        ss, rs = sems
        for rk in range(4):
            ref = dst.at[pl.ds(n * rk, n)]
            pl.when(r != rk)(lambda ref=ref, rk=rk: remote(
                src.at[0], ref, ss.at[0], rs.at[rk], to_x).wait_recv())

    def hand_sent(src, dst, sems, n):
        ss, rs = sems
        for zk in range(4):
            pl.when(r != zk)(lambda zk=zk: remote(
                src.at[zk], dst.at[pl.ds(0, n)], ss.at[zk], rs.at[0], to_x).wait_send())

    quarters[0].wait()
    out_q.finish()
    out_sems = (m["ho_s"], m["ho_r"])
    a_sems, b_sems = (m["hd_s"], m["hd_r"]), (m["hb_s"], m["hb_r"])
    for zk in range(4):
        hand(13, zk, m["zo"], m["wo_v"], out_sems, quarter_o)

    for k in range(1, 4):
        pl.when(z - k >= 0)(lambda k=k: remote(
            segs.at[0], segs.at[(z + 4 - k) % 4], m["su_s"].at[k - 1],
            m["su_r"].at[(z + 4 - k) % 4], to_x).wait_recv())

    summed = SeqSum(m["part"], [m[n] for n in SUM_NAMES])
    inv_all, att = m["inv_v"], m["att_v"]
    acc, q_seg = m["acc"], m["q_seg"]

    def attend_one(k, carry):
        b, e = order(k)
        s = 2 * b + e
        q_seg[...] = segment_columns(segs, z, s)

        def block(zk, diagonal):
            tile = kv[zk, s]
            p = exp_scores(q_all[s], tile, q_seg[...], segment_row(segs, zk, s), diagonal)
            ones = jnp.where(lanes(tile.shape) < HEAD_DIM, 1.0, tile.astype(F32)).astype(BF16)
            add = jnp.dot(p.astype(BF16), ones, preferred_element_type=F32)
            if diagonal:
                acc[...] = add
            else:
                acc[...] += add

        block(z, True)

        def step(i, inner):
            zk = z - 1 - i
            kv_arrival(zk, s).wait_recv()
            block(zk, False)
            return inner

        lax.fori_loop(0, z, step, 0)
        total = acc[...]
        inv = 1.0 / jnp.where(lanes(total.shape) < HEAD_DIM, total, 1.0)
        inv = jnp.where(lanes(total.shape) < HEAD_DIM, inv, roll(inv, 64))
        o = high_half(total * inv)
        lane = lanes((span, 128))
        inv_all[s] = jnp.where(lane < 32, inv[0:span], jnp.where(
            lane < 64, inv[span:2 * span], inv[2 * span:]))
        first, second, third = o[0:span], o[span:2 * span], o[2 * span:]
        att[s, :, 0:128] = (roll(first, 64) + second).astype(BF16)
        att[s, :, 128:192] = roll(third, 64)[:, 0:HEAD_DIM].astype(BF16)
        pl.when(k == 0)(lambda: handed(m["zo"], m["wo_v"], out_sems, quarter_o))
        out = jnp.dot(att[s], m["wo_v"][...], preferred_element_type=F32).astype(BF16)
        m["part"][pl.ds(2 * s, 2)] = out.reshape(2, rows, width)
        pl.when(k < 2)(lambda: summed.give(b))
        pl.when(k == 2)(summed.take_far)
        pl.when(k == 3)(summed.take_near)
        return carry

    lax.fori_loop(0, 4, attend_one, 0)
    down_a.second()
    gate_a.second()
    summed.middle()
    down_a.third()
    summed.finish()
    mid = m["tok"][...].astype(F32) + summed.out[...]
    m["mid"][...] = mid
    m["low"][...] = (mid * inverse_rms(mid) * m["g_two"][...]).astype(BF16)
    n2_all, cot_all = m["n2_v"], m["cot_v"]
    n2 = Gather(m["low"], n2_all, m["gc_s"], m["gc_r"], keep.at[20])
    n2.start()
    cot.finish()
    gate_a.third()
    down_b.pass_ends()
    gate_b.pass_ends()
    down_b.start_inner()
    gate_b.start_inner()
    n2.forward()
    down_a.finish()
    wda, wdb = wd_v.at[pl.ds(0, half_a)], wd_v.at[pl.ds(half_a, part - half_a)]
    for zk in range(4):
        hand(13, zk, m["za"], wda, a_sems, rows_a)
    n2.finish()
    gate_a.finish()
    handed(m["za"], wda, a_sems, rows_a)
    cross_a.wait_send()
    cross_b.wait_send()

    def feed_first(s, carry):
        at = pl.ds(pl.multiple_of(s * span, span), span)
        gu = jnp.dot(n2_all[pl.ds(2 * s, 2)].reshape(span, width), wgu[:, :cols_a],
                     preferred_element_type=F32)
        dh = last_dims(cot_all[pl.ds(2 * s, 2)].reshape(span, width), wd_v[0:half_a])
        hidden[at, 0:half_a], dgu[at, 0:half_a], dgu[at, half_a:cols_a] = swiglu(
            gu[:, :half_a], gu[:, half_a:], dh)
        return carry

    lax.fori_loop(0, 4, feed_first, 0)
    down_b.third()
    gate_b.third()
    down_b.pass_inner()
    gate_b.pass_inner()
    block_rows = 2 * own_rows
    gga, gdo, got_a = m["gga"], m["gdo"], m["got_a"]
    gate_sum = ChainSum(lambda zk: gga.at[zk], lambda at: m["gga_slot"].at[at], m["ys_s"],
                        m["ys_r"])
    down_sum = ChainSum(lambda zk: got_a.at[zk], lambda at: m["gda_slot"].at[at], m["yd_s"],
                        m["yd_r"])

    def grad_gate(zk, carry):
        cols = pl.ds(pl.multiple_of(zk * block_rows, 128), block_rows)
        left = n2_all[:, :, cols].reshape(8 * rows, block_rows)
        gga[zk] = first_dims(left, dgu[:, :cols_a]).astype(BF16)
        return carry

    lax.fori_loop(0, 4, grad_gate, 0)
    gate_sum.start()
    for j in range(0, half_a, 128):
        grad = first_dims(hidden[:, j:j + 128], cot_all[...].reshape(8 * rows, width))
        for h in range(128 // rows_a):
            gdo[j // rows_a + h, 0:rows_a] = grad[rows_a * h:rows_a * (h + 1)].astype(BF16)

    def spread_from(i):
        return gdo.at[i, pl.ds(0, rows_a)]

    def spread(i):
        return remote(spread_from(i), got_a.at[r], m["ha_s"].at[i], m["ha_r"].at[r],
                      device(base, i // 2, i % 2, z, x))

    for i in range(4):
        pl.when(r != i)(lambda i=i: spread(i).start())
    got_a[r] = gdo[r, 0:rows_a]

    def add(block, slot):
        block[...] = (block[...].astype(F32) + slot[...].astype(F32)).astype(BF16)

    gate_sum.first_hop(add)
    down_b.finish()
    for zk in range(4):
        hand(13, zk, m["zb"], wdb, b_sems, rows_b)
    gate_b.finish()
    handed(m["zb"], wdb, b_sems, rows_b)
    for i in range(4):
        pl.when(r != i)(lambda i=i: remote(
            spread_from(i), got_a.at[i], m["ha_s"].at[i], m["ha_r"].at[i], to_c).wait_recv())
    down_sum.start()
    gate_sum.second_hop(add)
    summed.sent()

    def total_in(block):
        def total(slots):
            value = block[...].astype(F32)
            for slot in slots:
                value = value + slot[...].astype(F32)
            block[...] = value.astype(BF16)
        return total

    parts, n2, cot_v, normed = m["part"], m["n2_v"], m["cot_v"], m["tok_all"]
    wd_v[pl.ds(part, 128 - rest)] = jnp.zeros((128 - rest, width), BF16)

    def feed(k, carry):
        b, e = order(k)
        s = 2 * b + e
        at = pl.ds(pl.multiple_of(s * span, span), span)
        gu = jnp.dot(n2[pl.ds(2 * s, 2)].reshape(span, width), wgu[:, cols_a:],
                     preferred_element_type=F32)
        dh = last_dims(cot_v[pl.ds(2 * s, 2)].reshape(span, width), wd_v[half_a:])
        (hidden[at, half_a:2 * half_a], dgu[at, cols_a:cols_a + half_a],
         dgu[at, cols_a + half_a:cols_a + 2 * half_a]) = swiglu(
            gu[:, :half_a], gu[:, half_a:2 * half_a], dh[:, :half_a])
        tile = gu[:, 2 * half_a:]
        gate, up, grad = low_half(tile), low_half(roll(tile, 64)), dh[:, half_a:]
        sigma = 1.0 / (1.0 + jnp.exp(-gate))
        active = gate * sigma
        hidden[at, 2 * half_a:] = (active * up).astype(BF16)
        d_gate = grad * up * sigma * (1.0 + gate * (1.0 - sigma))
        dgu[at, cols_a + 2 * half_a:] = (
            d_gate + roll(low_half(grad * active), 64)).astype(BF16)
        out = last_dims(dgu[at], wgu[...]).astype(BF16)
        parts[pl.ds(2 * s, 2)] = out.reshape(2, rows, width)
        pl.when(k < 2)(lambda: summed.give(b))
        pl.when(k == 2)(summed.take_far)
        pl.when(k == 3)(summed.take_near)
        return carry

    lax.fori_loop(0, 4, feed, 0)
    down_sum.first_hop(add)

    ggu = m["ggu"]
    gu_sum = ChainSum(lambda zk: ggu.at[zk], lambda at: m["gu_slot"].at[at], m["zg_s"], m["zg_r"])

    def farthest(i):
        up = z // 2
        return up * i + (1 - up) * (3 - i)

    def grad_gu(i, carry):
        zk = farthest(i)
        cols = pl.ds(pl.multiple_of(zk * block_rows, 128), block_rows)
        left = n2[:, :, cols].reshape(8 * rows, block_rows)
        ggu[zk] = first_dims(left, dgu[:, cols_a:]).astype(BF16)
        gu_sum.start_one(zk)
        return carry

    lax.fori_loop(0, 2, grad_gu, 0)
    summed.middle()
    lax.fori_loop(2, 4, grad_gu, 0)
    down_sum.second_hop(add)
    summed.finish()

    v = m["mid"][...]
    dv, gain_grad = norm_back(summed.out[...], v, inverse_rms(v), m["g_two"][...])
    m["row_two"][...] = gain_grad
    dmid = cot_v[t_own].astype(F32) + dv
    m["dmid"][...] = dmid
    m["low"][...] = dmid.astype(BF16)
    branch = Gather(m["low"], m["db"], m["gd_s"], m["gd_r"], keep.at[12])
    branch.start()

    got = m["got"]
    quarter_d = rows_b
    summed.sent()
    for i in range(4):
        pl.when(r != i)(lambda i=i: spread(i).wait_send())
    for j in range(0, half_a + 128, 128):
        at = half_a + j
        grad = first_dims(hidden[:, at:at + 128], cot_v[...].reshape(8 * rows, width))
        parts[j // 128] = grad.astype(BF16)
    for i in range(4):
        lo = quarter_d * i
        first, last = lo // rows, (lo + quarter_d - 1) // rows + 1
        span_rows = parts[first:last].reshape((last - first) * rows, width)
        gdo[i, 0:quarter_d] = span_rows[lo - first * rows:lo - first * rows + quarter_d]
    def give(i, lo, n, ss, rs):
        return remote(gdo.at[i, pl.ds(lo, n)], got.at[r, pl.ds(lo, n)], ss.at[i], rs.at[r],
                      device(base, i // 2, i % 2, z, x))

    def give_all(lo, n, ss, rs):
        for i in range(4):
            pl.when(r != i)(lambda i=i: give(i, lo, n, ss, rs).start())
        got[r, lo:lo + n] = gdo[r, lo:lo + n]

    def given(lo, n, ss, rs):
        for i in range(4):
            pl.when(r != i)(lambda i=i: remote(
                gdo.at[i, pl.ds(lo, n)], got.at[i, pl.ds(lo, n)], ss.at[i], rs.at[i],
                to_c).wait_recv())

    def give_sent(lo, n, ss, rs):
        for i in range(4):
            pl.when(r != i)(lambda i=i: give(i, lo, n, ss, rs).wait_send())

    branch.forward()
    give_all(0, quarter_d, m["he_s"], m["he_r"])
    gu_sum.first_hop(add)

    gate_sum.collect(total_in(gga.at[z]))
    down_sum.collect(total_in(got_a.at[z]))
    branch.finish()
    mixed = SeqSum(parts, [m[n] for n in SUM_NAMES])

    def down(k, carry):
        b, e = order(k)
        s = 2 * b + e
        out = jnp.dot(hidden[pl.ds(s * span, span)], wd_v[...], preferred_element_type=F32)
        parts[pl.ds(2 * s, 2)] = out.astype(BF16).reshape(2, rows, width)
        pl.when(k < 2)(lambda: mixed.give(b))
        pl.when(k == 2)(mixed.take_far)
        pl.when(k == 3)(mixed.take_near)
        return carry

    lax.fori_loop(0, 4, down, 0)

    def swap(src, out, ss, rs):
        return remote(src.at[pl.ds(own_rows * (1 - x), own_rows)], out.at[t_own], ss, rs, to_x)

    def keep_own(k, src, out):
        copy = pltpu.make_async_copy(src.at[pl.ds(own_rows * x, own_rows)], out.at[t_own],
                                     keep.at[k])
        copy.start()
        return copy

    def swapped(src, out, ss, rs):
        return remote(src.at[pl.ds(own_rows * x, own_rows)], out.at[2 * r + 1 - x], ss, rs, to_x)

    def pairs(out):
        return lambda i: out.at[pl.ds(2 * i, 2)]

    ga_out, gb_out, qkv_out = m["ga_g"], m["gb_g"], m["qkv_g"]
    ga_swap = swap(gga.at[z], ga_out, m["xs_s"], m["xs_r"])
    ga_swap.start()
    ga_keep = keep_own(14, gga.at[z], ga_out)
    da_keep = loaded(15, got_a.at[z], m["da_g"].at[r])
    ga_share = RepShare(pairs(ga_out), m["ra_s"], m["ra_r"])
    da_share = RepShare(lambda i: m["da_g"].at[i], m["rc_s"], m["rc_r"])


    wo, qkv, dkv = m["wo_v"], qkv_all, kv
    db, dqkv, do_v = m["db"], m["dqkv"], m["do"]
    own_kv = m["own_kv"]
    m["row_head"][...] = jnp.zeros((1, 128), F32)

    down_rest = ChainSum(lambda zk: got.at[zk, pl.ds(0, quarter_d)],
                         lambda at: m["down_slot"].at[at], m["zd_s"], m["zd_r"])

    def start_down():
        given(0, quarter_d, m["he_s"], m["he_r"])
        down_rest.start()

    def share_first():
        ga_keep.wait()
        da_keep.wait()
        swapped(gga.at[z], ga_out, m["xs_s"], m["xs_r"]).wait_recv()
        ga_share.start()
        da_share.start()

    kv_slot = m["kv_slot"]

    def kv_down(zk, s):
        return remote(dkv.at[zk, s], kv_slot.at[zk, s], m["zk_s"].at[zk, s], m["zk_r"].at[zk, s],
                      device(base, y, c, (z + 3) % 4, x))

    def kv_merge(k):
        b, e = order(k)
        s = 2 * b + e

        def one(zk, inner):
            kv_down(zk, s).wait_recv()
            dkv[zk, s] = (dkv[zk, s].astype(F32) + kv_slot[zk, s].astype(F32)).astype(BF16)
            kv_down(zk, s).start()
            return inner

        @pl.when((z == 1) | (z == 2))
        def _():
            lax.fori_loop(0, z, one, 0)

    def attend_back(k, carry):
        b, e = order(k)
        s = 2 * b + e
        grads = db[pl.ds(2 * s, 2)].reshape(span, width)
        d_att = last_dims(grads, wo[...])
        first = d_att[:, 0:128]
        third = jnp.concatenate([jnp.zeros((span, HEAD_DIM), F32), d_att[:, 128:192]], axis=1)
        d_out = [high_half(roll(first, 64)), high_half(first), third]
        att_a = att[s, :, 0:128].astype(F32)
        att_b = att[s, :, 128:192].astype(F32)
        att_b = jnp.concatenate([jnp.zeros((span, HEAD_DIM), F32), att_b], axis=1)
        deltas = []
        for j, o in enumerate((roll(att_a, 64), att_a, att_b)):
            inv = inv_all[s][:, 32 * j:32 * j + 1]
            part_j = (d_out[j].astype(BF16).astype(F32) * inv).astype(BF16)
            do_v[pl.ds(j * span, span)] = part_j
            deltas.append(jnp.sum(part_j.astype(F32) * o, axis=1, keepdims=True))
        delta = jnp.concatenate(deltas, axis=0)
        q_seg[...] = segment_columns(segs, z, s)
        acc[...] = jnp.zeros_like(acc)

        def block(zk, diagonal):
            tile = kv[zk, s]
            q = q_all[s]
            d_out = do_v[...]
            p = exp_scores(q, tile, q_seg[...], segment_row(segs, zk, s), diagonal)
            ds = (p * (last_dims(d_out, tile) - delta)).astype(BF16)
            acc[...] += jnp.dot(ds, tile, preferred_element_type=F32)
            return first_dims(ds, q) + first_dims(p.astype(BF16), d_out)

        def step(zk, inner):
            dkv[zk, s] = block(zk, False).astype(BF16)
            pl.when(z == 3)(lambda: kv_down(zk, s).start())
            return inner

        lax.fori_loop(0, z, step, 0)
        own_kv[s] = block(z, True)
        tiles = split_heads(qkv[s, :, 0:128], qkv[s, :, 128:256])
        back = []
        for j in range(GROUP):
            dy = rotated(low_half(acc[pl.ds(j * span, span)]) * HEAD_DIM ** (-0.5), cos, -sin)
            raw, gain_part = head_back(dy, tiles[j], qg[0:1])
            m["row_head"][...] += gain_part
            back.append(raw)
        dqkv[s, :, 0:128] = (back[0] + roll(back[1], 64)).astype(BF16)
        dqkv[s, :, 128:256] = back[2].astype(BF16)
        pl.when(k >= 1)(lambda: kv_merge(k - 1))
        pl.when(k == 0)(mixed.middle)
        pl.when(k == 1)(lambda: gu_sum.second_hop(add))
        pl.when(k == 2)(mixed.finish)
        pl.when(k == 2)(share_first)
        pl.when(k == 3)(start_down)
        return carry

    lax.fori_loop(0, 4, attend_back, 0)
    kv_merge(3)
    m["mixed"][...] = (m["mid"][...] + mixed.out[...]).astype(BF16)
    mixed.sent()
    free = m["free"]
    for to in (to_c, to_x, to_y):
        pl.semaphore_signal(free, inc=1, device_id=to, device_id_type=MESH)

    for j in range(0, width, 512):
        cols = slice(j, j + 512)
        grad = first_dims(att[...].reshape(8 * rows, Q_COLS),
                          db[:, :, cols].reshape(8 * rows, 512)).astype(BF16)
        for i in range(4):
            gdo[i, quarter_d:quarter_d + quarter_o, cols] = grad[quarter_o * i:quarter_o * (i + 1)]
    give_all(quarter_d, quarter_o, m["hf_s"], m["hf_r"])

    pl.semaphore_wait(free, 3)

    inputs = SeqSum(parts, [m[n] for n in SUM_NAMES])

    def finish_one(k, carry):
        b, e = order(k)
        s = 2 * b + e
        @pl.when(z < 3)
        def _():
            kv_down(z, s).wait_recv()
            own_kv[s] += kv_slot[z, s].astype(F32)

        total = own_kv[s]
        u = split_heads(qkv[s, :, 0:128], qkv[s, :, 128:256])[GROUP]
        dy = rotated(low_half(total), cos, -sin)
        raw, gain_part = head_back(dy, u, kg[0:1])
        m["row_head"][...] += roll(gain_part, 64)
        tile = dqkv[s, :, 128:256].astype(F32)
        dqkv[s, :, 128:256] = (low_half(tile) + roll(raw, 64)).astype(BF16)
        dqkv[s, :, 256:320] = roll(total, 64)[:, 0:HEAD_DIM].astype(BF16)
        out = last_dims(dqkv[s], wq[...]).astype(BF16)
        parts[pl.ds(2 * s, 2)] = out.reshape(2, rows, width)
        pl.when(k < 2)(lambda: inputs.give(b))
        pl.when(k == 2)(inputs.take_far)
        pl.when(k == 3)(inputs.take_near)
        return carry

    lax.fori_loop(0, 4, finish_one, 0)
    gqkv = m["gqkv"]
    qkv_sum = DirectBoth(lambda zk, a: gqkv.at[zk, pl.ds(own_rows * a, own_rows)],
                         lambda zk, a: m["qkv_slot"].at[zk, a], m["zq_s"], m["zq_r"])

    def grad_qkv(i, carry):
        zk = farthest(i)
        cols = pl.ds(pl.multiple_of(zk * block_rows, 128), block_rows)
        left = normed[:, :, cols].reshape(8 * rows, block_rows)
        gqkv[zk] = first_dims(left, dqkv[...].reshape(8 * rows, HEAD_COLS)).astype(BF16)
        qkv_sum.start(zk)
        return carry

    lax.fori_loop(0, 4, grad_qkv, 0)
    inputs.middle()
    given(quarter_d, quarter_o, m["hf_s"], m["hf_r"])
    out_sum = ChainSum(lambda zk: got.at[zk, pl.ds(quarter_d, quarter_o)],
                       lambda at: m["out_slot"].at[at], m["zo_s"], m["zo_r"])
    out_sum.start()


    gu_sum.collect(total_in(ggu.at[z]))
    gb_swap = swap(ggu.at[z], gb_out, m["xg_s"], m["xg_r"])
    gb_swap.start()
    gb_keep = keep_own(14, ggu.at[z], gb_out)
    ga_share.forward()
    da_share.forward()

    inputs.finish()
    v = m["tok"][...].astype(F32)
    dv, gain_grad = norm_back(inputs.out[...], v, inverse_rms(v), m["g_one"][...])
    m["input_grad"][...] = m["dmid"][...] + dv

    def gain_rows_of(k):
        return m["mid"].at[pl.ds(8 * k, 8)]

    gains_own = gain_rows_of(0)
    gains_own[0:1] = gain_grad
    gains_own[1:2] = m["row_two"][...]
    gains_own[2:3, 0:128] = m["row_head"][...]

    def gain_sum(k):
        return remote(gains_own, gain_rows_of(k), m["gm_s"].at[k - 1], m["gm_r"].at[k - 1],
                      mates[k - 1])

    for k in range(1, 8):
        gain_sum(k).start()

    gb_keep.wait()
    swapped(ggu.at[z], gb_out, m["xg_s"], m["xg_r"]).wait_recv()
    gb_share = RepShare(pairs(gb_out), m["rg_s"], m["rg_r"])
    gb_share.start()
    for k in range(1, 8):
        gain_sum(k).wait_recv()
    total = gains_own[...]
    for k in range(1, 8):
        total = total + gain_rows_of(k)[...]
    z_rows = m["z_rows"]
    z_rows[0] = total

    def gain_z(k):
        return remote(z_rows.at[0], z_rows.at[k], m["gz_s"].at[k - 1], m["gz_r"].at[k - 1],
                      device(base, y, c, (z + k) % 4, x))

    for k in range(1, 4):
        gain_z(k).start()

    down_rest.first_hop(add)
    out_sum.first_hop(add)

    qkv_own = m["qkv_slot"].at[z]
    total = gqkv[z, pl.ds(own_rows * x, own_rows)].astype(F32)
    for k in (1, 3, 2):
        qkv_sum.arrive((z + k) % 4, x)
        total = total + m["qkv_slot"][(z + k) % 4, x].astype(F32)
    qkv_own[x] = total.astype(BF16)
    total = jnp.zeros((own_rows, HEAD_COLS), F32)
    for k in (0, 1, 3, 2):
        qkv_sum.arrive((z + k) % 4, 1 - x)
        total = total + m["qkv_slot"][(z + k) % 4, 1 - x].astype(F32)
    qkv_own[1 - x] = total.astype(BF16)
    qkv_keep = loaded(16, qkv_own, pairs(qkv_out)(r))
    qkv_keep.wait()
    qkv_share = RepShare(pairs(qkv_out), m["rq_s"], m["rq_r"])
    qkv_share.start()

    down_rest.second_hop(add)
    out_sum.second_hop(add)
    down_rest.collect(total_in(got.at[z, pl.ds(0, quarter_d)]))
    db_keep = loaded(15, got.at[z, pl.ds(0, quarter_d)], m["db_g"].at[r])
    db_keep.wait()
    db_share = RepShare(lambda i: m["db_g"].at[i], m["rd_s"], m["rd_r"])
    db_share.start()
    out_own = got.at[z, pl.ds(quarter_d, quarter_o)]
    out_sum.collect(total_in(out_own))
    out_keep = loaded(0, out_own, m["out_g"].at[r])
    out_keep.wait()
    out_share = RepShare(lambda i: m["out_g"].at[i], m["re_s"], m["re_r"])
    out_share.start()
    gb_share.forward()
    db_share.forward()
    for k in range(1, 4):
        gain_z(k).wait_recv()
    m["gains_g"][...] = z_rows[0] + z_rows[1] + z_rows[2] + z_rows[3]
    out_share.forward()
    qkv_share.forward()
    shares = (ga_share, da_share, gb_share, db_share, out_share, qkv_share)
    for share in shares:
        share.finish()

    for share in shares:
        share.sent()
    for copy in (ga_swap, gb_swap):
        copy.wait_send()
    for k in range(1, 8):
        gain_sum(k).wait_send()
    for k in range(1, 4):
        gain_z(k).wait_send()
    for flow in (gu_sum, down_rest, qkv_sum, out_sum, inputs):
        flow.sent()
    give_sent(0, quarter_d, m["he_s"], m["he_r"])
    give_sent(quarter_d, quarter_o, m["hf_s"], m["hf_r"])

    def dkv_sent(s, carry):
        for zk in range(3):
            pl.when(z > zk)(lambda zk=zk: kv_down(zk, s).wait_send())
        return carry

    lax.fori_loop(0, 4, dkv_sent, 0)
    for flow in (near, flip, out_q, gate_a, gate_b, down_a, down_b, gate_sum, down_sum):
        flow.sent()
    over.wait_send()
    for k in range(1, 8):
        seg_copy(k).wait_send()
        gain_copy(k).wait_send()
    for k in range(1, 4):
        pl.when(z + k < 4)(lambda k=k: seg_up(k).wait_send())

    def kv_sent(s, carry):
        for d in (1, 2, 3):
            pl.when(z + d < 4)(lambda d=d: kv_copy(d, s).wait_send())
        return carry

    lax.fori_loop(0, 4, kv_sent, 0)
    hand_sent(m["zo"], m["wo_v"], out_sems, quarter_o)
    hand_sent(m["za"], wda, a_sems, rows_a)
    hand_sent(m["zb"], wdb, b_sems, rows_b)


SUM_NAMES = ("r1", "chip", "rx", "ry", "mine", "late", "sum_out", "sum_s", "sum_r")
IN = ("tok", "cot", "seg", "wq", "gains", "wgu", "wd", "wo", "qg", "kg", "cos", "sin")
OUT = ("mixed", "input_grad", "gains_g", "ga_g", "gb_g", "da_g", "db_g", "out_g", "qkv_g",
       "zo", "za", "zb", "gains_all")


def block_call(*args):
    shape = jax.ShapeDtypeStruct
    tok, _, seg, wq, gains, wgu, wd, wo = args[:8]
    rows, width = tok.shape
    span = 2 * rows
    own_rows = wq.shape[1]
    part = wgu.shape[1] // 16
    half_a = part // 256 * 128
    part_b = part - half_a
    cols_a, cols_b = 2 * half_a, 2 * half_a + 128
    quarter_a, quarter_d, quarter_o = half_a // 4, part_b // 4, own_rows // 4
    heads = GROUP * span
    outs = {
        "mixed": shape((rows, width), BF16),
        "input_grad": shape((rows, width), F32),
        "gains_g": shape((8, width), F32),
        "ga_g": shape((8, own_rows, cols_a), BF16),
        "gb_g": shape((8, own_rows, cols_b), BF16),
        "da_g": shape((4, quarter_a, width), BF16),
        "db_g": shape((4, quarter_d, width), BF16),
        "out_g": shape((4, quarter_o, width), BF16),
        "qkv_g": shape((8, own_rows, HEAD_COLS), BF16),
        "zo": shape((4, quarter_o, width), BF16),
        "za": shape((4, quarter_a, width), BF16),
        "zb": shape((4, quarter_d, width), BF16),
        "gains_all": shape((8,) + gains.shape, BF16),
    }
    buffers = {
        "tok_all": ((8, rows, width), BF16), "cot_v": ((8, rows, width), BF16),
        "n2_v": ((8, rows, width), BF16), "db": ((8, rows, width), BF16),
        "part": ((8, rows, width), BF16),
        "segs_v": ((4, 8) + seg.shape, seg.dtype), "gains_v": ((8,) + gains.shape, BF16),
        "wq_v": ((width, HEAD_COLS), BF16), "wo_v": ((Q_COLS, width), BF16),
        "wgu_v": ((width, cols_a + cols_b), BF16), "wd_v": ((2 * half_a + 128, width), BF16),
        "hidden": ((8 * rows, 2 * half_a + 128), BF16),
        "dgu": ((8 * rows, cols_a + cols_b), BF16),
        "qkv_v": ((4, span, 256), F32), "q_v": ((4, heads, 128), BF16),
        "kv_v": ((4, 4, span, 128), BF16), "kv_slot": ((3, 4, span, 128), BF16),
        "own_kv": ((4, span, 128), F32), "inv_v": ((4, span, 128), F32),
        "att_v": ((4, span, Q_COLS), BF16), "acc": ((heads, 128), F32),
        "do": ((heads, 128), BF16), "q_seg": ((span, span), jnp.int32),
        "dqkv": ((4, span, HEAD_COLS), BF16),
        "mid": ((rows, width), F32), "dmid": ((rows, width), F32), "low": ((rows, width), BF16),
        "g_one": ((1, width), F32), "g_two": ((1, width), F32),
        "gga": ((4, 2 * own_rows, cols_a), BF16), "gga_slot": ((5, 2 * own_rows, cols_a), BF16),
        "ggu": ((4, 2 * own_rows, cols_b), BF16), "gu_slot": ((5, 2 * own_rows, cols_b), BF16),
        "got_a": ((4, quarter_a, width), BF16),
        "gda_slot": ((5, quarter_a, width), BF16),
        "gdo": ((4, quarter_d + quarter_o, width), BF16),
        "got": ((4, quarter_d + quarter_o, width), BF16),
        "down_slot": ((5, quarter_d, width), BF16),
        "out_slot": ((5, quarter_o, width), BF16),
        "gqkv": ((4, 2 * own_rows, HEAD_COLS), BF16),
        "qkv_slot": ((4, 2, own_rows, HEAD_COLS), BF16),
        "row_two": ((1, width), F32), "row_head": ((1, 128), F32),
        "z_rows": ((4, 8, width), F32),
    }
    counts = {
        "ga": (8, 8), "gb": (8, 8), "gc": (8, 8), "gd": (8, 8), "sg": (7, 7), "gn": (7, 7),
        "gm": (7, 7), "gz": (3, 3), "wa": (6, 4), "wb": (6, 4), "wo": (6, 4), "wx": (1, 1),
        "xa": (1, 1), "xb": (1, 1), "xs": (1, 1), "xg": (1, 1), "ca": (5, 4), "cb": (5, 4),
        "da": (5, 4), "db": (5, 4), "ys": (4, 5), "yd": (4, 5), "zg": (4, 5), "zd": (4, 5),
        "zo": (4, 5), "zq": ((4, 2), (4, 2)), "zk": ((3, 4), (3, 4)), "kv": ((3, 4), (4, 4)),
        "su": (3, 4), "ha": (4, 4), "hb": (4, 4), "hd": (4, 4), "he": (4, 4), "hf": (4, 4),
        "ho": (4, 4), "ra": (3, 3), "rc": (3, 3), "rd": (3, 3), "re": (3, 3), "rg": (3, 3),
        "rq": (3, 3),
    }
    sem = pltpu.SemaphoreType.DMA
    many = lambda n: sem if n == 1 else sem(n if isinstance(n, tuple) else (n,))
    sems = {"keep": dma(21), "free": pltpu.SemaphoreType.REGULAR}
    for n, (send, recv) in counts.items():
        sems[n + "_s"], sems[n + "_r"] = many(send), many(recv)
    scratch = {n: pltpu.VMEM(*v) for n, v in buffers.items()}
    scratch.update(zip(SUM_NAMES, seq_scratch(width)))
    names = IN + OUT + tuple(scratch) + tuple(sems)
    got = pl.pallas_call(
        functools.partial(block_kernel, names),
        name="block",
        out_shape=tuple(outs[n] for n in OUT),
        in_specs=[ANY if n in ("cot", "wgu", "wd", "wo") else VMEM for n in IN],
        out_specs=tuple(VMEM if n in ("mixed", "input_grad", "gains_g") else ANY for n in OUT),
        scratch_shapes=list(scratch.values()) + list(sems.values()),
        compiler_params=params(0, 63),
    )(*args)
    return dict(zip(OUT, got))


def order_kernel(ga, gb, da, db, out, qkv, gu_o, down_o, out_o, qkv_o):
    which, i = pl.program_id(1), pl.program_id(0)
    half_a = ga.shape[2] // 2
    half_b = (gb.shape[2] - 128) // 2
    main = half_a + half_b
    low = lanes((ga.shape[1], 128)) < HEAD_DIM

    def at(start, n, step=128):
        return pl.ds(pl.multiple_of(start, step), n)

    def columns(w):
        first, second = gb[0, :, 2 * half_b:].astype(F32), gb[1, :, 2 * half_b:].astype(F32)
        if w == 0:
            tile = jnp.where(low, first, roll(second, 64))
        else:
            tile = jnp.where(low, roll(first, 64), second)
        gu_o[:, main:main + 128] = tile
        for k in range(2):
            lo = k * (main + 128)
            gu_o[:, lo:lo + half_a] = ga[k, :, w * half_a:(w + 1) * half_a].astype(F32)
            gu_o[:, lo + half_a:lo + main] = gb[k, :, w * half_b:(w + 1) * half_b].astype(F32)

    @pl.when(which == 0)
    def _():
        columns(0)
        x = lax.axis_index("grp") % 2
        part = down_o.shape[0]
        rows_a, rows_b = da.shape[1], db.shape[1]
        shift = (part - main) * x
        down_o[at(rows_a * i + shift, rows_a, 16)] = da[0].astype(F32)
        start = half_a + rows_b * i + shift
        down_o[at(start, 16, 16)] = db[0, 0:16].astype(F32)
        start = start + 16 - (i // 3) * x * part
        down_o[at(start, rows_b - 16, 16)] = db[0, 16:].astype(F32)

    @pl.when(which == 1)
    def _():
        columns(1)
        out_o[...] = out[0].astype(F32)
        a, b = qkv[0].astype(F32), qkv[1].astype(F32)
        q_cols, kv_cols = HEADS * HEAD_DIM, KV_HEADS * HEAD_DIM
        half = lambda v, w: jnp.where(low, v, w)
        a1, a2, b0, b1 = a[:, 128:256], a[:, 256:], b[:, 0:128], b[:, 128:256]
        qkv_o[:, at(i * 2 * Q_COLS, 128)] = a[:, 0:128]
        qkv_o[:, at(i * 2 * Q_COLS + 128, 128)] = half(a1, roll(b0, 64))
        qkv_o[:, at(i * 2 * Q_COLS + 256, 128)] = half(roll(b0, 64), roll(b1, 64))
        qkv_o[:, at(q_cols + i * 128, 128)] = half(roll(a1, 64), b1)
        qkv_o[:, at(q_cols + kv_cols + i * 128, 128)] = jnp.concatenate([a2, b[:, 256:]], axis=1)


def order_call(ga, gb, da, db, out, qkv):
    shape = jax.ShapeDtypeStruct
    _, own_rows, cols_a = ga.shape
    cols = cols_a + gb.shape[2]
    width = da.shape[2]
    part = 4 * (da.shape[1] + db.shape[1])
    qkv_cols = (HEADS + 2 * KV_HEADS) * HEAD_DIM
    block = lambda v, n: pl.BlockSpec((n,) + v.shape[1:], lambda i, w: (i, 0, 0))
    return pl.pallas_call(
        order_kernel,
        name="final_order",
        grid=(4, 2),
        out_shape=(
            shape((own_rows, 8 * cols), F32), shape((part, width), F32),
            shape((4 * out.shape[1], width), F32), shape((own_rows, qkv_cols), F32)),
        in_specs=[block(ga, 2), block(gb, 2), block(da, 1), block(db, 1), block(out, 1),
                  block(qkv, 2)],
        out_specs=(
            pl.BlockSpec((own_rows, cols), lambda i, w: (0, 4 * w + i)),
            pl.BlockSpec((part, width), lambda i, w: (0, 0)),
            pl.BlockSpec((out.shape[1], width), lambda i, w: (i, 0)),
            pl.BlockSpec((own_rows, qkv_cols), lambda i, w: (0, 0))),
        compiler_params=pltpu.CompilerParams(
            dimension_semantics=("arbitrary", "arbitrary"), vmem_limit_bytes=48 * 2**20),
    )(ga, gb, da, db, out, qkv)


def rope_tables(positions):
    half = HEAD_DIM // 2
    freq = jnp.exp(-jnp.log(THETA) * jnp.arange(half, dtype=F32) * 2.0 / HEAD_DIM)
    angle = positions.astype(F32)[:, None] * freq[None, :]
    cos, sin = jnp.cos(angle), jnp.sin(angle)
    zero = jnp.zeros_like(cos)
    return jnp.concatenate([cos, cos, zero, zero], 1), jnp.concatenate([-sin, sin, zero, zero], 1)


def over_quads(array):
    reps = lax.axis_size("rep")
    if reps == 4:
        return array
    rows = [[j + 4 * q for q in range(reps // 4)] for j in range(4)]
    return lax.psum(array, "rep", axis_index_groups=rows)


def local(tokens, attn_gain, w_qkv, q_gain, k_gain, w_out, ffn_gain, w_gate_up, w_down,
          cotangent, segment_ids):
    rows, width = tokens.shape
    _, y, c, z, x = here()
    r = 2 * y + c
    q_width, kv_width = HEADS * HEAD_DIM, KV_HEADS * HEAD_DIM
    own_rows = w_qkv.shape[0]
    span = 2 * rows
    cut = lax.dynamic_slice_in_dim

    q_pair = cut(w_qkv, 2 * Q_COLS * r, 2 * Q_COLS, 1)
    k_pair = cut(w_qkv, q_width + 2 * HEAD_DIM * r, 2 * HEAD_DIM, 1)
    v_pair = cut(w_qkv, q_width + kv_width + 2 * HEAD_DIM * r, 2 * HEAD_DIM, 1)
    wq = jnp.stack([
        jnp.concatenate([
            q_pair[:, i * Q_COLS:(i + 1) * Q_COLS],
            k_pair[:, i * HEAD_DIM:(i + 1) * HEAD_DIM],
            v_pair[:, i * HEAD_DIM:(i + 1) * HEAD_DIM]], 1)
        for i in range(2)])
    gains = jnp.zeros((16, 256), BF16)
    gains = gains.at[0, :own_rows].set(attn_gain).at[1, :own_rows].set(ffn_gain)
    seg = jnp.broadcast_to(segment_ids[None, :], (8, rows))
    cos, sin = rope_tables(span * z + jnp.arange(span, dtype=jnp.int32))

    def padded(gain):
        return jnp.zeros((8, 128), F32).at[:, :HEAD_DIM].set(gain.astype(F32)[None])

    qg, kg = padded(q_gain), padded(k_gain)
    g = block_call(tokens, cotangent, seg, wq, gains, w_gate_up, w_down, w_out, qg, kg, cos, sin)
    gu, down, out, qkv = order_call(
        *[over_quads(g[n]) for n in ("ga_g", "gb_g", "da_g", "db_g", "out_g", "qkv_g")])
    gains_sum = over_quads(g["gains_g"])
    place = 2 * z + x
    gain_one = cut(gains_sum[0], place * own_rows, own_rows, 0)
    gain_two = cut(gains_sum[1], place * own_rows, own_rows, 0)
    return (g["mixed"], g["input_grad"], gain_one, qkv, gains_sum[2, :HEAD_DIM],
            gains_sum[2, HEAD_DIM:2 * HEAD_DIM], out, gain_two, gu, down)


def solution(mesh):
    rows, split = P(("rep", "grp"), None), P("grp", None)
    return jax.shard_map(
        local,
        mesh=mesh,
        in_specs=(rows, P("grp"), split, P(), P(), split, P("grp"), split, split, rows,
                  P(("rep", "grp"))),
        out_specs=(rows, rows, P("grp"), split, P(), P(), split, P("grp"), split, split),
        check_vma=False,
    )
```

```python
import functools

import jax
import jax.numpy as jnp
from jax import lax
from jax.experimental import pallas as pl
from jax.experimental.pallas import tpu as pltpu
from jax.sharding import PartitionSpec as P

HEADS = 24
KV_HEADS = 8
HEAD_DIM = 64
GROUP = HEADS // KV_HEADS
Q_COLS = GROUP * HEAD_DIM
HEAD_COLS = Q_COLS + 2 * HEAD_DIM

EPS = 1e-05
THETA = 1000000.0
MESH = pl.DeviceIdType.MESH
F32 = jnp.float32
BF16 = jnp.bfloat16

VMEM = pl.BlockSpec(memory_space=pltpu.VMEM)
ANY = pl.BlockSpec(memory_space=pl.ANY)


def here():
    rep = lax.axis_index("rep")
    grp = lax.axis_index("grp")
    r = rep % 4
    return rep - r, r // 2, r % 2, grp // 2, grp % 2


def device(base, y, c, z, x):
    return {"rep": base + 2 * y + c, "grp": 2 * z + x}


def remote(src, dst, send, recv, to):
    return pltpu.make_async_remote_copy(
        src_ref=src, dst_ref=dst, send_sem=send, recv_sem=recv, device_id=to, device_id_type=MESH
    )


def greet(targets):
    barrier = pltpu.get_barrier_semaphore()
    for to in targets:
        pl.semaphore_signal(barrier, inc=1, device_id=to, device_id_type=MESH)
    pl.semaphore_wait(barrier, len(targets))


def neighbours():
    base, y, c, z, x = here()
    to_c = device(base, y, 1 - c, z, x)
    to_x = device(base, y, c, z, 1 - x)
    to_y = device(base, 1 - y, c, z, x)
    return to_c, to_x, to_y


class Gather:
    def __init__(self, src, out, send, recv, local):
        self.src, self.out, self.send, self.recv = src, out, send, recv
        _, y, c, _, x = here()
        self.to_c, self.to_x, self.to_y = neighbours()
        slot = lambda a, b, d: 4 * a + 2 * b + d
        self.own = slot(y, c, x)
        self.at_c, self.at_x, self.at_y = slot(y, 1 - c, x), slot(y, c, 1 - x), slot(1 - y, c, x)
        self.at_xc, self.at_yc = slot(y, 1 - c, 1 - x), slot(1 - y, 1 - c, x)
        self.at_xy, self.at_xyc = slot(1 - y, c, 1 - x), slot(1 - y, 1 - c, 1 - x)
        self.half = src.shape[0] // 2
        self.keep = pltpu.make_async_copy(src, out.at[self.own], local)

    def part(self, at, k):
        return self.out.at[at, pl.ds(k * self.half, self.half)]

    def copy(self, k):
        out, own = self.out, self.out.at[self.own]
        src, dst, to = (
            lambda: (self.src, own, self.to_x),
            lambda: (self.src, own, self.to_y),
            lambda: (self.src, own, self.to_c),
            lambda: (self.part(self.at_x, 0),) * 2 + (self.to_y,),
            lambda: (out.at[self.at_x],) * 2 + (self.to_c,),
            lambda: (self.part(self.at_y, 1),) * 2 + (self.to_x,),
            lambda: (out.at[self.at_y],) * 2 + (self.to_c,),
            lambda: (out.at[self.at_xy],) * 2 + (self.to_c,),
        )[k]()
        return remote(src, dst, self.send.at[k], self.recv.at[k], to)

    def arrive(self, k):
        out = self.out
        ref = (
            lambda: out.at[self.at_x], lambda: out.at[self.at_y], lambda: out.at[self.at_c],
            lambda: self.part(self.at_xy, 0), lambda: out.at[self.at_xc],
            lambda: self.part(self.at_xy, 1), lambda: out.at[self.at_yc],
            lambda: out.at[self.at_xyc],
        )[k]()
        remote(ref, ref, self.send.at[k], self.recv.at[k], self.to_c).wait_recv()

    def start(self):
        self.keep.start()
        for k in range(3):
            self.copy(k).start()

    def forward(self):
        self.arrive(0)
        self.copy(3).start()
        self.copy(4).start()
        self.arrive(1)
        self.copy(5).start()
        self.copy(6).start()

    def cross(self):
        self.arrive(3)
        self.arrive(5)
        self.copy(7).start()

    def finish(self):
        self.cross()
        for k in (2, 4, 6, 7):
            self.arrive(k)
        self.keep.wait()
        self.sent()

    def sent(self):
        for k in range(8):
            self.copy(k).wait_send()


def dma(n):
    return pltpu.SemaphoreType.DMA((n,))


def params(cid, limit=60):
    return pltpu.CompilerParams(
        collective_id=cid, has_side_effects=True, vmem_limit_bytes=limit * 2**20
    )


def inverse_rms(v):
    return lax.rsqrt(jnp.mean(v * v, axis=-1, keepdims=True) + EPS)


def norm_back(dy, v, inv, gain):
    scaled = dy * gain
    gain_grad = jnp.sum(dy * v * inv, axis=0, keepdims=True)
    inner = jnp.mean(scaled * v, axis=-1, keepdims=True)
    return inv * scaled - v * inv * inv * inv * inner, gain_grad


def when(cond):
    return pl.when(cond)


def lanes(shape):
    return lax.broadcasted_iota(jnp.int32, shape, len(shape) - 1)


def roll(v, by):
    return pltpu.roll(v, by % v.shape[-1], v.ndim - 1)


class Along:
    def __init__(self, src, slot, send, recv):
        self.src, self.slot, self.send, self.recv = src, slot, send, recv
        self.base, self.y, self.c, self.z, self.x = here()

    def at(self, zk, x):
        return device(self.base, self.y, self.c, zk, x)

    def copy(self, d):
        zk = (self.z + d + 4) % 4
        return remote(self.src, self.slot(self.z), self.send.at[d + 2], self.recv.at[self.z],
                      self.at(zk, self.x))

    def fits(self, d):
        return (self.z + d >= 0) & (self.z + d < 4)

    def first(self):
        for d in (2, -2):
            pl.when(self.fits(d))(lambda d=d: self.copy(d).start())
        pl.when(self.z == 2)(lambda: self.copy(1).start())
        pl.when(self.z == 1)(lambda: self.copy(-1).start())

    def second(self):
        pl.when(self.z < 2)(lambda: self.copy(1).start())
        pl.when(self.z >= 2)(lambda: self.copy(-1).start())

    def arrival(self, zk):
        ref = self.slot(zk)
        return remote(ref, ref, self.send.at[0], self.recv.at[zk], self.at(self.z, 1 - self.x))

    def passed(self, zk, to):
        ref = self.slot(zk)
        return remote(ref, ref, self.send.at[5], self.recv.at[zk], self.at(to, self.x))

    def forward(self):
        @pl.when(self.z == 2)
        def _():
            self.arrival(0).wait_recv()
            self.passed(0, 3).start()

        @pl.when(self.z == 1)
        def _():
            self.arrival(3).wait_recv()
            self.passed(3, 0).start()

    def wait(self, zk):
        early = ((self.z == 2) & (zk == 0)) | ((self.z == 1) & (zk == 3))
        due = jnp.logical_not(early) & (self.z != zk)
        pl.when(due)(lambda: self.arrival(zk).wait_recv())

    def finish(self):
        for zk in range(4):
            self.wait(zk)

    def sent(self):
        for d in (2, -2, 1, -1):
            pl.when(self.fits(d))(lambda d=d: self.copy(d).wait_send())
        pl.when(self.z == 2)(lambda: self.passed(0, 3).wait_send())
        pl.when(self.z == 1)(lambda: self.passed(3, 0).wait_send())


class Chain:
    def __init__(self, slot, send, recv):
        self.slot, self.send, self.recv = slot, send, recv
        self.base, self.y, self.c, self.z, self.x = here()

    def copy(self, k, zk, to):
        return remote(self.slot(zk), self.slot(zk), self.send.at[k], self.recv.at[zk],
                      device(self.base, self.y, self.c, to, self.x))

    def arrive(self, zk):
        self.copy(0, zk, self.z).wait_recv()

    def inner(self):
        return (self.z == 1) | (self.z == 2)

    def start_ends(self):
        pl.when(self.z == 0)(lambda: self.copy(0, 0, 1).start())
        pl.when(self.z == 3)(lambda: self.copy(1, 3, 2).start())

    def start_inner(self):
        z = self.z

        @pl.when(self.inner())
        def _():
            self.copy(0, z, z + 1).start()
            self.copy(1, z, z - 1).start()

    def pass_ends(self):
        @pl.when(self.z == 1)
        def _():
            self.arrive(0)
            self.copy(2, 0, 2).start()

        @pl.when(self.z == 2)
        def _():
            self.arrive(3)
            self.copy(3, 3, 1).start()

    def pass_inner(self):
        @pl.when(self.z == 1)
        def _():
            self.arrive(2)
            self.copy(3, 2, 0).start()

        @pl.when(self.z == 2)
        def _():
            self.arrive(1)
            self.copy(2, 1, 3).start()

    def second(self):
        self.pass_ends()
        self.pass_inner()

    def third(self):
        @pl.when(self.z == 2)
        def _():
            self.arrive(0)
            self.copy(4, 0, 3).start()

        @pl.when(self.z == 1)
        def _():
            self.arrive(3)
            self.copy(4, 3, 0).start()

    def finish(self):
        pl.when(self.z == 0)(lambda: [self.arrive(zk) for zk in (1, 2, 3)] and None)
        pl.when(self.z == 3)(lambda: [self.arrive(zk) for zk in (2, 1, 0)] and None)

    def sent(self):
        z = self.z
        pl.when(z < 3)(lambda: self.copy(0, z, z + 1).wait_send())
        pl.when(z > 0)(lambda: self.copy(1, z, z - 1).wait_send())

        @pl.when(self.inner())
        def _():
            self.copy(2, z - 1, z + 1).wait_send()
            self.copy(3, z + 1, z - 1).wait_send()
            self.copy(4, z, z + 1).wait_send()


class ChainSum:
    def __init__(self, block, slot, send, recv):
        self.block, self.slot, self.send, self.recv = block, slot, send, recv
        self.base, self.y, self.c, self.z, self.x = here()

    def copy(self, zk, to, at):
        return remote(self.block(zk), self.slot(at), self.send.at[zk], self.recv.at[at],
                      device(self.base, self.y, self.c, to, self.x))

    def arrive(self, at):
        self.copy(0, self.z, at).wait_recv()

    def start(self):
        @pl.when(self.z == 0)
        def _():
            for zk, at in ((3, 3), (2, 2), (1, 4)):
                self.copy(zk, 1, at).start()

        @pl.when(self.z == 3)
        def _():
            for zk in (0, 1, 2):
                self.copy(zk, 2, zk).start()

    def start_one(self, zk):
        for to, at in ((3, 3), (2, 2), (1, 4)):
            pl.when((self.z == 0) & (zk == to))(
                lambda to=to, at=at: self.copy(to, 1, at).start())
        for to in (0, 1, 2):
            pl.when((self.z == 3) & (zk == to))(lambda to=to: self.copy(to, 2, to).start())

    def first_hop(self, add, which=(0, 1)):
        @pl.when(self.z == 1)
        def _():
            for i in which:
                zk, at = ((3, 3), (2, 4))[i]
                self.arrive(zk)
                add(self.block(zk), self.slot(zk))
                self.copy(zk, 2, at).start()

        @pl.when(self.z == 2)
        def _():
            for zk in which:
                self.arrive(zk)
                add(self.block(zk), self.slot(zk))
                self.copy(zk, 1, zk).start()

    def second_hop(self, add):
        @pl.when(self.z == 1)
        def _():
            self.arrive(0)
            add(self.block(0), self.slot(0))
            self.copy(0, 0, 0).start()

        @pl.when(self.z == 2)
        def _():
            self.arrive(3)
            add(self.block(3), self.slot(3))
            self.copy(3, 3, 4).start()

    def collect(self, total):
        z = self.z

        def take(ats):
            for at in ats:
                self.arrive(at)
            total([self.slot(at) for at in ats])

        pl.when(z == 0)(lambda: take([0]))
        pl.when(z == 3)(lambda: take([4]))
        pl.when((z == 1) | (z == 2))(lambda: take([z, 4]))

    def sent(self):
        for zk in range(4):
            pl.when(self.z != zk)(lambda zk=zk: self.copy(zk, 0, 0).wait_send())


def layer_mates():
    base, y, c, z, x = here()
    return [
        device(base, (y + k // 4) % 2, (c + k // 2) % 2, z, (x + k) % 2) for k in range(1, 8)
    ]


def z_mates():
    base, y, c, z, x = here()
    return [device(base, y, c, (z + k // 2) % 4, (x + k) % 2) for k in range(2, 8)]


def rotated(u, cos, sin):
    lane = lanes(u.shape)
    return u * cos + jnp.where(lane < 32, roll(u, -32), roll(u, 32)) * sin


def low_half(v):
    return jnp.where(lanes(v.shape) < HEAD_DIM, v, 0.0)


def high_half(v):
    return jnp.where(lanes(v.shape) >= HEAD_DIM, v, 0.0)


def split_heads(tile_a, tile_b):
    return [low_half(tile_a), low_half(roll(tile_a, 64)), low_half(tile_b),
            low_half(roll(tile_b, 64))]


def head_inverse(u):
    return lax.rsqrt(jnp.sum(u * u, axis=-1, keepdims=True) * (1.0 / HEAD_DIM) + EPS)


def exp_scores(q, kv, q_seg, k_seg, diagonal):
    s = lax.dot_general(q, kv, (((1,), (1,)), ((), ())), preferred_element_type=F32)
    allowed = q_seg == k_seg
    if diagonal:
        row = lax.broadcasted_iota(jnp.int32, allowed.shape, 0)
        col = lax.broadcasted_iota(jnp.int32, allowed.shape, 1)
        allowed = allowed & (col <= row)
    n = allowed.shape[0]
    return jnp.concatenate([
        jnp.where(allowed, jnp.exp(s[n * j:n * (j + 1)]), 0.0) for j in range(GROUP)], axis=0)


def segment_row(segs, zk, s):
    return jnp.concatenate([segs[zk, 2 * s, 0:1], segs[zk, 2 * s + 1, 0:1]], axis=1)


def segment_columns(segs, zk, s):
    parts = []
    for i in range(2):
        row = jnp.broadcast_to(segs[zk, 2 * s + i, 0:1], (128, 128))
        parts.append(jnp.transpose(row))
    col = jnp.concatenate(parts, axis=0)
    return jnp.concatenate([col, col], axis=1)


class SeqSum:
    def __init__(self, part, scratch):
        self.part = part
        (self.r1, self.chip, self.rx, self.ry, self.mine, self.late, self.out,
         self.send, self.recv) = scratch
        _, self.y, self.c, _, self.x = here()
        self.to_c, self.to_x, self.to_y = neighbours()

    def copy(self, k, src, dst, to):
        return remote(src, dst, self.send.at[k], self.recv.at[k], to)

    def swap(self, b, a):
        at = 2 * b + a
        return self.copy(at, self.part.at[4 * b + 2 * (1 - self.c) + a], self.r1.at[at], self.to_c)

    def give(self, b):
        for a in range(2):
            self.swap(b, a).start()

    def along_x(self, b):
        at = 2 * b + 1 - self.x
        return self.copy(4 + b, self.chip.at[at, pl.ds(0, 64)], self.rx.at[b], self.to_x)

    def along_y(self, a):
        at = 2 * (1 - self.y) + a
        return self.copy(6 + a, self.chip.at[at, pl.ds(64, 64)], self.ry.at[a], self.to_y)

    def last_y(self):
        return self.copy(8, self.mine.at[0], self.late.at[0], self.to_y)

    def last_x(self):
        return self.copy(9, self.mine.at[1], self.late.at[1], self.to_x)

    def total(self, b, a):
        self.swap(b, a).wait_recv()
        at = 2 * b + a
        return self.part[4 * b + 2 * self.c + a].astype(F32) + self.r1[at].astype(F32)

    def take_far(self):
        b = 1 - self.y
        for a in (1 - self.x, self.x):
            self.chip[2 * b + a] = self.total(b, a).astype(BF16)
            self.along_y(a).start()
            if a is not self.x:
                self.along_x(b).start()

    def take_near(self):
        b, x = self.y, self.x
        self.chip[2 * b + 1 - x] = self.total(b, 1 - x).astype(BF16)
        self.along_x(b).start()
        self.out[...] = self.total(b, x)

    def middle(self):
        x, y = self.x, self.y
        self.along_x(1 - y).wait_recv()
        self.mine[0] = (
            self.chip[2 * (1 - y) + x, 0:64].astype(F32) + self.rx[1 - y].astype(F32)
        ).astype(BF16)
        self.last_y().start()
        self.along_y(1 - x).wait_recv()
        self.mine[1] = (
            self.chip[2 * y + 1 - x, 64:128].astype(F32) + self.ry[1 - x].astype(F32)
        ).astype(BF16)
        self.last_x().start()

    def finish(self):
        x, y = self.x, self.y
        self.along_x(y).wait_recv()
        self.along_y(x).wait_recv()
        self.last_y().wait_recv()
        self.last_x().wait_recv()
        self.out[0:64] += self.rx[y].astype(F32) + self.late[0].astype(F32)
        self.out[64:128] += self.ry[x].astype(F32) + self.late[1].astype(F32)

    def given(self):
        for b in range(2):
            for a in range(2):
                self.swap(b, a).wait_send()

    def passed(self):
        for b in range(2):
            self.along_x(b).wait_send()
            self.along_y(b).wait_send()
        self.last_y().wait_send()
        self.last_x().wait_send()

    def sent(self):
        self.given()
        self.passed()


def seq_scratch(width):
    return [
        pltpu.VMEM((4, 128, width), BF16),
        pltpu.VMEM((4, 128, width), BF16),
        pltpu.VMEM((2, 64, width), BF16),
        pltpu.VMEM((2, 64, width), BF16),
        pltpu.VMEM((2, 64, width), BF16),
        pltpu.VMEM((2, 64, width), BF16),
        pltpu.VMEM((128, width), F32),
        dma(10),
        dma(10),
    ]


def first_dims(left, right):
    return lax.dot_general(left, right, (((0,), (0,)), ((), ())), preferred_element_type=F32)


def last_dims(left, right):
    return lax.dot_general(left, right, (((1,), (1,)), ((), ())), preferred_element_type=F32)


def swiglu(gate, up, grad):
    sigma = 1.0 / (1.0 + jnp.exp(-gate))
    active = gate * sigma
    d_gate = grad * up * sigma * (1.0 + gate * (1.0 - sigma))
    return ((active * up).astype(BF16), d_gate.astype(BF16), (grad * active).astype(BF16))


class Direct:
    def __init__(self, block, slot, send, recv):
        self.block, self.slot, self.send, self.recv = block, slot, send, recv
        self.base, self.y, self.c, self.z, self.x = here()

    def copy(self, zk):
        return remote(self.block(zk), self.slot(self.z), self.send.at[zk], self.recv.at[self.z],
                      device(self.base, self.y, self.c, zk, self.x))

    def start(self, zk):
        pl.when(zk != self.z)(lambda: self.copy(zk).start())

    def take(self):
        for k in (1, 3, 2):
            zk = (self.z + k) % 4
            ref = self.slot(zk)
            remote(ref, ref, self.send.at[0], self.recv.at[zk],
                   device(self.base, self.y, self.c, zk, self.x)).wait_recv()
            yield ref[...].astype(F32)

    def sent(self):
        for zk in range(4):
            pl.when(self.z != zk)(lambda zk=zk: self.copy(zk).wait_send())


class DirectBoth:
    def __init__(self, half, slot, send, recv):
        self.half, self.slot, self.send, self.recv = half, slot, send, recv
        self.base, self.y, self.c, self.z, self.x = here()

    def copy(self, zk, a):
        return remote(self.half(zk, a), self.slot(self.z, self.x), self.send.at[zk, a],
                      self.recv.at[self.z, self.x], device(self.base, self.y, self.c, zk, a))

    def start(self, zk):
        self.copy(zk, 1 - self.x).start()
        pl.when(zk != self.z)(lambda: self.copy(zk, self.x).start())

    def arrive(self, zk, a):
        ref = self.slot(zk, a)
        remote(ref, ref, self.send.at[0, 0], self.recv.at[zk, a],
               device(self.base, self.y, self.c, self.z, 1 - self.x)).wait_recv()

    def sent(self):
        for k in range(1, 8):
            self.copy((self.z + k // 2) % 4, (self.x + k) % 2).wait_send()


class RepShare:
    def __init__(self, at, send, recv):
        self.at, self.send, self.recv = at, send, recv
        _, self.y, self.c, _, _ = here()
        self.to_c, _, self.to_y = neighbours()
        self.r = 2 * self.y + self.c

    def copy(self, k, r, to):
        return remote(self.at(r), self.at(r), self.send.at[k], self.recv.at[k], to)

    def start(self):
        self.copy(0, self.r, self.to_y).start()
        self.copy(1, self.r, self.to_c).start()

    def forward(self):
        other = 2 * (1 - self.y) + self.c
        self.copy(0, other, self.to_y).wait_recv()
        self.copy(2, other, self.to_c).start()

    def finish(self):
        self.copy(1, 2 * self.y + 1 - self.c, self.to_c).wait_recv()
        self.copy(2, 2 * (1 - self.y) + 1 - self.c, self.to_c).wait_recv()

    def sent(self):
        self.copy(0, self.r, self.to_y).wait_send()
        self.copy(1, self.r, self.to_c).wait_send()
        self.copy(2, self.r, self.to_c).wait_send()


def head_back(dy, u, gain):
    inv = head_inverse(u)
    scaled = dy * gain
    gain_grad = jnp.sum(dy * u * inv, axis=0, keepdims=True)
    inner = jnp.sum(scaled * u, axis=-1, keepdims=True) * (1.0 / HEAD_DIM)
    return inv * scaled - u * (inv * inv * inv * inner), gain_grad


def block_kernel(names, *refs):
    m = dict(zip(names, refs))
    base, y, c, z, x = here()
    r = 2 * y + c
    to_c, to_x, to_y = neighbours()
    greet(layer_mates() + z_mates())
    rows, width = m["tok"].shape
    quarter_o = m["wo"].shape[0] // 4
    own_rows = m["wq"].shape[1]
    half_cols = m["wgu"].shape[1] // 2
    piece = half_cols // 4
    part = piece // 2
    main = part // 128 * 128
    half_a = main // 2
    rows_a, rows_b, rest = half_a // 4, (part - half_a) // 4, part - main
    keep = m["keep"]
    own = 2 * z + x
    t_own = 2 * r + x

    def local_copy(k, src, dst):
        return pltpu.make_async_copy(src, dst, keep.at[k])

    hidden, dgu, wgu, wd_v = m["hidden"], m["dgu"], m["wgu_v"], m["wd_v"]
    cols_a = 2 * half_a
    cols_b = dgu.shape[1] - cols_a

    def raw(i):
        return dgu.at[pl.ds(i * own_rows, own_rows)]

    def pair(a, first, n):
        return dgu.at[pl.ds((2 + a) * own_rows, own_rows), pl.ds(first, n)]

    def loaded(k, src, dst):
        copy = local_copy(k, src, dst)
        copy.start()
        return copy

    tok = Gather(m["tok"], m["tok_all"], m["ga_s"], m["ga_r"], keep.at[0])
    cot = Gather(m["cot"], m["cot_v"], m["gb_s"], m["gb_r"], keep.at[1])
    segs = m["segs_v"]
    mates = layer_mates()

    def seg_copy(k):
        return remote(m["seg"], segs.at[z, t_own], m["sg_s"].at[k - 1], m["sg_r"].at[k - 1],
                      mates[k - 1])

    def gain_target(k):
        return device(base, y, c, (z + k // 2) % 4, (x + k) % 2)

    def gain_copy(k):
        return remote(m["gains"], m["gains_all"].at[own], m["gn_s"].at[k - 1],
                      m["gn_r"].at[k - 1], gain_target(k))

    wq = m["wq_v"]

    def wq_slot(zk, a):
        return wq.at[pl.ds((2 * zk + a) * own_rows, own_rows)]

    near = Along(m["wq"].at[x], lambda zk: wq_slot(zk, x), m["wa_s"], m["wa_r"])
    flip = Along(wq_slot(z, 1 - x), lambda zk: wq_slot(zk, 1 - x), m["wb_s"], m["wb_r"])
    over = remote(m["wq"].at[1 - x], wq_slot(z, x), m["wx_s"], m["wx_r"], to_x)
    over_in = remote(m["wq"].at[x], wq_slot(z, 1 - x), m["wx_s"], m["wx_r"], to_x)
    for k in range(1, 8):
        seg_copy(k).start()
    over.start()
    near.first()
    near.second()
    tok.start()
    local = [
        local_copy(2, m["wq"].at[x], wq_slot(z, x)),
        local_copy(3, m["gains"], m["gains_all"].at[own]),
        local_copy(4, m["seg"], segs.at[z, t_own]),
        local_copy(5, m["wgu"].at[:, pl.ds(piece * r, piece)], raw(0)),
        local_copy(6, m["wgu"].at[:, pl.ds(half_cols + piece * r, piece)], raw(1)),
    ]
    for copy in local:
        copy.start()
    for k in range(1, 8):
        gain_copy(k).start()
    out_q = Along(m["wo"].at[pl.ds(quarter_o * r, quarter_o)], lambda zk: m["zo"].at[zk],
                  m["wo_s"], m["wo_r"])
    last = r // 3
    tail_at = rest * x + half_a + rows_b * r + 16 - last * x * part
    quarters = [
        local_copy(7, m["wo"].at[pl.ds(quarter_o * r, quarter_o)], m["zo"].at[z]),
        local_copy(8, m["wd"].at[pl.ds(rest * x + rows_a * r, rows_a)], m["za"].at[z]),
        local_copy(13, m["wd"].at[pl.ds(rest * x + half_a + rows_b * r, 16)],
                   m["zb"].at[z, pl.ds(0, 16)]),
        local_copy(14, m["wd"].at[pl.ds(tail_at, rows_b - 16)],
                   m["zb"].at[z, pl.ds(16, rows_b - 16)]),
    ]
    for copy in quarters:
        copy.start()
    over_in.wait_recv()
    flip.first()
    flip.second()
    out_q.first()
    out_q.second()

    def seg_up(k):
        return remote(segs.at[z], segs.at[z], m["su_s"].at[k - 1], m["su_r"].at[z],
                      device(base, y, c, (z + k) % 4, x))

    for k in range(1, 8):
        seg_copy(k).wait_recv()
    local[2].wait()
    for k in range(3, 0, -1):
        pl.when(z + k < 4)(lambda k=k: seg_up(k).start())

    local[3].wait()
    local[4].wait()
    gate, up = raw(0), raw(1)
    for a in range(2):
        at = a * (piece - main)
        for i, src in enumerate((gate, up)):
            pair(a, i * half_a, half_a)[...] = src[:, at:at + half_a]
            pair(a, cols_a + i * half_a, half_a)[...] = src[:, at + half_a:at + main]
    g_tile = gate[:, main:main + 128].astype(F32)
    u_tile = up[:, main:main + 128].astype(F32)
    low = lanes(g_tile.shape) < HEAD_DIM
    pair(0, 2 * main, 128)[...] = jnp.where(low, g_tile, roll(u_tile, 64)).astype(BF16)
    pair(1, 2 * main, 128)[...] = jnp.where(low, roll(g_tile, 64), u_tile).astype(BF16)

    def unit(first, n):
        return lambda zk: wgu.at[pl.ds(2 * zk * own_rows, 2 * own_rows), pl.ds(first, n)]

    def crossing(first, n, ss, rs, k):
        cols = pl.ds(first, n)
        mine = wgu.at[pl.ds((2 * z + x) * own_rows, own_rows), cols]
        other = wgu.at[pl.ds((2 * z + 1 - x) * own_rows, own_rows), cols]
        return (remote(pair(1 - x, first, n), mine, ss, rs, to_x),
                remote(pair(x, first, n), other, ss, rs, to_x),
                local_copy(k, pair(x, first, n), mine))

    cross_a, cross_a_in, mine_a = crossing(0, cols_a, m["xa_s"], m["xa_r"], 5)
    cross_b, cross_b_in, mine_b = crossing(cols_a, cols_b, m["xb_s"], m["xb_r"], 6)
    gate_a = Chain(unit(0, cols_a), m["ca_s"], m["ca_r"])
    gate_b = Chain(unit(cols_a, cols_b), m["cb_s"], m["cb_r"])
    down_a = Chain(lambda zk: m["za"].at[zk], m["da_s"], m["da_r"])
    down_b = Chain(lambda zk: m["zb"].at[zk], m["db_s"], m["db_r"])
    tok.forward()
    for copy in (cross_a, mine_a, cross_b, mine_b):
        copy.start()
    near.forward()
    flip.forward()
    out_q.forward()
    tok.finish()
    cot.start()
    near.finish()
    flip.finish()
    for k in range(1, 8):
        at = 2 * ((z + 4 - k // 2) % 4) + (x + k) % 2
        remote(m["gains"], m["gains_all"].at[at], m["gn_s"].at[k - 1], m["gn_r"].at[k - 1],
               to_c).wait_recv()
    for k in (0, 1):
        local[k].wait()
    gather_gains = pltpu.make_async_copy(m["gains_all"], m["gains_v"], keep.at[3])
    gather_gains.start()
    gather_gains.wait()
    gain_rows = []
    for i in range(2):
        gain_rows.append(jnp.concatenate(
            [m["gains_v"][k, 0:16].astype(F32)[i:i + 1, :own_rows] for k in range(8)], axis=1))
    m["g_one"][...], m["g_two"][...] = gain_rows
    kv = m["kv_v"]
    q_all, qkv_all = m["q_v"], m["qkv_v"]
    qg, kg, cos, sin = m["qg"][...], m["kg"][...], m["cos"][...], m["sin"][...]
    span = 2 * rows

    def order(k):
        return (y + 1 + k) % 2, (c + 1 + k // 2) % 2

    def kv_copy(d, s):
        return remote(kv.at[z, s], kv.at[z, s], m["kv_s"].at[d - 1, s], m["kv_r"].at[z, s],
                      device(base, y, c, (z + d) % 4, x))

    def kv_arrival(zk, s):
        return remote(kv.at[zk, s], kv.at[zk, s], m["kv_s"].at[0, s], m["kv_r"].at[zk, s], to_x)

    def project(k, carry):
        b, e = order(k)
        s = 2 * b + e
        tokens = m["tok_all"][pl.ds(2 * s, 2)].reshape(span, width).astype(F32)
        normed = (tokens * inverse_rms(tokens) * m["g_one"][...]).astype(BF16)
        m["tok_all"][pl.ds(2 * s, 2)] = normed.reshape(2, rows, width)
        qkv = jnp.dot(normed, wq[...], preferred_element_type=F32)
        qkv_all[s] = qkv[:, 0:256]
        heads = split_heads(qkv[:, 0:128], qkv[:, 128:256])
        for j in range(GROUP):
            u = heads[j]
            u = rotated(u * head_inverse(u) * qg[0:1], cos, sin) * HEAD_DIM ** (-0.5)
            q_all[s, pl.ds(j * span, span)] = u.astype(BF16)
        u = heads[GROUP]
        u = rotated(u * head_inverse(u) * kg[0:1], cos, sin)
        v = jnp.concatenate([jnp.zeros((span, HEAD_DIM), F32), qkv[:, 256:320]], axis=1)
        kv[z, s] = (u + v).astype(BF16)
        for d in (3, 2, 1):
            pl.when(z + d < 4)(lambda d=d: kv_copy(d, s).start())
        return carry

    lax.fori_loop(0, 4, project, 0)
    for copy in quarters[1:]:
        copy.wait()
    down_a.start_ends()
    down_a.start_inner()
    for copy in (mine_a, mine_b):
        copy.wait()
    cross_a_in.wait_recv()
    gate_a.start_ends()
    gate_a.start_inner()
    cross_b_in.wait_recv()
    down_b.start_ends()
    gate_b.start_ends()
    cot.forward()

    def hand(k, zk, src, dst, sems, n):
        ss, rs = sems
        to = device(base, zk // 2, zk % 2, z, x)
        pl.when(r != zk)(lambda: remote(src.at[zk], dst.at[pl.ds(n * r, n)], ss.at[zk],
                                        rs.at[r], to).start())

        @pl.when(r == zk)
        def _():
            copy = local_copy(k, src.at[zk], dst.at[pl.ds(n * r, n)])
            copy.start()
            copy.wait()

    def handed(src, dst, sems, n):
        ss, rs = sems
        for rk in range(4):
            ref = dst.at[pl.ds(n * rk, n)]
            pl.when(r != rk)(lambda ref=ref, rk=rk: remote(
                src.at[0], ref, ss.at[0], rs.at[rk], to_x).wait_recv())

    def hand_sent(src, dst, sems, n):
        ss, rs = sems
        for zk in range(4):
            pl.when(r != zk)(lambda zk=zk: remote(
                src.at[zk], dst.at[pl.ds(0, n)], ss.at[zk], rs.at[0], to_x).wait_send())

    quarters[0].wait()
    out_q.finish()
    out_sems = (m["ho_s"], m["ho_r"])
    a_sems, b_sems = (m["hd_s"], m["hd_r"]), (m["hb_s"], m["hb_r"])
    for zk in range(4):
        hand(13, zk, m["zo"], m["wo_v"], out_sems, quarter_o)

    for k in range(1, 4):
        pl.when(z - k >= 0)(lambda k=k: remote(
            segs.at[0], segs.at[(z + 4 - k) % 4], m["su_s"].at[k - 1],
            m["su_r"].at[(z + 4 - k) % 4], to_x).wait_recv())

    summed = SeqSum(m["part"], [m[n] for n in SUM_NAMES])
    inv_all, att = m["inv_v"], m["att_v"]
    acc, q_seg = m["acc"], m["q_seg"]

    def attend_one(k, carry):
        b, e = order(k)
        s = 2 * b + e
        q_seg[...] = segment_columns(segs, z, s)

        def block(zk, diagonal):
            tile = kv[zk, s]
            p = exp_scores(q_all[s], tile, q_seg[...], segment_row(segs, zk, s), diagonal)
            ones = jnp.where(lanes(tile.shape) < HEAD_DIM, 1.0, tile.astype(F32)).astype(BF16)
            add = jnp.dot(p.astype(BF16), ones, preferred_element_type=F32)
            if diagonal:
                acc[...] = add
            else:
                acc[...] += add

        block(z, True)

        def step(i, inner):
            zk = z - 1 - i
            kv_arrival(zk, s).wait_recv()
            block(zk, False)
            return inner

        lax.fori_loop(0, z, step, 0)
        total = acc[...]
        inv = 1.0 / jnp.where(lanes(total.shape) < HEAD_DIM, total, 1.0)
        inv = jnp.where(lanes(total.shape) < HEAD_DIM, inv, roll(inv, 64))
        o = high_half(total * inv)
        lane = lanes((span, 128))
        inv_all[s] = jnp.where(lane < 32, inv[0:span], jnp.where(
            lane < 64, inv[span:2 * span], inv[2 * span:]))
        first, second, third = o[0:span], o[span:2 * span], o[2 * span:]
        att[s, :, 0:128] = (roll(first, 64) + second).astype(BF16)
        att[s, :, 128:192] = roll(third, 64)[:, 0:HEAD_DIM].astype(BF16)
        pl.when(k == 0)(lambda: handed(m["zo"], m["wo_v"], out_sems, quarter_o))
        out = jnp.dot(att[s], m["wo_v"][...], preferred_element_type=F32).astype(BF16)
        m["part"][pl.ds(2 * s, 2)] = out.reshape(2, rows, width)
        pl.when(k < 2)(lambda: summed.give(b))
        pl.when(k == 2)(summed.take_far)
        pl.when(k == 3)(summed.take_near)
        return carry

    lax.fori_loop(0, 4, attend_one, 0)
    down_a.second()
    gate_a.second()
    summed.middle()
    down_a.third()
    summed.finish()
    mid = m["tok"][...].astype(F32) + summed.out[...]
    m["mid"][...] = mid
    m["low"][...] = (mid * inverse_rms(mid) * m["g_two"][...]).astype(BF16)
    n2_all, cot_all = m["n2_v"], m["cot_v"]
    n2 = Gather(m["low"], n2_all, m["gc_s"], m["gc_r"], keep.at[20])
    n2.start()
    cot.finish()
    gate_a.third()
    down_b.pass_ends()
    gate_b.pass_ends()
    down_b.start_inner()
    gate_b.start_inner()
    n2.forward()
    down_a.finish()
    wda, wdb = wd_v.at[pl.ds(0, half_a)], wd_v.at[pl.ds(half_a, part - half_a)]
    for zk in range(4):
        hand(13, zk, m["za"], wda, a_sems, rows_a)
    n2.finish()
    gate_a.finish()
    handed(m["za"], wda, a_sems, rows_a)
    cross_a.wait_send()
    cross_b.wait_send()

    down_b.third()
    gate_b.third()

    def feed_first(s, carry):
        at = pl.ds(pl.multiple_of(s * span, span), span)
        gu = jnp.dot(n2_all[pl.ds(2 * s, 2)].reshape(span, width), wgu[:, :cols_a],
                     preferred_element_type=F32)
        dh = last_dims(cot_all[pl.ds(2 * s, 2)].reshape(span, width), wd_v[0:half_a])
        hidden[at, 0:half_a], dgu[at, 0:half_a], dgu[at, half_a:cols_a] = swiglu(
            gu[:, :half_a], gu[:, half_a:], dh)
        out = last_dims(dgu[at, 0:cols_a], wgu[:, :cols_a]).astype(BF16)
        m["part"][pl.ds(2 * s, 2)] = out.reshape(2, rows, width)
        return carry

    summed.given()
    lax.fori_loop(0, 4, feed_first, 0)
    down_b.pass_inner()
    gate_b.pass_inner()
    block_rows = 2 * own_rows
    gga, gdo, got_a = m["gga"], m["gdo"], m["got_a"]
    gate_sum = ChainSum(lambda zk: gga.at[zk], lambda at: m["gga_slot"].at[at], m["ys_s"],
                        m["ys_r"])
    down_sum = ChainSum(lambda zk: got_a.at[zk], lambda at: m["gda_slot"].at[at], m["yd_s"],
                        m["yd_r"])

    def grad_gate(zk, carry):
        cols = pl.ds(pl.multiple_of(zk * block_rows, 128), block_rows)
        left = n2_all[:, :, cols].reshape(8 * rows, block_rows)
        gga[zk] = first_dims(left, dgu[:, :cols_a]).astype(BF16)
        return carry

    lax.fori_loop(0, 4, grad_gate, 0)
    gate_sum.start()
    for j in range(0, half_a, 128):
        grad = first_dims(hidden[:, j:j + 128], cot_all[...].reshape(8 * rows, width))
        for h in range(128 // rows_a):
            gdo[j // rows_a + h, 0:rows_a] = grad[rows_a * h:rows_a * (h + 1)].astype(BF16)

    def spread_from(i):
        return gdo.at[i, pl.ds(0, rows_a)]

    def spread(i):
        return remote(spread_from(i), got_a.at[r], m["ha_s"].at[i], m["ha_r"].at[r],
                      device(base, i // 2, i % 2, z, x))

    for i in range(4):
        pl.when(r != i)(lambda i=i: spread(i).start())
    got_a[r] = gdo[r, 0:rows_a]

    def add(block, slot):
        block[...] = (block[...].astype(F32) + slot[...].astype(F32)).astype(BF16)

    gate_sum.first_hop(add)
    down_b.finish()
    for zk in range(4):
        hand(13, zk, m["zb"], wdb, b_sems, rows_b)
    gate_b.finish()
    handed(m["zb"], wdb, b_sems, rows_b)
    for i in range(4):
        pl.when(r != i)(lambda i=i: remote(
            spread_from(i), got_a.at[i], m["ha_s"].at[i], m["ha_r"].at[i], to_c).wait_recv())
    down_sum.start()
    gate_sum.second_hop(add)
    summed.passed()

    def total_in(block):
        def total(slots):
            value = block[...].astype(F32)
            for slot in slots:
                value = value + slot[...].astype(F32)
            block[...] = value.astype(BF16)
        return total

    parts, n2, cot_v, normed = m["part"], m["n2_v"], m["cot_v"], m["tok_all"]
    wd_v[pl.ds(part, 128 - rest)] = jnp.zeros((128 - rest, width), BF16)

    def feed(k, carry):
        b, e = order(k)
        s = 2 * b + e
        at = pl.ds(pl.multiple_of(s * span, span), span)
        gu = jnp.dot(n2[pl.ds(2 * s, 2)].reshape(span, width), wgu[:, cols_a:],
                     preferred_element_type=F32)
        dh = last_dims(cot_v[pl.ds(2 * s, 2)].reshape(span, width), wd_v[half_a:])
        (hidden[at, half_a:2 * half_a], dgu[at, cols_a:cols_a + half_a],
         dgu[at, cols_a + half_a:cols_a + 2 * half_a]) = swiglu(
            gu[:, :half_a], gu[:, half_a:2 * half_a], dh[:, :half_a])
        tile = gu[:, 2 * half_a:]
        gate, up, grad = low_half(tile), low_half(roll(tile, 64)), dh[:, half_a:]
        sigma = 1.0 / (1.0 + jnp.exp(-gate))
        active = gate * sigma
        hidden[at, 2 * half_a:] = (active * up).astype(BF16)
        d_gate = grad * up * sigma * (1.0 + gate * (1.0 - sigma))
        dgu[at, cols_a + 2 * half_a:] = (
            d_gate + roll(low_half(grad * active), 64)).astype(BF16)
        out = last_dims(dgu[at, cols_a:], wgu[:, cols_a:])
        out = out + parts[pl.ds(2 * s, 2)].reshape(span, width).astype(F32)
        parts[pl.ds(2 * s, 2)] = out.astype(BF16).reshape(2, rows, width)
        pl.when(k < 2)(lambda: summed.give(b))
        pl.when(k == 2)(summed.take_far)
        pl.when(k == 3)(summed.take_near)
        return carry

    lax.fori_loop(0, 4, feed, 0)
    down_sum.first_hop(add)

    ggu = m["ggu"]
    gu_sum = ChainSum(lambda zk: ggu.at[zk], lambda at: m["gu_slot"].at[at], m["zg_s"], m["zg_r"])

    def farthest(i):
        up = z // 2
        return up * i + (1 - up) * (3 - i)

    def grad_gu(i, carry):
        zk = farthest(i)
        cols = pl.ds(pl.multiple_of(zk * block_rows, 128), block_rows)
        left = n2[:, :, cols].reshape(8 * rows, block_rows)
        ggu[zk] = first_dims(left, dgu[:, cols_a:]).astype(BF16)
        gu_sum.start_one(zk)
        return carry

    lax.fori_loop(0, 2, grad_gu, 0)
    summed.middle()
    lax.fori_loop(2, 4, grad_gu, 0)
    down_sum.second_hop(add)
    summed.finish()

    v = m["mid"][...]
    dv, gain_grad = norm_back(summed.out[...], v, inverse_rms(v), m["g_two"][...])
    m["row_two"][...] = gain_grad
    dmid = cot_v[t_own].astype(F32) + dv
    m["dmid"][...] = dmid
    m["low"][...] = dmid.astype(BF16)
    branch = Gather(m["low"], m["db"], m["gd_s"], m["gd_r"], keep.at[12])
    branch.start()
    gu_sum.first_hop(add, (0,))

    got = m["got"]
    quarter_d = rows_b
    for i in range(4):
        pl.when(r != i)(lambda i=i: spread(i).wait_send())
    for j in range(0, half_a + 128, 128):
        at = half_a + j
        grad = first_dims(hidden[:, at:at + 128], cot_v[...].reshape(8 * rows, width))
        grad = grad.astype(BF16)
        for i in range(4):
            lo, hi = max(j, quarter_d * i), min(j + 128, quarter_d * (i + 1))
            if lo < hi:
                gdo[i, lo - quarter_d * i:hi - quarter_d * i] = grad[lo - j:hi - j]

    summed.sent()

    def down(s, carry):
        at = pl.ds(pl.multiple_of(s * span, span), span)
        out = jnp.dot(hidden[at], wd_v[...], preferred_element_type=F32)
        parts[pl.ds(2 * s, 2)] = out.astype(BF16).reshape(2, rows, width)
        return carry

    lax.fori_loop(0, 4, down, 0)
    mixed = SeqSum(parts, [m[n] for n in SUM_NAMES])

    def give(i, lo, n, ss, rs):
        return remote(gdo.at[i, pl.ds(lo, n)], got.at[r, pl.ds(lo, n)], ss.at[i], rs.at[r],
                      device(base, i // 2, i % 2, z, x))

    def give_all(lo, n, ss, rs):
        for i in range(4):
            pl.when(r != i)(lambda i=i: give(i, lo, n, ss, rs).start())
        got[r, lo:lo + n] = gdo[r, lo:lo + n]

    def given(lo, n, ss, rs):
        for i in range(4):
            pl.when(r != i)(lambda i=i: remote(
                gdo.at[i, pl.ds(lo, n)], got.at[i, pl.ds(lo, n)], ss.at[i], rs.at[i],
                to_c).wait_recv())

    def give_sent(lo, n, ss, rs):
        for i in range(4):
            pl.when(r != i)(lambda i=i: give(i, lo, n, ss, rs).wait_send())

    branch.forward()
    branch.arrive(2)
    branch.keep.wait()
    give_all(0, quarter_d, m["he_s"], m["he_r"])
    mixed.give(0)
    mixed.give(1)
    gu_sum.first_hop(add, (1,))

    def swap(src, out, ss, rs):
        return remote(src.at[pl.ds(own_rows * (1 - x), own_rows)], out.at[t_own], ss, rs, to_x)

    def keep_own(k, src, out):
        copy = pltpu.make_async_copy(src.at[pl.ds(own_rows * x, own_rows)], out.at[t_own],
                                     keep.at[k])
        copy.start()
        return copy

    def swapped(src, out, ss, rs):
        return remote(src.at[pl.ds(own_rows * x, own_rows)], out.at[2 * r + 1 - x], ss, rs, to_x)

    def pairs(out):
        return lambda i: out.at[pl.ds(2 * i, 2)]

    ga_out, gb_out, qkv_out = m["ga_g"], m["gb_g"], m["qkv_g"]
    ga_swap = swap(gga.at[z], ga_out, m["xs_s"], m["xs_r"])
    ga_keep = local_copy(14, gga.at[z, pl.ds(own_rows * x, own_rows)], ga_out.at[t_own])
    da_keep = local_copy(15, got_a.at[z], m["da_g"].at[r])
    ga_share = RepShare(pairs(ga_out), m["ra_s"], m["ra_r"])
    da_share = RepShare(lambda i: m["da_g"].at[i], m["rc_s"], m["rc_r"])


    wo, qkv, dkv = m["wo_v"], qkv_all, kv
    db, dqkv, do_v = m["db"], m["dqkv"], m["do"]
    own_kv = m["own_kv"]
    m["row_head"][...] = jnp.zeros((1, 128), F32)

    down_rest = ChainSum(lambda zk: got.at[zk, pl.ds(0, quarter_d)],
                         lambda at: m["down_slot"].at[at], m["zd_s"], m["zd_r"])

    def swap_first():
        gate_sum.collect(total_in(gga.at[z]))
        down_sum.collect(total_in(got_a.at[z]))
        for copy in (ga_swap, ga_keep, da_keep):
            copy.start()

    def share_first():
        ga_keep.wait()
        da_keep.wait()
        swapped(gga.at[z], ga_out, m["xs_s"], m["xs_r"]).wait_recv()
        ga_share.start()
        da_share.start()

    def order_back(k):
        return (y + k // 2) % 2, (c + 1 + k) % 2

    kv_slot = m["kv_slot"]

    def kv_down(zk, s):
        return remote(dkv.at[zk, s], kv_slot.at[zk, s], m["zk_s"].at[zk, s], m["zk_r"].at[zk, s],
                      device(base, y, c, (z + 3) % 4, x))

    def kv_merge(k):
        b, e = order_back(k)
        s = 2 * b + e

        def one(zk, inner):
            kv_down(zk, s).wait_recv()
            dkv[zk, s] = (dkv[zk, s].astype(F32) + kv_slot[zk, s].astype(F32)).astype(BF16)
            kv_down(zk, s).start()
            return inner

        @pl.when((z == 1) | (z == 2))
        def _():
            lax.fori_loop(0, z, one, 0)

    def attend_back(k, carry):
        pl.when(k == 0)(lambda: branch.arrive(4))
        pl.when(k == 1)(branch.cross)
        pl.when(k == 2)(lambda: [branch.arrive(6), branch.arrive(7)] and None)
        b, e = order_back(k)
        s = 2 * b + e
        grads = db[pl.ds(2 * s, 2)].reshape(span, width)
        d_att = last_dims(grads, wo[...])
        first = d_att[:, 0:128]
        third = jnp.concatenate([jnp.zeros((span, HEAD_DIM), F32), d_att[:, 128:192]], axis=1)
        d_out = [high_half(roll(first, 64)), high_half(first), third]
        att_a = att[s, :, 0:128].astype(F32)
        att_b = att[s, :, 128:192].astype(F32)
        att_b = jnp.concatenate([jnp.zeros((span, HEAD_DIM), F32), att_b], axis=1)
        deltas = []
        for j, o in enumerate((roll(att_a, 64), att_a, att_b)):
            inv = inv_all[s][:, 32 * j:32 * j + 1]
            part_j = (d_out[j].astype(BF16).astype(F32) * inv).astype(BF16)
            do_v[pl.ds(j * span, span)] = part_j
            deltas.append(jnp.sum(part_j.astype(F32) * o, axis=1, keepdims=True))
        delta = jnp.concatenate(deltas, axis=0)
        q_seg[...] = segment_columns(segs, z, s)
        acc[...] = jnp.zeros_like(acc)

        def block(zk, diagonal):
            tile = kv[zk, s]
            q = q_all[s]
            d_out = do_v[...]
            p = exp_scores(q, tile, q_seg[...], segment_row(segs, zk, s), diagonal)
            ds = (p * (last_dims(d_out, tile) - delta)).astype(BF16)
            acc[...] += jnp.dot(ds, tile, preferred_element_type=F32)
            return first_dims(ds, q) + first_dims(p.astype(BF16), d_out)

        def step(zk, inner):
            dkv[zk, s] = block(zk, False).astype(BF16)
            pl.when(z == 3)(lambda: kv_down(zk, s).start())
            return inner

        lax.fori_loop(0, z, step, 0)
        own_kv[s] = block(z, True)
        tiles = split_heads(qkv[s, :, 0:128], qkv[s, :, 128:256])
        back = []
        for j in range(GROUP):
            dy = rotated(low_half(acc[pl.ds(j * span, span)]) * HEAD_DIM ** (-0.5), cos, -sin)
            raw, gain_part = head_back(dy, tiles[j], qg[0:1])
            m["row_head"][...] += gain_part
            back.append(raw)
        dqkv[s, :, 0:128] = (back[0] + roll(back[1], 64)).astype(BF16)
        dqkv[s, :, 128:256] = back[2].astype(BF16)
        pl.when(k >= 1)(lambda: kv_merge(k - 1))
        pl.when(k == 0)(lambda: gu_sum.second_hop(add))
        pl.when(k == 0)(mixed.take_far)
        pl.when(k == 0)(mixed.take_near)
        pl.when(k == 1)(swap_first)
        pl.when(k == 2)(mixed.middle)
        pl.when(k == 3)(share_first)
        pl.when(k == 3)(lambda: given(0, quarter_d, m["he_s"], m["he_r"]))
        return carry

    lax.fori_loop(0, 4, attend_back, 0)
    kv_merge(3)
    down_rest.start()
    mixed.finish()
    m["mixed"][...] = (m["mid"][...] + mixed.out[...]).astype(BF16)
    mixed.sent()
    free = m["free"]
    for to in (to_c, to_x, to_y):
        pl.semaphore_signal(free, inc=1, device_id=to, device_id_type=MESH)

    for j in range(0, width, 512):
        cols = slice(j, j + 512)
        grad = first_dims(att[...].reshape(8 * rows, Q_COLS),
                          db[:, :, cols].reshape(8 * rows, 512)).astype(BF16)
        for i in range(4):
            gdo[i, quarter_d:quarter_d + quarter_o, cols] = grad[quarter_o * i:quarter_o * (i + 1)]
    give_all(quarter_d, quarter_o, m["hf_s"], m["hf_r"])
    gu_sum.collect(total_in(ggu.at[z]))
    gb_swap = swap(ggu.at[z], gb_out, m["xg_s"], m["xg_r"])
    gb_swap.start()
    gb_keep = keep_own(14, ggu.at[z], gb_out)

    pl.semaphore_wait(free, 3)

    inputs = SeqSum(parts, [m[n] for n in SUM_NAMES])

    def finish_one(k, carry):
        b, e = (y + (k + 1) // 2) % 2, (c + 1 + k // 2) % 2
        s = 2 * b + e
        @pl.when(z < 3)
        def _():
            kv_down(z, s).wait_recv()
            own_kv[s] += kv_slot[z, s].astype(F32)

        total = own_kv[s]
        u = split_heads(qkv[s, :, 0:128], qkv[s, :, 128:256])[GROUP]
        dy = rotated(low_half(total), cos, -sin)
        raw, gain_part = head_back(dy, u, kg[0:1])
        m["row_head"][...] += roll(gain_part, 64)
        tile = dqkv[s, :, 128:256].astype(F32)
        dqkv[s, :, 128:256] = (low_half(tile) + roll(raw, 64)).astype(BF16)
        dqkv[s, :, 256:320] = roll(total, 64)[:, 0:HEAD_DIM].astype(BF16)
        out = last_dims(dqkv[s], wq[...]).astype(BF16)
        parts[pl.ds(2 * s, 2)] = out.reshape(2, rows, width)
        pl.when(k < 2)(lambda: inputs.give(b))
        pl.when(k == 2)(inputs.take_far)
        pl.when(k == 3)(inputs.take_near)
        return carry

    lax.fori_loop(0, 4, finish_one, 0)
    down_rest.first_hop(add)
    gqkv = m["gqkv"]
    qkv_sum = DirectBoth(lambda zk, a: gqkv.at[zk, pl.ds(own_rows * a, own_rows)],
                         lambda zk, a: m["qkv_slot"].at[zk, a], m["zq_s"], m["zq_r"])

    def grad_qkv(i, carry):
        zk = farthest(i)
        cols = pl.ds(pl.multiple_of(zk * block_rows, 128), block_rows)
        left = normed[:, :, cols].reshape(8 * rows, block_rows)
        gqkv[zk] = first_dims(left, dqkv[...].reshape(8 * rows, HEAD_COLS)).astype(BF16)
        qkv_sum.start(zk)
        return carry

    lax.fori_loop(0, 4, grad_qkv, 0)
    inputs.middle()
    down_rest.second_hop(add)
    given(quarter_d, quarter_o, m["hf_s"], m["hf_r"])
    out_sum = Direct(lambda zk: got.at[zk, pl.ds(quarter_d, quarter_o)],
                     lambda zk: m["out_slot"].at[zk], m["zo_s"], m["zo_r"])

    def start_out(i, carry):
        out_sum.start(farthest(i))
        return carry

    lax.fori_loop(0, 4, start_out, 0)
    ga_share.forward()
    da_share.forward()

    inputs.finish()
    v = m["tok"][...].astype(F32)
    dv, gain_grad = norm_back(inputs.out[...], v, inverse_rms(v), m["g_one"][...])
    m["input_grad"][...] = m["dmid"][...] + dv

    def gain_rows_of(k):
        return m["mid"].at[pl.ds(8 * k, 8)]

    gains_own = gain_rows_of(0)
    gains_own[0:1] = gain_grad
    gains_own[1:2] = m["row_two"][...]
    gains_own[2:3, 0:128] = m["row_head"][...]

    def gain_sum(k):
        return remote(gains_own, gain_rows_of(k), m["gm_s"].at[k - 1], m["gm_r"].at[k - 1],
                      mates[k - 1])

    for k in range(1, 8):
        gain_sum(k).start()
    gb_keep.wait()
    swapped(ggu.at[z], gb_out, m["xg_s"], m["xg_r"]).wait_recv()
    gb_share = RepShare(pairs(gb_out), m["rg_s"], m["rg_r"])
    gb_share.start()

    down_rest.collect(total_in(got.at[z, pl.ds(0, quarter_d)]))
    db_keep = loaded(15, got.at[z, pl.ds(0, quarter_d)], m["db_g"].at[r])
    for k in range(1, 8):
        gain_sum(k).wait_recv()
    total = gains_own[...]
    for k in range(1, 8):
        total = total + gain_rows_of(k)[...]
    z_rows = m["z_rows"]
    z_rows[0] = total

    def gain_z(k):
        return remote(z_rows.at[0], z_rows.at[k], m["gz_s"].at[k - 1], m["gz_r"].at[k - 1],
                      device(base, y, c, (z + k) % 4, x))

    for k in range(1, 4):
        gain_z(k).start()
    db_keep.wait()
    db_share = RepShare(lambda i: m["db_g"].at[i], m["rd_s"], m["rd_r"])
    db_share.start()
    gb_share.forward()

    qkv_own = m["qkv_slot"].at[z]
    total = gqkv[z, pl.ds(own_rows * x, own_rows)].astype(F32)
    for k in (1, 3, 2):
        qkv_sum.arrive((z + k) % 4, x)
        total = total + m["qkv_slot"][(z + k) % 4, x].astype(F32)
    qkv_own[x] = total.astype(BF16)
    total = jnp.zeros((own_rows, HEAD_COLS), F32)
    for k in (0, 1, 3, 2):
        qkv_sum.arrive((z + k) % 4, 1 - x)
        total = total + m["qkv_slot"][(z + k) % 4, 1 - x].astype(F32)
    qkv_own[1 - x] = total.astype(BF16)
    qkv_keep = loaded(16, qkv_own, pairs(qkv_out)(r))
    qkv_keep.wait()
    qkv_share = RepShare(pairs(qkv_out), m["rq_s"], m["rq_r"])
    qkv_share.start()

    out_own = got.at[z, pl.ds(quarter_d, quarter_o)]
    total = out_own[...].astype(F32)
    for term in out_sum.take():
        total = total + term
    out_own[...] = total.astype(BF16)
    out_keep = loaded(0, out_own, m["out_g"].at[r])
    out_keep.wait()
    out_share = RepShare(lambda i: m["out_g"].at[i], m["re_s"], m["re_r"])
    out_share.start()
    db_share.forward()
    for k in range(1, 4):
        gain_z(k).wait_recv()
    m["gains_g"][...] = z_rows[0] + z_rows[1] + z_rows[2] + z_rows[3]
    qkv_share.forward()
    out_share.forward()
    shares = (ga_share, da_share, gb_share, db_share, out_share, qkv_share)
    for share in shares:
        share.finish()

    for share in shares:
        share.sent()
    for copy in (ga_swap, gb_swap):
        copy.wait_send()
    for k in range(1, 8):
        gain_sum(k).wait_send()
    for k in range(1, 4):
        gain_z(k).wait_send()
    for flow in (branch, gu_sum, down_rest, qkv_sum, out_sum, inputs):
        flow.sent()
    give_sent(0, quarter_d, m["he_s"], m["he_r"])
    give_sent(quarter_d, quarter_o, m["hf_s"], m["hf_r"])

    def dkv_sent(s, carry):
        for zk in range(3):
            pl.when(z > zk)(lambda zk=zk: kv_down(zk, s).wait_send())
        return carry

    lax.fori_loop(0, 4, dkv_sent, 0)
    for flow in (near, flip, out_q, gate_a, gate_b, down_a, down_b, gate_sum, down_sum):
        flow.sent()
    over.wait_send()
    for k in range(1, 8):
        seg_copy(k).wait_send()
        gain_copy(k).wait_send()
    for k in range(1, 4):
        pl.when(z + k < 4)(lambda k=k: seg_up(k).wait_send())

    def kv_sent(s, carry):
        for d in (1, 2, 3):
            pl.when(z + d < 4)(lambda d=d: kv_copy(d, s).wait_send())
        return carry

    lax.fori_loop(0, 4, kv_sent, 0)
    hand_sent(m["zo"], m["wo_v"], out_sems, quarter_o)
    hand_sent(m["za"], wda, a_sems, rows_a)
    hand_sent(m["zb"], wdb, b_sems, rows_b)


SUM_NAMES = ("r1", "chip", "rx", "ry", "mine", "late", "sum_out", "sum_s", "sum_r")
IN = ("tok", "cot", "seg", "wq", "gains", "wgu", "wd", "wo", "qg", "kg", "cos", "sin")
OUT = ("mixed", "input_grad", "gains_g", "ga_g", "gb_g", "da_g", "db_g", "out_g", "qkv_g",
       "zo", "za", "zb", "gains_all")


def block_call(*args):
    shape = jax.ShapeDtypeStruct
    tok, _, seg, wq, gains, wgu, wd, wo = args[:8]
    rows, width = tok.shape
    span = 2 * rows
    own_rows = wq.shape[1]
    part = wgu.shape[1] // 16
    half_a = part // 256 * 128
    part_b = part - half_a
    cols_a, cols_b = 2 * half_a, 2 * half_a + 128
    quarter_a, quarter_d, quarter_o = half_a // 4, part_b // 4, own_rows // 4
    heads = GROUP * span
    outs = {
        "mixed": shape((rows, width), BF16),
        "input_grad": shape((rows, width), F32),
        "gains_g": shape((8, width), F32),
        "ga_g": shape((8, own_rows, cols_a), BF16),
        "gb_g": shape((8, own_rows, cols_b), BF16),
        "da_g": shape((4, quarter_a, width), BF16),
        "db_g": shape((4, quarter_d, width), BF16),
        "out_g": shape((4, quarter_o, width), BF16),
        "qkv_g": shape((8, own_rows, HEAD_COLS), BF16),
        "zo": shape((4, quarter_o, width), BF16),
        "za": shape((4, quarter_a, width), BF16),
        "zb": shape((4, quarter_d, width), BF16),
        "gains_all": shape((8,) + gains.shape, BF16),
    }
    buffers = {
        "tok_all": ((8, rows, width), BF16), "cot_v": ((8, rows, width), BF16),
        "n2_v": ((8, rows, width), BF16), "db": ((8, rows, width), BF16),
        "part": ((8, rows, width), BF16),
        "segs_v": ((4, 8) + seg.shape, seg.dtype), "gains_v": ((8,) + gains.shape, BF16),
        "wq_v": ((width, HEAD_COLS), BF16), "wo_v": ((Q_COLS, width), BF16),
        "wgu_v": ((width, cols_a + cols_b), BF16), "wd_v": ((2 * half_a + 128, width), BF16),
        "hidden": ((8 * rows, 2 * half_a + 128), BF16),
        "dgu": ((8 * rows, cols_a + cols_b), BF16),
        "qkv_v": ((4, span, 256), F32), "q_v": ((4, heads, 128), BF16),
        "kv_v": ((4, 4, span, 128), BF16), "kv_slot": ((3, 4, span, 128), BF16),
        "own_kv": ((4, span, 128), F32), "inv_v": ((4, span, 128), F32),
        "att_v": ((4, span, Q_COLS), BF16), "acc": ((heads, 128), F32),
        "do": ((heads, 128), BF16), "q_seg": ((span, span), jnp.int32),
        "dqkv": ((4, span, HEAD_COLS), BF16),
        "mid": ((rows, width), F32), "dmid": ((rows, width), F32), "low": ((rows, width), BF16),
        "g_one": ((1, width), F32), "g_two": ((1, width), F32),
        "gga": ((4, 2 * own_rows, cols_a), BF16), "gga_slot": ((5, 2 * own_rows, cols_a), BF16),
        "ggu": ((4, 2 * own_rows, cols_b), BF16), "gu_slot": ((5, 2 * own_rows, cols_b), BF16),
        "got_a": ((4, quarter_a, width), BF16),
        "gda_slot": ((5, quarter_a, width), BF16),
        "gdo": ((4, quarter_d + quarter_o, width), BF16),
        "got": ((4, quarter_d + quarter_o, width), BF16),
        "down_slot": ((5, quarter_d, width), BF16),
        "out_slot": ((4, quarter_o, width), BF16),
        "gqkv": ((4, 2 * own_rows, HEAD_COLS), BF16),
        "qkv_slot": ((4, 2, own_rows, HEAD_COLS), BF16),
        "row_two": ((1, width), F32), "row_head": ((1, 128), F32),
        "z_rows": ((4, 8, width), F32),
    }
    counts = {
        "ga": (8, 8), "gb": (8, 8), "gc": (8, 8), "gd": (8, 8), "sg": (7, 7), "gn": (7, 7),
        "gm": (7, 7), "gz": (3, 3), "wa": (6, 4), "wb": (6, 4), "wo": (6, 4), "wx": (1, 1),
        "xa": (1, 1), "xb": (1, 1), "xs": (1, 1), "xg": (1, 1), "ca": (5, 4), "cb": (5, 4),
        "da": (5, 4), "db": (5, 4), "ys": (4, 5), "yd": (4, 5), "zg": (4, 5), "zd": (4, 5),
        "zo": (4, 4), "zq": ((4, 2), (4, 2)), "zk": ((3, 4), (3, 4)), "kv": ((3, 4), (4, 4)),
        "su": (3, 4), "ha": (4, 4), "hb": (4, 4), "hd": (4, 4), "he": (4, 4), "hf": (4, 4),
        "ho": (4, 4), "ra": (3, 3), "rc": (3, 3), "rd": (3, 3), "re": (3, 3), "rg": (3, 3),
        "rq": (3, 3),
    }
    sem = pltpu.SemaphoreType.DMA
    many = lambda n: sem if n == 1 else sem(n if isinstance(n, tuple) else (n,))
    sems = {"keep": dma(21), "free": pltpu.SemaphoreType.REGULAR}
    for n, (send, recv) in counts.items():
        sems[n + "_s"], sems[n + "_r"] = many(send), many(recv)
    scratch = {n: pltpu.VMEM(*v) for n, v in buffers.items()}
    scratch.update(zip(SUM_NAMES, seq_scratch(width)))
    names = IN + OUT + tuple(scratch) + tuple(sems)
    got = pl.pallas_call(
        functools.partial(block_kernel, names),
        name="block",
        out_shape=tuple(outs[n] for n in OUT),
        in_specs=[ANY if n in ("cot", "wgu", "wd", "wo") else VMEM for n in IN],
        out_specs=tuple(VMEM if n in ("mixed", "input_grad", "gains_g") else ANY for n in OUT),
        scratch_shapes=list(scratch.values()) + list(sems.values()),
        compiler_params=params(0, 63),
    )(*args)
    return dict(zip(OUT, got))


def order_kernel(ga, gb, da, db, out, qkv, gu_o, down_o, out_o, qkv_o):
    which, i = pl.program_id(1), pl.program_id(0)
    half_a = ga.shape[2] // 2
    half_b = (gb.shape[2] - 128) // 2
    main = half_a + half_b
    low = lanes((ga.shape[1], 128)) < HEAD_DIM

    def at(start, n, step=128):
        return pl.ds(pl.multiple_of(start, step), n)

    def columns(w):
        first, second = gb[0, :, 2 * half_b:].astype(F32), gb[1, :, 2 * half_b:].astype(F32)
        if w == 0:
            tile = jnp.where(low, first, roll(second, 64))
        else:
            tile = jnp.where(low, roll(first, 64), second)
        gu_o[:, main:main + 128] = tile
        for k in range(2):
            lo = k * (main + 128)
            gu_o[:, lo:lo + half_a] = ga[k, :, w * half_a:(w + 1) * half_a].astype(F32)
            gu_o[:, lo + half_a:lo + main] = gb[k, :, w * half_b:(w + 1) * half_b].astype(F32)

    @pl.when(which == 0)
    def _():
        columns(0)
        x = lax.axis_index("grp") % 2
        part = down_o.shape[0]
        rows_a, rows_b = da.shape[1], db.shape[1]
        shift = (part - main) * x
        down_o[at(rows_a * i + shift, rows_a, 16)] = da[0].astype(F32)
        start = half_a + rows_b * i + shift
        down_o[at(start, 16, 16)] = db[0, 0:16].astype(F32)
        start = start + 16 - (i // 3) * x * part
        down_o[at(start, rows_b - 16, 16)] = db[0, 16:].astype(F32)

    @pl.when(which == 1)
    def _():
        columns(1)
        out_o[...] = out[0].astype(F32)
        a, b = qkv[0].astype(F32), qkv[1].astype(F32)
        q_cols, kv_cols = HEADS * HEAD_DIM, KV_HEADS * HEAD_DIM
        half = lambda v, w: jnp.where(low, v, w)
        a1, a2, b0, b1 = a[:, 128:256], a[:, 256:], b[:, 0:128], b[:, 128:256]
        qkv_o[:, at(i * 2 * Q_COLS, 128)] = a[:, 0:128]
        qkv_o[:, at(i * 2 * Q_COLS + 128, 128)] = half(a1, roll(b0, 64))
        qkv_o[:, at(i * 2 * Q_COLS + 256, 128)] = half(roll(b0, 64), roll(b1, 64))
        qkv_o[:, at(q_cols + i * 128, 128)] = half(roll(a1, 64), b1)
        qkv_o[:, at(q_cols + kv_cols + i * 128, 128)] = jnp.concatenate([a2, b[:, 256:]], axis=1)


def order_call(ga, gb, da, db, out, qkv):
    shape = jax.ShapeDtypeStruct
    _, own_rows, cols_a = ga.shape
    cols = cols_a + gb.shape[2]
    width = da.shape[2]
    part = 4 * (da.shape[1] + db.shape[1])
    qkv_cols = (HEADS + 2 * KV_HEADS) * HEAD_DIM
    block = lambda v, n: pl.BlockSpec((n,) + v.shape[1:], lambda i, w: (i, 0, 0))
    return pl.pallas_call(
        order_kernel,
        name="final_order",
        grid=(4, 2),
        out_shape=(
            shape((own_rows, 8 * cols), F32), shape((part, width), F32),
            shape((4 * out.shape[1], width), F32), shape((own_rows, qkv_cols), F32)),
        in_specs=[block(ga, 2), block(gb, 2), block(da, 1), block(db, 1), block(out, 1),
                  block(qkv, 2)],
        out_specs=(
            pl.BlockSpec((own_rows, cols), lambda i, w: (0, 4 * w + i)),
            pl.BlockSpec((part, width), lambda i, w: (0, 0)),
            pl.BlockSpec((out.shape[1], width), lambda i, w: (i, 0)),
            pl.BlockSpec((own_rows, qkv_cols), lambda i, w: (0, 0))),
        compiler_params=pltpu.CompilerParams(
            dimension_semantics=("arbitrary", "arbitrary"), vmem_limit_bytes=48 * 2**20),
    )(ga, gb, da, db, out, qkv)


def rope_tables(positions):
    half = HEAD_DIM // 2
    freq = jnp.exp(-jnp.log(THETA) * jnp.arange(half, dtype=F32) * 2.0 / HEAD_DIM)
    angle = positions.astype(F32)[:, None] * freq[None, :]
    cos, sin = jnp.cos(angle), jnp.sin(angle)
    zero = jnp.zeros_like(cos)
    return jnp.concatenate([cos, cos, zero, zero], 1), jnp.concatenate([-sin, sin, zero, zero], 1)


def over_quads(array):
    reps = lax.axis_size("rep")
    if reps == 4:
        return array
    rows = [[j + 4 * q for q in range(reps // 4)] for j in range(4)]
    return lax.psum(array, "rep", axis_index_groups=rows)


def local(tokens, attn_gain, w_qkv, q_gain, k_gain, w_out, ffn_gain, w_gate_up, w_down,
          cotangent, segment_ids):
    rows, width = tokens.shape
    _, y, c, z, x = here()
    r = 2 * y + c
    q_width, kv_width = HEADS * HEAD_DIM, KV_HEADS * HEAD_DIM
    own_rows = w_qkv.shape[0]
    span = 2 * rows
    cut = lax.dynamic_slice_in_dim

    q_pair = cut(w_qkv, 2 * Q_COLS * r, 2 * Q_COLS, 1)
    k_pair = cut(w_qkv, q_width + 2 * HEAD_DIM * r, 2 * HEAD_DIM, 1)
    v_pair = cut(w_qkv, q_width + kv_width + 2 * HEAD_DIM * r, 2 * HEAD_DIM, 1)
    wq = jnp.stack([
        jnp.concatenate([
            q_pair[:, i * Q_COLS:(i + 1) * Q_COLS],
            k_pair[:, i * HEAD_DIM:(i + 1) * HEAD_DIM],
            v_pair[:, i * HEAD_DIM:(i + 1) * HEAD_DIM]], 1)
        for i in range(2)])
    gains = jnp.zeros((16, 256), BF16)
    gains = gains.at[0, :own_rows].set(attn_gain).at[1, :own_rows].set(ffn_gain)
    seg = jnp.broadcast_to(segment_ids[None, :], (8, rows))
    cos, sin = rope_tables(span * z + jnp.arange(span, dtype=jnp.int32))

    def padded(gain):
        return jnp.zeros((8, 128), F32).at[:, :HEAD_DIM].set(gain.astype(F32)[None])

    qg, kg = padded(q_gain), padded(k_gain)
    g = block_call(tokens, cotangent, seg, wq, gains, w_gate_up, w_down, w_out, qg, kg, cos, sin)
    gu, down, out, qkv = order_call(
        *[over_quads(g[n]) for n in ("ga_g", "gb_g", "da_g", "db_g", "out_g", "qkv_g")])
    gains_sum = over_quads(g["gains_g"])
    place = 2 * z + x
    gain_one = cut(gains_sum[0], place * own_rows, own_rows, 0)
    gain_two = cut(gains_sum[1], place * own_rows, own_rows, 0)
    return (g["mixed"], g["input_grad"], gain_one, qkv, gains_sum[2, :HEAD_DIM],
            gains_sum[2, HEAD_DIM:2 * HEAD_DIM], out, gain_two, gu, down)


def solution(mesh):
    rows, split = P(("rep", "grp"), None), P("grp", None)
    return jax.shard_map(
        local,
        mesh=mesh,
        in_specs=(rows, P("grp"), split, P(), P(), split, P("grp"), split, split, rows,
                  P(("rep", "grp"))),
        out_specs=(rows, rows, P("grp"), split, P(), P(), split, P("grp"), split, split),
        check_vma=False,
    )
```

```python
import functools

import jax
import jax.numpy as jnp
from jax import lax
from jax.experimental import pallas as pl
from jax.experimental.pallas import tpu as pltpu
from jax.sharding import PartitionSpec as P

HEADS = 24
KV_HEADS = 8
HEAD_DIM = 64
GROUP = HEADS // KV_HEADS
Q_COLS = GROUP * HEAD_DIM
HEAD_COLS = Q_COLS + 2 * HEAD_DIM

EPS = 1e-05
THETA = 1000000.0
MESH = pl.DeviceIdType.MESH
F32 = jnp.float32
BF16 = jnp.bfloat16

VMEM = pl.BlockSpec(memory_space=pltpu.VMEM)
ANY = pl.BlockSpec(memory_space=pl.ANY)


def here():
    rep = lax.axis_index("rep")
    grp = lax.axis_index("grp")
    r = rep % 4
    return rep - r, r // 2, r % 2, grp // 2, grp % 2


def device(base, y, c, z, x):
    return {"rep": base + 2 * y + c, "grp": 2 * z + x}


def remote(src, dst, send, recv, to):
    return pltpu.make_async_remote_copy(
        src_ref=src, dst_ref=dst, send_sem=send, recv_sem=recv, device_id=to, device_id_type=MESH
    )


def greet(targets):
    barrier = pltpu.get_barrier_semaphore()
    for to in targets:
        pl.semaphore_signal(barrier, inc=1, device_id=to, device_id_type=MESH)
    pl.semaphore_wait(barrier, len(targets))


def neighbours():
    base, y, c, z, x = here()
    to_c = device(base, y, 1 - c, z, x)
    to_x = device(base, y, c, z, 1 - x)
    to_y = device(base, 1 - y, c, z, x)
    return to_c, to_x, to_y


class Gather:
    def __init__(self, src, out, send, recv, local):
        self.src, self.out, self.send, self.recv = src, out, send, recv
        _, y, c, _, x = here()
        self.to_c, self.to_x, self.to_y = neighbours()
        slot = lambda a, b, d: 4 * a + 2 * b + d
        self.own = slot(y, c, x)
        self.at_c, self.at_x, self.at_y = slot(y, 1 - c, x), slot(y, c, 1 - x), slot(1 - y, c, x)
        self.at_xc, self.at_yc = slot(y, 1 - c, 1 - x), slot(1 - y, 1 - c, x)
        self.at_xy, self.at_xyc = slot(1 - y, c, 1 - x), slot(1 - y, 1 - c, 1 - x)
        self.half = src.shape[0] // 2
        self.keep = pltpu.make_async_copy(src, out.at[self.own], local)

    def part(self, at, k):
        return self.out.at[at, pl.ds(k * self.half, self.half)]

    def copy(self, k):
        out, own = self.out, self.out.at[self.own]
        src, dst, to = (
            lambda: (self.src, own, self.to_x),
            lambda: (self.src, own, self.to_y),
            lambda: (self.src, own, self.to_c),
            lambda: (self.part(self.at_x, 0),) * 2 + (self.to_y,),
            lambda: (out.at[self.at_x],) * 2 + (self.to_c,),
            lambda: (self.part(self.at_y, 1),) * 2 + (self.to_x,),
            lambda: (out.at[self.at_y],) * 2 + (self.to_c,),
            lambda: (out.at[self.at_xy],) * 2 + (self.to_c,),
        )[k]()
        return remote(src, dst, self.send.at[k], self.recv.at[k], to)

    def arrive(self, k):
        out = self.out
        ref = (
            lambda: out.at[self.at_x], lambda: out.at[self.at_y], lambda: out.at[self.at_c],
            lambda: self.part(self.at_xy, 0), lambda: out.at[self.at_xc],
            lambda: self.part(self.at_xy, 1), lambda: out.at[self.at_yc],
            lambda: out.at[self.at_xyc],
        )[k]()
        remote(ref, ref, self.send.at[k], self.recv.at[k], self.to_c).wait_recv()

    def start(self):
        self.keep.start()
        for k in range(3):
            self.copy(k).start()

    def forward(self):
        self.arrive(0)
        self.copy(3).start()
        self.copy(4).start()
        self.arrive(1)
        self.copy(5).start()
        self.copy(6).start()

    def cross(self):
        self.arrive(3)
        self.arrive(5)
        self.copy(7).start()

    def finish(self):
        self.cross()
        for k in (2, 4, 6, 7):
            self.arrive(k)
        self.keep.wait()
        self.sent()

    def sent(self):
        for k in range(8):
            self.copy(k).wait_send()


def dma(n):
    return pltpu.SemaphoreType.DMA((n,))


def params(cid, limit=60):
    return pltpu.CompilerParams(
        collective_id=cid, has_side_effects=True, vmem_limit_bytes=limit * 2**20
    )


def inverse_rms(v):
    return lax.rsqrt(jnp.mean(v * v, axis=-1, keepdims=True) + EPS)


def norm_back(dy, v, inv, gain):
    scaled = dy * gain
    gain_grad = jnp.sum(dy * v * inv, axis=0, keepdims=True)
    inner = jnp.mean(scaled * v, axis=-1, keepdims=True)
    return inv * scaled - v * inv * inv * inv * inner, gain_grad


def when(cond):
    return pl.when(cond)


def lanes(shape):
    return lax.broadcasted_iota(jnp.int32, shape, len(shape) - 1)


def roll(v, by):
    return pltpu.roll(v, by % v.shape[-1], v.ndim - 1)


class Along:
    def __init__(self, src, slot, send, recv):
        self.src, self.slot, self.send, self.recv = src, slot, send, recv
        self.base, self.y, self.c, self.z, self.x = here()

    def at(self, zk, x):
        return device(self.base, self.y, self.c, zk, x)

    def copy(self, d):
        zk = (self.z + d + 4) % 4
        return remote(self.src, self.slot(self.z), self.send.at[d + 2], self.recv.at[self.z],
                      self.at(zk, self.x))

    def fits(self, d):
        return (self.z + d >= 0) & (self.z + d < 4)

    def first(self):
        for d in (2, -2):
            pl.when(self.fits(d))(lambda d=d: self.copy(d).start())
        pl.when(self.z == 2)(lambda: self.copy(1).start())
        pl.when(self.z == 1)(lambda: self.copy(-1).start())

    def second(self):
        pl.when(self.z < 2)(lambda: self.copy(1).start())
        pl.when(self.z >= 2)(lambda: self.copy(-1).start())

    def arrival(self, zk):
        ref = self.slot(zk)
        return remote(ref, ref, self.send.at[0], self.recv.at[zk], self.at(self.z, 1 - self.x))

    def passed(self, zk, to):
        ref = self.slot(zk)
        return remote(ref, ref, self.send.at[5], self.recv.at[zk], self.at(to, self.x))

    def forward(self):
        @pl.when(self.z == 2)
        def _():
            self.arrival(0).wait_recv()
            self.passed(0, 3).start()

        @pl.when(self.z == 1)
        def _():
            self.arrival(3).wait_recv()
            self.passed(3, 0).start()

    def wait(self, zk):
        early = ((self.z == 2) & (zk == 0)) | ((self.z == 1) & (zk == 3))
        due = jnp.logical_not(early) & (self.z != zk)
        pl.when(due)(lambda: self.arrival(zk).wait_recv())

    def finish(self):
        for zk in range(4):
            self.wait(zk)

    def sent(self):
        for d in (2, -2, 1, -1):
            pl.when(self.fits(d))(lambda d=d: self.copy(d).wait_send())
        pl.when(self.z == 2)(lambda: self.passed(0, 3).wait_send())
        pl.when(self.z == 1)(lambda: self.passed(3, 0).wait_send())


class Chain:
    def __init__(self, slot, send, recv):
        self.slot, self.send, self.recv = slot, send, recv
        self.base, self.y, self.c, self.z, self.x = here()

    def copy(self, k, zk, to):
        return remote(self.slot(zk), self.slot(zk), self.send.at[k], self.recv.at[zk],
                      device(self.base, self.y, self.c, to, self.x))

    def arrive(self, zk):
        self.copy(0, zk, self.z).wait_recv()

    def inner(self):
        return (self.z == 1) | (self.z == 2)

    def start_ends(self):
        pl.when(self.z == 0)(lambda: self.copy(0, 0, 1).start())
        pl.when(self.z == 3)(lambda: self.copy(1, 3, 2).start())

    def start_inner(self):
        z = self.z

        @pl.when(self.inner())
        def _():
            self.copy(0, z, z + 1).start()
            self.copy(1, z, z - 1).start()

    def pass_ends(self):
        @pl.when(self.z == 1)
        def _():
            self.arrive(0)
            self.copy(2, 0, 2).start()

        @pl.when(self.z == 2)
        def _():
            self.arrive(3)
            self.copy(3, 3, 1).start()

    def pass_inner(self):
        @pl.when(self.z == 1)
        def _():
            self.arrive(2)
            self.copy(3, 2, 0).start()

        @pl.when(self.z == 2)
        def _():
            self.arrive(1)
            self.copy(2, 1, 3).start()

    def second(self):
        self.pass_ends()
        self.pass_inner()

    def third(self):
        @pl.when(self.z == 2)
        def _():
            self.arrive(0)
            self.copy(4, 0, 3).start()

        @pl.when(self.z == 1)
        def _():
            self.arrive(3)
            self.copy(4, 3, 0).start()

    def finish(self):
        pl.when(self.z == 0)(lambda: [self.arrive(zk) for zk in (1, 2, 3)] and None)
        pl.when(self.z == 3)(lambda: [self.arrive(zk) for zk in (2, 1, 0)] and None)

    def sent(self):
        z = self.z
        pl.when(z < 3)(lambda: self.copy(0, z, z + 1).wait_send())
        pl.when(z > 0)(lambda: self.copy(1, z, z - 1).wait_send())

        @pl.when(self.inner())
        def _():
            self.copy(2, z - 1, z + 1).wait_send()
            self.copy(3, z + 1, z - 1).wait_send()
            self.copy(4, z, z + 1).wait_send()


class ChainSum:
    def __init__(self, block, slot, send, recv):
        self.block, self.slot, self.send, self.recv = block, slot, send, recv
        self.base, self.y, self.c, self.z, self.x = here()

    def copy(self, zk, to, at):
        return remote(self.block(zk), self.slot(at), self.send.at[zk], self.recv.at[at],
                      device(self.base, self.y, self.c, to, self.x))

    def arrive(self, at):
        self.copy(0, self.z, at).wait_recv()

    def start(self):
        @pl.when(self.z == 0)
        def _():
            for zk, at in ((3, 3), (2, 2), (1, 4)):
                self.copy(zk, 1, at).start()

        @pl.when(self.z == 3)
        def _():
            for zk in (0, 1, 2):
                self.copy(zk, 2, zk).start()

    def start_one(self, zk):
        for to, at in ((3, 3), (2, 2), (1, 4)):
            pl.when((self.z == 0) & (zk == to))(
                lambda to=to, at=at: self.copy(to, 1, at).start())
        for to in (0, 1, 2):
            pl.when((self.z == 3) & (zk == to))(lambda to=to: self.copy(to, 2, to).start())

    def first_hop(self, add, which=(0, 1)):
        @pl.when(self.z == 1)
        def _():
            for i in which:
                zk, at = ((3, 3), (2, 4))[i]
                self.arrive(zk)
                add(self.block(zk), self.slot(zk))
                self.copy(zk, 2, at).start()

        @pl.when(self.z == 2)
        def _():
            for zk in which:
                self.arrive(zk)
                add(self.block(zk), self.slot(zk))
                self.copy(zk, 1, zk).start()

    def second_hop(self, add):
        @pl.when(self.z == 1)
        def _():
            self.arrive(0)
            add(self.block(0), self.slot(0))
            self.copy(0, 0, 0).start()

        @pl.when(self.z == 2)
        def _():
            self.arrive(3)
            add(self.block(3), self.slot(3))
            self.copy(3, 3, 4).start()

    def collect(self, total):
        z = self.z

        def take(ats):
            for at in ats:
                self.arrive(at)
            total([self.slot(at) for at in ats])

        pl.when(z == 0)(lambda: take([0]))
        pl.when(z == 3)(lambda: take([4]))
        pl.when((z == 1) | (z == 2))(lambda: take([z, 4]))

    def sent(self):
        for zk in range(4):
            pl.when(self.z != zk)(lambda zk=zk: self.copy(zk, 0, 0).wait_send())


def layer_mates():
    base, y, c, z, x = here()
    return [
        device(base, (y + k // 4) % 2, (c + k // 2) % 2, z, (x + k) % 2) for k in range(1, 8)
    ]


def z_mates():
    base, y, c, z, x = here()
    return [device(base, y, c, (z + k // 2) % 4, (x + k) % 2) for k in range(2, 8)]


def rotated(u, cos, sin):
    lane = lanes(u.shape)
    return u * cos + jnp.where(lane < 32, roll(u, -32), roll(u, 32)) * sin


def low_half(v):
    return jnp.where(lanes(v.shape) < HEAD_DIM, v, 0.0)


def high_half(v):
    return jnp.where(lanes(v.shape) >= HEAD_DIM, v, 0.0)


def split_heads(tile_a, tile_b):
    return [low_half(tile_a), low_half(roll(tile_a, 64)), low_half(tile_b),
            low_half(roll(tile_b, 64))]


def head_inverse(u):
    return lax.rsqrt(jnp.sum(u * u, axis=-1, keepdims=True) * (1.0 / HEAD_DIM) + EPS)


def exp_scores(q, kv, q_seg, k_seg, diagonal):
    s = lax.dot_general(q, kv, (((1,), (1,)), ((), ())), preferred_element_type=F32)
    allowed = q_seg == k_seg
    if diagonal:
        row = lax.broadcasted_iota(jnp.int32, allowed.shape, 0)
        col = lax.broadcasted_iota(jnp.int32, allowed.shape, 1)
        allowed = allowed & (col <= row)
    n = allowed.shape[0]
    return jnp.concatenate([
        jnp.where(allowed, jnp.exp(s[n * j:n * (j + 1)]), 0.0) for j in range(GROUP)], axis=0)


def segment_row(segs, zk, s):
    return jnp.concatenate([segs[zk, 2 * s, 0:1], segs[zk, 2 * s + 1, 0:1]], axis=1)


def segment_columns(segs, zk, s):
    parts = []
    for i in range(2):
        row = jnp.broadcast_to(segs[zk, 2 * s + i, 0:1], (128, 128))
        parts.append(jnp.transpose(row))
    col = jnp.concatenate(parts, axis=0)
    return jnp.concatenate([col, col], axis=1)


class SeqSum:
    def __init__(self, part, scratch):
        self.part = part
        (self.r1, self.chip, self.rx, self.ry, self.mine, self.late, self.out,
         self.send, self.recv) = scratch
        _, self.y, self.c, _, self.x = here()
        self.to_c, self.to_x, self.to_y = neighbours()

    def copy(self, k, src, dst, to):
        return remote(src, dst, self.send.at[k], self.recv.at[k], to)

    def swap(self, b, a):
        at = 2 * b + a
        return self.copy(at, self.part.at[4 * b + 2 * (1 - self.c) + a], self.r1.at[at], self.to_c)

    def give(self, b):
        for a in range(2):
            self.swap(b, a).start()

    def along_x(self, b):
        at = 2 * b + 1 - self.x
        return self.copy(4 + b, self.chip.at[at, pl.ds(0, 64)], self.rx.at[b], self.to_x)

    def along_y(self, a):
        at = 2 * (1 - self.y) + a
        return self.copy(6 + a, self.chip.at[at, pl.ds(64, 64)], self.ry.at[a], self.to_y)

    def last_y(self):
        return self.copy(8, self.mine.at[0], self.late.at[0], self.to_y)

    def last_x(self):
        return self.copy(9, self.mine.at[1], self.late.at[1], self.to_x)

    def total(self, b, a):
        self.swap(b, a).wait_recv()
        at = 2 * b + a
        return self.part[4 * b + 2 * self.c + a].astype(F32) + self.r1[at].astype(F32)

    def take_far(self):
        b = 1 - self.y
        for a in (1 - self.x, self.x):
            self.chip[2 * b + a] = self.total(b, a).astype(BF16)
            self.along_y(a).start()
            if a is not self.x:
                self.along_x(b).start()

    def take_near(self):
        b, x = self.y, self.x
        self.chip[2 * b + 1 - x] = self.total(b, 1 - x).astype(BF16)
        self.along_x(b).start()
        self.out[...] = self.total(b, x)

    def middle(self):
        x, y = self.x, self.y
        self.along_x(1 - y).wait_recv()
        self.mine[0] = (
            self.chip[2 * (1 - y) + x, 0:64].astype(F32) + self.rx[1 - y].astype(F32)
        ).astype(BF16)
        self.last_y().start()
        self.along_y(1 - x).wait_recv()
        self.mine[1] = (
            self.chip[2 * y + 1 - x, 64:128].astype(F32) + self.ry[1 - x].astype(F32)
        ).astype(BF16)
        self.last_x().start()

    def finish(self):
        x, y = self.x, self.y
        self.along_x(y).wait_recv()
        self.along_y(x).wait_recv()
        self.last_y().wait_recv()
        self.last_x().wait_recv()
        self.out[0:64] += self.rx[y].astype(F32) + self.late[0].astype(F32)
        self.out[64:128] += self.ry[x].astype(F32) + self.late[1].astype(F32)

    def given(self):
        for b in range(2):
            for a in range(2):
                self.swap(b, a).wait_send()

    def passed(self):
        for b in range(2):
            self.along_x(b).wait_send()
            self.along_y(b).wait_send()
        self.last_y().wait_send()
        self.last_x().wait_send()

    def sent(self):
        self.given()
        self.passed()


def seq_scratch(width):
    return [
        pltpu.VMEM((4, 128, width), BF16),
        pltpu.VMEM((4, 128, width), BF16),
        pltpu.VMEM((2, 64, width), BF16),
        pltpu.VMEM((2, 64, width), BF16),
        pltpu.VMEM((2, 64, width), BF16),
        pltpu.VMEM((2, 64, width), BF16),
        pltpu.VMEM((128, width), F32),
        dma(10),
        dma(10),
    ]


def first_dims(left, right):
    return lax.dot_general(left, right, (((0,), (0,)), ((), ())), preferred_element_type=F32)


def last_dims(left, right):
    return lax.dot_general(left, right, (((1,), (1,)), ((), ())), preferred_element_type=F32)


def swiglu(gate, up, grad):
    sigma = 1.0 / (1.0 + jnp.exp(-gate))
    active = gate * sigma
    d_gate = grad * up * sigma * (1.0 + gate * (1.0 - sigma))
    return ((active * up).astype(BF16), d_gate.astype(BF16), (grad * active).astype(BF16))


class Direct:
    def __init__(self, block, slot, send, recv):
        self.block, self.slot, self.send, self.recv = block, slot, send, recv
        self.base, self.y, self.c, self.z, self.x = here()

    def copy(self, zk):
        return remote(self.block(zk), self.slot(self.z), self.send.at[zk], self.recv.at[self.z],
                      device(self.base, self.y, self.c, zk, self.x))

    def start(self, zk):
        pl.when(zk != self.z)(lambda: self.copy(zk).start())

    def take(self):
        for k in (1, 3, 2):
            zk = (self.z + k) % 4
            ref = self.slot(zk)
            remote(ref, ref, self.send.at[0], self.recv.at[zk],
                   device(self.base, self.y, self.c, zk, self.x)).wait_recv()
            yield ref[...].astype(F32)

    def sent(self):
        for zk in range(4):
            pl.when(self.z != zk)(lambda zk=zk: self.copy(zk).wait_send())


class DirectBoth:
    def __init__(self, half, slot, send, recv):
        self.half, self.slot, self.send, self.recv = half, slot, send, recv
        self.base, self.y, self.c, self.z, self.x = here()

    def copy(self, zk, a):
        return remote(self.half(zk, a), self.slot(self.z, self.x), self.send.at[zk, a],
                      self.recv.at[self.z, self.x], device(self.base, self.y, self.c, zk, a))

    def start(self, zk):
        self.copy(zk, 1 - self.x).start()
        pl.when(zk != self.z)(lambda: self.copy(zk, self.x).start())

    def arrive(self, zk, a):
        ref = self.slot(zk, a)
        remote(ref, ref, self.send.at[0, 0], self.recv.at[zk, a],
               device(self.base, self.y, self.c, self.z, 1 - self.x)).wait_recv()

    def sent(self):
        for k in range(1, 8):
            self.copy((self.z + k // 2) % 4, (self.x + k) % 2).wait_send()


class RepShare:
    def __init__(self, at, send, recv):
        self.at, self.send, self.recv = at, send, recv
        _, self.y, self.c, _, _ = here()
        self.to_c, _, self.to_y = neighbours()
        self.r = 2 * self.y + self.c

    def copy(self, k, r, to):
        return remote(self.at(r), self.at(r), self.send.at[k], self.recv.at[k], to)

    def start(self):
        self.copy(0, self.r, self.to_y).start()
        self.copy(1, self.r, self.to_c).start()

    def forward(self):
        other = 2 * (1 - self.y) + self.c
        self.copy(0, other, self.to_y).wait_recv()
        self.copy(2, other, self.to_c).start()

    def finish(self):
        self.copy(1, 2 * self.y + 1 - self.c, self.to_c).wait_recv()
        self.copy(2, 2 * (1 - self.y) + 1 - self.c, self.to_c).wait_recv()

    def sent(self):
        self.copy(0, self.r, self.to_y).wait_send()
        self.copy(1, self.r, self.to_c).wait_send()
        self.copy(2, self.r, self.to_c).wait_send()


def head_back(dy, u, gain):
    inv = head_inverse(u)
    scaled = dy * gain
    gain_grad = jnp.sum(dy * u * inv, axis=0, keepdims=True)
    inner = jnp.sum(scaled * u, axis=-1, keepdims=True) * (1.0 / HEAD_DIM)
    return inv * scaled - u * (inv * inv * inv * inner), gain_grad


def block_kernel(names, *refs):
    m = dict(zip(names, refs))
    base, y, c, z, x = here()
    r = 2 * y + c
    to_c, to_x, to_y = neighbours()
    q_cols, kv_cols = HEADS * HEAD_DIM, KV_HEADS * HEAD_DIM
    raw_q = [
        pltpu.make_async_copy(m["wqkv"].at[:, pl.ds(first + n * r, n)],
                              m["wq_raw"].at[:, pl.ds(to, n)], m["keep"].at[k])
        for k, (first, to, n) in enumerate((
            (0, 0, 2 * Q_COLS), (q_cols, 2 * Q_COLS, 2 * HEAD_DIM),
            (q_cols + kv_cols, 2 * Q_COLS + 2 * HEAD_DIM, 2 * HEAD_DIM)))]
    for copy in raw_q:
        copy.start()
    small = m["small"][...].astype(F32)
    m["seg"][...] = jnp.broadcast_to(small[:, 512:640], (8, 128)).astype(jnp.int32)
    m["gains"][...] = jnp.concatenate(
        [small[:, 0:256], small[:, 256:512], jnp.zeros((14, 256), F32)], axis=0).astype(BF16)
    qg, kg = low_half(roll(small[:, 128:256], 64)), low_half(roll(small[:, 384:512], 64))
    greet(layer_mates() + z_mates())
    for copy in raw_q:
        copy.wait()
    tiles = [m["wq_raw"][:, 128 * i:128 * (i + 1)].astype(F32) for i in range(5)]
    low_lanes = lanes(tiles[0].shape) < HEAD_DIM
    half_of = lambda v, w: jnp.where(low_lanes, v, w).astype(BF16)
    q0, q1, q2, k_tile, v_tile = tiles
    m["wq"][0, :, 0:128] = q0.astype(BF16)
    m["wq"][0, :, 128:256] = half_of(q1, roll(k_tile, 64))
    m["wq"][0, :, 256:] = v_tile[:, 0:HEAD_DIM].astype(BF16)
    m["wq"][1, :, 0:128] = half_of(roll(q1, 64), roll(q2, 64))
    m["wq"][1, :, 128:256] = half_of(roll(q2, 64), k_tile)
    m["wq"][1, :, 256:] = roll(v_tile, 64)[:, 0:HEAD_DIM].astype(BF16)
    rows, width = m["tok"].shape
    quarter_o = m["wo"].shape[0] // 4
    own_rows = m["wqkv"].shape[0]
    half_cols = m["wgu"].shape[1] // 2
    piece = half_cols // 4
    part = piece // 2
    main = part // 128 * 128
    half_a = main // 2
    rows_a, rows_b, rest = half_a // 4, (part - half_a) // 4, part - main
    keep = m["keep"]
    own = 2 * z + x
    t_own = 2 * r + x

    def local_copy(k, src, dst):
        return pltpu.make_async_copy(src, dst, keep.at[k])

    hidden, dgu, wgu, wd_v = m["hidden"], m["dgu"], m["wgu_v"], m["wd_v"]
    cols_a = 2 * half_a
    cols_b = dgu.shape[1] - cols_a

    def raw(i):
        return dgu.at[pl.ds(i * own_rows, own_rows)]

    def pair(a, first, n):
        return dgu.at[pl.ds((2 + a) * own_rows, own_rows), pl.ds(first, n)]

    def loaded(k, src, dst):
        copy = local_copy(k, src, dst)
        copy.start()
        return copy

    tok = Gather(m["tok"], m["tok_all"], m["ga_s"], m["ga_r"], keep.at[0])
    cot = Gather(m["cot"], m["cot_v"], m["gb_s"], m["gb_r"], keep.at[1])
    segs = m["segs_v"]
    mates = layer_mates()

    def seg_copy(k):
        return remote(m["seg"], segs.at[z, t_own], m["sg_s"].at[k - 1], m["sg_r"].at[k - 1],
                      mates[k - 1])

    def gain_target(k):
        return device(base, y, c, (z + k // 2) % 4, (x + k) % 2)

    def gain_copy(k):
        return remote(m["gains"], m["gains_all"].at[own], m["gn_s"].at[k - 1],
                      m["gn_r"].at[k - 1], gain_target(k))

    wq = m["wq_v"]

    def wq_slot(zk, a):
        return wq.at[pl.ds((2 * zk + a) * own_rows, own_rows)]

    near = Along(m["wq"].at[x], lambda zk: wq_slot(zk, x), m["wa_s"], m["wa_r"])
    flip = Along(wq_slot(z, 1 - x), lambda zk: wq_slot(zk, 1 - x), m["wb_s"], m["wb_r"])
    over = remote(m["wq"].at[1 - x], wq_slot(z, x), m["wx_s"], m["wx_r"], to_x)
    over_in = remote(m["wq"].at[x], wq_slot(z, 1 - x), m["wx_s"], m["wx_r"], to_x)
    for k in range(1, 8):
        seg_copy(k).start()
    over.start()
    near.first()
    near.second()
    tok.start()
    local = [
        local_copy(2, m["wq"].at[x], wq_slot(z, x)),
        local_copy(3, m["gains"], m["gains_all"].at[own]),
        local_copy(4, m["seg"], segs.at[z, t_own]),
        local_copy(5, m["wgu"].at[:, pl.ds(piece * r, piece)], raw(0)),
        local_copy(6, m["wgu"].at[:, pl.ds(half_cols + piece * r, piece)], raw(1)),
    ]
    for copy in local:
        copy.start()
    for k in range(1, 8):
        gain_copy(k).start()
    out_q = Along(m["wo"].at[pl.ds(quarter_o * r, quarter_o)], lambda zk: m["zo"].at[zk],
                  m["wo_s"], m["wo_r"])
    last = r // 3
    tail_at = rest * x + half_a + rows_b * r + 16 - last * x * part
    quarters = [
        local_copy(7, m["wo"].at[pl.ds(quarter_o * r, quarter_o)], m["zo"].at[z]),
        local_copy(8, m["wd"].at[pl.ds(rest * x + rows_a * r, rows_a)], m["za"].at[z]),
        local_copy(13, m["wd"].at[pl.ds(rest * x + half_a + rows_b * r, 16)],
                   m["zb"].at[z, pl.ds(0, 16)]),
        local_copy(14, m["wd"].at[pl.ds(tail_at, rows_b - 16)],
                   m["zb"].at[z, pl.ds(16, rows_b - 16)]),
    ]
    for copy in quarters:
        copy.start()
    over_in.wait_recv()
    flip.first()
    flip.second()
    out_q.first()
    out_q.second()

    def seg_up(k):
        return remote(segs.at[z], segs.at[z], m["su_s"].at[k - 1], m["su_r"].at[z],
                      device(base, y, c, (z + k) % 4, x))

    for k in range(1, 8):
        seg_copy(k).wait_recv()
    local[2].wait()
    for k in range(3, 0, -1):
        pl.when(z + k < 4)(lambda k=k: seg_up(k).start())

    local[3].wait()
    local[4].wait()
    gate, up = raw(0), raw(1)
    for a in range(2):
        at = a * (piece - main)
        for i, src in enumerate((gate, up)):
            pair(a, i * half_a, half_a)[...] = src[:, at:at + half_a]
            pair(a, cols_a + i * half_a, half_a)[...] = src[:, at + half_a:at + main]
    g_tile = gate[:, main:main + 128].astype(F32)
    u_tile = up[:, main:main + 128].astype(F32)
    low = lanes(g_tile.shape) < HEAD_DIM
    pair(0, 2 * main, 128)[...] = jnp.where(low, g_tile, roll(u_tile, 64)).astype(BF16)
    pair(1, 2 * main, 128)[...] = jnp.where(low, roll(g_tile, 64), u_tile).astype(BF16)

    def unit(first, n):
        return lambda zk: wgu.at[pl.ds(2 * zk * own_rows, 2 * own_rows), pl.ds(first, n)]

    def crossing(first, n, ss, rs, k):
        cols = pl.ds(first, n)
        mine = wgu.at[pl.ds((2 * z + x) * own_rows, own_rows), cols]
        other = wgu.at[pl.ds((2 * z + 1 - x) * own_rows, own_rows), cols]
        return (remote(pair(1 - x, first, n), mine, ss, rs, to_x),
                remote(pair(x, first, n), other, ss, rs, to_x),
                local_copy(k, pair(x, first, n), mine))

    cross_a, cross_a_in, mine_a = crossing(0, cols_a, m["xa_s"], m["xa_r"], 5)
    cross_b, cross_b_in, mine_b = crossing(cols_a, cols_b, m["xb_s"], m["xb_r"], 6)
    gate_a = Chain(unit(0, cols_a), m["ca_s"], m["ca_r"])
    gate_b = Chain(unit(cols_a, cols_b), m["cb_s"], m["cb_r"])
    down_a = Chain(lambda zk: m["za"].at[zk], m["da_s"], m["da_r"])
    down_b = Chain(lambda zk: m["zb"].at[zk], m["db_s"], m["db_r"])
    tok.forward()
    for copy in (cross_a, mine_a, cross_b, mine_b):
        copy.start()
    near.forward()
    flip.forward()
    out_q.forward()
    tok.finish()
    cot.start()
    near.finish()
    flip.finish()
    for k in range(1, 8):
        at = 2 * ((z + 4 - k // 2) % 4) + (x + k) % 2
        remote(m["gains"], m["gains_all"].at[at], m["gn_s"].at[k - 1], m["gn_r"].at[k - 1],
               to_c).wait_recv()
    for k in (0, 1):
        local[k].wait()
    gather_gains = pltpu.make_async_copy(m["gains_all"], m["gains_v"], keep.at[3])
    gather_gains.start()
    gather_gains.wait()
    gain_rows = []
    for i in range(2):
        gain_rows.append(jnp.concatenate(
            [m["gains_v"][k, 0:16].astype(F32)[i:i + 1, :own_rows] for k in range(8)], axis=1))
    m["g_one"][...], m["g_two"][...] = gain_rows
    kv = m["kv_v"]
    q_all, qkv_all = m["q_v"], m["qkv_v"]
    cos, sin = low_half(m["rope"][...]), low_half(roll(m["rope"][...], 64))
    span = 2 * rows

    def order(k):
        return (y + 1 + k) % 2, (c + 1 + k // 2) % 2

    def kv_copy(d, s):
        return remote(kv.at[z, s], kv.at[z, s], m["kv_s"].at[d - 1, s], m["kv_r"].at[z, s],
                      device(base, y, c, (z + d) % 4, x))

    def kv_arrival(zk, s):
        return remote(kv.at[zk, s], kv.at[zk, s], m["kv_s"].at[0, s], m["kv_r"].at[zk, s], to_x)

    def project(k, carry):
        b, e = order(k)
        s = 2 * b + e
        tokens = m["tok_all"][pl.ds(2 * s, 2)].reshape(span, width).astype(F32)
        normed = (tokens * inverse_rms(tokens) * m["g_one"][...]).astype(BF16)
        m["tok_all"][pl.ds(2 * s, 2)] = normed.reshape(2, rows, width)
        qkv = jnp.dot(normed, wq[...], preferred_element_type=F32)
        qkv_all[s] = qkv[:, 0:256]
        heads = split_heads(qkv[:, 0:128], qkv[:, 128:256])
        for j in range(GROUP):
            u = heads[j]
            u = rotated(u * head_inverse(u) * qg, cos, sin) * HEAD_DIM ** (-0.5)
            q_all[s, pl.ds(j * span, span)] = u.astype(BF16)
        u = heads[GROUP]
        u = rotated(u * head_inverse(u) * kg, cos, sin)
        v = jnp.concatenate([jnp.zeros((span, HEAD_DIM), F32), qkv[:, 256:320]], axis=1)
        kv[z, s] = (u + v).astype(BF16)
        for d in (3, 2, 1):
            pl.when(z + d < 4)(lambda d=d: kv_copy(d, s).start())
        return carry

    lax.fori_loop(0, 4, project, 0)
    for copy in quarters[1:]:
        copy.wait()
    down_a.start_ends()
    down_a.start_inner()
    for copy in (mine_a, mine_b):
        copy.wait()
    cross_a_in.wait_recv()
    gate_a.start_ends()
    gate_a.start_inner()
    cross_b_in.wait_recv()
    down_b.start_ends()
    gate_b.start_ends()
    cot.forward()

    def hand(k, zk, src, dst, sems, n):
        ss, rs = sems
        to = device(base, zk // 2, zk % 2, z, x)
        pl.when(r != zk)(lambda: remote(src.at[zk], dst.at[pl.ds(n * r, n)], ss.at[zk],
                                        rs.at[r], to).start())

        @pl.when(r == zk)
        def _():
            copy = local_copy(k, src.at[zk], dst.at[pl.ds(n * r, n)])
            copy.start()
            copy.wait()

    def handed(src, dst, sems, n):
        ss, rs = sems
        for rk in range(4):
            ref = dst.at[pl.ds(n * rk, n)]
            pl.when(r != rk)(lambda ref=ref, rk=rk: remote(
                src.at[0], ref, ss.at[0], rs.at[rk], to_x).wait_recv())

    def hand_sent(src, dst, sems, n):
        ss, rs = sems
        for zk in range(4):
            pl.when(r != zk)(lambda zk=zk: remote(
                src.at[zk], dst.at[pl.ds(0, n)], ss.at[zk], rs.at[0], to_x).wait_send())

    quarters[0].wait()
    out_q.finish()
    out_sems = (m["ho_s"], m["ho_r"])
    a_sems, b_sems = (m["hd_s"], m["hd_r"]), (m["hb_s"], m["hb_r"])
    for zk in range(4):
        hand(13, zk, m["zo"], m["wo_v"], out_sems, quarter_o)

    for k in range(1, 4):
        pl.when(z - k >= 0)(lambda k=k: remote(
            segs.at[0], segs.at[(z + 4 - k) % 4], m["su_s"].at[k - 1],
            m["su_r"].at[(z + 4 - k) % 4], to_x).wait_recv())

    summed = SeqSum(m["part"], [m[n] for n in SUM_NAMES])
    inv_all, att = m["inv_v"], m["att_v"]
    acc, q_seg = m["acc"], m["q_seg"]

    def attend_one(k, carry):
        b, e = order(k)
        s = 2 * b + e
        q_seg[...] = segment_columns(segs, z, s)

        def block(zk, diagonal):
            tile = kv[zk, s]
            p = exp_scores(q_all[s], tile, q_seg[...], segment_row(segs, zk, s), diagonal)
            ones = jnp.where(lanes(tile.shape) < HEAD_DIM, 1.0, tile.astype(F32)).astype(BF16)
            add = jnp.dot(p.astype(BF16), ones, preferred_element_type=F32)
            if diagonal:
                acc[...] = add
            else:
                acc[...] += add

        block(z, True)

        def step(i, inner):
            zk = z - 1 - i
            kv_arrival(zk, s).wait_recv()
            block(zk, False)
            return inner

        lax.fori_loop(0, z, step, 0)
        total = acc[...]
        inv = 1.0 / jnp.where(lanes(total.shape) < HEAD_DIM, total, 1.0)
        inv = jnp.where(lanes(total.shape) < HEAD_DIM, inv, roll(inv, 64))
        o = high_half(total * inv)
        lane = lanes((span, 128))
        inv_all[s] = jnp.where(lane < 32, inv[0:span], jnp.where(
            lane < 64, inv[span:2 * span], inv[2 * span:]))
        first, second, third = o[0:span], o[span:2 * span], o[2 * span:]
        att[s, :, 0:128] = (roll(first, 64) + second).astype(BF16)
        att[s, :, 128:192] = roll(third, 64)[:, 0:HEAD_DIM].astype(BF16)
        pl.when(k == 0)(lambda: handed(m["zo"], m["wo_v"], out_sems, quarter_o))
        out = jnp.dot(att[s], m["wo_v"][...], preferred_element_type=F32).astype(BF16)
        m["part"][pl.ds(2 * s, 2)] = out.reshape(2, rows, width)
        pl.when(k < 2)(lambda: summed.give(b))
        pl.when(k == 2)(summed.take_far)
        pl.when(k == 3)(summed.take_near)
        return carry

    lax.fori_loop(0, 4, attend_one, 0)
    down_a.second()
    gate_a.second()
    summed.middle()
    down_a.third()
    summed.finish()
    mid = m["tok"][...].astype(F32) + summed.out[...]
    m["mid"][...] = mid
    m["low"][...] = (mid * inverse_rms(mid) * m["g_two"][...]).astype(BF16)
    n2_all, cot_all = m["n2_v"], m["cot_v"]
    n2 = Gather(m["low"], n2_all, m["gc_s"], m["gc_r"], keep.at[20])
    n2.start()
    cot.finish()
    gate_a.third()
    down_b.pass_ends()
    gate_b.pass_ends()
    down_b.start_inner()
    gate_b.start_inner()
    n2.forward()
    down_a.finish()
    wda, wdb = wd_v.at[pl.ds(0, half_a)], wd_v.at[pl.ds(half_a, part - half_a)]
    for zk in range(4):
        hand(13, zk, m["za"], wda, a_sems, rows_a)
    n2.finish()
    gate_a.finish()
    handed(m["za"], wda, a_sems, rows_a)
    cross_a.wait_send()
    cross_b.wait_send()

    down_b.third()
    gate_b.third()

    def feed_first(s, carry):
        at = pl.ds(pl.multiple_of(s * span, span), span)
        gu = jnp.dot(n2_all[pl.ds(2 * s, 2)].reshape(span, width), wgu[:, :cols_a],
                     preferred_element_type=F32)
        dh = last_dims(cot_all[pl.ds(2 * s, 2)].reshape(span, width), wd_v[0:half_a])
        hidden[at, 0:half_a], dgu[at, 0:half_a], dgu[at, half_a:cols_a] = swiglu(
            gu[:, :half_a], gu[:, half_a:], dh)
        out = last_dims(dgu[at, 0:cols_a], wgu[:, :cols_a]).astype(BF16)
        m["part"][pl.ds(2 * s, 2)] = out.reshape(2, rows, width)
        return carry

    summed.given()
    lax.fori_loop(0, 4, feed_first, 0)
    down_b.pass_inner()
    gate_b.pass_inner()
    block_rows = 2 * own_rows
    gga, gdo, got_a = m["gga"], m["gdo"], m["got_a"]
    gate_sum = ChainSum(lambda zk: gga.at[zk], lambda at: m["gga_slot"].at[at], m["ys_s"],
                        m["ys_r"])
    down_sum = ChainSum(lambda zk: got_a.at[zk], lambda at: m["gda_slot"].at[at], m["yd_s"],
                        m["yd_r"])

    def grad_gate(zk, carry):
        cols = pl.ds(pl.multiple_of(zk * block_rows, 128), block_rows)
        left = n2_all[:, :, cols].reshape(8 * rows, block_rows)
        gga[zk] = first_dims(left, dgu[:, :cols_a]).astype(BF16)
        return carry

    lax.fori_loop(0, 4, grad_gate, 0)
    gate_sum.start()
    for j in range(0, half_a, 128):
        grad = first_dims(hidden[:, j:j + 128], cot_all[...].reshape(8 * rows, width))
        for h in range(128 // rows_a):
            gdo[j // rows_a + h, 0:rows_a] = grad[rows_a * h:rows_a * (h + 1)].astype(BF16)

    def spread_from(i):
        return gdo.at[i, pl.ds(0, rows_a)]

    def spread(i):
        return remote(spread_from(i), got_a.at[r], m["ha_s"].at[i], m["ha_r"].at[r],
                      device(base, i // 2, i % 2, z, x))

    for i in range(4):
        pl.when(r != i)(lambda i=i: spread(i).start())
    got_a[r] = gdo[r, 0:rows_a]

    def add(block, slot):
        block[...] = (block[...].astype(F32) + slot[...].astype(F32)).astype(BF16)

    gate_sum.first_hop(add)
    down_b.finish()
    for zk in range(4):
        hand(13, zk, m["zb"], wdb, b_sems, rows_b)
    gate_b.finish()
    handed(m["zb"], wdb, b_sems, rows_b)
    for i in range(4):
        pl.when(r != i)(lambda i=i: remote(
            spread_from(i), got_a.at[i], m["ha_s"].at[i], m["ha_r"].at[i], to_c).wait_recv())
    down_sum.start()
    gate_sum.second_hop(add)
    summed.passed()

    def total_in(block):
        def total(slots):
            value = block[...].astype(F32)
            for slot in slots:
                value = value + slot[...].astype(F32)
            block[...] = value.astype(BF16)
        return total

    parts, n2, cot_v, normed = m["part"], m["n2_v"], m["cot_v"], m["tok_all"]
    wd_v[pl.ds(part, 128 - rest)] = jnp.zeros((128 - rest, width), BF16)

    def feed(k, carry):
        b, e = order(k)
        s = 2 * b + e
        at = pl.ds(pl.multiple_of(s * span, span), span)
        gu = jnp.dot(n2[pl.ds(2 * s, 2)].reshape(span, width), wgu[:, cols_a:],
                     preferred_element_type=F32)
        dh = last_dims(cot_v[pl.ds(2 * s, 2)].reshape(span, width), wd_v[half_a:])
        (hidden[at, half_a:2 * half_a], dgu[at, cols_a:cols_a + half_a],
         dgu[at, cols_a + half_a:cols_a + 2 * half_a]) = swiglu(
            gu[:, :half_a], gu[:, half_a:2 * half_a], dh[:, :half_a])
        tile = gu[:, 2 * half_a:]
        gate, up, grad = low_half(tile), low_half(roll(tile, 64)), dh[:, half_a:]
        sigma = 1.0 / (1.0 + jnp.exp(-gate))
        active = gate * sigma
        hidden[at, 2 * half_a:] = (active * up).astype(BF16)
        d_gate = grad * up * sigma * (1.0 + gate * (1.0 - sigma))
        dgu[at, cols_a + 2 * half_a:] = (
            d_gate + roll(low_half(grad * active), 64)).astype(BF16)
        out = last_dims(dgu[at, cols_a:], wgu[:, cols_a:])
        out = out + parts[pl.ds(2 * s, 2)].reshape(span, width).astype(F32)
        parts[pl.ds(2 * s, 2)] = out.astype(BF16).reshape(2, rows, width)
        pl.when(k < 2)(lambda: summed.give(b))
        pl.when(k == 2)(summed.take_far)
        pl.when(k == 3)(summed.take_near)
        return carry

    lax.fori_loop(0, 4, feed, 0)
    down_sum.first_hop(add)

    ggu = m["ggu"]
    gu_sum = ChainSum(lambda zk: ggu.at[zk], lambda at: m["gu_slot"].at[at], m["zg_s"], m["zg_r"])

    def farthest(i):
        up = z // 2
        return up * i + (1 - up) * (3 - i)

    def grad_gu(i, carry):
        zk = farthest(i)
        cols = pl.ds(pl.multiple_of(zk * block_rows, 128), block_rows)
        left = n2[:, :, cols].reshape(8 * rows, block_rows)
        ggu[zk] = first_dims(left, dgu[:, cols_a:]).astype(BF16)
        gu_sum.start_one(zk)
        return carry

    lax.fori_loop(0, 2, grad_gu, 0)
    summed.middle()
    lax.fori_loop(2, 4, grad_gu, 0)
    down_sum.second_hop(add)
    summed.finish()

    v = m["mid"][...]
    dv, gain_grad = norm_back(summed.out[...], v, inverse_rms(v), m["g_two"][...])
    m["row_two"][...] = gain_grad
    dmid = cot_v[t_own].astype(F32) + dv
    m["dmid"][...] = dmid
    m["low"][...] = dmid.astype(BF16)
    branch = Gather(m["low"], m["db"], m["gd_s"], m["gd_r"], keep.at[12])
    branch.start()
    gu_sum.first_hop(add, (0,))

    got = m["got"]
    quarter_d = rows_b
    for i in range(4):
        pl.when(r != i)(lambda i=i: spread(i).wait_send())
    for j in range(0, half_a + 128, 128):
        at = half_a + j
        grad = first_dims(hidden[:, at:at + 128], cot_v[...].reshape(8 * rows, width))
        grad = grad.astype(BF16)
        for i in range(4):
            lo, hi = max(j, quarter_d * i), min(j + 128, quarter_d * (i + 1))
            if lo < hi:
                gdo[i, lo - quarter_d * i:hi - quarter_d * i] = grad[lo - j:hi - j]

    summed.sent()

    def down(s, carry):
        at = pl.ds(pl.multiple_of(s * span, span), span)
        out = jnp.dot(hidden[at], wd_v[...], preferred_element_type=F32)
        parts[pl.ds(2 * s, 2)] = out.astype(BF16).reshape(2, rows, width)
        return carry

    lax.fori_loop(0, 4, down, 0)
    mixed = SeqSum(parts, [m[n] for n in SUM_NAMES])

    def give(i, lo, n, ss, rs):
        return remote(gdo.at[i, pl.ds(lo, n)], got.at[r, pl.ds(lo, n)], ss.at[i], rs.at[r],
                      device(base, i // 2, i % 2, z, x))

    def give_all(lo, n, ss, rs):
        for i in range(4):
            pl.when(r != i)(lambda i=i: give(i, lo, n, ss, rs).start())
        got[r, lo:lo + n] = gdo[r, lo:lo + n]

    def given(lo, n, ss, rs):
        for i in range(4):
            pl.when(r != i)(lambda i=i: remote(
                gdo.at[i, pl.ds(lo, n)], got.at[i, pl.ds(lo, n)], ss.at[i], rs.at[i],
                to_c).wait_recv())

    def give_sent(lo, n, ss, rs):
        for i in range(4):
            pl.when(r != i)(lambda i=i: give(i, lo, n, ss, rs).wait_send())

    branch.forward()
    branch.arrive(2)
    branch.keep.wait()
    give_all(0, quarter_d, m["he_s"], m["he_r"])
    mixed.give(0)
    mixed.give(1)
    gu_sum.first_hop(add, (1,))

    def swap(src, out, ss, rs):
        return remote(src.at[pl.ds(own_rows * (1 - x), own_rows)], out.at[t_own], ss, rs, to_x)

    def keep_own(k, src, out):
        copy = pltpu.make_async_copy(src.at[pl.ds(own_rows * x, own_rows)], out.at[t_own],
                                     keep.at[k])
        copy.start()
        return copy

    def swapped(src, out, ss, rs):
        return remote(src.at[pl.ds(own_rows * x, own_rows)], out.at[2 * r + 1 - x], ss, rs, to_x)

    def pairs(out):
        return lambda i: out.at[pl.ds(2 * i, 2)]

    ga_out, gb_out, qkv_out = m["ga_g"], m["gb_g"], m["qkv_g"]
    ga_swap = swap(gga.at[z], ga_out, m["xs_s"], m["xs_r"])
    ga_keep = local_copy(14, gga.at[z, pl.ds(own_rows * x, own_rows)], ga_out.at[t_own])
    da_keep = local_copy(15, got_a.at[z], m["da_g"].at[r])
    ga_share = RepShare(pairs(ga_out), m["ra_s"], m["ra_r"])
    da_share = RepShare(lambda i: m["da_g"].at[i], m["rc_s"], m["rc_r"])


    wo, qkv, dkv = m["wo_v"], qkv_all, kv
    db, dqkv, do_v = m["db"], m["dqkv"], m["do"]
    own_kv = m["own_kv"]
    m["row_head"][...] = jnp.zeros((1, 128), F32)

    down_rest = ChainSum(lambda zk: got.at[zk, pl.ds(0, quarter_d)],
                         lambda at: m["down_slot"].at[at], m["zd_s"], m["zd_r"])

    def swap_first():
        gate_sum.collect(total_in(gga.at[z]))
        down_sum.collect(total_in(got_a.at[z]))
        for copy in (ga_swap, ga_keep, da_keep):
            copy.start()

    def share_first():
        ga_keep.wait()
        da_keep.wait()
        swapped(gga.at[z], ga_out, m["xs_s"], m["xs_r"]).wait_recv()
        ga_share.start()
        da_share.start()

    def order_back(k):
        return (y + k // 2) % 2, (c + 1 + k) % 2

    kv_slot = m["kv_slot"]

    def kv_down(zk, s):
        return remote(dkv.at[zk, s], kv_slot.at[zk, s], m["zk_s"].at[zk, s], m["zk_r"].at[zk, s],
                      device(base, y, c, (z + 3) % 4, x))

    def kv_merge(k):
        b, e = order_back(k)
        s = 2 * b + e

        def one(zk, inner):
            kv_down(zk, s).wait_recv()
            dkv[zk, s] = (dkv[zk, s].astype(F32) + kv_slot[zk, s].astype(F32)).astype(BF16)
            kv_down(zk, s).start()
            return inner

        @pl.when((z == 1) | (z == 2))
        def _():
            lax.fori_loop(0, z, one, 0)

    def attend_back(k, carry):
        pl.when(k == 0)(lambda: branch.arrive(4))
        pl.when(k == 1)(branch.cross)
        pl.when(k == 2)(lambda: [branch.arrive(6), branch.arrive(7)] and None)
        b, e = order_back(k)
        s = 2 * b + e
        grads = db[pl.ds(2 * s, 2)].reshape(span, width)
        d_att = last_dims(grads, wo[...])
        first = d_att[:, 0:128]
        third = jnp.concatenate([jnp.zeros((span, HEAD_DIM), F32), d_att[:, 128:192]], axis=1)
        d_out = [high_half(roll(first, 64)), high_half(first), third]
        att_a = att[s, :, 0:128].astype(F32)
        att_b = att[s, :, 128:192].astype(F32)
        att_b = jnp.concatenate([jnp.zeros((span, HEAD_DIM), F32), att_b], axis=1)
        deltas = []
        for j, o in enumerate((roll(att_a, 64), att_a, att_b)):
            inv = inv_all[s][:, 32 * j:32 * j + 1]
            part_j = (d_out[j].astype(BF16).astype(F32) * inv).astype(BF16)
            do_v[pl.ds(j * span, span)] = part_j
            deltas.append(jnp.sum(part_j.astype(F32) * o, axis=1, keepdims=True))
        delta = jnp.concatenate(deltas, axis=0)
        q_seg[...] = segment_columns(segs, z, s)
        acc[...] = jnp.zeros_like(acc)

        def block(zk, diagonal):
            tile = kv[zk, s]
            q = q_all[s]
            d_out = do_v[...]
            p = exp_scores(q, tile, q_seg[...], segment_row(segs, zk, s), diagonal)
            ds = (p * (last_dims(d_out, tile) - delta)).astype(BF16)
            acc[...] += jnp.dot(ds, tile, preferred_element_type=F32)
            return first_dims(ds, q) + first_dims(p.astype(BF16), d_out)

        def step(zk, inner):
            dkv[zk, s] = block(zk, False).astype(BF16)
            pl.when(z == 3)(lambda: kv_down(zk, s).start())
            return inner

        lax.fori_loop(0, z, step, 0)
        own_kv[s] = block(z, True)
        tiles = split_heads(qkv[s, :, 0:128], qkv[s, :, 128:256])
        back = []
        for j in range(GROUP):
            dy = rotated(low_half(acc[pl.ds(j * span, span)]) * HEAD_DIM ** (-0.5), cos, -sin)
            raw, gain_part = head_back(dy, tiles[j], qg)
            m["row_head"][...] += gain_part
            back.append(raw)
        dqkv[s, :, 0:128] = (back[0] + roll(back[1], 64)).astype(BF16)
        dqkv[s, :, 128:256] = back[2].astype(BF16)
        pl.when(k >= 1)(lambda: kv_merge(k - 1))
        pl.when(k == 0)(lambda: gu_sum.second_hop(add))
        pl.when(k == 0)(mixed.take_far)
        pl.when(k == 0)(mixed.take_near)
        pl.when(k == 1)(swap_first)
        pl.when(k == 2)(mixed.middle)
        pl.when(k == 3)(share_first)
        pl.when(k == 3)(lambda: given(0, quarter_d, m["he_s"], m["he_r"]))
        return carry

    lax.fori_loop(0, 4, attend_back, 0)
    kv_merge(3)
    down_rest.start()
    mixed.finish()
    branch.sent()
    m["low"][...] = (m["mid"][...] + mixed.out[...]).astype(BF16)
    mixed_out = loaded(17, m["low"], m["mixed"])
    mixed.sent()
    free = m["free"]
    for to in (to_c, to_x, to_y):
        pl.semaphore_signal(free, inc=1, device_id=to, device_id_type=MESH)

    for j in range(0, width, 512):
        cols = slice(j, j + 512)
        grad = first_dims(att[...].reshape(8 * rows, Q_COLS),
                          db[:, :, cols].reshape(8 * rows, 512)).astype(BF16)
        for i in range(4):
            gdo[i, quarter_d:quarter_d + quarter_o, cols] = grad[quarter_o * i:quarter_o * (i + 1)]
    give_all(quarter_d, quarter_o, m["hf_s"], m["hf_r"])
    gu_sum.collect(total_in(ggu.at[z]))
    gb_swap = swap(ggu.at[z], gb_out, m["xg_s"], m["xg_r"])
    gb_swap.start()
    gb_keep = keep_own(14, ggu.at[z], gb_out)

    pl.semaphore_wait(free, 3)

    inputs = SeqSum(parts, [m[n] for n in SUM_NAMES])

    def finish_one(k, carry):
        b, e = (y + (k + 1) // 2) % 2, (c + 1 + k // 2) % 2
        s = 2 * b + e
        @pl.when(z < 3)
        def _():
            kv_down(z, s).wait_recv()
            own_kv[s] += kv_slot[z, s].astype(F32)

        total = own_kv[s]
        u = split_heads(qkv[s, :, 0:128], qkv[s, :, 128:256])[GROUP]
        dy = rotated(low_half(total), cos, -sin)
        raw, gain_part = head_back(dy, u, kg)
        m["row_head"][...] += roll(gain_part, 64)
        tile = dqkv[s, :, 128:256].astype(F32)
        dqkv[s, :, 128:256] = (low_half(tile) + roll(raw, 64)).astype(BF16)
        dqkv[s, :, 256:320] = roll(total, 64)[:, 0:HEAD_DIM].astype(BF16)
        out = last_dims(dqkv[s], wq[...]).astype(BF16)
        parts[pl.ds(2 * s, 2)] = out.reshape(2, rows, width)
        pl.when(k < 2)(lambda: inputs.give(b))
        pl.when(k == 2)(inputs.take_far)
        pl.when(k == 3)(inputs.take_near)
        return carry

    lax.fori_loop(0, 4, finish_one, 0)
    down_rest.first_hop(add)
    gqkv = m["gqkv"]
    qkv_sum = DirectBoth(lambda zk, a: gqkv.at[zk, pl.ds(own_rows * a, own_rows)],
                         lambda zk, a: m["qkv_slot"].at[zk, a], m["zq_s"], m["zq_r"])

    def grad_qkv(i, carry):
        zk = farthest(i)
        cols = pl.ds(pl.multiple_of(zk * block_rows, 128), block_rows)
        left = normed[:, :, cols].reshape(8 * rows, block_rows)
        gqkv[zk] = first_dims(left, dqkv[...].reshape(8 * rows, HEAD_COLS)).astype(BF16)
        qkv_sum.start(zk)
        return carry

    lax.fori_loop(0, 4, grad_qkv, 0)
    inputs.middle()
    down_rest.second_hop(add)
    given(quarter_d, quarter_o, m["hf_s"], m["hf_r"])
    out_sum = Direct(lambda zk: got.at[zk, pl.ds(quarter_d, quarter_o)],
                     lambda zk: m["out_slot"].at[zk], m["zo_s"], m["zo_r"])

    def start_out(i, carry):
        out_sum.start(farthest(i))
        return carry

    lax.fori_loop(0, 4, start_out, 0)
    ga_share.forward()
    da_share.forward()

    inputs.finish()
    v = m["tok"][...].astype(F32)
    dv, gain_grad = norm_back(inputs.out[...], v, inverse_rms(v), m["g_one"][...])
    m["dmid"][...] += dv
    grad_out = loaded(18, m["dmid"], m["input_grad"])

    def gain_rows_of(k):
        return m["mid"].at[pl.ds(8 * k, 8)]

    gains_own = gain_rows_of(0)
    gains_own[0:1] = gain_grad
    gains_own[1:2] = m["row_two"][...]
    gains_own[2:3, 0:128] = m["row_head"][...]

    def gain_sum(k):
        return remote(gains_own, gain_rows_of(k), m["gm_s"].at[k - 1], m["gm_r"].at[k - 1],
                      mates[k - 1])

    for k in range(1, 8):
        gain_sum(k).start()
    gb_keep.wait()
    swapped(ggu.at[z], gb_out, m["xg_s"], m["xg_r"]).wait_recv()
    gb_share = RepShare(pairs(gb_out), m["rg_s"], m["rg_r"])
    gb_share.start()

    down_rest.collect(total_in(got.at[z, pl.ds(0, quarter_d)]))
    db_keep = loaded(15, got.at[z, pl.ds(0, quarter_d)], m["db_g"].at[r])
    for k in range(1, 8):
        gain_sum(k).wait_recv()
    total = gains_own[...]
    for k in range(1, 8):
        total = total + gain_rows_of(k)[...]
    z_rows = m["z_rows"]
    z_rows[0] = total

    def gain_z(k):
        return remote(z_rows.at[0], z_rows.at[k], m["gz_s"].at[k - 1], m["gz_r"].at[k - 1],
                      device(base, y, c, (z + k) % 4, x))

    for k in range(1, 4):
        gain_z(k).start()
    db_keep.wait()
    db_share = RepShare(lambda i: m["db_g"].at[i], m["rd_s"], m["rd_r"])
    db_share.start()
    gb_share.forward()

    qkv_own = m["qkv_slot"].at[z]
    total = gqkv[z, pl.ds(own_rows * x, own_rows)].astype(F32)
    for k in (1, 3, 2):
        qkv_sum.arrive((z + k) % 4, x)
        total = total + m["qkv_slot"][(z + k) % 4, x].astype(F32)
    qkv_own[x] = total.astype(BF16)
    total = jnp.zeros((own_rows, HEAD_COLS), F32)
    for k in (0, 1, 3, 2):
        qkv_sum.arrive((z + k) % 4, 1 - x)
        total = total + m["qkv_slot"][(z + k) % 4, 1 - x].astype(F32)
    qkv_own[1 - x] = total.astype(BF16)
    qkv_keep = loaded(16, qkv_own, pairs(qkv_out)(r))
    qkv_keep.wait()
    qkv_share = RepShare(pairs(qkv_out), m["rq_s"], m["rq_r"])
    qkv_share.start()

    out_own = got.at[z, pl.ds(quarter_d, quarter_o)]
    total = out_own[...].astype(F32)
    for term in out_sum.take():
        total = total + term
    out_own[...] = total.astype(BF16)
    out_keep = loaded(0, out_own, m["out_g"].at[r])
    out_keep.wait()
    out_share = RepShare(lambda i: m["out_g"].at[i], m["re_s"], m["re_r"])
    out_share.start()
    db_share.forward()
    for k in range(1, 4):
        gain_z(k).wait_recv()
    m["gains_g"][...] = z_rows[0] + z_rows[1] + z_rows[2] + z_rows[3]
    qkv_share.forward()
    out_share.forward()
    shares = (ga_share, da_share, gb_share, db_share, out_share, qkv_share)
    for share in shares:
        share.finish()

    for share in shares:
        share.sent()
    for copy in (ga_swap, gb_swap):
        copy.wait_send()
    for k in range(1, 8):
        gain_sum(k).wait_send()
    for k in range(1, 4):
        gain_z(k).wait_send()
    mixed_out.wait()
    grad_out.wait()
    for flow in (gu_sum, down_rest, qkv_sum, out_sum, inputs):
        flow.sent()
    give_sent(0, quarter_d, m["he_s"], m["he_r"])
    give_sent(quarter_d, quarter_o, m["hf_s"], m["hf_r"])

    def dkv_sent(s, carry):
        for zk in range(3):
            pl.when(z > zk)(lambda zk=zk: kv_down(zk, s).wait_send())
        return carry

    lax.fori_loop(0, 4, dkv_sent, 0)
    for flow in (near, flip, out_q, gate_a, gate_b, down_a, down_b, gate_sum, down_sum):
        flow.sent()
    over.wait_send()
    for k in range(1, 8):
        seg_copy(k).wait_send()
        gain_copy(k).wait_send()
    for k in range(1, 4):
        pl.when(z + k < 4)(lambda k=k: seg_up(k).wait_send())

    def kv_sent(s, carry):
        for d in (1, 2, 3):
            pl.when(z + d < 4)(lambda d=d: kv_copy(d, s).wait_send())
        return carry

    lax.fori_loop(0, 4, kv_sent, 0)
    hand_sent(m["zo"], m["wo_v"], out_sems, quarter_o)
    hand_sent(m["za"], wda, a_sems, rows_a)
    hand_sent(m["zb"], wdb, b_sems, rows_b)


SUM_NAMES = ("r1", "chip", "rx", "ry", "mine", "late", "sum_out", "sum_s", "sum_r")
IN = ("tok", "cot", "small", "wqkv", "wgu", "wd", "wo", "rope")
OUT = ("mixed", "input_grad", "gains_g", "ga_g", "gb_g", "da_g", "db_g", "out_g", "qkv_g",
       "zo", "za", "zb", "gains_all")


def block_call(*args):
    shape = jax.ShapeDtypeStruct
    tok, _, _, wqkv, wgu, wd, wo = args[:7]
    rows, width = tok.shape
    span = 2 * rows
    own_rows = wqkv.shape[0]
    seg, gains = shape((8, rows), jnp.int32), shape((16, 256), BF16)
    part = wgu.shape[1] // 16
    half_a = part // 256 * 128
    part_b = part - half_a
    cols_a, cols_b = 2 * half_a, 2 * half_a + 128
    quarter_a, quarter_d, quarter_o = half_a // 4, part_b // 4, own_rows // 4
    heads = GROUP * span
    outs = {
        "mixed": shape((rows, width), BF16),
        "input_grad": shape((rows, width), F32),
        "gains_g": shape((8, width), F32),
        "ga_g": shape((8, own_rows, cols_a), BF16),
        "gb_g": shape((8, own_rows, cols_b), BF16),
        "da_g": shape((4, quarter_a, width), BF16),
        "db_g": shape((4, quarter_d, width), BF16),
        "out_g": shape((4, quarter_o, width), BF16),
        "qkv_g": shape((8, own_rows, HEAD_COLS), BF16),
        "zo": shape((4, quarter_o, width), BF16),
        "za": shape((4, quarter_a, width), BF16),
        "zb": shape((4, quarter_d, width), BF16),
        "gains_all": shape((8,) + gains.shape, BF16),
    }
    buffers = {
        "tok_all": ((8, rows, width), BF16), "cot_v": ((8, rows, width), BF16),
        "n2_v": ((8, rows, width), BF16), "db": ((8, rows, width), BF16),
        "part": ((8, rows, width), BF16),
        "seg": (seg.shape, seg.dtype), "gains": (gains.shape, BF16),
        "wq": ((2, own_rows, HEAD_COLS), BF16), "wq_raw": ((own_rows, 640), BF16),
        "segs_v": ((4, 8) + seg.shape, seg.dtype), "gains_v": ((8,) + gains.shape, BF16),
        "wq_v": ((width, HEAD_COLS), BF16), "wo_v": ((Q_COLS, width), BF16),
        "wgu_v": ((width, cols_a + cols_b), BF16), "wd_v": ((2 * half_a + 128, width), BF16),
        "hidden": ((8 * rows, 2 * half_a + 128), BF16),
        "dgu": ((8 * rows, cols_a + cols_b), BF16),
        "qkv_v": ((4, span, 256), F32), "q_v": ((4, heads, 128), BF16),
        "kv_v": ((4, 4, span, 128), BF16), "kv_slot": ((3, 4, span, 128), BF16),
        "own_kv": ((4, span, 128), F32), "inv_v": ((4, span, 128), F32),
        "att_v": ((4, span, Q_COLS), BF16), "acc": ((heads, 128), F32),
        "do": ((heads, 128), BF16), "q_seg": ((span, span), jnp.int32),
        "dqkv": ((4, span, HEAD_COLS), BF16),
        "mid": ((rows, width), F32), "dmid": ((rows, width), F32), "low": ((rows, width), BF16),
        "g_one": ((1, width), F32), "g_two": ((1, width), F32),
        "gga": ((4, 2 * own_rows, cols_a), BF16), "gga_slot": ((5, 2 * own_rows, cols_a), BF16),
        "ggu": ((4, 2 * own_rows, cols_b), BF16), "gu_slot": ((5, 2 * own_rows, cols_b), BF16),
        "got_a": ((4, quarter_a, width), BF16),
        "gda_slot": ((5, quarter_a, width), BF16),
        "gdo": ((4, quarter_d + quarter_o, width), BF16),
        "got": ((4, quarter_d + quarter_o, width), BF16),
        "down_slot": ((5, quarter_d, width), BF16),
        "out_slot": ((4, quarter_o, width), BF16),
        "gqkv": ((4, 2 * own_rows, HEAD_COLS), BF16),
        "qkv_slot": ((4, 2, own_rows, HEAD_COLS), BF16),
        "row_two": ((1, width), F32), "row_head": ((1, 128), F32),
        "z_rows": ((4, 8, width), F32),
    }
    counts = {
        "ga": (8, 8), "gb": (8, 8), "gc": (8, 8), "gd": (8, 8), "sg": (7, 7), "gn": (7, 7),
        "gm": (7, 7), "gz": (3, 3), "wa": (6, 4), "wb": (6, 4), "wo": (6, 4), "wx": (1, 1),
        "xa": (1, 1), "xb": (1, 1), "xs": (1, 1), "xg": (1, 1), "ca": (5, 4), "cb": (5, 4),
        "da": (5, 4), "db": (5, 4), "ys": (4, 5), "yd": (4, 5), "zg": (4, 5), "zd": (4, 5),
        "zo": (4, 4), "zq": ((4, 2), (4, 2)), "zk": ((3, 4), (3, 4)), "kv": ((3, 4), (4, 4)),
        "su": (3, 4), "ha": (4, 4), "hb": (4, 4), "hd": (4, 4), "he": (4, 4), "hf": (4, 4),
        "ho": (4, 4), "ra": (3, 3), "rc": (3, 3), "rd": (3, 3), "re": (3, 3), "rg": (3, 3),
        "rq": (3, 3),
    }
    sem = pltpu.SemaphoreType.DMA
    many = lambda n: sem if n == 1 else sem(n if isinstance(n, tuple) else (n,))
    sems = {"keep": dma(21), "free": pltpu.SemaphoreType.REGULAR}
    for n, (send, recv) in counts.items():
        sems[n + "_s"], sems[n + "_r"] = many(send), many(recv)
    scratch = {n: pltpu.VMEM(*v) for n, v in buffers.items()}
    scratch.update(zip(SUM_NAMES, seq_scratch(width)))
    names = IN + OUT + tuple(scratch) + tuple(sems)
    got = pl.pallas_call(
        functools.partial(block_kernel, names),
        name="block",
        out_shape=tuple(outs[n] for n in OUT),
        in_specs=[ANY if n in ("cot", "wqkv", "wgu", "wd", "wo") else VMEM for n in IN],
        out_specs=tuple(VMEM if n == "gains_g" else ANY for n in OUT),
        scratch_shapes=list(scratch.values()) + list(sems.values()),
        compiler_params=params(0, 63),
    )(*args)
    return dict(zip(OUT, got))


def order_kernel(names, *refs):
    m = dict(zip(names, refs))
    half_a = m["ga"].shape[2] // 2
    half_b = (m["gb"].shape[2] - 128) // 2
    main = half_a + half_b
    cols = 2 * main + 128
    own_rows = m["ga"].shape[1]
    low = lanes((own_rows, 128)) < HEAD_DIM
    x = lax.axis_index("grp") % 2

    def fetch(k, src, dst):
        copy = pltpu.make_async_copy(src, dst, m["load"].at[k])
        copy.start()
        return copy

    def store(k, src, dst):
        copy = pltpu.make_async_copy(src, dst, m["save"].at[k])
        copy.start()
        return copy

    ga, gb = m["ga_v"], m["gb_v"]
    pair = lambda i: pl.ds(2 * i, 2)
    wide = [(fetch(2 * i, m["ga"].at[pair(i)], ga.at[pair(i)]),
             fetch(2 * i + 1, m["gb"].at[pair(i)], gb.at[pair(i)])) for i in range(4)]
    rest = {n: fetch(8 + k, m[n], m[n + "_v"])
            for k, n in enumerate(("db", "qkv", "da", "out", "ig", "mixed"))}
    saved = []
    for i in range(4):
        for copy in wide[i]:
            copy.wait()
        first, second = ga.at[2 * i], ga.at[2 * i + 1]
        tiles = [gb[2 * i + k, :, 2 * half_b:].astype(F32) for k in range(2)]
        for w in range(2):
            to = m["gu_v"].at[4 * w + i]
            for k in range(2):
                lo = k * (main + 128)
                to[:, lo:lo + half_a] = ga[2 * i + k, :, w * half_a:(w + 1) * half_a].astype(F32)
                to[:, lo + half_a:lo + main] = (
                    gb[2 * i + k, :, w * half_b:(w + 1) * half_b].astype(F32))
            if w == 0:
                to[:, main:main + 128] = jnp.where(low, tiles[0], roll(tiles[1], 64))
            else:
                to[:, main:main + 128] = jnp.where(low, roll(tiles[0], 64), tiles[1])
            saved.append(store(
                4 * w + i, to, m["gu_o"].at[:, pl.ds((4 * w + i) * cols, cols)]))

    rest["da"].wait()
    rest["db"].wait()
    da, db, down = m["da_v"], m["db_v"], m["down_v"]
    part = down.shape[0]
    rows_a, rows_b = da.shape[1], db.shape[1]
    shift = (part - main) * x

    def at(start, n):
        return pl.ds(pl.multiple_of(start, 16), n)

    for i in range(4):
        down[at(rows_a * i + shift, rows_a)] = da[i].astype(F32)
        start = half_a + rows_b * i + shift
        down[at(start, 16)] = db[i, 0:16].astype(F32)
        down[at(start + 16 - (i // 3) * x * part, rows_b - 16)] = db[i, 16:].astype(F32)
    saved.append(store(8, down, m["down_o"]))
    rest["qkv"].wait()
    qkv_v, qkv_f = m["qkv_v"], m["qkv_f"]
    q_cols, kv_cols = HEADS * HEAD_DIM, KV_HEADS * HEAD_DIM
    half = lambda v, w: jnp.where(low, v, w)
    for i in range(4):
        a, b = qkv_v[2 * i].astype(F32), qkv_v[2 * i + 1].astype(F32)
        a1, a2, b0, b1 = a[:, 128:256], a[:, 256:], b[:, 0:128], b[:, 128:256]
        lo = i * 2 * Q_COLS
        qkv_f[:, lo:lo + 128] = a[:, 0:128]
        qkv_f[:, lo + 128:lo + 256] = half(a1, roll(b0, 64))
        qkv_f[:, lo + 256:lo + 384] = half(roll(b0, 64), roll(b1, 64))
        lo = q_cols + i * 128
        qkv_f[:, lo:lo + 128] = half(roll(a1, 64), b1)
        lo = lo + kv_cols
        qkv_f[:, lo:lo + 128] = jnp.concatenate([a2, b[:, 256:]], axis=1)
    saved.append(store(9, qkv_f, m["qkv_o"]))
    rest["out"].wait()
    n = m["out_v"].shape[1]
    for i in range(4):
        m["out_f"][n * i:n * (i + 1)] = m["out_v"][i].astype(F32)
    saved.append(store(10, m["out_f"], m["out_o"]))
    for k, n in ((11, "ig"), (12, "mixed")):
        rest[n].wait()
        saved.append(store(k, m[n + "_v"], m[n + "_o"]))
    gains = m["gains"][...]
    width = gains.shape[1]
    turned = pltpu.roll(gains, (width - own_rows * lax.axis_index("grp")) % width, 1)
    m["one_o"][...] = turned[0:1, 0:own_rows]
    m["two_o"][...] = turned[1:2, 0:own_rows]
    m["q_o"][...] = gains[2:3, 0:HEAD_DIM]
    m["k_o"][...] = gains[2:3, HEAD_DIM:2 * HEAD_DIM]
    for copy in saved:
        copy.wait()


def order_call(g):
    shape = jax.ShapeDtypeStruct
    ga, gb, da, db, out, qkv, mixed, ig = (g[n] for n in ORDER_IN)
    _, own_rows, cols_a = ga.shape
    cols = cols_a + gb.shape[2]
    width = da.shape[2]
    part = 4 * (da.shape[1] + db.shape[1])
    qkv_cols = (HEADS + 2 * KV_HEADS) * HEAD_DIM
    outs = {
        "gu_o": shape((own_rows, 8 * cols), F32), "down_o": shape((part, width), F32),
        "out_o": shape((own_rows, width), F32), "qkv_o": shape((own_rows, qkv_cols), F32),
        "ig_o": shape(ig.shape, F32), "mixed_o": shape(mixed.shape, BF16),
        "one_o": shape((1, own_rows), F32), "two_o": shape((1, own_rows), F32),
        "q_o": shape((1, HEAD_DIM), F32), "k_o": shape((1, HEAD_DIM), F32),
    }
    ins = ("ga", "gb", "da", "db", "out", "qkv", "mixed", "ig")
    scratch = {n + "_v": pltpu.VMEM(v.shape, v.dtype)
               for n, v in zip(ins, (ga, gb, da, db, out, qkv, mixed, ig))}
    scratch["gu_v"] = pltpu.VMEM((8, own_rows, cols), F32)
    scratch["down_v"] = pltpu.VMEM((part, width), F32)
    scratch["out_f"] = pltpu.VMEM((own_rows, width), F32)
    scratch["qkv_f"] = pltpu.VMEM((own_rows, qkv_cols), F32)
    scratch["load"], scratch["save"] = dma(14), dma(13)
    names = ins + ("gains",) + tuple(outs) + tuple(scratch)
    got = pl.pallas_call(
        functools.partial(order_kernel, names),
        name="final_order",
        out_shape=tuple(outs.values()),
        in_specs=[ANY] * 8 + [VMEM],
        out_specs=(ANY,) * 6 + (VMEM,) * 4,
        scratch_shapes=list(scratch.values()),
        compiler_params=pltpu.CompilerParams(vmem_limit_bytes=62 * 2**20),
    )(ga, gb, da, db, out, qkv, mixed, ig, g["gains_g"])
    return dict(zip(outs, got))


ORDER_IN = ("ga_g", "gb_g", "da_g", "db_g", "out_g", "qkv_g", "mixed", "input_grad")


def rope_table(start, rows):
    half = HEAD_DIM // 2
    lane = lax.broadcasted_iota(jnp.int32, (rows, 4 * half), 1)
    freq = jnp.exp(-jnp.log(THETA) * (lane % half).astype(F32) * 2.0 / HEAD_DIM)
    position = start + lax.broadcasted_iota(jnp.int32, (rows, 4 * half), 0)
    angle = position.astype(F32) * freq
    sine = jnp.sin(angle)
    return jnp.where(lane < 2 * half, jnp.cos(angle), jnp.where(lane < 3 * half, -sine, sine))


def over_quads(array):
    reps = lax.axis_size("rep")
    if reps == 4:
        return array
    rows = [[j + 4 * q for q in range(reps // 4)] for j in range(4)]
    return lax.psum(array, "rep", axis_index_groups=rows)


def local(tokens, attn_gain, w_qkv, q_gain, k_gain, w_out, ffn_gain, w_gate_up, w_down,
          cotangent, segment_ids):
    rows, width = tokens.shape
    _, y, c, z, x = here()
    r = 2 * y + c
    span = 2 * rows
    rope = rope_table(span * z, span)
    parts = (attn_gain, q_gain, ffn_gain, k_gain, segment_ids)
    total = sum(v.shape[0] for v in parts)
    small, at = 0.0, 0
    for v in parts:
        n = v.shape[0]
        small = small + jnp.pad(v.astype(F32)[None], ((0, 0), (at, total - at - n)))
        at += n
    g = block_call(tokens, cotangent, small, w_qkv, w_gate_up, w_down, w_out, rope)
    g = {n: over_quads(v) if n.endswith("_g") else v for n, v in g.items()}
    o = order_call(g)
    flat = lambda n: o[n].reshape(-1)
    return (o["mixed_o"], o["ig_o"], flat("one_o"), o["qkv_o"], flat("q_o"), flat("k_o"),
            o["out_o"], flat("two_o"), o["gu_o"], o["down_o"])


def solution(mesh):
    rows, split = P(("rep", "grp"), None), P("grp", None)
    return jax.shard_map(
        local,
        mesh=mesh,
        in_specs=(rows, P("grp"), split, P(), P(), split, P("grp"), split, split, rows,
                  P(("rep", "grp"))),
        out_specs=(rows, rows, P("grp"), split, P(), P(), split, P("grp"), split, split),
        check_vma=False,
    )
```

```python
import functools

import jax
import jax.numpy as jnp
from jax import lax
from jax.experimental import pallas as pl
from jax.experimental.pallas import tpu as pltpu
from jax.sharding import PartitionSpec as P

HEADS = 24
KV_HEADS = 8
HEAD_DIM = 64
GROUP = HEADS // KV_HEADS
Q_COLS = GROUP * HEAD_DIM
HEAD_COLS = Q_COLS + 2 * HEAD_DIM

EPS = 1e-05
THETA = 1000000.0
MESH = pl.DeviceIdType.MESH
F32 = jnp.float32
BF16 = jnp.bfloat16

VMEM = pl.BlockSpec(memory_space=pltpu.VMEM)
ANY = pl.BlockSpec(memory_space=pl.ANY)


def here():
    rep = lax.axis_index("rep")
    grp = lax.axis_index("grp")
    r = rep % 4
    return rep - r, r // 2, r % 2, grp // 2, grp % 2


def device(base, y, c, z, x):
    return {"rep": base + 2 * y + c, "grp": 2 * z + x}


def remote(src, dst, send, recv, to):
    return pltpu.make_async_remote_copy(
        src_ref=src, dst_ref=dst, send_sem=send, recv_sem=recv, device_id=to, device_id_type=MESH
    )


def greet(targets):
    barrier = pltpu.get_barrier_semaphore()
    for to in targets:
        pl.semaphore_signal(barrier, inc=1, device_id=to, device_id_type=MESH)
    pl.semaphore_wait(barrier, len(targets))


def neighbours():
    base, y, c, z, x = here()
    to_c = device(base, y, 1 - c, z, x)
    to_x = device(base, y, c, z, 1 - x)
    to_y = device(base, 1 - y, c, z, x)
    return to_c, to_x, to_y


class Gather:
    def __init__(self, src, out, send, recv, local):
        self.src, self.out, self.send, self.recv = src, out, send, recv
        _, y, c, _, x = here()
        self.to_c, self.to_x, self.to_y = neighbours()
        slot = lambda a, b, d: 4 * a + 2 * b + d
        self.own = slot(y, c, x)
        self.at_c, self.at_x, self.at_y = slot(y, 1 - c, x), slot(y, c, 1 - x), slot(1 - y, c, x)
        self.at_xc, self.at_yc = slot(y, 1 - c, 1 - x), slot(1 - y, 1 - c, x)
        self.at_xy, self.at_xyc = slot(1 - y, c, 1 - x), slot(1 - y, 1 - c, 1 - x)
        self.half = src.shape[0] // 2
        self.keep = pltpu.make_async_copy(src, out.at[self.own], local)

    def part(self, at, k):
        return self.out.at[at, pl.ds(k * self.half, self.half)]

    def copy(self, k):
        out, own = self.out, self.out.at[self.own]
        src, dst, to = (
            lambda: (self.src, own, self.to_x),
            lambda: (self.src, own, self.to_y),
            lambda: (self.src, own, self.to_c),
            lambda: (self.part(self.at_x, 0),) * 2 + (self.to_y,),
            lambda: (out.at[self.at_x],) * 2 + (self.to_c,),
            lambda: (self.part(self.at_y, 1),) * 2 + (self.to_x,),
            lambda: (out.at[self.at_y],) * 2 + (self.to_c,),
            lambda: (out.at[self.at_xy],) * 2 + (self.to_c,),
        )[k]()
        return remote(src, dst, self.send.at[k], self.recv.at[k], to)

    def arrive(self, k):
        out = self.out
        ref = (
            lambda: out.at[self.at_x], lambda: out.at[self.at_y], lambda: out.at[self.at_c],
            lambda: self.part(self.at_xy, 0), lambda: out.at[self.at_xc],
            lambda: self.part(self.at_xy, 1), lambda: out.at[self.at_yc],
            lambda: out.at[self.at_xyc],
        )[k]()
        remote(ref, ref, self.send.at[k], self.recv.at[k], self.to_c).wait_recv()

    def start(self):
        self.keep.start()
        for k in range(3):
            self.copy(k).start()

    def forward(self):
        self.arrive(0)
        self.copy(3).start()
        self.copy(4).start()
        self.arrive(1)
        self.copy(5).start()
        self.copy(6).start()

    def cross(self):
        self.arrive(3)
        self.arrive(5)
        self.copy(7).start()

    def finish(self):
        self.cross()
        for k in (2, 4, 6, 7):
            self.arrive(k)
        self.keep.wait()
        self.sent()

    def sent(self):
        for k in range(8):
            self.copy(k).wait_send()


def dma(n):
    return pltpu.SemaphoreType.DMA((n,))


def params(cid, limit=60):
    return pltpu.CompilerParams(
        collective_id=cid, has_side_effects=True, vmem_limit_bytes=limit * 2**20
    )


def inverse_rms(v):
    return lax.rsqrt(jnp.mean(v * v, axis=-1, keepdims=True) + EPS)


def norm_back(dy, v, inv, gain):
    scaled = dy * gain
    gain_grad = jnp.sum(dy * v * inv, axis=0, keepdims=True)
    inner = jnp.mean(scaled * v, axis=-1, keepdims=True)
    return inv * scaled - v * inv * inv * inv * inner, gain_grad


def when(cond):
    return pl.when(cond)


def lanes(shape):
    return lax.broadcasted_iota(jnp.int32, shape, len(shape) - 1)


def roll(v, by):
    return pltpu.roll(v, by % v.shape[-1], v.ndim - 1)


class Along:
    def __init__(self, src, slot, send, recv):
        self.src, self.slot, self.send, self.recv = src, slot, send, recv
        self.base, self.y, self.c, self.z, self.x = here()

    def at(self, zk, x):
        return device(self.base, self.y, self.c, zk, x)

    def copy(self, d):
        zk = (self.z + d + 4) % 4
        return remote(self.src, self.slot(self.z), self.send.at[d + 2], self.recv.at[self.z],
                      self.at(zk, self.x))

    def fits(self, d):
        return (self.z + d >= 0) & (self.z + d < 4)

    def first(self):
        for d in (2, -2):
            pl.when(self.fits(d))(lambda d=d: self.copy(d).start())
        pl.when(self.z == 2)(lambda: self.copy(1).start())
        pl.when(self.z == 1)(lambda: self.copy(-1).start())

    def second(self):
        pl.when(self.z < 2)(lambda: self.copy(1).start())
        pl.when(self.z >= 2)(lambda: self.copy(-1).start())

    def arrival(self, zk):
        ref = self.slot(zk)
        return remote(ref, ref, self.send.at[0], self.recv.at[zk], self.at(self.z, 1 - self.x))

    def passed(self, zk, to):
        ref = self.slot(zk)
        return remote(ref, ref, self.send.at[5], self.recv.at[zk], self.at(to, self.x))

    def forward(self):
        @pl.when(self.z == 2)
        def _():
            self.arrival(0).wait_recv()
            self.passed(0, 3).start()

        @pl.when(self.z == 1)
        def _():
            self.arrival(3).wait_recv()
            self.passed(3, 0).start()

    def wait(self, zk):
        early = ((self.z == 2) & (zk == 0)) | ((self.z == 1) & (zk == 3))
        due = jnp.logical_not(early) & (self.z != zk)
        pl.when(due)(lambda: self.arrival(zk).wait_recv())

    def finish(self):
        for zk in range(4):
            self.wait(zk)

    def sent(self):
        for d in (2, -2, 1, -1):
            pl.when(self.fits(d))(lambda d=d: self.copy(d).wait_send())
        pl.when(self.z == 2)(lambda: self.passed(0, 3).wait_send())
        pl.when(self.z == 1)(lambda: self.passed(3, 0).wait_send())


class Chain:
    def __init__(self, slot, send, recv):
        self.slot, self.send, self.recv = slot, send, recv
        self.base, self.y, self.c, self.z, self.x = here()

    def copy(self, k, zk, to):
        return remote(self.slot(zk), self.slot(zk), self.send.at[k], self.recv.at[zk],
                      device(self.base, self.y, self.c, to, self.x))

    def arrive(self, zk):
        self.copy(0, zk, self.z).wait_recv()

    def inner(self):
        return (self.z == 1) | (self.z == 2)

    def start_ends(self):
        pl.when(self.z == 0)(lambda: self.copy(0, 0, 1).start())
        pl.when(self.z == 3)(lambda: self.copy(1, 3, 2).start())

    def start_inner(self):
        z = self.z

        @pl.when(self.inner())
        def _():
            self.copy(0, z, z + 1).start()
            self.copy(1, z, z - 1).start()

    def pass_ends(self):
        @pl.when(self.z == 1)
        def _():
            self.arrive(0)
            self.copy(2, 0, 2).start()

        @pl.when(self.z == 2)
        def _():
            self.arrive(3)
            self.copy(3, 3, 1).start()

    def pass_inner(self):
        @pl.when(self.z == 1)
        def _():
            self.arrive(2)
            self.copy(3, 2, 0).start()

        @pl.when(self.z == 2)
        def _():
            self.arrive(1)
            self.copy(2, 1, 3).start()

    def second(self):
        self.pass_ends()
        self.pass_inner()

    def third(self):
        @pl.when(self.z == 2)
        def _():
            self.arrive(0)
            self.copy(4, 0, 3).start()

        @pl.when(self.z == 1)
        def _():
            self.arrive(3)
            self.copy(4, 3, 0).start()

    def finish(self):
        pl.when(self.z == 0)(lambda: [self.arrive(zk) for zk in (1, 2, 3)] and None)
        pl.when(self.z == 3)(lambda: [self.arrive(zk) for zk in (2, 1, 0)] and None)

    def sent(self):
        z = self.z
        pl.when(z < 3)(lambda: self.copy(0, z, z + 1).wait_send())
        pl.when(z > 0)(lambda: self.copy(1, z, z - 1).wait_send())

        @pl.when(self.inner())
        def _():
            self.copy(2, z - 1, z + 1).wait_send()
            self.copy(3, z + 1, z - 1).wait_send()
            self.copy(4, z, z + 1).wait_send()


class ChainSum:
    def __init__(self, block, slot, send, recv):
        self.block, self.slot, self.send, self.recv = block, slot, send, recv
        self.base, self.y, self.c, self.z, self.x = here()

    def copy(self, zk, to, at):
        return remote(self.block(zk), self.slot(at), self.send.at[zk], self.recv.at[at],
                      device(self.base, self.y, self.c, to, self.x))

    def arrive(self, at):
        self.copy(0, self.z, at).wait_recv()

    def start(self):
        @pl.when(self.z == 0)
        def _():
            for zk, at in ((3, 3), (2, 2), (1, 4)):
                self.copy(zk, 1, at).start()

        @pl.when(self.z == 3)
        def _():
            for zk in (0, 1, 2):
                self.copy(zk, 2, zk).start()

    def start_one(self, zk):
        for to, at in ((3, 3), (2, 2), (1, 4)):
            pl.when((self.z == 0) & (zk == to))(
                lambda to=to, at=at: self.copy(to, 1, at).start())
        for to in (0, 1, 2):
            pl.when((self.z == 3) & (zk == to))(lambda to=to: self.copy(to, 2, to).start())

    def first_hop(self, add, which=(0, 1)):
        @pl.when(self.z == 1)
        def _():
            for i in which:
                zk, at = ((3, 3), (2, 4))[i]
                self.arrive(zk)
                add(self.block(zk), self.slot(zk))
                self.copy(zk, 2, at).start()

        @pl.when(self.z == 2)
        def _():
            for zk in which:
                self.arrive(zk)
                add(self.block(zk), self.slot(zk))
                self.copy(zk, 1, zk).start()

    def second_hop(self, add, inner=(1, 2)):
        for z, zk, to, at in ((1, 0, 0, 0), (2, 3, 3, 4)):
            if z not in inner:
                continue

            @pl.when(self.z == z)
            def _():
                self.arrive(zk)
                add(self.block(zk), self.slot(zk))
                self.copy(zk, to, at).start()

    def collect(self, total):
        z = self.z

        def take(ats):
            for at in ats:
                self.arrive(at)
            total([self.slot(at) for at in ats])

        pl.when(z == 0)(lambda: take([0]))
        pl.when(z == 3)(lambda: take([4]))
        pl.when((z == 1) | (z == 2))(lambda: take([z, 4]))

    def sent(self):
        for zk in range(4):
            pl.when(self.z != zk)(lambda zk=zk: self.copy(zk, 0, 0).wait_send())


def layer_mates():
    base, y, c, z, x = here()
    return [
        device(base, (y + k // 4) % 2, (c + k // 2) % 2, z, (x + k) % 2) for k in range(1, 8)
    ]


def z_mates():
    base, y, c, z, x = here()
    return [device(base, y, c, (z + k // 2) % 4, (x + k) % 2) for k in range(2, 8)]


def rotated(u, cos, sin):
    lane = lanes(u.shape)
    return u * cos + jnp.where(lane < 32, roll(u, -32), roll(u, 32)) * sin


def low_half(v):
    return jnp.where(lanes(v.shape) < HEAD_DIM, v, 0.0)


def high_half(v):
    return jnp.where(lanes(v.shape) >= HEAD_DIM, v, 0.0)


def split_heads(tile_a, tile_b):
    return [low_half(tile_a), low_half(roll(tile_a, 64)), low_half(tile_b),
            low_half(roll(tile_b, 64))]


def head_inverse(u):
    return lax.rsqrt(jnp.sum(u * u, axis=-1, keepdims=True) * (1.0 / HEAD_DIM) + EPS)


def exp_scores(q, kv, q_seg, k_seg, diagonal):
    s = lax.dot_general(q, kv, (((1,), (1,)), ((), ())), preferred_element_type=F32)
    allowed = q_seg == k_seg
    if diagonal:
        row = lax.broadcasted_iota(jnp.int32, allowed.shape, 0)
        col = lax.broadcasted_iota(jnp.int32, allowed.shape, 1)
        allowed = allowed & (col <= row)
    n = allowed.shape[0]
    return jnp.concatenate([
        jnp.where(allowed, jnp.exp(s[n * j:n * (j + 1)]), 0.0) for j in range(GROUP)], axis=0)


def segment_row(segs, zk, s):
    return jnp.concatenate([segs[zk, 2 * s, 0:1], segs[zk, 2 * s + 1, 0:1]], axis=1)


def segment_columns(segs, zk, s):
    parts = []
    for i in range(2):
        row = jnp.broadcast_to(segs[zk, 2 * s + i, 0:1], (128, 128))
        parts.append(jnp.transpose(row))
    col = jnp.concatenate(parts, axis=0)
    return jnp.concatenate([col, col], axis=1)


class SeqSum:
    def __init__(self, part, scratch, by_x=False):
        self.part, self.by_x = part, by_x
        (self.r1, self.chip, self.rx, self.mine, self.late, self.out,
         self.send, self.recv) = scratch
        _, self.y, self.c, _, self.x = here()
        self.to_c, self.to_x, self.to_y = neighbours()
        rows = part.shape[1]
        self.top = pl.ds(0, rows if by_x else rows // 2)
        self.low = pl.ds(rows // 2, rows // 2)

    def copy(self, k, src, dst, to):
        return remote(src, dst, self.send.at[k], self.recv.at[k], to)

    def swap(self, b, a):
        at = 2 * b + a
        return self.copy(at, self.part.at[4 * b + 2 * (1 - self.c) + a], self.r1.at[at], self.to_c)

    def give(self, b):
        for a in range(2):
            self.swap(b, a).start()

    def along_x(self, b):
        at = 2 * b + 1 - self.x
        return self.copy(4 + b, self.chip.at[at, self.top], self.rx.at[b, self.top], self.to_x)

    def along_y(self, a):
        at = 2 * (1 - self.y) + a
        return self.copy(6 + a, self.chip.at[at, self.low], self.rx.at[a, self.low], self.to_y)

    def last_y(self):
        return self.copy(8, self.mine.at[self.top], self.late.at[self.top], self.to_y)

    def last_x(self):
        return self.copy(9, self.mine.at[self.low], self.late.at[self.low], self.to_x)

    def total(self, b, a):
        self.swap(b, a).wait_recv()
        at = 2 * b + a
        return self.part[4 * b + 2 * self.c + a].astype(F32) + self.r1[at].astype(F32)

    def take_far(self):
        b = 1 - self.y
        for a in (1 - self.x, self.x):
            self.chip[2 * b + a] = self.total(b, a).astype(BF16)
            if a is not self.x:
                self.along_x(b).start()
            if not self.by_x:
                self.along_y(a).start()

    def take_near(self):
        b, x = self.y, self.x
        self.chip[2 * b + 1 - x] = self.total(b, 1 - x).astype(BF16)
        self.along_x(b).start()
        self.out[...] = self.total(b, x)

    def middle(self):
        x, y, top, low = self.x, self.y, self.top, self.low
        self.along_x(1 - y).wait_recv()
        self.mine[top] = (
            self.chip[2 * (1 - y) + x, top].astype(F32) + self.rx[1 - y, top].astype(F32)
        ).astype(BF16)
        self.last_y().start()
        if self.by_x:
            return
        self.along_y(1 - x).wait_recv()
        self.mine[low] = (
            self.chip[2 * y + 1 - x, low].astype(F32) + self.rx[1 - x, low].astype(F32)
        ).astype(BF16)
        self.last_x().start()

    def finish(self):
        x, y, top, low = self.x, self.y, self.top, self.low
        self.along_x(y).wait_recv()
        self.last_y().wait_recv()
        self.out[top] += self.rx[y, top].astype(F32) + self.late[top].astype(F32)
        if self.by_x:
            return
        self.along_y(x).wait_recv()
        self.last_x().wait_recv()
        self.out[low] += self.rx[x, low].astype(F32) + self.late[low].astype(F32)

    def given(self):
        for b in range(2):
            for a in range(2):
                self.swap(b, a).wait_send()

    def passed(self):
        for b in range(2):
            self.along_x(b).wait_send()
            if not self.by_x:
                self.along_y(b).wait_send()
        self.last_y().wait_send()
        if not self.by_x:
            self.last_x().wait_send()

    def sent(self):
        self.given()
        self.passed()


def seq_scratch(width):
    return [
        pltpu.VMEM((4, 128, width), BF16),
        pltpu.VMEM((4, 128, width), BF16),
        pltpu.VMEM((2, 128, width), BF16),
        pltpu.VMEM((128, width), BF16),
        pltpu.VMEM((128, width), BF16),
        pltpu.VMEM((128, width), F32),
        dma(10),
        dma(10),
    ]


def first_dims(left, right):
    return lax.dot_general(left, right, (((0,), (0,)), ((), ())), preferred_element_type=F32)


def last_dims(left, right):
    return lax.dot_general(left, right, (((1,), (1,)), ((), ())), preferred_element_type=F32)


def swiglu(gate, up, grad):
    sigma = 1.0 / (1.0 + jnp.exp(-gate))
    active = gate * sigma
    d_gate = grad * up * sigma * (1.0 + gate * (1.0 - sigma))
    return ((active * up).astype(BF16), d_gate.astype(BF16), (grad * active).astype(BF16))


class Direct:
    def __init__(self, block, slot, send, recv):
        self.block, self.slot, self.send, self.recv = block, slot, send, recv
        self.base, self.y, self.c, self.z, self.x = here()

    def copy(self, zk):
        return remote(self.block(zk), self.slot(self.z), self.send.at[zk], self.recv.at[self.z],
                      device(self.base, self.y, self.c, zk, self.x))

    def start(self, zk):
        pl.when(zk != self.z)(lambda: self.copy(zk).start())

    def take(self):
        for k in (1, 3, 2):
            zk = (self.z + k) % 4
            ref = self.slot(zk)
            remote(ref, ref, self.send.at[0], self.recv.at[zk],
                   device(self.base, self.y, self.c, zk, self.x)).wait_recv()
            yield ref[...].astype(F32)

    def sent(self):
        for zk in range(4):
            pl.when(self.z != zk)(lambda zk=zk: self.copy(zk).wait_send())


class RepShare:
    def __init__(self, at, send, recv):
        self.at, self.send, self.recv = at, send, recv
        _, self.y, self.c, _, _ = here()
        self.to_c, _, self.to_y = neighbours()
        self.r = 2 * self.y + self.c

    def copy(self, k, r, to):
        return remote(self.at(r), self.at(r), self.send.at[k], self.recv.at[k], to)

    def start(self):
        self.copy(0, self.r, self.to_y).start()
        self.copy(1, self.r, self.to_c).start()

    def forward(self):
        other = 2 * (1 - self.y) + self.c
        self.copy(0, other, self.to_y).wait_recv()
        self.copy(2, other, self.to_c).start()

    def finish(self):
        self.copy(1, 2 * self.y + 1 - self.c, self.to_c).wait_recv()
        self.copy(2, 2 * (1 - self.y) + 1 - self.c, self.to_c).wait_recv()

    def sent(self):
        self.copy(0, self.r, self.to_y).wait_send()
        self.copy(1, self.r, self.to_c).wait_send()
        self.copy(2, self.r, self.to_c).wait_send()


def head_back(dy, u, gain):
    inv = head_inverse(u)
    scaled = dy * gain
    gain_grad = jnp.sum(dy * u * inv, axis=0, keepdims=True)
    inner = jnp.sum(scaled * u, axis=-1, keepdims=True) * (1.0 / HEAD_DIM)
    return inv * scaled - u * (inv * inv * inv * inner), gain_grad


def block_kernel(names, *refs):
    m = dict(zip(names, refs))
    base, y, c, z, x = here()
    r = 2 * y + c
    to_c, to_x, to_y = neighbours()
    q_cols, kv_cols = HEADS * HEAD_DIM, KV_HEADS * HEAD_DIM
    raw_q = [
        pltpu.make_async_copy(m["wqkv"].at[:, pl.ds(first + n * r, n)],
                              m["wq_raw"].at[:, pl.ds(to, n)], m["keep"].at[k])
        for k, (first, to, n) in enumerate((
            (0, 0, 2 * Q_COLS), (q_cols, 2 * Q_COLS, 2 * HEAD_DIM),
            (q_cols + kv_cols, 2 * Q_COLS + 2 * HEAD_DIM, 2 * HEAD_DIM)))]
    for copy in raw_q:
        copy.start()
    small = m["small"][...].astype(F32)
    m["seg"][...] = jnp.broadcast_to(small[:, 512:640], (8, 128)).astype(jnp.int32)
    m["gains"][...] = jnp.concatenate(
        [small[:, 0:256], small[:, 256:512], jnp.zeros((14, 256), F32)], axis=0).astype(BF16)
    qg, kg = low_half(roll(small[:, 128:256], 64)), low_half(roll(small[:, 384:512], 64))
    greet(layer_mates() + z_mates())
    for copy in raw_q:
        copy.wait()
    tiles = [m["wq_raw"][:, 128 * i:128 * (i + 1)].astype(F32) for i in range(5)]
    low_lanes = lanes(tiles[0].shape) < HEAD_DIM
    half_of = lambda v, w: jnp.where(low_lanes, v, w).astype(BF16)
    q0, q1, q2, k_tile, v_tile = tiles
    m["wq"][0, :, 0:128] = q0.astype(BF16)
    m["wq"][0, :, 128:256] = half_of(q1, roll(k_tile, 64))
    m["wq"][0, :, 256:] = v_tile[:, 0:HEAD_DIM].astype(BF16)
    m["wq"][1, :, 0:128] = half_of(roll(q1, 64), roll(q2, 64))
    m["wq"][1, :, 128:256] = half_of(roll(q2, 64), k_tile)
    m["wq"][1, :, 256:] = roll(v_tile, 64)[:, 0:HEAD_DIM].astype(BF16)
    rows, width = m["tok"].shape
    quarter_o = m["wo"].shape[0] // 4
    own_rows = m["wqkv"].shape[0]
    half_cols = m["wgu"].shape[1] // 2
    piece = half_cols // 4
    part = piece // 2
    main = part // 128 * 128
    half_a = main // 2
    rows_a, rows_b, rest = half_a // 4, (part - half_a) // 4, part - main
    keep = m["keep"]
    own = 2 * z + x
    t_own = 2 * r + x

    def local_copy(k, src, dst):
        return pltpu.make_async_copy(src, dst, keep.at[k])

    hidden, dgu, wgu, wd_v = m["hidden"], m["dgu"], m["wgu_v"], m["wd_v"]
    cols_a = 2 * half_a
    cols_b = dgu.shape[1] - cols_a

    def raw(i):
        return dgu.at[pl.ds(i * own_rows, own_rows)]

    def pair(a, first, n):
        return dgu.at[pl.ds((2 + a) * own_rows, own_rows), pl.ds(first, n)]

    def loaded(k, src, dst):
        copy = local_copy(k, src, dst)
        copy.start()
        return copy

    tok = Gather(m["tok"], m["tok_all"], m["ga_s"], m["ga_r"], keep.at[0])
    cot = Gather(m["cot"], m["cot_v"], m["gb_s"], m["gb_r"], keep.at[1])
    segs = m["segs_v"]
    mates = layer_mates()

    def seg_copy(k):
        return remote(m["seg"], segs.at[z, t_own], m["sg_s"].at[k - 1], m["sg_r"].at[k - 1],
                      mates[k - 1])

    def gain_target(k):
        return device(base, y, c, (z + k // 2) % 4, (x + k) % 2)

    def gain_copy(k):
        return remote(m["gains"], m["gains_all"].at[own], m["gn_s"].at[k - 1],
                      m["gn_r"].at[k - 1], gain_target(k))

    wq = m["wq_v"]

    def wq_slot(zk, a):
        return wq.at[pl.ds((2 * zk + a) * own_rows, own_rows)]

    near = Along(m["wq"].at[x], lambda zk: wq_slot(zk, x), m["wa_s"], m["wa_r"])
    flip = Along(wq_slot(z, 1 - x), lambda zk: wq_slot(zk, 1 - x), m["wb_s"], m["wb_r"])
    over = remote(m["wq"].at[1 - x], wq_slot(z, x), m["wx_s"], m["wx_r"], to_x)
    over_in = remote(m["wq"].at[x], wq_slot(z, 1 - x), m["wx_s"], m["wx_r"], to_x)
    for k in range(1, 8):
        seg_copy(k).start()
    over.start()
    near.first()
    near.second()
    tok.start()
    local = [
        local_copy(2, m["wq"].at[x], wq_slot(z, x)),
        local_copy(3, m["gains"], m["gains_all"].at[own]),
        local_copy(4, m["seg"], segs.at[z, t_own]),
        local_copy(5, m["wgu"].at[:, pl.ds(piece * r, piece)], raw(0)),
        local_copy(6, m["wgu"].at[:, pl.ds(half_cols + piece * r, piece)], raw(1)),
    ]
    for copy in local:
        copy.start()
    for k in range(1, 8):
        gain_copy(k).start()
    out_q = Along(m["wo"].at[pl.ds(quarter_o * r, quarter_o)], lambda zk: m["zo"].at[zk],
                  m["wo_s"], m["wo_r"])
    last = r // 3
    tail_at = rest * x + half_a + rows_b * r + 16 - last * x * part
    quarters = [
        local_copy(7, m["wo"].at[pl.ds(quarter_o * r, quarter_o)], m["zo"].at[z]),
        local_copy(8, m["wd"].at[pl.ds(rest * x + rows_a * r, rows_a)], m["za"].at[z]),
        local_copy(13, m["wd"].at[pl.ds(rest * x + half_a + rows_b * r, 16)],
                   m["zb"].at[z, pl.ds(0, 16)]),
        local_copy(14, m["wd"].at[pl.ds(tail_at, rows_b - 16)],
                   m["zb"].at[z, pl.ds(16, rows_b - 16)]),
    ]
    for copy in quarters:
        copy.start()
    over_in.wait_recv()
    flip.first()
    flip.second()
    out_q.first()
    out_q.second()

    def seg_up(k):
        return remote(segs.at[z], segs.at[z], m["su_s"].at[k - 1], m["su_r"].at[z],
                      device(base, y, c, (z + k) % 4, x))

    for k in range(1, 8):
        seg_copy(k).wait_recv()
    local[2].wait()
    for k in range(3, 0, -1):
        pl.when(z + k < 4)(lambda k=k: seg_up(k).start())

    local[3].wait()
    local[4].wait()
    gate, up = raw(0), raw(1)
    for a in range(2):
        at = a * (piece - main)
        for i, src in enumerate((gate, up)):
            pair(a, i * half_a, half_a)[...] = src[:, at:at + half_a]
            pair(a, cols_a + i * half_a, half_a)[...] = src[:, at + half_a:at + main]
    g_tile = gate[:, main:main + 128].astype(F32)
    u_tile = up[:, main:main + 128].astype(F32)
    low = lanes(g_tile.shape) < HEAD_DIM
    pair(0, 2 * main, 128)[...] = jnp.where(low, g_tile, roll(u_tile, 64)).astype(BF16)
    pair(1, 2 * main, 128)[...] = jnp.where(low, roll(g_tile, 64), u_tile).astype(BF16)

    def unit(first, n):
        return lambda zk: wgu.at[pl.ds(2 * zk * own_rows, 2 * own_rows), pl.ds(first, n)]

    def crossing(first, n, ss, rs, k):
        cols = pl.ds(first, n)
        mine = wgu.at[pl.ds((2 * z + x) * own_rows, own_rows), cols]
        other = wgu.at[pl.ds((2 * z + 1 - x) * own_rows, own_rows), cols]
        return (remote(pair(1 - x, first, n), mine, ss, rs, to_x),
                remote(pair(x, first, n), other, ss, rs, to_x),
                local_copy(k, pair(x, first, n), mine))

    cross_a, cross_a_in, mine_a = crossing(0, cols_a, m["xa_s"], m["xa_r"], 5)
    cross_b, cross_b_in, mine_b = crossing(cols_a, cols_b, m["xb_s"], m["xb_r"], 6)
    gate_a = Chain(unit(0, cols_a), m["ca_s"], m["ca_r"])
    gate_b = Chain(unit(cols_a, cols_b), m["cb_s"], m["cb_r"])
    down_a = Chain(lambda zk: m["za"].at[zk], m["da_s"], m["da_r"])
    down_b = Chain(lambda zk: m["zb"].at[zk], m["db_s"], m["db_r"])
    tok.forward()
    for copy in (cross_a, mine_a, cross_b, mine_b):
        copy.start()
    near.forward()
    flip.forward()
    out_q.forward()
    tok.finish()
    cot.start()
    near.finish()
    flip.finish()
    for k in range(1, 8):
        at = 2 * ((z + 4 - k // 2) % 4) + (x + k) % 2
        remote(m["gains"], m["gains_all"].at[at], m["gn_s"].at[k - 1], m["gn_r"].at[k - 1],
               to_c).wait_recv()
    for k in (0, 1):
        local[k].wait()
    gather_gains = pltpu.make_async_copy(m["gains_all"], m["gains_v"], keep.at[3])
    gather_gains.start()
    gather_gains.wait()
    gain_rows = []
    for i in range(2):
        gain_rows.append(jnp.concatenate(
            [m["gains_v"][k, 0:16].astype(F32)[i:i + 1, :own_rows] for k in range(8)], axis=1))
    m["g_one"][...], m["g_two"][...] = gain_rows
    kv = m["kv_v"]
    q_all, qkv_all = m["q_v"], m["qkv_v"]
    cos, sin = low_half(m["rope"][...]), low_half(roll(m["rope"][...], 64))
    span = 2 * rows

    def order(k):
        return (y + 1 + k) % 2, (c + 1 + k // 2) % 2

    def kv_copy(d, s):
        return remote(kv.at[z, s], kv.at[z, s], m["kv_s"].at[d - 1, s], m["kv_r"].at[z, s],
                      device(base, y, c, (z + d) % 4, x))

    def kv_arrival(zk, s):
        return remote(kv.at[zk, s], kv.at[zk, s], m["kv_s"].at[0, s], m["kv_r"].at[zk, s], to_x)

    def project(k, carry):
        b, e = order(k)
        s = 2 * b + e
        tokens = m["tok_all"][pl.ds(2 * s, 2)].reshape(span, width).astype(F32)
        normed = (tokens * inverse_rms(tokens) * m["g_one"][...]).astype(BF16)
        m["tok_all"][pl.ds(2 * s, 2)] = normed.reshape(2, rows, width)
        qkv = jnp.dot(normed, wq[...], preferred_element_type=F32)
        qkv_all[s] = qkv[:, 0:256]
        heads = split_heads(qkv[:, 0:128], qkv[:, 128:256])
        for j in range(GROUP):
            u = heads[j]
            u = rotated(u * head_inverse(u) * qg, cos, sin) * HEAD_DIM ** (-0.5)
            q_all[s, pl.ds(j * span, span)] = u.astype(BF16)
        u = heads[GROUP]
        u = rotated(u * head_inverse(u) * kg, cos, sin)
        v = jnp.concatenate([jnp.zeros((span, HEAD_DIM), F32), qkv[:, 256:320]], axis=1)
        kv[z, s] = (u + v).astype(BF16)
        for d in (3, 2, 1):
            pl.when(z + d < 4)(lambda d=d: kv_copy(d, s).start())
        return carry

    lax.fori_loop(0, 4, project, 0)
    for copy in quarters[1:]:
        copy.wait()
    down_a.start_ends()
    down_a.start_inner()
    for copy in (mine_a, mine_b):
        copy.wait()
    cross_a_in.wait_recv()
    gate_a.start_ends()
    gate_a.start_inner()
    cross_b_in.wait_recv()
    down_b.start_ends()
    gate_b.start_ends()
    cot.forward()

    def hand(k, zk, src, dst, sems, n):
        ss, rs = sems
        to = device(base, zk // 2, zk % 2, z, x)
        pl.when(r != zk)(lambda: remote(src.at[zk], dst.at[pl.ds(n * r, n)], ss.at[zk],
                                        rs.at[r], to).start())

        @pl.when(r == zk)
        def _():
            copy = local_copy(k, src.at[zk], dst.at[pl.ds(n * r, n)])
            copy.start()
            copy.wait()

    def handed(src, dst, sems, n):
        ss, rs = sems
        for rk in range(4):
            ref = dst.at[pl.ds(n * rk, n)]
            pl.when(r != rk)(lambda ref=ref, rk=rk: remote(
                src.at[0], ref, ss.at[0], rs.at[rk], to_x).wait_recv())

    def hand_sent(src, dst, sems, n):
        ss, rs = sems
        for zk in range(4):
            pl.when(r != zk)(lambda zk=zk: remote(
                src.at[zk], dst.at[pl.ds(0, n)], ss.at[zk], rs.at[0], to_x).wait_send())

    quarters[0].wait()
    out_q.finish()
    out_sems = (m["ho_s"], m["ho_r"])
    a_sems, b_sems = (m["hd_s"], m["hd_r"]), (m["hb_s"], m["hb_r"])
    for zk in range(4):
        hand(13, zk, m["zo"], m["wo_v"], out_sems, quarter_o)

    for k in range(1, 4):
        pl.when(z - k >= 0)(lambda k=k: remote(
            segs.at[0], segs.at[(z + 4 - k) % 4], m["su_s"].at[k - 1],
            m["su_r"].at[(z + 4 - k) % 4], to_x).wait_recv())

    summed = SeqSum(m["part"], [m[n] for n in SUM_NAMES])
    inv_all, att = m["inv_v"], m["att_v"]
    acc, q_seg = m["acc"], m["q_seg"]

    def attend_one(k, carry):
        b, e = order(k)
        s = 2 * b + e
        q_seg[...] = segment_columns(segs, z, s)

        def block(zk, diagonal):
            tile = kv[zk, s]
            p = exp_scores(q_all[s], tile, q_seg[...], segment_row(segs, zk, s), diagonal)
            ones = jnp.where(lanes(tile.shape) < HEAD_DIM, 1.0, tile.astype(F32)).astype(BF16)
            add = jnp.dot(p.astype(BF16), ones, preferred_element_type=F32)
            if diagonal:
                acc[...] = add
            else:
                acc[...] += add

        block(z, True)

        def step(i, inner):
            zk = z - 1 - i
            kv_arrival(zk, s).wait_recv()
            block(zk, False)
            return inner

        lax.fori_loop(0, z, step, 0)
        total = acc[...]
        inv = 1.0 / jnp.where(lanes(total.shape) < HEAD_DIM, total, 1.0)
        inv = jnp.where(lanes(total.shape) < HEAD_DIM, inv, roll(inv, 64))
        o = high_half(total * inv)
        lane = lanes((span, 128))
        inv_all[s] = jnp.where(lane < 32, inv[0:span], jnp.where(
            lane < 64, inv[span:2 * span], inv[2 * span:]))
        first, second, third = o[0:span], o[span:2 * span], o[2 * span:]
        att[s, :, 0:128] = (roll(first, 64) + second).astype(BF16)
        att[s, :, 128:192] = roll(third, 64)[:, 0:HEAD_DIM].astype(BF16)
        pl.when(k == 0)(lambda: handed(m["zo"], m["wo_v"], out_sems, quarter_o))
        out = jnp.dot(att[s], m["wo_v"][...], preferred_element_type=F32).astype(BF16)
        m["part"][pl.ds(2 * s, 2)] = out.reshape(2, rows, width)
        pl.when(k < 2)(lambda: summed.give(b))
        pl.when(k == 2)(summed.take_far)
        pl.when(k == 3)(summed.take_near)
        return carry

    lax.fori_loop(0, 4, attend_one, 0)
    down_a.second()
    gate_a.second()
    summed.middle()
    down_a.third()
    summed.finish()
    mid = m["tok"][...].astype(F32) + summed.out[...]
    m["mid"][...] = mid
    m["low"][...] = (mid * inverse_rms(mid) * m["g_two"][...]).astype(BF16)
    n2_all, cot_all = m["n2_v"], m["cot_v"]
    n2 = Gather(m["low"], n2_all, m["gc_s"], m["gc_r"], keep.at[20])
    n2.start()
    cot.finish()
    gate_a.third()
    down_b.pass_ends()
    gate_b.pass_ends()
    down_b.start_inner()
    gate_b.start_inner()
    n2.forward()
    down_a.finish()
    wda, wdb = wd_v.at[pl.ds(0, half_a)], wd_v.at[pl.ds(half_a, part - half_a)]
    for zk in range(4):
        hand(13, zk, m["za"], wda, a_sems, rows_a)
    n2.finish()
    gate_a.finish()
    handed(m["za"], wda, a_sems, rows_a)
    cross_a.wait_send()
    cross_b.wait_send()

    down_b.third()
    gate_b.third()

    def feed_first(s, carry):
        at = pl.ds(pl.multiple_of(s * span, span), span)
        gu = jnp.dot(n2_all[pl.ds(2 * s, 2)].reshape(span, width), wgu[:, :cols_a],
                     preferred_element_type=F32)
        dh = last_dims(cot_all[pl.ds(2 * s, 2)].reshape(span, width), wd_v[0:half_a])
        hidden[at, 0:half_a], dgu[at, 0:half_a], dgu[at, half_a:cols_a] = swiglu(
            gu[:, :half_a], gu[:, half_a:], dh)
        out = last_dims(dgu[at, 0:cols_a], wgu[:, :cols_a]).astype(BF16)
        m["part"][pl.ds(2 * s, 2)] = out.reshape(2, rows, width)
        return carry

    summed.given()
    lax.fori_loop(0, 4, feed_first, 0)
    down_b.pass_inner()
    gate_b.pass_inner()
    block_rows = 2 * own_rows
    gga, gdo, got_a = m["gga"], m["gdo"], m["got_a"]
    gate_sum = ChainSum(lambda zk: gga.at[zk], lambda at: m["gga_slot"].at[at], m["ys_s"],
                        m["ys_r"])
    down_sum = ChainSum(lambda zk: got_a.at[zk], lambda at: m["gda_slot"].at[at], m["yd_s"],
                        m["yd_r"])

    def grad_gate(zk, carry):
        cols = pl.ds(pl.multiple_of(zk * block_rows, 128), block_rows)
        left = n2_all[:, :, cols].reshape(8 * rows, block_rows)
        gga[zk] = first_dims(left, dgu[:, :cols_a]).astype(BF16)
        return carry

    lax.fori_loop(0, 4, grad_gate, 0)
    gate_sum.start()
    for j in range(0, half_a, 128):
        grad = first_dims(hidden[:, j:j + 128], cot_all[...].reshape(8 * rows, width))
        for h in range(128 // rows_a):
            gdo[j // rows_a + h, 0:rows_a] = grad[rows_a * h:rows_a * (h + 1)].astype(BF16)

    def spread_from(i):
        return gdo.at[i, pl.ds(0, rows_a)]

    def spread(i):
        return remote(spread_from(i), got_a.at[r], m["ha_s"].at[i], m["ha_r"].at[r],
                      device(base, i // 2, i % 2, z, x))

    for i in range(4):
        pl.when(r != i)(lambda i=i: spread(i).start())
    got_a[r] = gdo[r, 0:rows_a]

    def add(block, slot):
        block[...] = (block[...].astype(F32) + slot[...].astype(F32)).astype(BF16)

    gate_sum.first_hop(add)
    down_b.finish()
    for zk in range(4):
        hand(13, zk, m["zb"], wdb, b_sems, rows_b)
    gate_b.finish()
    gate_sum.second_hop(add)
    handed(m["zb"], wdb, b_sems, rows_b)
    for i in range(4):
        pl.when(r != i)(lambda i=i: remote(
            spread_from(i), got_a.at[i], m["ha_s"].at[i], m["ha_r"].at[i], to_c).wait_recv())
    down_sum.start()
    summed.passed()

    def total_in(block):
        def total(slots):
            value = block[...].astype(F32)
            for slot in slots:
                value = value + slot[...].astype(F32)
            block[...] = value.astype(BF16)
        return total

    parts, n2, cot_v, normed = m["part"], m["n2_v"], m["cot_v"], m["tok_all"]
    wd_v[pl.ds(part, 128 - rest)] = jnp.zeros((128 - rest, width), BF16)

    def feed(k, carry):
        b, e = order(k)
        s = 2 * b + e
        at = pl.ds(pl.multiple_of(s * span, span), span)
        gu = jnp.dot(n2[pl.ds(2 * s, 2)].reshape(span, width), wgu[:, cols_a:],
                     preferred_element_type=F32)
        dh = last_dims(cot_v[pl.ds(2 * s, 2)].reshape(span, width), wd_v[half_a:])
        (hidden[at, half_a:2 * half_a], dgu[at, cols_a:cols_a + half_a],
         dgu[at, cols_a + half_a:cols_a + 2 * half_a]) = swiglu(
            gu[:, :half_a], gu[:, half_a:2 * half_a], dh[:, :half_a])
        tile = gu[:, 2 * half_a:]
        gate, up, grad = low_half(tile), low_half(roll(tile, 64)), dh[:, half_a:]
        sigma = 1.0 / (1.0 + jnp.exp(-gate))
        active = gate * sigma
        hidden[at, 2 * half_a:] = (active * up).astype(BF16)
        d_gate = grad * up * sigma * (1.0 + gate * (1.0 - sigma))
        dgu[at, cols_a + 2 * half_a:] = (
            d_gate + roll(low_half(grad * active), 64)).astype(BF16)
        out = last_dims(dgu[at, cols_a:], wgu[:, cols_a:])
        out = out + parts[pl.ds(2 * s, 2)].reshape(span, width).astype(F32)
        parts[pl.ds(2 * s, 2)] = out.astype(BF16).reshape(2, rows, width)
        pl.when(k < 2)(lambda: summed.give(b))
        pl.when(k == 2)(summed.take_far)
        pl.when(k == 3)(summed.take_near)
        return carry

    lax.fori_loop(0, 4, feed, 0)
    down_sum.first_hop(add)

    ggu = m["ggu"]
    gu_sum = ChainSum(lambda zk: ggu.at[zk], lambda at: m["gu_slot"].at[at], m["zg_s"], m["zg_r"])

    def farthest(i):
        up = z // 2
        return up * i + (1 - up) * (3 - i)

    def grad_gu(i, carry):
        zk = farthest(i)
        cols = pl.ds(pl.multiple_of(zk * block_rows, 128), block_rows)
        left = n2[:, :, cols].reshape(8 * rows, block_rows)
        ggu[zk] = first_dims(left, dgu[:, cols_a:]).astype(BF16)
        pl.when(i < 2)(lambda: gu_sum.start_one(zk))
        return carry

    lax.fori_loop(0, 2, grad_gu, 0)
    summed.middle()
    lax.fori_loop(2, 4, grad_gu, 0)
    down_sum.second_hop(add)
    summed.finish()

    v = m["mid"][...]
    dv, gain_grad = norm_back(summed.out[...], v, inverse_rms(v), m["g_two"][...])
    m["row_two"][...] = gain_grad
    dmid = cot_v[t_own].astype(F32) + dv
    m["dmid"][...] = dmid
    m["low"][...] = dmid.astype(BF16)
    branch = Gather(m["low"], m["db"], m["gd_s"], m["gd_r"], keep.at[12])
    branch.start()
    gu_sum.first_hop(add, (0,))

    got = m["got"]
    quarter_d = rows_b
    for i in range(4):
        pl.when(r != i)(lambda i=i: spread(i).wait_send())
    for j in range(0, half_a + 128, 128):
        at = half_a + j
        grad = first_dims(hidden[:, at:at + 128], cot_v[...].reshape(8 * rows, width))
        grad = grad.astype(BF16)
        for i in range(4):
            lo, hi = max(j, quarter_d * i), min(j + 128, quarter_d * (i + 1))
            if lo < hi:
                gdo[i, lo - quarter_d * i:hi - quarter_d * i] = grad[lo - j:hi - j]

    summed.sent()

    def down(s, carry):
        at = pl.ds(pl.multiple_of(s * span, span), span)
        out = jnp.dot(hidden[at], wd_v[...], preferred_element_type=F32)
        parts[pl.ds(2 * s, 2)] = out.astype(BF16).reshape(2, rows, width)
        return carry

    lax.fori_loop(0, 4, down, 0)
    mixed = SeqSum(parts, [m[n] for n in SUM_NAMES], by_x=True)

    def give(i, lo, n, ss, rs):
        return remote(gdo.at[i, pl.ds(lo, n)], got.at[r, pl.ds(lo, n)], ss.at[i], rs.at[r],
                      device(base, i // 2, i % 2, z, x))

    def give_all(lo, n, ss, rs):
        for i in range(4):
            pl.when(r != i)(lambda i=i: give(i, lo, n, ss, rs).start())
        got[r, lo:lo + n] = gdo[r, lo:lo + n]

    def given(lo, n, ss, rs):
        for i in range(4):
            pl.when(r != i)(lambda i=i: remote(
                gdo.at[i, pl.ds(lo, n)], got.at[i, pl.ds(lo, n)], ss.at[i], rs.at[i],
                to_c).wait_recv())

    def give_sent(lo, n, ss, rs):
        for i in range(4):
            pl.when(r != i)(lambda i=i: give(i, lo, n, ss, rs).wait_send())

    def swap(src, out, ss, rs):
        return remote(src.at[pl.ds(own_rows * (1 - x), own_rows)], out.at[t_own], ss, rs, to_x)

    def keep_own(k, src, out):
        copy = pltpu.make_async_copy(src.at[pl.ds(own_rows * x, own_rows)], out.at[t_own],
                                     keep.at[k])
        copy.start()
        return copy

    def swapped(src, out, ss, rs):
        return remote(src.at[pl.ds(own_rows * x, own_rows)], out.at[2 * r + 1 - x], ss, rs, to_x)

    def pairs(out):
        return lambda i: out.at[pl.ds(2 * i, 2)]

    ga_out, gb_out, qkv_out = m["ga_g"], m["gb_g"], m["qkv_g"]
    ga_swap = swap(gga.at[z], ga_out, m["xs_s"], m["xs_r"])
    ga_keep = local_copy(14, gga.at[z, pl.ds(own_rows * x, own_rows)], ga_out.at[t_own])
    da_keep = local_copy(15, got_a.at[z], m["da_g"].at[r])
    ga_share = RepShare(pairs(ga_out), m["ra_s"], m["ra_r"])
    da_share = RepShare(lambda i: m["da_g"].at[i], m["rc_s"], m["rc_r"])

    def swap_first():
        gate_sum.collect(total_in(gga.at[z]))
        down_sum.collect(total_in(got_a.at[z]))
        for copy in (ga_swap, ga_keep, da_keep):
            copy.start()

    branch.forward()
    branch.arrive(2)
    branch.keep.wait()
    give_all(0, quarter_d, m["he_s"], m["he_r"])
    mixed.give(0)
    mixed.give(1)
    swap_first()
    gu_sum.first_hop(add, (1,))

    wo, qkv, dkv = m["wo_v"], qkv_all, kv
    db, dqkv, do_v = m["db"], m["dqkv"], m["do"]
    own_kv = m["own_kv"]
    m["row_head"][...] = jnp.zeros((1, 128), F32)

    down_rest = ChainSum(lambda zk: got.at[zk, pl.ds(0, quarter_d)],
                         lambda at: m["down_slot"].at[at], m["zd_s"], m["zd_r"])

    def share_first():
        ga_keep.wait()
        da_keep.wait()
        swapped(gga.at[z], ga_out, m["xs_s"], m["xs_r"]).wait_recv()
        ga_share.start()
        da_share.start()

    def order_back(k):
        return (y + k // 2) % 2, (c + 1 + k) % 2

    kv_slot = m["kv_slot"]

    def kv_down(zk, s):
        return remote(dkv.at[zk, s], kv_slot.at[zk, s], m["zk_s"].at[zk, s], m["zk_r"].at[zk, s],
                      device(base, y, c, (z + 3) % 4, x))

    def kv_merge(k):
        b, e = order_back(k)
        s = 2 * b + e

        def one(zk, inner):
            kv_down(zk, s).wait_recv()
            dkv[zk, s] = (dkv[zk, s].astype(F32) + kv_slot[zk, s].astype(F32)).astype(BF16)
            kv_down(zk, s).start()
            return inner

        @pl.when((z == 1) | (z == 2))
        def _():
            lax.fori_loop(0, z, one, 0)

    def attend_back(k, carry):
        pl.when(k == 0)(lambda: branch.arrive(4))
        pl.when(k == 1)(branch.cross)
        pl.when(k == 2)(lambda: [branch.arrive(6), branch.arrive(7)] and None)
        b, e = order_back(k)
        s = 2 * b + e
        grads = db[pl.ds(2 * s, 2)].reshape(span, width)
        d_att = last_dims(grads, wo[...])
        first = d_att[:, 0:128]
        third = jnp.concatenate([jnp.zeros((span, HEAD_DIM), F32), d_att[:, 128:192]], axis=1)
        d_out = [high_half(roll(first, 64)), high_half(first), third]
        att_a = att[s, :, 0:128].astype(F32)
        att_b = att[s, :, 128:192].astype(F32)
        att_b = jnp.concatenate([jnp.zeros((span, HEAD_DIM), F32), att_b], axis=1)
        deltas = []
        for j, o in enumerate((roll(att_a, 64), att_a, att_b)):
            inv = inv_all[s][:, 32 * j:32 * j + 1]
            part_j = (d_out[j].astype(BF16).astype(F32) * inv).astype(BF16)
            do_v[pl.ds(j * span, span)] = part_j
            deltas.append(jnp.sum(part_j.astype(F32) * o, axis=1, keepdims=True))
        delta = jnp.concatenate(deltas, axis=0)
        q_seg[...] = segment_columns(segs, z, s)
        acc[...] = jnp.zeros_like(acc)

        def block(zk, diagonal):
            tile = kv[zk, s]
            q = q_all[s]
            d_out = do_v[...]
            p = exp_scores(q, tile, q_seg[...], segment_row(segs, zk, s), diagonal)
            ds = (p * (last_dims(d_out, tile) - delta)).astype(BF16)
            acc[...] += jnp.dot(ds, tile, preferred_element_type=F32)
            return first_dims(ds, q) + first_dims(p.astype(BF16), d_out)

        def step(zk, inner):
            dkv[zk, s] = block(zk, False).astype(BF16)
            pl.when(z == 3)(lambda: kv_down(zk, s).start())
            return inner

        lax.fori_loop(0, z, step, 0)
        own_kv[s] = block(z, True)
        tiles = split_heads(qkv[s, :, 0:128], qkv[s, :, 128:256])
        back = []
        for j in range(GROUP):
            dy = rotated(low_half(acc[pl.ds(j * span, span)]) * HEAD_DIM ** (-0.5), cos, -sin)
            raw, gain_part = head_back(dy, tiles[j], qg)
            m["row_head"][...] += gain_part
            back.append(raw)
        dqkv[s, :, 0:128] = (back[0] + roll(back[1], 64)).astype(BF16)
        dqkv[s, :, 128:256] = back[2].astype(BF16)
        pl.when(k >= 1)(lambda: kv_merge(k - 1))
        pl.when(k == 0)(lambda: gu_sum.second_hop(add))
        pl.when(k == 0)(mixed.take_far)
        pl.when(k == 0)(mixed.take_near)
        pl.when(k == 1)(share_first)
        pl.when(k == 3)(mixed.middle)
        pl.when(k == 3)(lambda: given(0, quarter_d, m["he_s"], m["he_r"]))
        return carry

    lax.fori_loop(0, 4, attend_back, 0)
    kv_merge(3)
    gu_sum.start_one(farthest(2))
    down_rest.start()
    for j in range(0, width, 512):
        cols = slice(j, j + 512)
        grad = first_dims(att[...].reshape(8 * rows, Q_COLS),
                          db[:, :, cols].reshape(8 * rows, 512)).astype(BF16)
        for i in range(4):
            gdo[i, quarter_d:quarter_d + quarter_o, cols] = grad[quarter_o * i:quarter_o * (i + 1)]
    give_all(quarter_d, quarter_o, m["hf_s"], m["hf_r"])
    mixed.given()
    inputs = SeqSum(parts, [m[n] for n in SUM_NAMES], by_x=True)

    def finish_one(k, carry):
        b, e = (y + (k + 1) // 2) % 2, (c + 1 + k // 2) % 2
        s = 2 * b + e
        @pl.when(z < 3)
        def _():
            kv_down(z, s).wait_recv()
            own_kv[s] += kv_slot[z, s].astype(F32)

        total = own_kv[s]
        u = split_heads(qkv[s, :, 0:128], qkv[s, :, 128:256])[GROUP]
        dy = rotated(low_half(total), cos, -sin)
        raw, gain_part = head_back(dy, u, kg)
        m["row_head"][...] += roll(gain_part, 64)
        tile = dqkv[s, :, 128:256].astype(F32)
        dqkv[s, :, 128:256] = (low_half(tile) + roll(raw, 64)).astype(BF16)
        dqkv[s, :, 256:320] = roll(total, 64)[:, 0:HEAD_DIM].astype(BF16)
        out = last_dims(dqkv[s], wq[...]).astype(BF16)
        parts[pl.ds(2 * s, 2)] = out.reshape(2, rows, width)
        return carry

    lax.fori_loop(0, 4, finish_one, 0)
    gqkv = m["gqkv"]
    qkv_sum = Direct(lambda zk: gqkv.at[zk], lambda zk: m["qkv_slot"].at[zk], m["zq_s"],
                     m["zq_r"])

    def grad_qkv(i, carry):
        zk = farthest(i)
        cols = pl.ds(pl.multiple_of(zk * block_rows, 128), block_rows)
        left = normed[:, :, cols].reshape(8 * rows, block_rows)
        gqkv[zk] = first_dims(left, dqkv[...].reshape(8 * rows, HEAD_COLS)).astype(BF16)
        qkv_sum.start(zk)
        return carry

    lax.fori_loop(0, 4, grad_qkv, 0)
    gu_sum.collect(total_in(ggu.at[z]))
    gb_swap = swap(ggu.at[z], gb_out, m["xg_s"], m["xg_r"])
    gb_swap.start()
    gb_keep = keep_own(14, ggu.at[z], gb_out)
    mixed.finish()
    branch.sent()
    m["low"][...] = (m["mid"][...] + mixed.out[...]).astype(BF16)
    mixed_out = loaded(17, m["low"], m["mixed"])
    mixed.passed()
    free = m["free"]
    for to in (to_c, to_x, to_y):
        pl.semaphore_signal(free, inc=1, device_id=to, device_id_type=MESH)

    pl.semaphore_wait(free, 3)
    inputs.give(0)
    inputs.give(1)
    inputs.take_far()
    inputs.take_near()
    gb_keep.wait()
    swapped(ggu.at[z], gb_out, m["xg_s"], m["xg_r"]).wait_recv()
    gb_share = RepShare(pairs(gb_out), m["rg_s"], m["rg_r"])
    gb_share.start()
    down_rest.first_hop(add)
    inputs.middle()
    down_rest.second_hop(add, (1,))
    given(quarter_d, quarter_o, m["hf_s"], m["hf_r"])
    out_sum = Direct(lambda zk: got.at[zk, pl.ds(quarter_d, quarter_o)],
                     lambda zk: m["out_slot"].at[zk], m["zo_s"], m["zo_r"])

    def start_out(i, carry):
        out_sum.start(farthest(i))
        return carry

    lax.fori_loop(0, 4, start_out, 0)
    ga_share.forward()
    da_share.forward()

    inputs.finish()
    v = m["tok"][...].astype(F32)
    dv, gain_grad = norm_back(inputs.out[...], v, inverse_rms(v), m["g_one"][...])
    m["dmid"][...] += dv
    grad_out = loaded(18, m["dmid"], m["input_grad"])

    def gain_rows_of(k):
        return m["mid"].at[pl.ds(8 * k, 8)]

    gains_own = gain_rows_of(0)
    gains_own[0:1] = gain_grad
    gains_own[1:2] = m["row_two"][...]
    gains_own[2:3, 0:128] = m["row_head"][...]

    def gain_sum(k):
        return remote(gains_own, gain_rows_of(k), m["gm_s"].at[k - 1], m["gm_r"].at[k - 1],
                      mates[k - 1])

    for k in range(1, 8):
        gain_sum(k).start()

    down_rest.second_hop(add, (2,))

    total = gqkv[z].astype(F32)
    for term in qkv_sum.take():
        total = total + term
    gqkv[z] = total.astype(BF16)
    qkv_swap = swap(gqkv.at[z], qkv_out, m["xq_s"], m["xq_r"])
    qkv_swap.start()
    qkv_keep = keep_own(16, gqkv.at[z], qkv_out)
    qkv_share = RepShare(pairs(qkv_out), m["rq_s"], m["rq_r"])

    down_rest.collect(total_in(got.at[z, pl.ds(0, quarter_d)]))
    db_keep = loaded(15, got.at[z, pl.ds(0, quarter_d)], m["db_g"].at[r])
    db_keep.wait()
    db_share = RepShare(lambda i: m["db_g"].at[i], m["rd_s"], m["rd_r"])
    db_share.start()
    for k in range(1, 8):
        gain_sum(k).wait_recv()
    total = gains_own[...]
    for k in range(1, 8):
        total = total + gain_rows_of(k)[...]
    z_rows = m["z_rows"]
    z_rows[0] = total

    def gain_z(k):
        return remote(z_rows.at[0], z_rows.at[k], m["gz_s"].at[k - 1], m["gz_r"].at[k - 1],
                      device(base, y, c, (z + k) % 4, x))

    for k in range(1, 4):
        gain_z(k).start()
    gb_share.forward()
    qkv_keep.wait()
    swapped(gqkv.at[z], qkv_out, m["xq_s"], m["xq_r"]).wait_recv()
    qkv_share.start()
    out_own = got.at[z, pl.ds(quarter_d, quarter_o)]
    total = out_own[...].astype(F32)
    for term in out_sum.take():
        total = total + term
    out_own[...] = total.astype(BF16)
    out_keep = loaded(0, out_own, m["out_g"].at[r])
    out_keep.wait()
    out_share = RepShare(lambda i: m["out_g"].at[i], m["re_s"], m["re_r"])
    out_share.start()
    db_share.forward()
    for k in range(1, 4):
        gain_z(k).wait_recv()
    m["gains_g"][...] = z_rows[0] + z_rows[1] + z_rows[2] + z_rows[3]
    qkv_share.forward()
    out_share.forward()
    shares = (ga_share, da_share, gb_share, db_share, out_share, qkv_share)
    for share in shares:
        share.finish()

    for share in shares:
        share.sent()
    for copy in (ga_swap, gb_swap, qkv_swap):
        copy.wait_send()
    for k in range(1, 8):
        gain_sum(k).wait_send()
    for k in range(1, 4):
        gain_z(k).wait_send()
    mixed_out.wait()
    grad_out.wait()
    for flow in (gu_sum, down_rest, qkv_sum, out_sum, inputs):
        flow.sent()
    give_sent(0, quarter_d, m["he_s"], m["he_r"])
    give_sent(quarter_d, quarter_o, m["hf_s"], m["hf_r"])

    def dkv_sent(s, carry):
        for zk in range(3):
            pl.when(z > zk)(lambda zk=zk: kv_down(zk, s).wait_send())
        return carry

    lax.fori_loop(0, 4, dkv_sent, 0)
    for flow in (near, flip, out_q, gate_a, gate_b, down_a, down_b, gate_sum, down_sum):
        flow.sent()
    over.wait_send()
    for k in range(1, 8):
        seg_copy(k).wait_send()
        gain_copy(k).wait_send()
    for k in range(1, 4):
        pl.when(z + k < 4)(lambda k=k: seg_up(k).wait_send())

    def kv_sent(s, carry):
        for d in (1, 2, 3):
            pl.when(z + d < 4)(lambda d=d: kv_copy(d, s).wait_send())
        return carry

    lax.fori_loop(0, 4, kv_sent, 0)
    hand_sent(m["zo"], m["wo_v"], out_sems, quarter_o)
    hand_sent(m["za"], wda, a_sems, rows_a)
    hand_sent(m["zb"], wdb, b_sems, rows_b)


SUM_NAMES = ("r1", "chip", "rx", "mine", "late", "sum_out", "sum_s", "sum_r")
IN = ("tok", "cot", "small", "wqkv", "wgu", "wd", "wo", "rope")
OUT = ("mixed", "input_grad", "gains_g", "ga_g", "gb_g", "da_g", "db_g", "out_g", "qkv_g",
       "zo", "za", "zb", "gains_all")


def block_call(*args):
    shape = jax.ShapeDtypeStruct
    tok, _, _, wqkv, wgu, wd, wo = args[:7]
    rows, width = tok.shape
    span = 2 * rows
    own_rows = wqkv.shape[0]
    seg, gains = shape((8, rows), jnp.int32), shape((16, 256), BF16)
    part = wgu.shape[1] // 16
    half_a = part // 256 * 128
    part_b = part - half_a
    cols_a, cols_b = 2 * half_a, 2 * half_a + 128
    quarter_a, quarter_d, quarter_o = half_a // 4, part_b // 4, own_rows // 4
    heads = GROUP * span
    outs = {
        "mixed": shape((rows, width), BF16),
        "input_grad": shape((rows, width), F32),
        "gains_g": shape((8, width), F32),
        "ga_g": shape((8, own_rows, cols_a), BF16),
        "gb_g": shape((8, own_rows, cols_b), BF16),
        "da_g": shape((4, quarter_a, width), BF16),
        "db_g": shape((4, quarter_d, width), BF16),
        "out_g": shape((4, quarter_o, width), BF16),
        "qkv_g": shape((8, own_rows, HEAD_COLS), BF16),
        "zo": shape((4, quarter_o, width), BF16),
        "za": shape((4, quarter_a, width), BF16),
        "zb": shape((4, quarter_d, width), BF16),
        "gains_all": shape((8,) + gains.shape, BF16),
    }
    buffers = {
        "tok_all": ((8, rows, width), BF16), "cot_v": ((8, rows, width), BF16),
        "n2_v": ((8, rows, width), BF16), "db": ((8, rows, width), BF16),
        "part": ((8, rows, width), BF16),
        "seg": (seg.shape, seg.dtype), "gains": (gains.shape, BF16),
        "wq": ((2, own_rows, HEAD_COLS), BF16), "wq_raw": ((own_rows, 640), BF16),
        "segs_v": ((4, 8) + seg.shape, seg.dtype), "gains_v": ((8,) + gains.shape, BF16),
        "wq_v": ((width, HEAD_COLS), BF16), "wo_v": ((Q_COLS, width), BF16),
        "wgu_v": ((width, cols_a + cols_b), BF16), "wd_v": ((2 * half_a + 128, width), BF16),
        "hidden": ((8 * rows, 2 * half_a + 128), BF16),
        "dgu": ((8 * rows, cols_a + cols_b), BF16),
        "qkv_v": ((4, span, 256), F32), "q_v": ((4, heads, 128), BF16),
        "kv_v": ((4, 4, span, 128), BF16), "kv_slot": ((3, 4, span, 128), BF16),
        "own_kv": ((4, span, 128), F32), "inv_v": ((4, span, 128), F32),
        "att_v": ((4, span, Q_COLS), BF16), "acc": ((heads, 128), F32),
        "do": ((heads, 128), BF16), "q_seg": ((span, span), jnp.int32),
        "dqkv": ((4, span, HEAD_COLS), BF16),
        "mid": ((rows, width), F32), "dmid": ((rows, width), F32), "low": ((rows, width), BF16),
        "g_one": ((1, width), F32), "g_two": ((1, width), F32),
        "gga": ((4, 2 * own_rows, cols_a), BF16), "gga_slot": ((5, 2 * own_rows, cols_a), BF16),
        "ggu": ((4, 2 * own_rows, cols_b), BF16), "gu_slot": ((5, 2 * own_rows, cols_b), BF16),
        "got_a": ((4, quarter_a, width), BF16),
        "gda_slot": ((5, quarter_a, width), BF16),
        "gdo": ((4, quarter_d + quarter_o, width), BF16),
        "got": ((4, quarter_d + quarter_o, width), BF16),
        "down_slot": ((5, quarter_d, width), BF16),
        "out_slot": ((4, quarter_o, width), BF16),
        "gqkv": ((4, 2 * own_rows, HEAD_COLS), BF16),
        "qkv_slot": ((4, 2 * own_rows, HEAD_COLS), BF16),
        "row_two": ((1, width), F32), "row_head": ((1, 128), F32),
        "z_rows": ((4, 8, width), F32),
    }
    counts = {
        "ga": (8, 8), "gb": (8, 8), "gc": (8, 8), "gd": (8, 8), "sg": (7, 7), "gn": (7, 7),
        "gm": (7, 7), "gz": (3, 3), "wa": (6, 4), "wb": (6, 4), "wo": (6, 4), "wx": (1, 1),
        "xa": (1, 1), "xb": (1, 1), "xs": (1, 1), "xg": (1, 1), "ca": (5, 4), "cb": (5, 4),
        "da": (5, 4), "db": (5, 4), "ys": (4, 5), "yd": (4, 5), "zg": (4, 5), "zd": (4, 5),
        "zo": (4, 4), "zq": (4, 4), "xq": (1, 1), "zk": ((3, 4), (3, 4)), "kv": ((3, 4), (4, 4)),
        "su": (3, 4), "ha": (4, 4), "hb": (4, 4), "hd": (4, 4), "he": (4, 4), "hf": (4, 4),
        "ho": (4, 4), "ra": (3, 3), "rc": (3, 3), "rd": (3, 3), "re": (3, 3), "rg": (3, 3),
        "rq": (3, 3),
    }
    sem = pltpu.SemaphoreType.DMA
    many = lambda n: sem if n == 1 else sem(n if isinstance(n, tuple) else (n,))
    sems = {"keep": dma(21), "free": pltpu.SemaphoreType.REGULAR}
    for n, (send, recv) in counts.items():
        sems[n + "_s"], sems[n + "_r"] = many(send), many(recv)
    scratch = {n: pltpu.VMEM(*v) for n, v in buffers.items()}
    scratch.update(zip(SUM_NAMES, seq_scratch(width)))
    names = IN + OUT + tuple(scratch) + tuple(sems)
    got = pl.pallas_call(
        functools.partial(block_kernel, names),
        name="block",
        out_shape=tuple(outs[n] for n in OUT),
        in_specs=[ANY if n in ("cot", "wqkv", "wgu", "wd", "wo") else VMEM for n in IN],
        out_specs=tuple(VMEM if n == "gains_g" else ANY for n in OUT),
        scratch_shapes=list(scratch.values()) + list(sems.values()),
        compiler_params=params(0, 63),
    )(*args)
    return dict(zip(OUT, got))


def order_kernel(names, *refs):
    m = dict(zip(names, refs))
    half_a = m["ga"].shape[2] // 2
    half_b = (m["gb"].shape[2] - 128) // 2
    main = half_a + half_b
    cols = 2 * main + 128
    own_rows = m["ga"].shape[1]
    low = lanes((own_rows, 128)) < HEAD_DIM
    x = lax.axis_index("grp") % 2

    def fetch(k, src, dst):
        copy = pltpu.make_async_copy(src, dst, m["load"].at[k])
        copy.start()
        return copy

    def store(k, src, dst):
        copy = pltpu.make_async_copy(src, dst, m["save"].at[k])
        copy.start()
        return copy

    ga, gb = m["ga_v"], m["gb_v"]
    pair = lambda i: pl.ds(2 * i, 2)
    wide = [(fetch(2 * i, m["ga"].at[pair(i)], ga.at[pair(i)]),
             fetch(2 * i + 1, m["gb"].at[pair(i)], gb.at[pair(i)])) for i in range(4)]
    rest = {n: fetch(8 + k, m[n], m[n + "_v"])
            for k, n in enumerate(("db", "qkv", "da", "out", "ig", "mixed"))}
    saved = []
    for i in range(4):
        for copy in wide[i]:
            copy.wait()
        first, second = ga.at[2 * i], ga.at[2 * i + 1]
        tiles = [gb[2 * i + k, :, 2 * half_b:].astype(F32) for k in range(2)]
        for w in range(2):
            to = m["gu_v"].at[4 * w + i]
            for k in range(2):
                lo = k * (main + 128)
                to[:, lo:lo + half_a] = ga[2 * i + k, :, w * half_a:(w + 1) * half_a].astype(F32)
                to[:, lo + half_a:lo + main] = (
                    gb[2 * i + k, :, w * half_b:(w + 1) * half_b].astype(F32))
            if w == 0:
                to[:, main:main + 128] = jnp.where(low, tiles[0], roll(tiles[1], 64))
            else:
                to[:, main:main + 128] = jnp.where(low, roll(tiles[0], 64), tiles[1])
            saved.append(store(
                4 * w + i, to, m["gu_o"].at[:, pl.ds((4 * w + i) * cols, cols)]))

    rest["da"].wait()
    rest["db"].wait()
    da, db, down = m["da_v"], m["db_v"], m["down_v"]
    part = down.shape[0]
    rows_a, rows_b = da.shape[1], db.shape[1]
    shift = (part - main) * x

    def at(start, n):
        return pl.ds(pl.multiple_of(start, 16), n)

    for i in range(4):
        down[at(rows_a * i + shift, rows_a)] = da[i].astype(F32)
        start = half_a + rows_b * i + shift
        down[at(start, 16)] = db[i, 0:16].astype(F32)
        down[at(start + 16 - (i // 3) * x * part, rows_b - 16)] = db[i, 16:].astype(F32)
    saved.append(store(8, down, m["down_o"]))
    rest["qkv"].wait()
    qkv_v, qkv_f = m["qkv_v"], m["qkv_f"]
    q_cols, kv_cols = HEADS * HEAD_DIM, KV_HEADS * HEAD_DIM
    half = lambda v, w: jnp.where(low, v, w)
    for i in range(4):
        a, b = qkv_v[2 * i].astype(F32), qkv_v[2 * i + 1].astype(F32)
        a1, a2, b0, b1 = a[:, 128:256], a[:, 256:], b[:, 0:128], b[:, 128:256]
        lo = i * 2 * Q_COLS
        qkv_f[:, lo:lo + 128] = a[:, 0:128]
        qkv_f[:, lo + 128:lo + 256] = half(a1, roll(b0, 64))
        qkv_f[:, lo + 256:lo + 384] = half(roll(b0, 64), roll(b1, 64))
        lo = q_cols + i * 128
        qkv_f[:, lo:lo + 128] = half(roll(a1, 64), b1)
        lo = lo + kv_cols
        qkv_f[:, lo:lo + 128] = jnp.concatenate([a2, b[:, 256:]], axis=1)
    saved.append(store(9, qkv_f, m["qkv_o"]))
    rest["out"].wait()
    n = m["out_v"].shape[1]
    for i in range(4):
        m["out_f"][n * i:n * (i + 1)] = m["out_v"][i].astype(F32)
    saved.append(store(10, m["out_f"], m["out_o"]))
    for k, n in ((11, "ig"), (12, "mixed")):
        rest[n].wait()
        saved.append(store(k, m[n + "_v"], m[n + "_o"]))
    gains = m["gains"][...]
    width = gains.shape[1]
    turned = pltpu.roll(gains, (width - own_rows * lax.axis_index("grp")) % width, 1)
    m["one_o"][...] = turned[0:1, 0:own_rows]
    m["two_o"][...] = turned[1:2, 0:own_rows]
    m["q_o"][...] = gains[2:3, 0:HEAD_DIM]
    m["k_o"][...] = gains[2:3, HEAD_DIM:2 * HEAD_DIM]
    for copy in saved:
        copy.wait()


def order_call(g):
    shape = jax.ShapeDtypeStruct
    ga, gb, da, db, out, qkv, mixed, ig = (g[n] for n in ORDER_IN)
    _, own_rows, cols_a = ga.shape
    cols = cols_a + gb.shape[2]
    width = da.shape[2]
    part = 4 * (da.shape[1] + db.shape[1])
    qkv_cols = (HEADS + 2 * KV_HEADS) * HEAD_DIM
    outs = {
        "gu_o": shape((own_rows, 8 * cols), F32), "down_o": shape((part, width), F32),
        "out_o": shape((own_rows, width), F32), "qkv_o": shape((own_rows, qkv_cols), F32),
        "ig_o": shape(ig.shape, F32), "mixed_o": shape(mixed.shape, BF16),
        "one_o": shape((1, own_rows), F32), "two_o": shape((1, own_rows), F32),
        "q_o": shape((1, HEAD_DIM), F32), "k_o": shape((1, HEAD_DIM), F32),
    }
    ins = ("ga", "gb", "da", "db", "out", "qkv", "mixed", "ig")
    scratch = {n + "_v": pltpu.VMEM(v.shape, v.dtype)
               for n, v in zip(ins, (ga, gb, da, db, out, qkv, mixed, ig))}
    scratch["gu_v"] = pltpu.VMEM((8, own_rows, cols), F32)
    scratch["down_v"] = pltpu.VMEM((part, width), F32)
    scratch["out_f"] = pltpu.VMEM((own_rows, width), F32)
    scratch["qkv_f"] = pltpu.VMEM((own_rows, qkv_cols), F32)
    scratch["load"], scratch["save"] = dma(14), dma(13)
    names = ins + ("gains",) + tuple(outs) + tuple(scratch)
    got = pl.pallas_call(
        functools.partial(order_kernel, names),
        name="final_order",
        out_shape=tuple(outs.values()),
        in_specs=[ANY] * 8 + [VMEM],
        out_specs=(ANY,) * 6 + (VMEM,) * 4,
        scratch_shapes=list(scratch.values()),
        compiler_params=pltpu.CompilerParams(vmem_limit_bytes=62 * 2**20),
    )(ga, gb, da, db, out, qkv, mixed, ig, g["gains_g"])
    return dict(zip(outs, got))


ORDER_IN = ("ga_g", "gb_g", "da_g", "db_g", "out_g", "qkv_g", "mixed", "input_grad")


def rope_table(start, rows):
    half = HEAD_DIM // 2
    lane = lax.broadcasted_iota(jnp.int32, (rows, 4 * half), 1)
    freq = jnp.exp(-jnp.log(THETA) * (lane % half).astype(F32) * 2.0 / HEAD_DIM)
    position = start + lax.broadcasted_iota(jnp.int32, (rows, 4 * half), 0)
    angle = position.astype(F32) * freq
    sine = jnp.sin(angle)
    return jnp.where(lane < 2 * half, jnp.cos(angle), jnp.where(lane < 3 * half, -sine, sine))


def over_quads(array):
    reps = lax.axis_size("rep")
    if reps == 4:
        return array
    rows = [[j + 4 * q for q in range(reps // 4)] for j in range(4)]
    return lax.psum(array, "rep", axis_index_groups=rows)


def local(tokens, attn_gain, w_qkv, q_gain, k_gain, w_out, ffn_gain, w_gate_up, w_down,
          cotangent, segment_ids):
    rows, width = tokens.shape
    _, y, c, z, x = here()
    r = 2 * y + c
    span = 2 * rows
    rope = rope_table(span * z, span)
    parts = (attn_gain, q_gain, ffn_gain, k_gain, segment_ids)
    total = sum(v.shape[0] for v in parts)
    small, at = 0.0, 0
    for v in parts:
        n = v.shape[0]
        small = small + jnp.pad(v.astype(F32)[None], ((0, 0), (at, total - at - n)))
        at += n
    g = block_call(tokens, cotangent, small, w_qkv, w_gate_up, w_down, w_out, rope)
    g = {n: over_quads(v) if n.endswith("_g") else v for n, v in g.items()}
    o = order_call(g)
    flat = lambda n: o[n].reshape(-1)
    return (o["mixed_o"], o["ig_o"], flat("one_o"), o["qkv_o"], flat("q_o"), flat("k_o"),
            o["out_o"], flat("two_o"), o["gu_o"], o["down_o"])


def solution(mesh):
    rows, split = P(("rep", "grp"), None), P("grp", None)
    return jax.shard_map(
        local,
        mesh=mesh,
        in_specs=(rows, P("grp"), split, P(), P(), split, P("grp"), split, split, rows,
                  P(("rep", "grp"))),
        out_specs=(rows, rows, P("grp"), split, P(), P(), split, P("grp"), split, split),
        check_vma=False,
    )
```

```python
import functools

import jax
import jax.numpy as jnp
from jax import lax
from jax.experimental import pallas as pl
from jax.experimental.pallas import tpu as pltpu
from jax.sharding import PartitionSpec as P

HEADS = 24
KV_HEADS = 8
HEAD_DIM = 64
GROUP = HEADS // KV_HEADS
Q_COLS = GROUP * HEAD_DIM
HEAD_COLS = Q_COLS + 2 * HEAD_DIM

EPS = 1e-05
THETA = 1000000.0
MESH = pl.DeviceIdType.MESH
F32 = jnp.float32
BF16 = jnp.bfloat16

VMEM = pl.BlockSpec(memory_space=pltpu.VMEM)
ANY = pl.BlockSpec(memory_space=pl.ANY)


def here():
    rep = lax.axis_index("rep")
    grp = lax.axis_index("grp")
    r = rep % 4
    return rep - r, r // 2, r % 2, grp // 2, grp % 2


def device(base, y, c, z, x):
    return {"rep": base + 2 * y + c, "grp": 2 * z + x}


def remote(src, dst, send, recv, to):
    return pltpu.make_async_remote_copy(
        src_ref=src, dst_ref=dst, send_sem=send, recv_sem=recv, device_id=to, device_id_type=MESH
    )


def greet(targets):
    barrier = pltpu.get_barrier_semaphore()
    for to in targets:
        pl.semaphore_signal(barrier, inc=1, device_id=to, device_id_type=MESH)
    pl.semaphore_wait(barrier, len(targets))


def neighbours():
    base, y, c, z, x = here()
    to_c = device(base, y, 1 - c, z, x)
    to_x = device(base, y, c, z, 1 - x)
    to_y = device(base, 1 - y, c, z, x)
    return to_c, to_x, to_y


class Gather:
    def __init__(self, src, out, send, recv, local):
        self.src, self.out, self.send, self.recv = src, out, send, recv
        _, y, c, _, x = here()
        self.to_c, self.to_x, self.to_y = neighbours()
        slot = lambda a, b, d: 4 * a + 2 * b + d
        self.own = slot(y, c, x)
        self.at_c, self.at_x, self.at_y = slot(y, 1 - c, x), slot(y, c, 1 - x), slot(1 - y, c, x)
        self.at_xc, self.at_yc = slot(y, 1 - c, 1 - x), slot(1 - y, 1 - c, x)
        self.at_xy, self.at_xyc = slot(1 - y, c, 1 - x), slot(1 - y, 1 - c, 1 - x)
        self.half = src.shape[0] // 2
        self.keep = pltpu.make_async_copy(src, out.at[self.own], local)

    def part(self, at, k):
        return self.out.at[at, pl.ds(k * self.half, self.half)]

    def copy(self, k):
        out, own = self.out, self.out.at[self.own]
        src, dst, to = (
            lambda: (self.src, own, self.to_x),
            lambda: (self.src, own, self.to_y),
            lambda: (self.src, own, self.to_c),
            lambda: (self.part(self.at_x, 0),) * 2 + (self.to_y,),
            lambda: (out.at[self.at_x],) * 2 + (self.to_c,),
            lambda: (self.part(self.at_y, 1),) * 2 + (self.to_x,),
            lambda: (out.at[self.at_y],) * 2 + (self.to_c,),
            lambda: (out.at[self.at_xy],) * 2 + (self.to_c,),
        )[k]()
        return remote(src, dst, self.send.at[k], self.recv.at[k], to)

    def arrive(self, k):
        out = self.out
        ref = (
            lambda: out.at[self.at_x], lambda: out.at[self.at_y], lambda: out.at[self.at_c],
            lambda: self.part(self.at_xy, 0), lambda: out.at[self.at_xc],
            lambda: self.part(self.at_xy, 1), lambda: out.at[self.at_yc],
            lambda: out.at[self.at_xyc],
        )[k]()
        remote(ref, ref, self.send.at[k], self.recv.at[k], self.to_c).wait_recv()

    def start(self):
        self.keep.start()
        for k in range(3):
            self.copy(k).start()

    def forward(self):
        self.arrive(0)
        self.copy(3).start()
        self.copy(4).start()
        self.arrive(1)
        self.copy(5).start()
        self.copy(6).start()

    def cross(self):
        self.arrive(3)
        self.arrive(5)
        self.copy(7).start()

    def finish(self):
        self.cross()
        for k in (2, 4, 6, 7):
            self.arrive(k)
        self.keep.wait()
        self.sent()

    def sent(self):
        for k in range(8):
            self.copy(k).wait_send()


def dma(n):
    return pltpu.SemaphoreType.DMA((n,))


def params(cid, limit=60):
    return pltpu.CompilerParams(
        collective_id=cid, has_side_effects=True, vmem_limit_bytes=limit * 2**20
    )


def inverse_rms(v):
    return lax.rsqrt(jnp.mean(v * v, axis=-1, keepdims=True) + EPS)


def norm_back(dy, v, inv, gain):
    scaled = dy * gain
    gain_grad = jnp.sum(dy * v * inv, axis=0, keepdims=True)
    inner = jnp.mean(scaled * v, axis=-1, keepdims=True)
    return inv * scaled - v * inv * inv * inv * inner, gain_grad


def when(cond):
    return pl.when(cond)


def lanes(shape):
    return lax.broadcasted_iota(jnp.int32, shape, len(shape) - 1)


def roll(v, by):
    return pltpu.roll(v, by % v.shape[-1], v.ndim - 1)


class Along:
    def __init__(self, src, slot, send, recv):
        self.src, self.slot, self.send, self.recv = src, slot, send, recv
        self.base, self.y, self.c, self.z, self.x = here()

    def at(self, zk, x):
        return device(self.base, self.y, self.c, zk, x)

    def copy(self, d):
        zk = (self.z + d + 4) % 4
        return remote(self.src, self.slot(self.z), self.send.at[d + 2], self.recv.at[self.z],
                      self.at(zk, self.x))

    def fits(self, d):
        return (self.z + d >= 0) & (self.z + d < 4)

    def first(self):
        for d in (2, -2):
            pl.when(self.fits(d))(lambda d=d: self.copy(d).start())
        pl.when(self.z == 2)(lambda: self.copy(1).start())
        pl.when(self.z == 1)(lambda: self.copy(-1).start())

    def second(self):
        pl.when(self.z < 2)(lambda: self.copy(1).start())
        pl.when(self.z >= 2)(lambda: self.copy(-1).start())

    def arrival(self, zk):
        ref = self.slot(zk)
        return remote(ref, ref, self.send.at[0], self.recv.at[zk], self.at(self.z, 1 - self.x))

    def passed(self, zk, to):
        ref = self.slot(zk)
        return remote(ref, ref, self.send.at[5], self.recv.at[zk], self.at(to, self.x))

    def forward(self):
        @pl.when(self.z == 2)
        def _():
            self.arrival(0).wait_recv()
            self.passed(0, 3).start()

        @pl.when(self.z == 1)
        def _():
            self.arrival(3).wait_recv()
            self.passed(3, 0).start()

    def wait(self, zk):
        early = ((self.z == 2) & (zk == 0)) | ((self.z == 1) & (zk == 3))
        due = jnp.logical_not(early) & (self.z != zk)
        pl.when(due)(lambda: self.arrival(zk).wait_recv())

    def finish(self):
        for zk in range(4):
            self.wait(zk)

    def sent(self):
        for d in (2, -2, 1, -1):
            pl.when(self.fits(d))(lambda d=d: self.copy(d).wait_send())
        pl.when(self.z == 2)(lambda: self.passed(0, 3).wait_send())
        pl.when(self.z == 1)(lambda: self.passed(3, 0).wait_send())


class Chain:
    def __init__(self, slot, send, recv):
        self.slot, self.send, self.recv = slot, send, recv
        self.base, self.y, self.c, self.z, self.x = here()

    def copy(self, k, zk, to):
        return remote(self.slot(zk), self.slot(zk), self.send.at[k], self.recv.at[zk],
                      device(self.base, self.y, self.c, to, self.x))

    def arrive(self, zk):
        self.copy(0, zk, self.z).wait_recv()

    def inner(self):
        return (self.z == 1) | (self.z == 2)

    def start_ends(self):
        pl.when(self.z == 0)(lambda: self.copy(0, 0, 1).start())
        pl.when(self.z == 3)(lambda: self.copy(1, 3, 2).start())

    def start_inner(self):
        z = self.z

        @pl.when(self.inner())
        def _():
            self.copy(0, z, z + 1).start()
            self.copy(1, z, z - 1).start()

    def pass_ends(self):
        @pl.when(self.z == 1)
        def _():
            self.arrive(0)
            self.copy(2, 0, 2).start()

        @pl.when(self.z == 2)
        def _():
            self.arrive(3)
            self.copy(3, 3, 1).start()

    def pass_inner(self):
        @pl.when(self.z == 1)
        def _():
            self.arrive(2)
            self.copy(3, 2, 0).start()

        @pl.when(self.z == 2)
        def _():
            self.arrive(1)
            self.copy(2, 1, 3).start()

    def second(self):
        self.pass_ends()
        self.pass_inner()

    def third(self):
        @pl.when(self.z == 2)
        def _():
            self.arrive(0)
            self.copy(4, 0, 3).start()

        @pl.when(self.z == 1)
        def _():
            self.arrive(3)
            self.copy(4, 3, 0).start()

    def finish(self):
        pl.when(self.z == 0)(lambda: [self.arrive(zk) for zk in (1, 2, 3)] and None)
        pl.when(self.z == 3)(lambda: [self.arrive(zk) for zk in (2, 1, 0)] and None)

    def sent(self):
        z = self.z
        pl.when(z < 3)(lambda: self.copy(0, z, z + 1).wait_send())
        pl.when(z > 0)(lambda: self.copy(1, z, z - 1).wait_send())

        @pl.when(self.inner())
        def _():
            self.copy(2, z - 1, z + 1).wait_send()
            self.copy(3, z + 1, z - 1).wait_send()
            self.copy(4, z, z + 1).wait_send()


class ChainSum:
    def __init__(self, block, slot, send, recv):
        self.block, self.slot, self.send, self.recv = block, slot, send, recv
        self.base, self.y, self.c, self.z, self.x = here()

    def copy(self, zk, to, at):
        return remote(self.block(zk), self.slot(at), self.send.at[zk], self.recv.at[at],
                      device(self.base, self.y, self.c, to, self.x))

    def arrive(self, at):
        self.copy(0, self.z, at).wait_recv()

    def start(self):
        @pl.when(self.z == 0)
        def _():
            for zk, at in ((3, 3), (2, 2), (1, 4)):
                self.copy(zk, 1, at).start()

        @pl.when(self.z == 3)
        def _():
            for zk in (0, 1, 2):
                self.copy(zk, 2, zk).start()

    def start_one(self, zk):
        for to, at in ((3, 3), (2, 2), (1, 4)):
            pl.when((self.z == 0) & (zk == to))(
                lambda to=to, at=at: self.copy(to, 1, at).start())
        for to in (0, 1, 2):
            pl.when((self.z == 3) & (zk == to))(lambda to=to: self.copy(to, 2, to).start())

    def first_hop(self, add, which=(0, 1)):
        @pl.when(self.z == 1)
        def _():
            for i in which:
                zk, at = ((3, 3), (2, 4))[i]
                self.arrive(zk)
                add(self.block(zk), self.slot(zk))
                self.copy(zk, 2, at).start()

        @pl.when(self.z == 2)
        def _():
            for zk in which:
                self.arrive(zk)
                add(self.block(zk), self.slot(zk))
                self.copy(zk, 1, zk).start()

    def second_hop(self, add, inner=(1, 2)):
        for z, zk, to, at in ((1, 0, 0, 0), (2, 3, 3, 4)):
            if z not in inner:
                continue

            @pl.when(self.z == z)
            def _():
                self.arrive(zk)
                add(self.block(zk), self.slot(zk))
                self.copy(zk, to, at).start()

    def collect(self, total):
        z = self.z

        def take(ats):
            for at in ats:
                self.arrive(at)
            total([self.slot(at) for at in ats])

        pl.when(z == 0)(lambda: take([0]))
        pl.when(z == 3)(lambda: take([4]))
        pl.when((z == 1) | (z == 2))(lambda: take([z, 4]))

    def sent(self):
        for zk in range(4):
            pl.when(self.z != zk)(lambda zk=zk: self.copy(zk, 0, 0).wait_send())


def layer_mates():
    base, y, c, z, x = here()
    return [
        device(base, (y + k // 4) % 2, (c + k // 2) % 2, z, (x + k) % 2) for k in range(1, 8)
    ]


def z_mates():
    base, y, c, z, x = here()
    return [device(base, y, c, (z + k // 2) % 4, (x + k) % 2) for k in range(2, 8)]


def rotated(u, cos, sin):
    lane = lanes(u.shape)
    return u * cos + jnp.where(lane < 32, roll(u, -32), roll(u, 32)) * sin


def low_half(v):
    return jnp.where(lanes(v.shape) < HEAD_DIM, v, 0.0)


def high_half(v):
    return jnp.where(lanes(v.shape) >= HEAD_DIM, v, 0.0)


def split_heads(tile_a, tile_b):
    return [low_half(tile_a), low_half(roll(tile_a, 64)), low_half(tile_b),
            low_half(roll(tile_b, 64))]


def head_inverse(u):
    return lax.rsqrt(jnp.sum(u * u, axis=-1, keepdims=True) * (1.0 / HEAD_DIM) + EPS)


def exp_scores(q, kv, q_seg, k_seg, diagonal):
    s = lax.dot_general(q, kv, (((1,), (1,)), ((), ())), preferred_element_type=F32)
    allowed = q_seg == k_seg
    if diagonal:
        row = lax.broadcasted_iota(jnp.int32, allowed.shape, 0)
        col = lax.broadcasted_iota(jnp.int32, allowed.shape, 1)
        allowed = allowed & (col <= row)
    n = allowed.shape[0]
    return jnp.concatenate([
        jnp.where(allowed, jnp.exp(s[n * j:n * (j + 1)]), 0.0) for j in range(GROUP)], axis=0)


def segment_row(segs, zk, s):
    return jnp.concatenate([segs[zk, 2 * s, 0:1], segs[zk, 2 * s + 1, 0:1]], axis=1)


def segment_columns(segs, zk, s):
    parts = []
    for i in range(2):
        row = jnp.broadcast_to(segs[zk, 2 * s + i, 0:1], (128, 128))
        parts.append(jnp.transpose(row))
    col = jnp.concatenate(parts, axis=0)
    return jnp.concatenate([col, col], axis=1)


class SeqSum:
    def __init__(self, part, scratch, by_x=False):
        self.part, self.by_x = part, by_x
        (self.r1, self.chip, self.rx, self.mine, self.late, self.out,
         self.send, self.recv) = scratch
        _, self.y, self.c, _, self.x = here()
        self.to_c, self.to_x, self.to_y = neighbours()
        rows = part.shape[1]
        self.top = pl.ds(0, rows if by_x else rows // 2)
        self.low = pl.ds(rows // 2, rows // 2)

    def copy(self, k, src, dst, to):
        return remote(src, dst, self.send.at[k], self.recv.at[k], to)

    def swap(self, b, a):
        at = 2 * b + a
        return self.copy(at, self.part.at[4 * b + 2 * (1 - self.c) + a], self.r1.at[at], self.to_c)

    def give(self, b):
        for a in range(2):
            self.swap(b, a).start()

    def along_x(self, b):
        at = 2 * b + 1 - self.x
        return self.copy(4 + b, self.chip.at[at, self.top], self.rx.at[b, self.top], self.to_x)

    def along_y(self, a):
        at = 2 * (1 - self.y) + a
        return self.copy(6 + a, self.chip.at[at, self.low], self.rx.at[a, self.low], self.to_y)

    def last_y(self):
        return self.copy(8, self.mine.at[self.top], self.late.at[self.top], self.to_y)

    def last_x(self):
        return self.copy(9, self.mine.at[self.low], self.late.at[self.low], self.to_x)

    def total(self, b, a):
        self.swap(b, a).wait_recv()
        at = 2 * b + a
        return self.part[4 * b + 2 * self.c + a].astype(F32) + self.r1[at].astype(F32)

    def take_far(self):
        b = 1 - self.y
        for a in (1 - self.x, self.x):
            self.chip[2 * b + a] = self.total(b, a).astype(BF16)
            if a is not self.x:
                self.along_x(b).start()
            if not self.by_x:
                self.along_y(a).start()

    def take_near(self):
        b, x = self.y, self.x
        self.chip[2 * b + 1 - x] = self.total(b, 1 - x).astype(BF16)
        self.along_x(b).start()
        self.out[...] = self.total(b, x)

    def middle(self):
        x, y, top, low = self.x, self.y, self.top, self.low
        self.along_x(1 - y).wait_recv()
        self.mine[top] = (
            self.chip[2 * (1 - y) + x, top].astype(F32) + self.rx[1 - y, top].astype(F32)
        ).astype(BF16)
        self.last_y().start()
        if self.by_x:
            return
        self.along_y(1 - x).wait_recv()
        self.mine[low] = (
            self.chip[2 * y + 1 - x, low].astype(F32) + self.rx[1 - x, low].astype(F32)
        ).astype(BF16)
        self.last_x().start()

    def finish(self):
        x, y, top, low = self.x, self.y, self.top, self.low
        self.along_x(y).wait_recv()
        self.last_y().wait_recv()
        self.out[top] += self.rx[y, top].astype(F32) + self.late[top].astype(F32)
        if self.by_x:
            return
        self.along_y(x).wait_recv()
        self.last_x().wait_recv()
        self.out[low] += self.rx[x, low].astype(F32) + self.late[low].astype(F32)

    def given(self):
        for b in range(2):
            for a in range(2):
                self.swap(b, a).wait_send()

    def passed(self):
        for b in range(2):
            self.along_x(b).wait_send()
            if not self.by_x:
                self.along_y(b).wait_send()
        self.last_y().wait_send()
        if not self.by_x:
            self.last_x().wait_send()

    def sent(self):
        self.given()
        self.passed()


def seq_scratch(width):
    return [
        pltpu.VMEM((4, 128, width), BF16),
        pltpu.VMEM((4, 128, width), BF16),
        pltpu.VMEM((2, 128, width), BF16),
        pltpu.VMEM((128, width), BF16),
        pltpu.VMEM((128, width), BF16),
        pltpu.VMEM((128, width), F32),
        dma(10),
        dma(10),
    ]


def first_dims(left, right):
    return lax.dot_general(left, right, (((0,), (0,)), ((), ())), preferred_element_type=F32)


def last_dims(left, right):
    return lax.dot_general(left, right, (((1,), (1,)), ((), ())), preferred_element_type=F32)


def swiglu(gate, up, grad):
    sigma = 1.0 / (1.0 + jnp.exp(-gate))
    active = gate * sigma
    d_gate = grad * up * sigma * (1.0 + gate * (1.0 - sigma))
    return ((active * up).astype(BF16), d_gate.astype(BF16), (grad * active).astype(BF16))


class Direct:
    def __init__(self, block, slot, send, recv):
        self.block, self.slot, self.send, self.recv = block, slot, send, recv
        self.base, self.y, self.c, self.z, self.x = here()

    def copy(self, zk):
        return remote(self.block(zk), self.slot(self.z), self.send.at[zk], self.recv.at[self.z],
                      device(self.base, self.y, self.c, zk, self.x))

    def start(self, zk):
        pl.when(zk != self.z)(lambda: self.copy(zk).start())

    def take(self):
        for k in (1, 3, 2):
            zk = (self.z + k) % 4
            ref = self.slot(zk)
            remote(ref, ref, self.send.at[0], self.recv.at[zk],
                   device(self.base, self.y, self.c, zk, self.x)).wait_recv()
            yield ref[...].astype(F32)

    def sent(self):
        for zk in range(4):
            pl.when(self.z != zk)(lambda zk=zk: self.copy(zk).wait_send())


class RepShare:
    def __init__(self, at, send, recv):
        self.at, self.send, self.recv = at, send, recv
        _, self.y, self.c, _, _ = here()
        self.to_c, _, self.to_y = neighbours()
        self.r = 2 * self.y + self.c

    def copy(self, k, r, to):
        return remote(self.at(r), self.at(r), self.send.at[k], self.recv.at[k], to)

    def start(self):
        self.copy(0, self.r, self.to_y).start()
        self.copy(1, self.r, self.to_c).start()

    def forward(self):
        other = 2 * (1 - self.y) + self.c
        self.copy(0, other, self.to_y).wait_recv()
        self.copy(2, other, self.to_c).start()

    def finish(self):
        self.copy(1, 2 * self.y + 1 - self.c, self.to_c).wait_recv()
        self.copy(2, 2 * (1 - self.y) + 1 - self.c, self.to_c).wait_recv()

    def sent(self):
        self.copy(0, self.r, self.to_y).wait_send()
        self.copy(1, self.r, self.to_c).wait_send()
        self.copy(2, self.r, self.to_c).wait_send()


def head_back(dy, u, gain):
    inv = head_inverse(u)
    scaled = dy * gain
    gain_grad = jnp.sum(dy * u * inv, axis=0, keepdims=True)
    inner = jnp.sum(scaled * u, axis=-1, keepdims=True) * (1.0 / HEAD_DIM)
    return inv * scaled - u * (inv * inv * inv * inner), gain_grad


def rope_table(start, rows):
    half = HEAD_DIM // 2
    lane = lax.broadcasted_iota(jnp.int32, (rows, 4 * half), 1)
    freq = jnp.exp(-jnp.log(THETA) * (lane % half).astype(F32) * 2.0 / HEAD_DIM)
    position = start + lax.broadcasted_iota(jnp.int32, (rows, 4 * half), 0)
    angle = position.astype(F32) * freq
    sine = jnp.sin(angle)
    return jnp.where(lane < 2 * half, jnp.cos(angle), jnp.where(lane < 3 * half, -sine, sine))


def block_kernel(names, *refs):
    m = dict(zip(names, refs))
    base, y, c, z, x = here()
    r = 2 * y + c
    to_c, to_x, to_y = neighbours()
    q_cols, kv_cols = HEADS * HEAD_DIM, KV_HEADS * HEAD_DIM
    raw_q = [
        pltpu.make_async_copy(m["wqkv"].at[:, pl.ds(first + n * r, n)],
                              m["wq_raw"].at[:, pl.ds(to, n)], m["keep"].at[k])
        for k, (first, to, n) in enumerate((
            (0, 0, 2 * Q_COLS), (q_cols, 2 * Q_COLS, 2 * HEAD_DIM),
            (q_cols + kv_cols, 2 * Q_COLS + 2 * HEAD_DIM, 2 * HEAD_DIM)))]
    for copy in raw_q:
        copy.start()
    small = m["small"][...].astype(F32)
    m["seg"][...] = jnp.broadcast_to(small[:, 512:640], (8, 128)).astype(jnp.int32)
    m["gains"][...] = jnp.concatenate(
        [small[:, 0:256], small[:, 256:512], jnp.zeros((14, 256), F32)], axis=0).astype(BF16)
    qg, kg = low_half(roll(small[:, 128:256], 64)), low_half(roll(small[:, 384:512], 64))
    greet(layer_mates() + z_mates())
    for copy in raw_q:
        copy.wait()
    tiles = [m["wq_raw"][:, 128 * i:128 * (i + 1)].astype(F32) for i in range(5)]
    low_lanes = lanes(tiles[0].shape) < HEAD_DIM
    half_of = lambda v, w: jnp.where(low_lanes, v, w).astype(BF16)
    q0, q1, q2, k_tile, v_tile = tiles
    m["wq"][0, :, 0:128] = q0.astype(BF16)
    m["wq"][0, :, 128:256] = half_of(q1, roll(k_tile, 64))
    m["wq"][0, :, 256:] = v_tile[:, 0:HEAD_DIM].astype(BF16)
    m["wq"][1, :, 0:128] = half_of(roll(q1, 64), roll(q2, 64))
    m["wq"][1, :, 128:256] = half_of(roll(q2, 64), k_tile)
    m["wq"][1, :, 256:] = roll(v_tile, 64)[:, 0:HEAD_DIM].astype(BF16)
    rows, width = m["tok"].shape
    quarter_o = m["wo"].shape[0] // 4
    own_rows = m["wqkv"].shape[0]
    half_cols = m["wgu"].shape[1] // 2
    piece = half_cols // 4
    part = piece // 2
    main = part // 128 * 128
    half_a = main // 2
    rows_a, rows_b, rest = half_a // 4, (part - half_a) // 4, part - main
    keep = m["keep"]
    own = 2 * z + x
    t_own = 2 * r + x

    def local_copy(k, src, dst):
        return pltpu.make_async_copy(src, dst, keep.at[k])

    hidden, dgu, wgu, wd_v = m["hidden"], m["dgu"], m["wgu_v"], m["wd_v"]
    cols_a = 2 * half_a
    cols_b = dgu.shape[1] - cols_a

    def raw(i):
        return dgu.at[pl.ds(i * own_rows, own_rows)]

    def pair(a, first, n):
        return dgu.at[pl.ds((2 + a) * own_rows, own_rows), pl.ds(first, n)]

    def loaded(k, src, dst):
        copy = local_copy(k, src, dst)
        copy.start()
        return copy

    tok = Gather(m["tok"], m["tok_all"], m["ga_s"], m["ga_r"], keep.at[0])
    cot = Gather(m["cot"], m["cot_v"], m["gb_s"], m["gb_r"], keep.at[1])
    segs = m["segs_v"]
    mates = layer_mates()

    def seg_copy(k):
        return remote(m["seg"], segs.at[z, t_own], m["sg_s"].at[k - 1], m["sg_r"].at[k - 1],
                      mates[k - 1])

    def gain_target(k):
        return device(base, y, c, (z + k // 2) % 4, (x + k) % 2)

    def gain_copy(k):
        return remote(m["gains"], m["gains_all"].at[own], m["gn_s"].at[k - 1],
                      m["gn_r"].at[k - 1], gain_target(k))

    wq = m["wq_v"]

    def wq_slot(zk, a):
        return wq.at[pl.ds((2 * zk + a) * own_rows, own_rows)]

    near = Along(m["wq"].at[x], lambda zk: wq_slot(zk, x), m["wa_s"], m["wa_r"])
    flip = Along(wq_slot(z, 1 - x), lambda zk: wq_slot(zk, 1 - x), m["wb_s"], m["wb_r"])
    over = remote(m["wq"].at[1 - x], wq_slot(z, x), m["wx_s"], m["wx_r"], to_x)
    over_in = remote(m["wq"].at[x], wq_slot(z, 1 - x), m["wx_s"], m["wx_r"], to_x)
    for k in range(1, 8):
        seg_copy(k).start()
    over.start()
    near.first()
    near.second()
    tok.start()
    local = [
        local_copy(2, m["wq"].at[x], wq_slot(z, x)),
        local_copy(3, m["gains"], m["gains_all"].at[own]),
        local_copy(4, m["seg"], segs.at[z, t_own]),
        local_copy(5, m["wgu"].at[:, pl.ds(piece * r, piece)], raw(0)),
        local_copy(6, m["wgu"].at[:, pl.ds(half_cols + piece * r, piece)], raw(1)),
    ]
    for copy in local:
        copy.start()
    for k in range(1, 8):
        gain_copy(k).start()
    out_q = Along(m["wo"].at[pl.ds(quarter_o * r, quarter_o)], lambda zk: m["zo"].at[zk],
                  m["wo_s"], m["wo_r"])
    last = r // 3
    tail_at = rest * x + half_a + rows_b * r + 16 - last * x * part
    quarters = [
        local_copy(7, m["wo"].at[pl.ds(quarter_o * r, quarter_o)], m["zo"].at[z]),
        local_copy(8, m["wd"].at[pl.ds(rest * x + rows_a * r, rows_a)], m["za"].at[z]),
        local_copy(13, m["wd"].at[pl.ds(rest * x + half_a + rows_b * r, 16)],
                   m["zb"].at[z, pl.ds(0, 16)]),
        local_copy(14, m["wd"].at[pl.ds(tail_at, rows_b - 16)],
                   m["zb"].at[z, pl.ds(16, rows_b - 16)]),
    ]
    for copy in quarters:
        copy.start()
    over_in.wait_recv()
    flip.first()
    flip.second()
    out_q.first()
    out_q.second()

    def seg_up(k):
        return remote(segs.at[z], segs.at[z], m["su_s"].at[k - 1], m["su_r"].at[z],
                      device(base, y, c, (z + k) % 4, x))

    for k in range(1, 8):
        seg_copy(k).wait_recv()
    local[2].wait()
    for k in range(3, 0, -1):
        pl.when(z + k < 4)(lambda k=k: seg_up(k).start())

    local[3].wait()
    local[4].wait()
    gate, up = raw(0), raw(1)
    for a in range(2):
        at = a * (piece - main)
        for i, src in enumerate((gate, up)):
            pair(a, i * half_a, half_a)[...] = src[:, at:at + half_a]
            pair(a, cols_a + i * half_a, half_a)[...] = src[:, at + half_a:at + main]
    g_tile = gate[:, main:main + 128].astype(F32)
    u_tile = up[:, main:main + 128].astype(F32)
    low = lanes(g_tile.shape) < HEAD_DIM
    pair(0, 2 * main, 128)[...] = jnp.where(low, g_tile, roll(u_tile, 64)).astype(BF16)
    pair(1, 2 * main, 128)[...] = jnp.where(low, roll(g_tile, 64), u_tile).astype(BF16)

    def unit(first, n):
        return lambda zk: wgu.at[pl.ds(2 * zk * own_rows, 2 * own_rows), pl.ds(first, n)]

    def crossing(first, n, ss, rs, k):
        cols = pl.ds(first, n)
        mine = wgu.at[pl.ds((2 * z + x) * own_rows, own_rows), cols]
        other = wgu.at[pl.ds((2 * z + 1 - x) * own_rows, own_rows), cols]
        return (remote(pair(1 - x, first, n), mine, ss, rs, to_x),
                remote(pair(x, first, n), other, ss, rs, to_x),
                local_copy(k, pair(x, first, n), mine))

    cross_a, cross_a_in, mine_a = crossing(0, cols_a, m["xa_s"], m["xa_r"], 5)
    cross_b, cross_b_in, mine_b = crossing(cols_a, cols_b, m["xb_s"], m["xb_r"], 6)
    gate_a = Chain(unit(0, cols_a), m["ca_s"], m["ca_r"])
    gate_b = Chain(unit(cols_a, cols_b), m["cb_s"], m["cb_r"])
    down_a = Chain(lambda zk: m["za"].at[zk], m["da_s"], m["da_r"])
    down_b = Chain(lambda zk: m["zb"].at[zk], m["db_s"], m["db_r"])
    m["rope"][...] = rope_table(2 * rows * z, 2 * rows)
    tok.forward()
    for copy in (cross_a, mine_a, cross_b, mine_b):
        copy.start()
    near.forward()
    flip.forward()
    out_q.forward()
    tok.finish()
    cot.start()
    near.finish()
    flip.finish()
    for k in range(1, 8):
        at = 2 * ((z + 4 - k // 2) % 4) + (x + k) % 2
        remote(m["gains"], m["gains_all"].at[at], m["gn_s"].at[k - 1], m["gn_r"].at[k - 1],
               to_c).wait_recv()
    for k in (0, 1):
        local[k].wait()
    gather_gains = pltpu.make_async_copy(m["gains_all"], m["gains_v"], keep.at[3])
    gather_gains.start()
    gather_gains.wait()
    gain_rows = []
    for i in range(2):
        gain_rows.append(jnp.concatenate(
            [m["gains_v"][k, 0:16].astype(F32)[i:i + 1, :own_rows] for k in range(8)], axis=1))
    m["g_one"][...], m["g_two"][...] = gain_rows
    kv = m["kv_v"]
    q_all, qkv_all = m["q_v"], m["qkv_v"]
    cos, sin = low_half(m["rope"][...]), low_half(roll(m["rope"][...], 64))
    span = 2 * rows

    def order(k):
        return (y + 1 + k) % 2, (c + 1 + k // 2) % 2

    def kv_copy(d, s):
        return remote(kv.at[z, s], kv.at[z, s], m["kv_s"].at[d - 1, s], m["kv_r"].at[z, s],
                      device(base, y, c, (z + d) % 4, x))

    def kv_arrival(zk, s):
        return remote(kv.at[zk, s], kv.at[zk, s], m["kv_s"].at[0, s], m["kv_r"].at[zk, s], to_x)

    def project(k, carry):
        b, e = order(k)
        s = 2 * b + e
        tokens = m["tok_all"][pl.ds(2 * s, 2)].reshape(span, width).astype(F32)
        normed = (tokens * inverse_rms(tokens) * m["g_one"][...]).astype(BF16)
        m["tok_all"][pl.ds(2 * s, 2)] = normed.reshape(2, rows, width)
        qkv = jnp.dot(normed, wq[...], preferred_element_type=F32)
        qkv_all[s] = qkv[:, 0:256]
        heads = split_heads(qkv[:, 0:128], qkv[:, 128:256])
        for j in range(GROUP):
            u = heads[j]
            u = rotated(u * head_inverse(u) * qg, cos, sin) * HEAD_DIM ** (-0.5)
            q_all[s, pl.ds(j * span, span)] = u.astype(BF16)
        u = heads[GROUP]
        u = rotated(u * head_inverse(u) * kg, cos, sin)
        v = jnp.concatenate([jnp.zeros((span, HEAD_DIM), F32), qkv[:, 256:320]], axis=1)
        kv[z, s] = (u + v).astype(BF16)
        for d in (3, 2, 1):
            pl.when(z + d < 4)(lambda d=d: kv_copy(d, s).start())
        return carry

    lax.fori_loop(0, 4, project, 0)
    for copy in quarters[1:]:
        copy.wait()
    down_a.start_ends()
    down_a.start_inner()
    for copy in (mine_a, mine_b):
        copy.wait()
    cross_a_in.wait_recv()
    gate_a.start_ends()
    gate_a.start_inner()
    cross_b_in.wait_recv()
    down_b.start_ends()
    gate_b.start_ends()
    cot.forward()

    def hand(k, zk, src, dst, sems, n):
        ss, rs = sems
        to = device(base, zk // 2, zk % 2, z, x)
        pl.when(r != zk)(lambda: remote(src.at[zk], dst.at[pl.ds(n * r, n)], ss.at[zk],
                                        rs.at[r], to).start())

        @pl.when(r == zk)
        def _():
            copy = local_copy(k, src.at[zk], dst.at[pl.ds(n * r, n)])
            copy.start()
            copy.wait()

    def handed(src, dst, sems, n):
        ss, rs = sems
        for rk in range(4):
            ref = dst.at[pl.ds(n * rk, n)]
            pl.when(r != rk)(lambda ref=ref, rk=rk: remote(
                src.at[0], ref, ss.at[0], rs.at[rk], to_x).wait_recv())

    def hand_sent(src, dst, sems, n):
        ss, rs = sems
        for zk in range(4):
            pl.when(r != zk)(lambda zk=zk: remote(
                src.at[zk], dst.at[pl.ds(0, n)], ss.at[zk], rs.at[0], to_x).wait_send())

    quarters[0].wait()
    out_q.finish()
    out_sems = (m["ho_s"], m["ho_r"])
    a_sems, b_sems = (m["hd_s"], m["hd_r"]), (m["hb_s"], m["hb_r"])
    for zk in range(4):
        hand(13, zk, m["zo"], m["wo_v"], out_sems, quarter_o)

    for k in range(1, 4):
        pl.when(z - k >= 0)(lambda k=k: remote(
            segs.at[0], segs.at[(z + 4 - k) % 4], m["su_s"].at[k - 1],
            m["su_r"].at[(z + 4 - k) % 4], to_x).wait_recv())

    summed = SeqSum(m["part"], [m[n] for n in SUM_NAMES])
    inv_all, att = m["inv_v"], m["att_v"]
    acc, q_seg = m["acc"], m["q_seg"]

    def attend_one(k, carry):
        b, e = order(k)
        s = 2 * b + e
        q_seg[...] = segment_columns(segs, z, s)

        def block(zk, diagonal):
            tile = kv[zk, s]
            p = exp_scores(q_all[s], tile, q_seg[...], segment_row(segs, zk, s), diagonal)
            ones = jnp.where(lanes(tile.shape) < HEAD_DIM, 1.0, tile.astype(F32)).astype(BF16)
            add = jnp.dot(p.astype(BF16), ones, preferred_element_type=F32)
            if diagonal:
                acc[...] = add
            else:
                acc[...] += add

        block(z, True)

        def step(i, inner):
            zk = z - 1 - i
            kv_arrival(zk, s).wait_recv()
            block(zk, False)
            return inner

        lax.fori_loop(0, z, step, 0)
        total = acc[...]
        inv = 1.0 / jnp.where(lanes(total.shape) < HEAD_DIM, total, 1.0)
        inv = jnp.where(lanes(total.shape) < HEAD_DIM, inv, roll(inv, 64))
        o = high_half(total * inv)
        lane = lanes((span, 128))
        inv_all[s] = jnp.where(lane < 32, inv[0:span], jnp.where(
            lane < 64, inv[span:2 * span], inv[2 * span:]))
        first, second, third = o[0:span], o[span:2 * span], o[2 * span:]
        att[s, :, 0:128] = (roll(first, 64) + second).astype(BF16)
        att[s, :, 128:192] = roll(third, 64)[:, 0:HEAD_DIM].astype(BF16)
        pl.when(k == 0)(lambda: handed(m["zo"], m["wo_v"], out_sems, quarter_o))
        out = jnp.dot(att[s], m["wo_v"][...], preferred_element_type=F32).astype(BF16)
        m["part"][pl.ds(2 * s, 2)] = out.reshape(2, rows, width)
        pl.when(k < 2)(lambda: summed.give(b))
        pl.when(k == 2)(summed.take_far)
        pl.when(k == 3)(summed.take_near)
        return carry

    lax.fori_loop(0, 4, attend_one, 0)
    down_a.second()
    gate_a.second()
    summed.middle()
    down_a.third()
    summed.finish()
    mid = m["tok"][...].astype(F32) + summed.out[...]
    m["mid"][...] = mid
    m["low"][...] = (mid * inverse_rms(mid) * m["g_two"][...]).astype(BF16)
    n2_all, cot_all = m["n2_v"], m["cot_v"]
    n2 = Gather(m["low"], n2_all, m["gc_s"], m["gc_r"], keep.at[20])
    n2.start()
    cot.finish()
    gate_a.third()
    down_b.pass_ends()
    gate_b.pass_ends()
    down_b.start_inner()
    gate_b.start_inner()
    n2.forward()
    down_a.finish()
    wda, wdb = wd_v.at[pl.ds(0, half_a)], wd_v.at[pl.ds(half_a, part - half_a)]
    for zk in range(4):
        hand(13, zk, m["za"], wda, a_sems, rows_a)
    n2.finish()
    gate_a.finish()
    handed(m["za"], wda, a_sems, rows_a)
    cross_a.wait_send()
    cross_b.wait_send()

    down_b.third()
    gate_b.third()

    def feed_first(s, carry):
        at = pl.ds(pl.multiple_of(s * span, span), span)
        gu = jnp.dot(n2_all[pl.ds(2 * s, 2)].reshape(span, width), wgu[:, :cols_a],
                     preferred_element_type=F32)
        dh = last_dims(cot_all[pl.ds(2 * s, 2)].reshape(span, width), wd_v[0:half_a])
        hidden[at, 0:half_a], dgu[at, 0:half_a], dgu[at, half_a:cols_a] = swiglu(
            gu[:, :half_a], gu[:, half_a:], dh)
        out = last_dims(dgu[at, 0:cols_a], wgu[:, :cols_a]).astype(BF16)
        m["part"][pl.ds(2 * s, 2)] = out.reshape(2, rows, width)
        return carry

    summed.given()
    lax.fori_loop(0, 4, feed_first, 0)
    down_b.pass_inner()
    gate_b.pass_inner()
    block_rows = 2 * own_rows
    gga, gdo, got_a = m["gga"], m["gdo"], m["got_a"]
    gate_sum = ChainSum(lambda zk: gga.at[zk], lambda at: m["gga_slot"].at[at], m["ys_s"],
                        m["ys_r"])
    down_sum = ChainSum(lambda zk: got_a.at[zk], lambda at: m["gda_slot"].at[at], m["yd_s"],
                        m["yd_r"])

    def grad_gate(zk, carry):
        cols = pl.ds(pl.multiple_of(zk * block_rows, 128), block_rows)
        left = n2_all[:, :, cols].reshape(8 * rows, block_rows)
        gga[zk] = first_dims(left, dgu[:, :cols_a]).astype(BF16)
        return carry

    lax.fori_loop(0, 4, grad_gate, 0)
    gate_sum.start()
    for j in range(0, half_a, 128):
        grad = first_dims(hidden[:, j:j + 128], cot_all[...].reshape(8 * rows, width))
        for h in range(128 // rows_a):
            gdo[j // rows_a + h, 0:rows_a] = grad[rows_a * h:rows_a * (h + 1)].astype(BF16)

    def spread_from(i):
        return gdo.at[i, pl.ds(0, rows_a)]

    def spread(i):
        return remote(spread_from(i), got_a.at[r], m["ha_s"].at[i], m["ha_r"].at[r],
                      device(base, i // 2, i % 2, z, x))

    for i in range(4):
        pl.when(r != i)(lambda i=i: spread(i).start())
    got_a[r] = gdo[r, 0:rows_a]

    def add(block, slot):
        block[...] = (block[...].astype(F32) + slot[...].astype(F32)).astype(BF16)

    gate_sum.first_hop(add)
    down_b.finish()
    for zk in range(4):
        hand(13, zk, m["zb"], wdb, b_sems, rows_b)
    gate_b.finish()
    gate_sum.second_hop(add)
    handed(m["zb"], wdb, b_sems, rows_b)
    for i in range(4):
        pl.when(r != i)(lambda i=i: remote(
            spread_from(i), got_a.at[i], m["ha_s"].at[i], m["ha_r"].at[i], to_c).wait_recv())
    down_sum.start()
    summed.passed()

    def total_in(block):
        def total(slots):
            value = block[...].astype(F32)
            for slot in slots:
                value = value + slot[...].astype(F32)
            block[...] = value.astype(BF16)
        return total

    parts, n2, cot_v, normed = m["part"], m["n2_v"], m["cot_v"], m["tok_all"]
    wd_v[pl.ds(part, 128 - rest)] = jnp.zeros((128 - rest, width), BF16)

    def feed(k, carry):
        b, e = order(k)
        s = 2 * b + e
        at = pl.ds(pl.multiple_of(s * span, span), span)
        gu = jnp.dot(n2[pl.ds(2 * s, 2)].reshape(span, width), wgu[:, cols_a:],
                     preferred_element_type=F32)
        dh = last_dims(cot_v[pl.ds(2 * s, 2)].reshape(span, width), wd_v[half_a:])
        (hidden[at, half_a:2 * half_a], dgu[at, cols_a:cols_a + half_a],
         dgu[at, cols_a + half_a:cols_a + 2 * half_a]) = swiglu(
            gu[:, :half_a], gu[:, half_a:2 * half_a], dh[:, :half_a])
        tile = gu[:, 2 * half_a:]
        gate, up, grad = low_half(tile), low_half(roll(tile, 64)), dh[:, half_a:]
        sigma = 1.0 / (1.0 + jnp.exp(-gate))
        active = gate * sigma
        hidden[at, 2 * half_a:] = (active * up).astype(BF16)
        d_gate = grad * up * sigma * (1.0 + gate * (1.0 - sigma))
        dgu[at, cols_a + 2 * half_a:] = (
            d_gate + roll(low_half(grad * active), 64)).astype(BF16)
        out = last_dims(dgu[at, cols_a:], wgu[:, cols_a:])
        out = out + parts[pl.ds(2 * s, 2)].reshape(span, width).astype(F32)
        parts[pl.ds(2 * s, 2)] = out.astype(BF16).reshape(2, rows, width)
        pl.when(k < 2)(lambda: summed.give(b))
        pl.when(k == 2)(summed.take_far)
        pl.when(k == 3)(summed.take_near)
        return carry

    lax.fori_loop(0, 4, feed, 0)
    down_sum.first_hop(add)

    ggu = m["ggu"]
    gu_sum = ChainSum(lambda zk: ggu.at[zk], lambda at: m["gu_slot"].at[at], m["zg_s"], m["zg_r"])

    def farthest(i):
        up = z // 2
        return up * i + (1 - up) * (3 - i)

    def grad_gu(i, carry):
        zk = farthest(i)
        cols = pl.ds(pl.multiple_of(zk * block_rows, 128), block_rows)
        left = n2[:, :, cols].reshape(8 * rows, block_rows)
        ggu[zk] = first_dims(left, dgu[:, cols_a:]).astype(BF16)
        pl.when(i < 2)(lambda: gu_sum.start_one(zk))
        return carry

    lax.fori_loop(0, 2, grad_gu, 0)
    summed.middle()
    lax.fori_loop(2, 4, grad_gu, 0)
    down_sum.second_hop(add)
    summed.finish()

    v = m["mid"][...]
    dv, gain_grad = norm_back(summed.out[...], v, inverse_rms(v), m["g_two"][...])
    m["row_two"][...] = gain_grad
    dmid = cot_v[t_own].astype(F32) + dv
    m["dmid"][...] = dmid
    m["low"][...] = dmid.astype(BF16)
    branch = Gather(m["low"], m["db"], m["gd_s"], m["gd_r"], keep.at[12])
    branch.start()
    gu_sum.first_hop(add, (0,))

    got = m["got"]
    quarter_d = rows_b
    for i in range(4):
        pl.when(r != i)(lambda i=i: spread(i).wait_send())
    for j in range(0, half_a + 128, 128):
        at = half_a + j
        grad = first_dims(hidden[:, at:at + 128], cot_v[...].reshape(8 * rows, width))
        grad = grad.astype(BF16)
        for i in range(4):
            lo, hi = max(j, quarter_d * i), min(j + 128, quarter_d * (i + 1))
            if lo < hi:
                gdo[i, lo - quarter_d * i:hi - quarter_d * i] = grad[lo - j:hi - j]

    summed.sent()

    def down(s, carry):
        at = pl.ds(pl.multiple_of(s * span, span), span)
        out = jnp.dot(hidden[at], wd_v[...], preferred_element_type=F32)
        parts[pl.ds(2 * s, 2)] = out.astype(BF16).reshape(2, rows, width)
        return carry

    lax.fori_loop(0, 4, down, 0)
    mixed = SeqSum(parts, [m[n] for n in SUM_NAMES], by_x=True)

    def give(i, lo, n, ss, rs):
        return remote(gdo.at[i, pl.ds(lo, n)], got.at[r, pl.ds(lo, n)], ss.at[i], rs.at[r],
                      device(base, i // 2, i % 2, z, x))

    def give_all(lo, n, ss, rs):
        for i in range(4):
            pl.when(r != i)(lambda i=i: give(i, lo, n, ss, rs).start())
        got[r, lo:lo + n] = gdo[r, lo:lo + n]

    def given(lo, n, ss, rs):
        for i in range(4):
            pl.when(r != i)(lambda i=i: remote(
                gdo.at[i, pl.ds(lo, n)], got.at[i, pl.ds(lo, n)], ss.at[i], rs.at[i],
                to_c).wait_recv())

    def give_sent(lo, n, ss, rs):
        for i in range(4):
            pl.when(r != i)(lambda i=i: give(i, lo, n, ss, rs).wait_send())

    def swap(src, out, ss, rs):
        return remote(src.at[pl.ds(own_rows * (1 - x), own_rows)], out.at[t_own], ss, rs, to_x)

    def keep_own(k, src, out):
        copy = pltpu.make_async_copy(src.at[pl.ds(own_rows * x, own_rows)], out.at[t_own],
                                     keep.at[k])
        copy.start()
        return copy

    def swapped(src, out, ss, rs):
        return remote(src.at[pl.ds(own_rows * x, own_rows)], out.at[2 * r + 1 - x], ss, rs, to_x)

    def pairs(out):
        return lambda i: out.at[pl.ds(2 * i, 2)]

    ga_out, gb_out, qkv_out = m["ga_g"], m["gb_g"], m["qkv_g"]
    ga_swap = swap(gga.at[z], ga_out, m["xs_s"], m["xs_r"])
    ga_keep = local_copy(14, gga.at[z, pl.ds(own_rows * x, own_rows)], ga_out.at[t_own])
    da_keep = local_copy(15, got_a.at[z], m["da_g"].at[r])
    ga_share = RepShare(pairs(ga_out), m["ra_s"], m["ra_r"])
    da_share = RepShare(lambda i: m["da_g"].at[i], m["rc_s"], m["rc_r"])

    def swap_first():
        gate_sum.collect(total_in(gga.at[z]))
        down_sum.collect(total_in(got_a.at[z]))
        for copy in (ga_swap, ga_keep, da_keep):
            copy.start()

    branch.forward()
    branch.arrive(2)
    branch.keep.wait()
    give_all(0, quarter_d, m["he_s"], m["he_r"])
    mixed.give(0)
    mixed.give(1)
    swap_first()
    gu_sum.first_hop(add, (1,))

    wo, qkv, dkv = m["wo_v"], qkv_all, kv
    db, dqkv, do_v = m["db"], m["dqkv"], m["do"]
    own_kv = m["own_kv"]
    m["row_head"][...] = jnp.zeros((1, 128), F32)

    down_rest = ChainSum(lambda zk: got.at[zk, pl.ds(0, quarter_d)],
                         lambda at: m["down_slot"].at[at], m["zd_s"], m["zd_r"])

    def share_first():
        ga_keep.wait()
        da_keep.wait()
        swapped(gga.at[z], ga_out, m["xs_s"], m["xs_r"]).wait_recv()
        ga_share.start()
        da_share.start()

    def order_back(k):
        return (y + k // 2) % 2, (c + 1 + k) % 2

    kv_slot = m["kv_slot"]

    def kv_down(zk, s):
        return remote(dkv.at[zk, s], kv_slot.at[zk, s], m["zk_s"].at[zk, s], m["zk_r"].at[zk, s],
                      device(base, y, c, (z + 3) % 4, x))

    def kv_merge(k):
        b, e = order_back(k)
        s = 2 * b + e

        def one(zk, inner):
            kv_down(zk, s).wait_recv()
            dkv[zk, s] = (dkv[zk, s].astype(F32) + kv_slot[zk, s].astype(F32)).astype(BF16)
            kv_down(zk, s).start()
            return inner

        @pl.when((z == 1) | (z == 2))
        def _():
            lax.fori_loop(0, z, one, 0)

    def attend_back(k, carry):
        pl.when(k == 0)(lambda: branch.arrive(4))
        pl.when(k == 1)(branch.cross)
        pl.when(k == 2)(lambda: [branch.arrive(6), branch.arrive(7)] and None)
        b, e = order_back(k)
        s = 2 * b + e
        grads = db[pl.ds(2 * s, 2)].reshape(span, width)
        d_att = last_dims(grads, wo[...])
        first = d_att[:, 0:128]
        third = jnp.concatenate([jnp.zeros((span, HEAD_DIM), F32), d_att[:, 128:192]], axis=1)
        d_out = [high_half(roll(first, 64)), high_half(first), third]
        att_a = att[s, :, 0:128].astype(F32)
        att_b = att[s, :, 128:192].astype(F32)
        att_b = jnp.concatenate([jnp.zeros((span, HEAD_DIM), F32), att_b], axis=1)
        deltas = []
        for j, o in enumerate((roll(att_a, 64), att_a, att_b)):
            inv = inv_all[s][:, 32 * j:32 * j + 1]
            part_j = (d_out[j].astype(BF16).astype(F32) * inv).astype(BF16)
            do_v[pl.ds(j * span, span)] = part_j
            deltas.append(jnp.sum(part_j.astype(F32) * o, axis=1, keepdims=True))
        delta = jnp.concatenate(deltas, axis=0)
        m["q_t"][...] = jnp.transpose(q_all[s].astype(F32)).astype(BF16)
        m["do_t"][...] = jnp.transpose(do_v[...].astype(F32)).astype(BF16)
        q_seg[...] = segment_columns(segs, z, s)
        acc[...] = jnp.zeros_like(acc)

        def block(zk, diagonal):
            tile = kv[zk, s]
            q = q_all[s]
            d_out = do_v[...]
            p = exp_scores(q, tile, q_seg[...], segment_row(segs, zk, s), diagonal)
            ds = (p * (last_dims(d_out, tile) - delta)).astype(BF16)
            acc[...] += jnp.dot(ds, tile, preferred_element_type=F32)
            both = jnp.dot(m["q_t"][...], ds, preferred_element_type=F32)
            both = both + jnp.dot(m["do_t"][...], p.astype(BF16), preferred_element_type=F32)
            return jnp.transpose(both)

        def step(zk, inner):
            dkv[zk, s] = block(zk, False).astype(BF16)
            pl.when(z == 3)(lambda: kv_down(zk, s).start())
            return inner

        lax.fori_loop(0, z, step, 0)
        own_kv[s] = block(z, True)
        tiles = split_heads(qkv[s, :, 0:128], qkv[s, :, 128:256])
        back = []
        for j in range(GROUP):
            dy = rotated(low_half(acc[pl.ds(j * span, span)]) * HEAD_DIM ** (-0.5), cos, -sin)
            raw, gain_part = head_back(dy, tiles[j], qg)
            m["row_head"][...] += gain_part
            back.append(raw)
        dqkv[s, :, 0:128] = (back[0] + roll(back[1], 64)).astype(BF16)
        dqkv[s, :, 128:256] = back[2].astype(BF16)
        pl.when(k >= 1)(lambda: kv_merge(k - 1))
        pl.when(k == 0)(lambda: gu_sum.second_hop(add))
        pl.when(k == 0)(mixed.take_far)
        pl.when(k == 0)(mixed.take_near)
        pl.when(k == 1)(share_first)
        pl.when(k == 3)(mixed.middle)
        pl.when(k == 3)(lambda: given(0, quarter_d, m["he_s"], m["he_r"]))
        return carry

    lax.fori_loop(0, 4, attend_back, 0)
    kv_merge(3)
    gu_sum.start_one(farthest(2))
    down_rest.start()
    inputs = SeqSum(parts, [m[n] for n in SUM_NAMES], by_x=True)

    def finish_one(k, carry):
        b, e = (y + (k + 1) // 2) % 2, (c + 1 + k // 2) % 2
        s = 2 * b + e
        @pl.when(z < 3)
        def _():
            kv_down(z, s).wait_recv()
            own_kv[s] += kv_slot[z, s].astype(F32)

        total = own_kv[s]
        u = split_heads(qkv[s, :, 0:128], qkv[s, :, 128:256])[GROUP]
        dy = rotated(low_half(total), cos, -sin)
        raw, gain_part = head_back(dy, u, kg)
        m["row_head"][...] += roll(gain_part, 64)
        tile = dqkv[s, :, 128:256].astype(F32)
        dqkv[s, :, 128:256] = (low_half(tile) + roll(raw, 64)).astype(BF16)
        dqkv[s, :, 256:320] = roll(total, 64)[:, 0:HEAD_DIM].astype(BF16)
        return carry

    lax.fori_loop(0, 4, finish_one, 0)
    gqkv = m["gqkv"]
    qkv_sum = Direct(lambda zk: gqkv.at[zk], lambda zk: m["qkv_slot"].at[zk], m["zq_s"],
                     m["zq_r"])

    def grad_qkv(i, carry):
        zk = farthest(i)
        cols = pl.ds(pl.multiple_of(zk * block_rows, 128), block_rows)
        left = normed[:, :, cols].reshape(8 * rows, block_rows)
        gqkv[zk] = first_dims(left, dqkv[...].reshape(8 * rows, HEAD_COLS)).astype(BF16)
        qkv_sum.start(zk)
        return carry

    lax.fori_loop(0, 4, grad_qkv, 0)

    for j in range(0, width, 512):
        cols = slice(j, j + 512)
        grad = first_dims(att[...].reshape(8 * rows, Q_COLS),
                          db[:, :, cols].reshape(8 * rows, 512)).astype(BF16)
        for i in range(4):
            gdo[i, quarter_d:quarter_d + quarter_o, cols] = grad[quarter_o * i:quarter_o * (i + 1)]
    give_all(quarter_d, quarter_o, m["hf_s"], m["hf_r"])
    mixed.given()

    def back_in(s, carry):
        out = last_dims(dqkv[s], wq[...]).astype(BF16)
        parts[pl.ds(2 * s, 2)] = out.reshape(2, rows, width)
        return carry

    lax.fori_loop(0, 4, back_in, 0)
    gu_sum.collect(total_in(ggu.at[z]))
    gb_swap = swap(ggu.at[z], gb_out, m["xg_s"], m["xg_r"])
    gb_swap.start()
    gb_keep = keep_own(14, ggu.at[z], gb_out)
    mixed.finish()
    branch.sent()
    m["low"][...] = (m["mid"][...] + mixed.out[...]).astype(BF16)
    mixed_out = loaded(17, m["low"], m["mixed"])
    mixed.passed()
    free = m["free"]
    for to in (to_c, to_x, to_y):
        pl.semaphore_signal(free, inc=1, device_id=to, device_id_type=MESH)

    pl.semaphore_wait(free, 3)
    inputs.give(0)
    inputs.give(1)
    inputs.take_far()
    inputs.take_near()
    gb_keep.wait()
    swapped(ggu.at[z], gb_out, m["xg_s"], m["xg_r"]).wait_recv()
    gb_share = RepShare(pairs(gb_out), m["rg_s"], m["rg_r"])
    gb_share.start()
    down_rest.first_hop(add)
    inputs.middle()
    down_rest.second_hop(add, (1,))
    given(quarter_d, quarter_o, m["hf_s"], m["hf_r"])
    out_sum = Direct(lambda zk: got.at[zk, pl.ds(quarter_d, quarter_o)],
                     lambda zk: m["out_slot"].at[zk], m["zo_s"], m["zo_r"])

    def start_out(i, carry):
        out_sum.start(farthest(i))
        return carry

    lax.fori_loop(0, 4, start_out, 0)
    ga_share.forward()
    da_share.forward()

    inputs.finish()
    v = m["tok"][...].astype(F32)
    dv, gain_grad = norm_back(inputs.out[...], v, inverse_rms(v), m["g_one"][...])
    m["dmid"][...] += dv
    grad_out = loaded(18, m["dmid"], m["input_grad"])

    def gain_rows_of(k):
        return m["mid"].at[pl.ds(8 * k, 8)]

    gains_own = gain_rows_of(0)
    gains_own[0:1] = gain_grad
    gains_own[1:2] = m["row_two"][...]
    gains_own[2:3, 0:128] = m["row_head"][...]

    def gain_sum(k):
        return remote(gains_own, gain_rows_of(k), m["gm_s"].at[k - 1], m["gm_r"].at[k - 1],
                      mates[k - 1])

    for k in range(1, 8):
        gain_sum(k).start()

    down_rest.second_hop(add, (2,))

    total = gqkv[z].astype(F32)
    for term in qkv_sum.take():
        total = total + term
    gqkv[z] = total.astype(BF16)
    qkv_swap = swap(gqkv.at[z], qkv_out, m["xq_s"], m["xq_r"])
    qkv_swap.start()
    qkv_keep = keep_own(16, gqkv.at[z], qkv_out)
    qkv_share = RepShare(pairs(qkv_out), m["rq_s"], m["rq_r"])

    down_rest.collect(total_in(got.at[z, pl.ds(0, quarter_d)]))
    db_keep = loaded(15, got.at[z, pl.ds(0, quarter_d)], m["db_g"].at[r])
    db_keep.wait()
    db_share = RepShare(lambda i: m["db_g"].at[i], m["rd_s"], m["rd_r"])
    db_share.start()
    for k in range(1, 8):
        gain_sum(k).wait_recv()
    total = gains_own[...]
    for k in range(1, 8):
        total = total + gain_rows_of(k)[...]
    z_rows = m["z_rows"]
    z_rows[0] = total

    def gain_z(k):
        return remote(z_rows.at[0], z_rows.at[k], m["gz_s"].at[k - 1], m["gz_r"].at[k - 1],
                      device(base, y, c, (z + k) % 4, x))

    for k in range(1, 4):
        gain_z(k).start()
    gb_share.forward()
    qkv_keep.wait()
    swapped(gqkv.at[z], qkv_out, m["xq_s"], m["xq_r"]).wait_recv()
    qkv_share.start()
    out_own = got.at[z, pl.ds(quarter_d, quarter_o)]
    total = out_own[...].astype(F32)
    for term in out_sum.take():
        total = total + term
    out_own[...] = total.astype(BF16)
    out_keep = loaded(0, out_own, m["out_g"].at[r])
    out_keep.wait()
    out_share = RepShare(lambda i: m["out_g"].at[i], m["re_s"], m["re_r"])
    out_share.start()
    db_share.forward()
    for k in range(1, 4):
        gain_z(k).wait_recv()
    m["gains_g"][...] = z_rows[0] + z_rows[1] + z_rows[2] + z_rows[3]
    qkv_share.forward()
    out_share.forward()
    shares = (ga_share, da_share, gb_share, db_share, out_share, qkv_share)
    for share in shares:
        share.finish()

    for share in shares:
        share.sent()
    for copy in (ga_swap, gb_swap, qkv_swap):
        copy.wait_send()
    for k in range(1, 8):
        gain_sum(k).wait_send()
    for k in range(1, 4):
        gain_z(k).wait_send()
    mixed_out.wait()
    grad_out.wait()
    for flow in (gu_sum, down_rest, qkv_sum, out_sum, inputs):
        flow.sent()
    give_sent(0, quarter_d, m["he_s"], m["he_r"])
    give_sent(quarter_d, quarter_o, m["hf_s"], m["hf_r"])

    def dkv_sent(s, carry):
        for zk in range(3):
            pl.when(z > zk)(lambda zk=zk: kv_down(zk, s).wait_send())
        return carry

    lax.fori_loop(0, 4, dkv_sent, 0)
    for flow in (near, flip, out_q, gate_a, gate_b, down_a, down_b, gate_sum, down_sum):
        flow.sent()
    over.wait_send()
    for k in range(1, 8):
        seg_copy(k).wait_send()
        gain_copy(k).wait_send()
    for k in range(1, 4):
        pl.when(z + k < 4)(lambda k=k: seg_up(k).wait_send())

    def kv_sent(s, carry):
        for d in (1, 2, 3):
            pl.when(z + d < 4)(lambda d=d: kv_copy(d, s).wait_send())
        return carry

    lax.fori_loop(0, 4, kv_sent, 0)
    hand_sent(m["zo"], m["wo_v"], out_sems, quarter_o)
    hand_sent(m["za"], wda, a_sems, rows_a)
    hand_sent(m["zb"], wdb, b_sems, rows_b)


SUM_NAMES = ("r1", "chip", "rx", "mine", "late", "sum_out", "sum_s", "sum_r")
IN = ("tok", "cot", "small", "wqkv", "wgu", "wd", "wo")
OUT = ("mixed", "input_grad", "gains_g", "ga_g", "gb_g", "da_g", "db_g", "out_g", "qkv_g",
       "zo", "za", "zb", "gains_all")


def block_call(*args):
    shape = jax.ShapeDtypeStruct
    tok, _, _, wqkv, wgu, wd, wo = args[:7]
    rows, width = tok.shape
    span = 2 * rows
    own_rows = wqkv.shape[0]
    seg, gains = shape((8, rows), jnp.int32), shape((16, 256), BF16)
    part = wgu.shape[1] // 16
    half_a = part // 256 * 128
    part_b = part - half_a
    cols_a, cols_b = 2 * half_a, 2 * half_a + 128
    quarter_a, quarter_d, quarter_o = half_a // 4, part_b // 4, own_rows // 4
    heads = GROUP * span
    outs = {
        "mixed": shape((rows, width), BF16),
        "input_grad": shape((rows, width), F32),
        "gains_g": shape((8, width), F32),
        "ga_g": shape((8, own_rows, cols_a), BF16),
        "gb_g": shape((8, own_rows, cols_b), BF16),
        "da_g": shape((4, quarter_a, width), BF16),
        "db_g": shape((4, quarter_d, width), BF16),
        "out_g": shape((4, quarter_o, width), BF16),
        "qkv_g": shape((8, own_rows, HEAD_COLS), BF16),
        "zo": shape((4, quarter_o, width), BF16),
        "za": shape((4, quarter_a, width), BF16),
        "zb": shape((4, quarter_d, width), BF16),
        "gains_all": shape((8,) + gains.shape, BF16),
    }
    buffers = {
        "tok_all": ((8, rows, width), BF16), "cot_v": ((8, rows, width), BF16),
        "n2_v": ((8, rows, width), BF16), "db": ((8, rows, width), BF16),
        "part": ((8, rows, width), BF16),
        "rope": ((span, 128), F32), "seg": (seg.shape, seg.dtype), "gains": (gains.shape, BF16),
        "wq": ((2, own_rows, HEAD_COLS), BF16), "wq_raw": ((own_rows, 640), BF16),
        "segs_v": ((4, 8) + seg.shape, seg.dtype), "gains_v": ((8,) + gains.shape, BF16),
        "wq_v": ((width, HEAD_COLS), BF16), "wo_v": ((Q_COLS, width), BF16),
        "wgu_v": ((width, cols_a + cols_b), BF16), "wd_v": ((2 * half_a + 128, width), BF16),
        "hidden": ((8 * rows, 2 * half_a + 128), BF16),
        "dgu": ((8 * rows, cols_a + cols_b), BF16),
        "qkv_v": ((4, span, 256), F32), "q_v": ((4, heads, 128), BF16),
        "kv_v": ((4, 4, span, 128), BF16), "kv_slot": ((3, 4, span, 128), BF16),
        "own_kv": ((4, span, 128), F32), "inv_v": ((4, span, 128), F32),
        "att_v": ((4, span, Q_COLS), BF16), "acc": ((heads, 128), F32),
        "do": ((heads, 128), BF16), "q_t": ((128, heads), BF16), "do_t": ((128, heads), BF16), "q_seg": ((span, span), jnp.int32),
        "dqkv": ((4, span, HEAD_COLS), BF16),
        "mid": ((rows, width), F32), "dmid": ((rows, width), F32), "low": ((rows, width), BF16),
        "g_one": ((1, width), F32), "g_two": ((1, width), F32),
        "gga": ((4, 2 * own_rows, cols_a), BF16), "gga_slot": ((5, 2 * own_rows, cols_a), BF16),
        "ggu": ((4, 2 * own_rows, cols_b), BF16), "gu_slot": ((5, 2 * own_rows, cols_b), BF16),
        "got_a": ((4, quarter_a, width), BF16),
        "gda_slot": ((5, quarter_a, width), BF16),
        "gdo": ((4, quarter_d + quarter_o, width), BF16),
        "got": ((4, quarter_d + quarter_o, width), BF16),
        "down_slot": ((5, quarter_d, width), BF16),
        "out_slot": ((4, quarter_o, width), BF16),
        "gqkv": ((4, 2 * own_rows, HEAD_COLS), BF16),
        "qkv_slot": ((4, 2 * own_rows, HEAD_COLS), BF16),
        "row_two": ((1, width), F32), "row_head": ((1, 128), F32),
        "z_rows": ((4, 8, width), F32),
    }
    counts = {
        "ga": (8, 8), "gb": (8, 8), "gc": (8, 8), "gd": (8, 8), "sg": (7, 7), "gn": (7, 7),
        "gm": (7, 7), "gz": (3, 3), "wa": (6, 4), "wb": (6, 4), "wo": (6, 4), "wx": (1, 1),
        "xa": (1, 1), "xb": (1, 1), "xs": (1, 1), "xg": (1, 1), "ca": (5, 4), "cb": (5, 4),
        "da": (5, 4), "db": (5, 4), "ys": (4, 5), "yd": (4, 5), "zg": (4, 5), "zd": (4, 5),
        "zo": (4, 4), "zq": (4, 4), "xq": (1, 1), "zk": ((3, 4), (3, 4)), "kv": ((3, 4), (4, 4)),
        "su": (3, 4), "ha": (4, 4), "hb": (4, 4), "hd": (4, 4), "he": (4, 4), "hf": (4, 4),
        "ho": (4, 4), "ra": (3, 3), "rc": (3, 3), "rd": (3, 3), "re": (3, 3), "rg": (3, 3),
        "rq": (3, 3),
    }
    sem = pltpu.SemaphoreType.DMA
    many = lambda n: sem if n == 1 else sem(n if isinstance(n, tuple) else (n,))
    sems = {"keep": dma(21), "free": pltpu.SemaphoreType.REGULAR}
    for n, (send, recv) in counts.items():
        sems[n + "_s"], sems[n + "_r"] = many(send), many(recv)
    scratch = {n: pltpu.VMEM(*v) for n, v in buffers.items()}
    scratch.update(zip(SUM_NAMES, seq_scratch(width)))
    names = IN + OUT + tuple(scratch) + tuple(sems)
    got = pl.pallas_call(
        functools.partial(block_kernel, names),
        name="block",
        out_shape=tuple(outs[n] for n in OUT),
        in_specs=[ANY if n in ("cot", "wqkv", "wgu", "wd", "wo") else VMEM for n in IN],
        out_specs=tuple(VMEM if n == "gains_g" else ANY for n in OUT),
        scratch_shapes=list(scratch.values()) + list(sems.values()),
        compiler_params=params(0, 63),
    )(*args)
    return dict(zip(OUT, got))


def order_kernel(names, *refs):
    m = dict(zip(names, refs))
    half_a = m["ga"].shape[2] // 2
    half_b = (m["gb"].shape[2] - 128) // 2
    main = half_a + half_b
    cols = 2 * main + 128
    own_rows = m["ga"].shape[1]
    low = lanes((own_rows, 128)) < HEAD_DIM
    x = lax.axis_index("grp") % 2

    def fetch(k, src, dst):
        copy = pltpu.make_async_copy(src, dst, m["load"].at[k])
        copy.start()
        return copy

    def store(k, src, dst):
        copy = pltpu.make_async_copy(src, dst, m["save"].at[k])
        copy.start()
        return copy

    ga, gb = m["ga_v"], m["gb_v"]
    pair = lambda i: pl.ds(2 * i, 2)
    wide = [(fetch(2 * i, m["ga"].at[pair(i)], ga.at[pair(i)]),
             fetch(2 * i + 1, m["gb"].at[pair(i)], gb.at[pair(i)])) for i in range(4)]
    rest = {n: fetch(8 + k, m[n], m[n + "_v"])
            for k, n in enumerate(("db", "qkv", "da", "out", "ig", "mixed"))}
    saved = []
    for i in range(4):
        for copy in wide[i]:
            copy.wait()
        first, second = ga.at[2 * i], ga.at[2 * i + 1]
        tiles = [gb[2 * i + k, :, 2 * half_b:].astype(F32) for k in range(2)]
        for w in range(2):
            to = m["gu_v"].at[4 * w + i]
            for k in range(2):
                lo = k * (main + 128)
                to[:, lo:lo + half_a] = ga[2 * i + k, :, w * half_a:(w + 1) * half_a].astype(F32)
                to[:, lo + half_a:lo + main] = (
                    gb[2 * i + k, :, w * half_b:(w + 1) * half_b].astype(F32))
            if w == 0:
                to[:, main:main + 128] = jnp.where(low, tiles[0], roll(tiles[1], 64))
            else:
                to[:, main:main + 128] = jnp.where(low, roll(tiles[0], 64), tiles[1])
            saved.append(store(
                4 * w + i, to, m["gu_o"].at[:, pl.ds((4 * w + i) * cols, cols)]))

    rest["da"].wait()
    rest["db"].wait()
    da, db, down = m["da_v"], m["db_v"], m["down_v"]
    part = down.shape[0]
    rows_a, rows_b = da.shape[1], db.shape[1]
    shift = (part - main) * x

    def at(start, n):
        return pl.ds(pl.multiple_of(start, 16), n)

    for i in range(4):
        down[at(rows_a * i + shift, rows_a)] = da[i].astype(F32)
        start = half_a + rows_b * i + shift
        down[at(start, 16)] = db[i, 0:16].astype(F32)
        down[at(start + 16 - (i // 3) * x * part, rows_b - 16)] = db[i, 16:].astype(F32)
    saved.append(store(8, down, m["down_o"]))
    rest["qkv"].wait()
    qkv_v, qkv_f = m["qkv_v"], m["qkv_f"]
    q_cols, kv_cols = HEADS * HEAD_DIM, KV_HEADS * HEAD_DIM
    half = lambda v, w: jnp.where(low, v, w)
    for i in range(4):
        a, b = qkv_v[2 * i].astype(F32), qkv_v[2 * i + 1].astype(F32)
        a1, a2, b0, b1 = a[:, 128:256], a[:, 256:], b[:, 0:128], b[:, 128:256]
        lo = i * 2 * Q_COLS
        qkv_f[:, lo:lo + 128] = a[:, 0:128]
        qkv_f[:, lo + 128:lo + 256] = half(a1, roll(b0, 64))
        qkv_f[:, lo + 256:lo + 384] = half(roll(b0, 64), roll(b1, 64))
        lo = q_cols + i * 128
        qkv_f[:, lo:lo + 128] = half(roll(a1, 64), b1)
        lo = lo + kv_cols
        qkv_f[:, lo:lo + 128] = jnp.concatenate([a2, b[:, 256:]], axis=1)
    saved.append(store(9, qkv_f, m["qkv_o"]))
    rest["out"].wait()
    n = m["out_v"].shape[1]
    for i in range(4):
        m["out_f"][n * i:n * (i + 1)] = m["out_v"][i].astype(F32)
    saved.append(store(10, m["out_f"], m["out_o"]))
    for k, n in ((11, "ig"), (12, "mixed")):
        rest[n].wait()
        saved.append(store(k, m[n + "_v"], m[n + "_o"]))
    gains = m["gains"][...]
    width = gains.shape[1]
    turned = pltpu.roll(gains, (width - own_rows * lax.axis_index("grp")) % width, 1)
    m["one_o"][...] = turned[0:1, 0:own_rows]
    m["two_o"][...] = turned[1:2, 0:own_rows]
    m["q_o"][...] = gains[2:3, 0:HEAD_DIM]
    m["k_o"][...] = gains[2:3, HEAD_DIM:2 * HEAD_DIM]
    for copy in saved:
        copy.wait()


def order_call(g):
    shape = jax.ShapeDtypeStruct
    ga, gb, da, db, out, qkv, mixed, ig = (g[n] for n in ORDER_IN)
    _, own_rows, cols_a = ga.shape
    cols = cols_a + gb.shape[2]
    width = da.shape[2]
    part = 4 * (da.shape[1] + db.shape[1])
    qkv_cols = (HEADS + 2 * KV_HEADS) * HEAD_DIM
    outs = {
        "gu_o": shape((own_rows, 8 * cols), F32), "down_o": shape((part, width), F32),
        "out_o": shape((own_rows, width), F32), "qkv_o": shape((own_rows, qkv_cols), F32),
        "ig_o": shape(ig.shape, F32), "mixed_o": shape(mixed.shape, BF16),
        "one_o": shape((1, own_rows), F32), "two_o": shape((1, own_rows), F32),
        "q_o": shape((1, HEAD_DIM), F32), "k_o": shape((1, HEAD_DIM), F32),
    }
    ins = ("ga", "gb", "da", "db", "out", "qkv", "mixed", "ig")
    scratch = {n + "_v": pltpu.VMEM(v.shape, v.dtype)
               for n, v in zip(ins, (ga, gb, da, db, out, qkv, mixed, ig))}
    scratch["gu_v"] = pltpu.VMEM((8, own_rows, cols), F32)
    scratch["down_v"] = pltpu.VMEM((part, width), F32)
    scratch["out_f"] = pltpu.VMEM((own_rows, width), F32)
    scratch["qkv_f"] = pltpu.VMEM((own_rows, qkv_cols), F32)
    scratch["load"], scratch["save"] = dma(14), dma(13)
    names = ins + ("gains",) + tuple(outs) + tuple(scratch)
    got = pl.pallas_call(
        functools.partial(order_kernel, names),
        name="final_order",
        out_shape=tuple(outs.values()),
        in_specs=[ANY] * 8 + [VMEM],
        out_specs=(ANY,) * 6 + (VMEM,) * 4,
        scratch_shapes=list(scratch.values()),
        compiler_params=pltpu.CompilerParams(vmem_limit_bytes=62 * 2**20),
    )(ga, gb, da, db, out, qkv, mixed, ig, g["gains_g"])
    return dict(zip(outs, got))


ORDER_IN = ("ga_g", "gb_g", "da_g", "db_g", "out_g", "qkv_g", "mixed", "input_grad")


def over_quads(array):
    reps = lax.axis_size("rep")
    if reps == 4:
        return array
    rows = [[j + 4 * q for q in range(reps // 4)] for j in range(4)]
    return lax.psum(array, "rep", axis_index_groups=rows)


def local(tokens, attn_gain, w_qkv, q_gain, k_gain, w_out, ffn_gain, w_gate_up, w_down,
          cotangent, segment_ids):
    rows, width = tokens.shape
    parts = (attn_gain, q_gain, ffn_gain, k_gain, segment_ids)
    total = sum(v.shape[0] for v in parts)
    small, at = 0.0, 0
    for v in parts:
        n = v.shape[0]
        small = small + jnp.pad(v.astype(F32), (at, total - at - n))
        at += n
    g = block_call(
        tokens, cotangent, small.reshape(1, -1), w_qkv, w_gate_up, w_down, w_out)
    g = {n: over_quads(v) if n.endswith("_g") else v for n, v in g.items()}
    o = order_call(g)
    flat = lambda n: o[n].reshape(-1)
    return (o["mixed_o"], o["ig_o"], flat("one_o"), o["qkv_o"], flat("q_o"), flat("k_o"),
            o["out_o"], flat("two_o"), o["gu_o"], o["down_o"])


def solution(mesh):
    rows, split = P(("rep", "grp"), None), P("grp", None)
    return jax.shard_map(
        local,
        mesh=mesh,
        in_specs=(rows, P("grp"), split, P(), P(), split, P("grp"), split, split, rows,
                  P(("rep", "grp"))),
        out_specs=(rows, rows, P("grp"), split, P(), P(), split, P("grp"), split, split),
        check_vma=False,
    )
```

```python
import functools

import jax
import jax.numpy as jnp
from jax import lax
from jax.experimental import pallas as pl
from jax.experimental.pallas import tpu as pltpu
from jax.sharding import PartitionSpec as P

HEADS = 24
KV_HEADS = 8
HEAD_DIM = 64
GROUP = HEADS // KV_HEADS
Q_COLS = GROUP * HEAD_DIM
HEAD_COLS = Q_COLS + 2 * HEAD_DIM

EPS = 1e-05
THETA = 1000000.0
MESH = pl.DeviceIdType.MESH
F32 = jnp.float32
BF16 = jnp.bfloat16

VMEM = pl.BlockSpec(memory_space=pltpu.VMEM)
ANY = pl.BlockSpec(memory_space=pl.ANY)


def here():
    rep = lax.axis_index("rep")
    grp = lax.axis_index("grp")
    r = rep % 4
    return rep - r, r // 2, r % 2, grp // 2, grp % 2


def device(base, y, c, z, x):
    return {"rep": base + 2 * y + c, "grp": 2 * z + x}


def remote(src, dst, send, recv, to):
    return pltpu.make_async_remote_copy(
        src_ref=src, dst_ref=dst, send_sem=send, recv_sem=recv, device_id=to, device_id_type=MESH
    )


def greet(targets):
    barrier = pltpu.get_barrier_semaphore()
    for to in targets:
        pl.semaphore_signal(barrier, inc=1, device_id=to, device_id_type=MESH)
    pl.semaphore_wait(barrier, len(targets))


def neighbours():
    base, y, c, z, x = here()
    to_c = device(base, y, 1 - c, z, x)
    to_x = device(base, y, c, z, 1 - x)
    to_y = device(base, 1 - y, c, z, x)
    return to_c, to_x, to_y


class Gather:
    def __init__(self, src, out, send, recv, local):
        self.src, self.out, self.send, self.recv = src, out, send, recv
        _, y, c, _, x = here()
        self.to_c, self.to_x, self.to_y = neighbours()
        slot = lambda a, b, d: 4 * a + 2 * b + d
        self.own = slot(y, c, x)
        self.at_c, self.at_x, self.at_y = slot(y, 1 - c, x), slot(y, c, 1 - x), slot(1 - y, c, x)
        self.at_xc, self.at_yc = slot(y, 1 - c, 1 - x), slot(1 - y, 1 - c, x)
        self.at_xy, self.at_xyc = slot(1 - y, c, 1 - x), slot(1 - y, 1 - c, 1 - x)
        self.half = src.shape[0] // 2
        self.keep = pltpu.make_async_copy(src, out.at[self.own], local)

    def part(self, at, k):
        return self.out.at[at, pl.ds(k * self.half, self.half)]

    def copy(self, k):
        out, own = self.out, self.out.at[self.own]
        src, dst, to = (
            lambda: (self.src, own, self.to_x),
            lambda: (self.src, own, self.to_y),
            lambda: (self.src, own, self.to_c),
            lambda: (self.part(self.at_x, 0),) * 2 + (self.to_y,),
            lambda: (out.at[self.at_x],) * 2 + (self.to_c,),
            lambda: (self.part(self.at_y, 1),) * 2 + (self.to_x,),
            lambda: (out.at[self.at_y],) * 2 + (self.to_c,),
            lambda: (out.at[self.at_xy],) * 2 + (self.to_c,),
        )[k]()
        return remote(src, dst, self.send.at[k], self.recv.at[k], to)

    def arrive(self, k):
        out = self.out
        ref = (
            lambda: out.at[self.at_x], lambda: out.at[self.at_y], lambda: out.at[self.at_c],
            lambda: self.part(self.at_xy, 0), lambda: out.at[self.at_xc],
            lambda: self.part(self.at_xy, 1), lambda: out.at[self.at_yc],
            lambda: out.at[self.at_xyc],
        )[k]()
        remote(ref, ref, self.send.at[k], self.recv.at[k], self.to_c).wait_recv()

    def start(self):
        self.keep.start()
        for k in range(3):
            self.copy(k).start()

    def forward(self):
        self.arrive(0)
        self.copy(3).start()
        self.copy(4).start()
        self.arrive(1)
        self.copy(5).start()
        self.copy(6).start()

    def cross(self):
        self.arrive(3)
        self.arrive(5)
        self.copy(7).start()

    def finish(self):
        self.cross()
        for k in (2, 4, 6, 7):
            self.arrive(k)
        self.keep.wait()
        self.sent()

    def sent(self):
        for k in range(8):
            self.copy(k).wait_send()


def dma(n):
    return pltpu.SemaphoreType.DMA((n,))


def params(cid, limit=60):
    return pltpu.CompilerParams(
        collective_id=cid, has_side_effects=True, vmem_limit_bytes=limit * 2**20
    )


def inverse_rms(v):
    return lax.rsqrt(jnp.mean(v * v, axis=-1, keepdims=True) + EPS)


def norm_back(dy, v, inv, gain):
    scaled = dy * gain
    gain_grad = jnp.sum(dy * v * inv, axis=0, keepdims=True)
    inner = jnp.mean(scaled * v, axis=-1, keepdims=True)
    return inv * scaled - v * inv * inv * inv * inner, gain_grad


def when(cond):
    return pl.when(cond)


def lanes(shape):
    return lax.broadcasted_iota(jnp.int32, shape, len(shape) - 1)


def roll(v, by):
    return pltpu.roll(v, by % v.shape[-1], v.ndim - 1)


class Along:
    def __init__(self, src, slot, send, recv):
        self.src, self.slot, self.send, self.recv = src, slot, send, recv
        self.base, self.y, self.c, self.z, self.x = here()

    def at(self, zk, x):
        return device(self.base, self.y, self.c, zk, x)

    def copy(self, d):
        zk = (self.z + d + 4) % 4
        return remote(self.src, self.slot(self.z), self.send.at[d + 2], self.recv.at[self.z],
                      self.at(zk, self.x))

    def fits(self, d):
        return (self.z + d >= 0) & (self.z + d < 4)

    def first(self):
        for d in (2, -2):
            pl.when(self.fits(d))(lambda d=d: self.copy(d).start())
        pl.when(self.z == 2)(lambda: self.copy(1).start())
        pl.when(self.z == 1)(lambda: self.copy(-1).start())

    def second(self):
        pl.when(self.z < 2)(lambda: self.copy(1).start())
        pl.when(self.z >= 2)(lambda: self.copy(-1).start())

    def arrival(self, zk):
        ref = self.slot(zk)
        return remote(ref, ref, self.send.at[0], self.recv.at[zk], self.at(self.z, 1 - self.x))

    def passed(self, zk, to):
        ref = self.slot(zk)
        return remote(ref, ref, self.send.at[5], self.recv.at[zk], self.at(to, self.x))

    def forward(self):
        @pl.when(self.z == 2)
        def _():
            self.arrival(0).wait_recv()
            self.passed(0, 3).start()

        @pl.when(self.z == 1)
        def _():
            self.arrival(3).wait_recv()
            self.passed(3, 0).start()

    def wait(self, zk):
        early = ((self.z == 2) & (zk == 0)) | ((self.z == 1) & (zk == 3))
        due = jnp.logical_not(early) & (self.z != zk)
        pl.when(due)(lambda: self.arrival(zk).wait_recv())

    def finish(self):
        for zk in range(4):
            self.wait(zk)

    def sent(self):
        for d in (2, -2, 1, -1):
            pl.when(self.fits(d))(lambda d=d: self.copy(d).wait_send())
        pl.when(self.z == 2)(lambda: self.passed(0, 3).wait_send())
        pl.when(self.z == 1)(lambda: self.passed(3, 0).wait_send())


class Chain:
    def __init__(self, slot, send, recv):
        self.slot, self.send, self.recv = slot, send, recv
        self.base, self.y, self.c, self.z, self.x = here()

    def copy(self, k, zk, to):
        return remote(self.slot(zk), self.slot(zk), self.send.at[k], self.recv.at[zk],
                      device(self.base, self.y, self.c, to, self.x))

    def arrive(self, zk):
        self.copy(0, zk, self.z).wait_recv()

    def inner(self):
        return (self.z == 1) | (self.z == 2)

    def start_ends(self):
        pl.when(self.z == 0)(lambda: self.copy(0, 0, 1).start())
        pl.when(self.z == 3)(lambda: self.copy(1, 3, 2).start())

    def start_inner(self):
        z = self.z

        @pl.when(self.inner())
        def _():
            self.copy(0, z, z + 1).start()
            self.copy(1, z, z - 1).start()

    def pass_ends(self):
        @pl.when(self.z == 1)
        def _():
            self.arrive(0)
            self.copy(2, 0, 2).start()

        @pl.when(self.z == 2)
        def _():
            self.arrive(3)
            self.copy(3, 3, 1).start()

    def pass_inner(self):
        @pl.when(self.z == 1)
        def _():
            self.arrive(2)
            self.copy(3, 2, 0).start()

        @pl.when(self.z == 2)
        def _():
            self.arrive(1)
            self.copy(2, 1, 3).start()

    def second(self):
        self.pass_ends()
        self.pass_inner()

    def third(self):
        @pl.when(self.z == 2)
        def _():
            self.arrive(0)
            self.copy(4, 0, 3).start()

        @pl.when(self.z == 1)
        def _():
            self.arrive(3)
            self.copy(4, 3, 0).start()

    def finish(self):
        pl.when(self.z == 0)(lambda: [self.arrive(zk) for zk in (1, 2, 3)] and None)
        pl.when(self.z == 3)(lambda: [self.arrive(zk) for zk in (2, 1, 0)] and None)

    def sent(self):
        z = self.z
        pl.when(z < 3)(lambda: self.copy(0, z, z + 1).wait_send())
        pl.when(z > 0)(lambda: self.copy(1, z, z - 1).wait_send())

        @pl.when(self.inner())
        def _():
            self.copy(2, z - 1, z + 1).wait_send()
            self.copy(3, z + 1, z - 1).wait_send()
            self.copy(4, z, z + 1).wait_send()


class ChainSum:
    def __init__(self, block, slot, send, recv):
        self.block, self.slot, self.send, self.recv = block, slot, send, recv
        self.base, self.y, self.c, self.z, self.x = here()

    def copy(self, zk, to, at):
        return remote(self.block(zk), self.slot(at), self.send.at[zk], self.recv.at[at],
                      device(self.base, self.y, self.c, to, self.x))

    def arrive(self, at):
        self.copy(0, self.z, at).wait_recv()

    def start(self):
        @pl.when(self.z == 0)
        def _():
            for zk, at in ((3, 3), (2, 2), (1, 4)):
                self.copy(zk, 1, at).start()

        @pl.when(self.z == 3)
        def _():
            for zk in (0, 1, 2):
                self.copy(zk, 2, zk).start()

    def start_one(self, zk):
        for to, at in ((3, 3), (2, 2), (1, 4)):
            pl.when((self.z == 0) & (zk == to))(
                lambda to=to, at=at: self.copy(to, 1, at).start())
        for to in (0, 1, 2):
            pl.when((self.z == 3) & (zk == to))(lambda to=to: self.copy(to, 2, to).start())

    def first_hop(self, add, which=(0, 1)):
        @pl.when(self.z == 1)
        def _():
            for i in which:
                zk, at = ((3, 3), (2, 4))[i]
                self.arrive(zk)
                add(self.block(zk), self.slot(zk))
                self.copy(zk, 2, at).start()

        @pl.when(self.z == 2)
        def _():
            for zk in which:
                self.arrive(zk)
                add(self.block(zk), self.slot(zk))
                self.copy(zk, 1, zk).start()

    def second_hop(self, add, inner=(1, 2)):
        for z, zk, to, at in ((1, 0, 0, 0), (2, 3, 3, 4)):
            if z not in inner:
                continue

            @pl.when(self.z == z)
            def _():
                self.arrive(zk)
                add(self.block(zk), self.slot(zk))
                self.copy(zk, to, at).start()

    def collect(self, total):
        z = self.z

        def take(ats):
            for at in ats:
                self.arrive(at)
            total([self.slot(at) for at in ats])

        pl.when(z == 0)(lambda: take([0]))
        pl.when(z == 3)(lambda: take([4]))
        pl.when((z == 1) | (z == 2))(lambda: take([z, 4]))

    def sent(self):
        for zk in range(4):
            pl.when(self.z != zk)(lambda zk=zk: self.copy(zk, 0, 0).wait_send())


def layer_mates():
    base, y, c, z, x = here()
    return [
        device(base, (y + k // 4) % 2, (c + k // 2) % 2, z, (x + k) % 2) for k in range(1, 8)
    ]


def z_mates():
    base, y, c, z, x = here()
    return [device(base, y, c, (z + k // 2) % 4, (x + k) % 2) for k in range(2, 8)]


def rotated(u, cos, sin):
    lane = lanes(u.shape)
    return u * cos + jnp.where(lane < 32, roll(u, -32), roll(u, 32)) * sin


def low_half(v):
    return jnp.where(lanes(v.shape) < HEAD_DIM, v, 0.0)


def high_half(v):
    return jnp.where(lanes(v.shape) >= HEAD_DIM, v, 0.0)


def split_heads(tile_a, tile_b):
    return [low_half(tile_a), low_half(roll(tile_a, 64)), low_half(tile_b),
            low_half(roll(tile_b, 64))]


def head_inverse(u):
    return lax.rsqrt(jnp.sum(u * u, axis=-1, keepdims=True) * (1.0 / HEAD_DIM) + EPS)


def exp_scores(q, kv, q_seg, k_seg, diagonal):
    s = lax.dot_general(q, kv, (((1,), (1,)), ((), ())), preferred_element_type=F32)
    allowed = q_seg == k_seg
    if diagonal:
        row = lax.broadcasted_iota(jnp.int32, allowed.shape, 0)
        col = lax.broadcasted_iota(jnp.int32, allowed.shape, 1)
        allowed = allowed & (col <= row)
    n = allowed.shape[0]
    return jnp.concatenate([
        jnp.where(allowed, jnp.exp(s[n * j:n * (j + 1)]), 0.0) for j in range(GROUP)], axis=0)


def segment_row(segs, zk, s):
    return jnp.concatenate([segs[zk, 2 * s, 0:1], segs[zk, 2 * s + 1, 0:1]], axis=1)


def segment_columns(segs, zk, s):
    parts = []
    for i in range(2):
        row = jnp.broadcast_to(segs[zk, 2 * s + i, 0:1], (128, 128))
        parts.append(jnp.transpose(row))
    col = jnp.concatenate(parts, axis=0)
    return jnp.concatenate([col, col], axis=1)


class SeqSum:
    def __init__(self, part, scratch, by_x=False):
        self.part, self.by_x = part, by_x
        (self.r1, self.chip, self.rx, self.mine, self.late, self.out,
         self.send, self.recv) = scratch
        _, self.y, self.c, _, self.x = here()
        self.to_c, self.to_x, self.to_y = neighbours()
        rows = part.shape[1]
        self.top = pl.ds(0, rows if by_x else rows // 2)
        self.low = pl.ds(rows // 2, rows // 2)

    def copy(self, k, src, dst, to):
        return remote(src, dst, self.send.at[k], self.recv.at[k], to)

    def swap(self, b, a):
        at = 2 * b + a
        return self.copy(at, self.part.at[4 * b + 2 * (1 - self.c) + a], self.r1.at[at], self.to_c)

    def give(self, b):
        for a in range(2):
            self.swap(b, a).start()

    def along_x(self, b):
        at = 2 * b + 1 - self.x
        return self.copy(4 + b, self.chip.at[at, self.top], self.rx.at[b, self.top], self.to_x)

    def along_y(self, a):
        at = 2 * (1 - self.y) + a
        return self.copy(6 + a, self.chip.at[at, self.low], self.rx.at[a, self.low], self.to_y)

    def last_y(self):
        return self.copy(8, self.mine.at[self.top], self.late.at[self.top], self.to_y)

    def last_x(self):
        return self.copy(9, self.mine.at[self.low], self.late.at[self.low], self.to_x)

    def total(self, b, a):
        self.swap(b, a).wait_recv()
        at = 2 * b + a
        return self.part[4 * b + 2 * self.c + a].astype(F32) + self.r1[at].astype(F32)

    def take_far(self):
        b = 1 - self.y
        for a in (1 - self.x, self.x):
            self.chip[2 * b + a] = self.total(b, a).astype(BF16)
            if a is not self.x:
                self.along_x(b).start()
            if not self.by_x:
                self.along_y(a).start()

    def take_near(self):
        b, x = self.y, self.x
        self.chip[2 * b + 1 - x] = self.total(b, 1 - x).astype(BF16)
        self.along_x(b).start()
        self.out[...] = self.total(b, x)

    def middle(self):
        x, y, top, low = self.x, self.y, self.top, self.low
        self.along_x(1 - y).wait_recv()
        self.mine[top] = (
            self.chip[2 * (1 - y) + x, top].astype(F32) + self.rx[1 - y, top].astype(F32)
        ).astype(BF16)
        self.last_y().start()
        if self.by_x:
            return
        self.along_y(1 - x).wait_recv()
        self.mine[low] = (
            self.chip[2 * y + 1 - x, low].astype(F32) + self.rx[1 - x, low].astype(F32)
        ).astype(BF16)
        self.last_x().start()

    def finish(self):
        x, y, top, low = self.x, self.y, self.top, self.low
        self.along_x(y).wait_recv()
        self.last_y().wait_recv()
        self.out[top] += self.rx[y, top].astype(F32) + self.late[top].astype(F32)
        if self.by_x:
            return
        self.along_y(x).wait_recv()
        self.last_x().wait_recv()
        self.out[low] += self.rx[x, low].astype(F32) + self.late[low].astype(F32)

    def given(self):
        for b in range(2):
            for a in range(2):
                self.swap(b, a).wait_send()

    def passed(self):
        for b in range(2):
            self.along_x(b).wait_send()
            if not self.by_x:
                self.along_y(b).wait_send()
        self.last_y().wait_send()
        if not self.by_x:
            self.last_x().wait_send()

    def sent(self):
        self.given()
        self.passed()


def seq_scratch(width):
    return [
        pltpu.VMEM((4, 128, width), BF16),
        pltpu.VMEM((4, 128, width), BF16),
        pltpu.VMEM((2, 128, width), BF16),
        pltpu.VMEM((128, width), BF16),
        pltpu.VMEM((128, width), BF16),
        pltpu.VMEM((128, width), F32),
        dma(10),
        dma(10),
    ]


def first_dims(left, right):
    return lax.dot_general(left, right, (((0,), (0,)), ((), ())), preferred_element_type=F32)


def last_dims(left, right):
    return lax.dot_general(left, right, (((1,), (1,)), ((), ())), preferred_element_type=F32)


def swiglu(gate, up, grad):
    sigma = 1.0 / (1.0 + jnp.exp(-gate))
    active = gate * sigma
    d_gate = grad * up * sigma * (1.0 + gate * (1.0 - sigma))
    return ((active * up).astype(BF16), d_gate.astype(BF16), (grad * active).astype(BF16))


class Direct:
    def __init__(self, block, slot, send, recv):
        self.block, self.slot, self.send, self.recv = block, slot, send, recv
        self.base, self.y, self.c, self.z, self.x = here()

    def copy(self, zk):
        return remote(self.block(zk), self.slot(self.z), self.send.at[zk], self.recv.at[self.z],
                      device(self.base, self.y, self.c, zk, self.x))

    def start(self, zk):
        pl.when(zk != self.z)(lambda: self.copy(zk).start())

    def take(self):
        for k in (1, 3, 2):
            zk = (self.z + k) % 4
            ref = self.slot(zk)
            remote(ref, ref, self.send.at[0], self.recv.at[zk],
                   device(self.base, self.y, self.c, zk, self.x)).wait_recv()
            yield ref[...].astype(F32)

    def sent(self):
        for zk in range(4):
            pl.when(self.z != zk)(lambda zk=zk: self.copy(zk).wait_send())


class RepShare:
    def __init__(self, at, send, recv):
        self.at, self.send, self.recv = at, send, recv
        _, self.y, self.c, _, _ = here()
        self.to_c, _, self.to_y = neighbours()
        self.r = 2 * self.y + self.c

    def copy(self, k, r, to):
        return remote(self.at(r), self.at(r), self.send.at[k], self.recv.at[k], to)

    def start(self):
        self.copy(0, self.r, self.to_y).start()
        self.copy(1, self.r, self.to_c).start()

    def forward(self):
        other = 2 * (1 - self.y) + self.c
        self.copy(0, other, self.to_y).wait_recv()
        self.copy(2, other, self.to_c).start()

    def finish(self):
        self.copy(1, 2 * self.y + 1 - self.c, self.to_c).wait_recv()
        self.copy(2, 2 * (1 - self.y) + 1 - self.c, self.to_c).wait_recv()

    def sent(self):
        self.copy(0, self.r, self.to_y).wait_send()
        self.copy(1, self.r, self.to_c).wait_send()
        self.copy(2, self.r, self.to_c).wait_send()


def head_back(dy, u, gain):
    inv = head_inverse(u)
    scaled = dy * gain
    gain_grad = jnp.sum(dy * u * inv, axis=0, keepdims=True)
    inner = jnp.sum(scaled * u, axis=-1, keepdims=True) * (1.0 / HEAD_DIM)
    return inv * scaled - u * (inv * inv * inv * inner), gain_grad


def rope_table(start, rows):
    half = HEAD_DIM // 2
    lane = lax.broadcasted_iota(jnp.int32, (rows, 4 * half), 1)
    freq = jnp.exp(-jnp.log(THETA) * (lane % half).astype(F32) * 2.0 / HEAD_DIM)
    position = start + lax.broadcasted_iota(jnp.int32, (rows, 4 * half), 0)
    angle = position.astype(F32) * freq
    sine = jnp.sin(angle)
    return jnp.where(lane < 2 * half, jnp.cos(angle), jnp.where(lane < 3 * half, -sine, sine))


def block_kernel(names, *refs):
    m = dict(zip(names, refs))
    base, y, c, z, x = here()
    r = 2 * y + c
    to_c, to_x, to_y = neighbours()
    q_cols, kv_cols = HEADS * HEAD_DIM, KV_HEADS * HEAD_DIM
    raw_q = [
        pltpu.make_async_copy(m["wqkv"].at[:, pl.ds(first + n * r, n)],
                              m["wq_raw"].at[:, pl.ds(to, n)], m["keep"].at[k])
        for k, (first, to, n) in enumerate((
            (0, 0, 2 * Q_COLS), (q_cols, 2 * Q_COLS, 2 * HEAD_DIM),
            (q_cols + kv_cols, 2 * Q_COLS + 2 * HEAD_DIM, 2 * HEAD_DIM)))]
    for copy in raw_q:
        copy.start()
    tok_load = pltpu.make_async_copy(m["tok"], m["tok_v"], m["keep"].at[19])
    tok_load.start()
    small = m["small"][...].astype(F32)
    m["seg"][...] = jnp.broadcast_to(small[:, 512:640], (8, 128)).astype(jnp.int32)
    m["gains"][...] = jnp.concatenate(
        [small[:, 0:256], small[:, 256:512], jnp.zeros((14, 256), F32)], axis=0).astype(BF16)
    qg, kg = low_half(roll(small[:, 128:256], 64)), low_half(roll(small[:, 384:512], 64))
    greet(layer_mates() + z_mates())
    for copy in raw_q:
        copy.wait()
    tiles = [m["wq_raw"][:, 128 * i:128 * (i + 1)].astype(F32) for i in range(5)]
    low_lanes = lanes(tiles[0].shape) < HEAD_DIM
    half_of = lambda v, w: jnp.where(low_lanes, v, w).astype(BF16)
    q0, q1, q2, k_tile, v_tile = tiles
    m["wq"][0, :, 0:128] = q0.astype(BF16)
    m["wq"][0, :, 128:256] = half_of(q1, roll(k_tile, 64))
    m["wq"][0, :, 256:] = v_tile[:, 0:HEAD_DIM].astype(BF16)
    m["wq"][1, :, 0:128] = half_of(roll(q1, 64), roll(q2, 64))
    m["wq"][1, :, 128:256] = half_of(roll(q2, 64), k_tile)
    m["wq"][1, :, 256:] = roll(v_tile, 64)[:, 0:HEAD_DIM].astype(BF16)
    rows, width = m["tok"].shape
    quarter_o = m["wo"].shape[0] // 4
    own_rows = m["wqkv"].shape[0]
    half_cols = m["wgu"].shape[1] // 2
    piece = half_cols // 4
    part = piece // 2
    main = part // 128 * 128
    half_a = main // 2
    rows_a, rows_b, rest = half_a // 4, (part - half_a) // 4, part - main
    keep = m["keep"]
    own = 2 * z + x
    t_own = 2 * r + x

    def local_copy(k, src, dst):
        return pltpu.make_async_copy(src, dst, keep.at[k])

    hidden, dgu, wgu, wd_v = m["hidden"], m["dgu"], m["wgu_v"], m["wd_v"]
    cols_a = 2 * half_a
    cols_b = dgu.shape[1] - cols_a

    def raw(i):
        return dgu.at[pl.ds(i * own_rows, own_rows)]

    def pair(a, first, n):
        return dgu.at[pl.ds((2 + a) * own_rows, own_rows), pl.ds(first, n)]

    def loaded(k, src, dst):
        copy = local_copy(k, src, dst)
        copy.start()
        return copy

    tok = Gather(m["tok"], m["tok_all"], m["ga_s"], m["ga_r"], keep.at[0])
    cot = Gather(m["cot"], m["cot_v"], m["gb_s"], m["gb_r"], keep.at[1])
    segs = m["segs_v"]
    mates = layer_mates()

    def seg_copy(k):
        return remote(m["seg"], segs.at[z, t_own], m["sg_s"].at[k - 1], m["sg_r"].at[k - 1],
                      mates[k - 1])

    def gain_target(k):
        return device(base, y, c, (z + k // 2) % 4, (x + k) % 2)

    def gain_copy(k):
        return remote(m["gains"], m["gains_all"].at[own], m["gn_s"].at[k - 1],
                      m["gn_r"].at[k - 1], gain_target(k))

    wq = m["wq_v"]

    def wq_slot(zk, a):
        return wq.at[pl.ds((2 * zk + a) * own_rows, own_rows)]

    near = Along(m["wq"].at[x], lambda zk: wq_slot(zk, x), m["wa_s"], m["wa_r"])
    flip = Along(wq_slot(z, 1 - x), lambda zk: wq_slot(zk, 1 - x), m["wb_s"], m["wb_r"])
    over = remote(m["wq"].at[1 - x], wq_slot(z, x), m["wx_s"], m["wx_r"], to_x)
    over_in = remote(m["wq"].at[x], wq_slot(z, 1 - x), m["wx_s"], m["wx_r"], to_x)
    over.start()
    near.first()
    near.second()
    tok.start()
    for k in range(1, 8):
        seg_copy(k).start()
    local = [
        local_copy(2, m["wq"].at[x], wq_slot(z, x)),
        local_copy(3, m["gains"], m["gains_all"].at[own]),
        local_copy(4, m["seg"], segs.at[z, t_own]),
        local_copy(5, m["wgu"].at[:, pl.ds(piece * r, piece)], raw(0)),
        local_copy(6, m["wgu"].at[:, pl.ds(half_cols + piece * r, piece)], raw(1)),
    ]
    for copy in local:
        copy.start()
    for k in range(1, 8):
        gain_copy(k).start()
    out_q = Along(m["wo"].at[pl.ds(quarter_o * r, quarter_o)], lambda zk: m["zo"].at[zk],
                  m["wo_s"], m["wo_r"])
    last = r // 3
    tail_at = rest * x + half_a + rows_b * r + 16 - last * x * part
    quarters = [
        local_copy(7, m["wo"].at[pl.ds(quarter_o * r, quarter_o)], m["zo"].at[z]),
        local_copy(8, m["wd"].at[pl.ds(rest * x + rows_a * r, rows_a)], m["za"].at[z]),
        local_copy(13, m["wd"].at[pl.ds(rest * x + half_a + rows_b * r, 16)],
                   m["zb"].at[z, pl.ds(0, 16)]),
        local_copy(14, m["wd"].at[pl.ds(tail_at, rows_b - 16)],
                   m["zb"].at[z, pl.ds(16, rows_b - 16)]),
    ]
    for copy in quarters:
        copy.start()
    over_in.wait_recv()
    flip.first()
    flip.second()
    out_q.first()
    out_q.second()

    def seg_up(k):
        return remote(segs.at[z], segs.at[z], m["su_s"].at[k - 1], m["su_r"].at[z],
                      device(base, y, c, (z + k) % 4, x))

    for k in range(1, 8):
        seg_copy(k).wait_recv()
    local[2].wait()
    for k in range(3, 0, -1):
        pl.when(z + k < 4)(lambda k=k: seg_up(k).start())

    local[3].wait()
    local[4].wait()
    gate, up = raw(0), raw(1)
    for a in range(2):
        at = a * (piece - main)
        for i, src in enumerate((gate, up)):
            pair(a, i * half_a, half_a)[...] = src[:, at:at + half_a]
            pair(a, cols_a + i * half_a, half_a)[...] = src[:, at + half_a:at + main]
    g_tile = gate[:, main:main + 128].astype(F32)
    u_tile = up[:, main:main + 128].astype(F32)
    low = lanes(g_tile.shape) < HEAD_DIM
    pair(0, 2 * main, 128)[...] = jnp.where(low, g_tile, roll(u_tile, 64)).astype(BF16)
    pair(1, 2 * main, 128)[...] = jnp.where(low, roll(g_tile, 64), u_tile).astype(BF16)

    def unit(first, n):
        return lambda zk: wgu.at[pl.ds(2 * zk * own_rows, 2 * own_rows), pl.ds(first, n)]

    def crossing(first, n, ss, rs, k):
        cols = pl.ds(first, n)
        mine = wgu.at[pl.ds((2 * z + x) * own_rows, own_rows), cols]
        other = wgu.at[pl.ds((2 * z + 1 - x) * own_rows, own_rows), cols]
        return (remote(pair(1 - x, first, n), mine, ss, rs, to_x),
                remote(pair(x, first, n), other, ss, rs, to_x),
                local_copy(k, pair(x, first, n), mine))

    cross_a, cross_a_in, mine_a = crossing(0, cols_a, m["xa_s"], m["xa_r"], 5)
    cross_b, cross_b_in, mine_b = crossing(cols_a, cols_b, m["xb_s"], m["xb_r"], 6)
    gate_a = Chain(unit(0, cols_a), m["ca_s"], m["ca_r"])
    gate_b = Chain(unit(cols_a, cols_b), m["cb_s"], m["cb_r"])
    down_a = Chain(lambda zk: m["za"].at[zk], m["da_s"], m["da_r"])
    down_b = Chain(lambda zk: m["zb"].at[zk], m["db_s"], m["db_r"])
    m["rope"][...] = rope_table(2 * rows * z, 2 * rows)
    tok.forward()
    for copy in (cross_a, mine_a, cross_b, mine_b):
        copy.start()
    near.forward()
    flip.forward()
    out_q.forward()
    tok.finish()
    cot.start()
    near.finish()
    flip.finish()
    for k in range(1, 8):
        at = 2 * ((z + 4 - k // 2) % 4) + (x + k) % 2
        remote(m["gains"], m["gains_all"].at[at], m["gn_s"].at[k - 1], m["gn_r"].at[k - 1],
               to_c).wait_recv()
    for k in (0, 1):
        local[k].wait()
    gather_gains = pltpu.make_async_copy(m["gains_all"], m["gains_v"], keep.at[3])
    gather_gains.start()
    gather_gains.wait()
    gain_rows = []
    for i in range(2):
        gain_rows.append(jnp.concatenate(
            [m["gains_v"][k, 0:16].astype(F32)[i:i + 1, :own_rows] for k in range(8)], axis=1))
    m["g_one"][...], m["g_two"][...] = gain_rows
    kv = m["kv_v"]
    q_all, qkv_all = m["q_v"], m["qkv_v"]
    cos, sin = low_half(m["rope"][...]), low_half(roll(m["rope"][...], 64))
    span = 2 * rows

    def order(k):
        return (y + 1 + k) % 2, (c + 1 + k // 2) % 2

    def kv_copy(d, s):
        return remote(kv.at[z, s], kv.at[z, s], m["kv_s"].at[d - 1, s], m["kv_r"].at[z, s],
                      device(base, y, c, (z + d) % 4, x))

    def kv_arrival(zk, s):
        return remote(kv.at[zk, s], kv.at[zk, s], m["kv_s"].at[0, s], m["kv_r"].at[zk, s], to_x)

    def project(k, carry):
        b, e = order(k)
        s = 2 * b + e
        tokens = m["tok_all"][pl.ds(2 * s, 2)].reshape(span, width).astype(F32)
        normed = (tokens * inverse_rms(tokens) * m["g_one"][...]).astype(BF16)
        m["tok_all"][pl.ds(2 * s, 2)] = normed.reshape(2, rows, width)
        qkv = jnp.dot(normed, wq[...], preferred_element_type=F32)
        qkv_all[s] = qkv[:, 0:256]
        heads = split_heads(qkv[:, 0:128], qkv[:, 128:256])
        for j in range(GROUP):
            u = heads[j]
            u = rotated(u * head_inverse(u) * qg, cos, sin) * HEAD_DIM ** (-0.5)
            q_all[s, pl.ds(j * span, span)] = u.astype(BF16)
        u = heads[GROUP]
        u = rotated(u * head_inverse(u) * kg, cos, sin)
        v = jnp.concatenate([jnp.zeros((span, HEAD_DIM), F32), qkv[:, 256:320]], axis=1)
        kv[z, s] = (u + v).astype(BF16)
        for d in (3, 2, 1):
            pl.when(z + d < 4)(lambda d=d: kv_copy(d, s).start())
        return carry

    lax.fori_loop(0, 4, project, 0)
    for copy in quarters[1:]:
        copy.wait()
    down_a.start_ends()
    down_a.start_inner()
    for copy in (mine_a, mine_b):
        copy.wait()
    cross_a_in.wait_recv()
    gate_a.start_ends()
    gate_a.start_inner()
    cross_b_in.wait_recv()
    down_b.start_ends()
    gate_b.start_ends()
    cot.forward()

    def hand(k, zk, src, dst, sems, n):
        ss, rs = sems
        to = device(base, zk // 2, zk % 2, z, x)
        pl.when(r != zk)(lambda: remote(src.at[zk], dst.at[pl.ds(n * r, n)], ss.at[zk],
                                        rs.at[r], to).start())

        @pl.when(r == zk)
        def _():
            copy = local_copy(k, src.at[zk], dst.at[pl.ds(n * r, n)])
            copy.start()
            copy.wait()

    def handed(src, dst, sems, n):
        ss, rs = sems
        for rk in range(4):
            ref = dst.at[pl.ds(n * rk, n)]
            pl.when(r != rk)(lambda ref=ref, rk=rk: remote(
                src.at[0], ref, ss.at[0], rs.at[rk], to_x).wait_recv())

    def hand_sent(src, dst, sems, n):
        ss, rs = sems
        for zk in range(4):
            pl.when(r != zk)(lambda zk=zk: remote(
                src.at[zk], dst.at[pl.ds(0, n)], ss.at[zk], rs.at[0], to_x).wait_send())

    quarters[0].wait()
    out_q.finish()
    out_sems = (m["ho_s"], m["ho_r"])
    a_sems, b_sems = (m["hd_s"], m["hd_r"]), (m["hb_s"], m["hb_r"])
    for zk in range(4):
        hand(13, zk, m["zo"], m["wo_v"], out_sems, quarter_o)

    for k in range(1, 4):
        pl.when(z - k >= 0)(lambda k=k: remote(
            segs.at[0], segs.at[(z + 4 - k) % 4], m["su_s"].at[k - 1],
            m["su_r"].at[(z + 4 - k) % 4], to_x).wait_recv())

    summed = SeqSum(m["part"], [m[n] for n in SUM_NAMES])
    inv_all, att = m["inv_v"], m["att_v"]
    acc, q_seg = m["acc"], m["q_seg"]

    def attend_one(k, carry):
        b, e = order(k)
        s = 2 * b + e
        q_seg[...] = segment_columns(segs, z, s)

        def block(zk, diagonal):
            tile = kv[zk, s]
            p = exp_scores(q_all[s], tile, q_seg[...], segment_row(segs, zk, s), diagonal)
            ones = jnp.where(lanes(tile.shape) < HEAD_DIM, 1.0, tile.astype(F32)).astype(BF16)
            add = jnp.dot(p.astype(BF16), ones, preferred_element_type=F32)
            if diagonal:
                acc[...] = add
            else:
                acc[...] += add

        block(z, True)

        def step(i, inner):
            zk = z - 1 - i
            kv_arrival(zk, s).wait_recv()
            block(zk, False)
            return inner

        lax.fori_loop(0, z, step, 0)
        total = acc[...]
        inv = 1.0 / jnp.where(lanes(total.shape) < HEAD_DIM, total, 1.0)
        inv = jnp.where(lanes(total.shape) < HEAD_DIM, inv, roll(inv, 64))
        o = high_half(total * inv)
        lane = lanes((span, 128))
        inv_all[s] = jnp.where(lane < 32, inv[0:span], jnp.where(
            lane < 64, inv[span:2 * span], inv[2 * span:]))
        first, second, third = o[0:span], o[span:2 * span], o[2 * span:]
        att[s, :, 0:128] = (roll(first, 64) + second).astype(BF16)
        att[s, :, 128:192] = roll(third, 64)[:, 0:HEAD_DIM].astype(BF16)
        pl.when(k == 0)(lambda: handed(m["zo"], m["wo_v"], out_sems, quarter_o))
        out = jnp.dot(att[s], m["wo_v"][...], preferred_element_type=F32).astype(BF16)
        m["part"][pl.ds(2 * s, 2)] = out.reshape(2, rows, width)
        pl.when(k < 2)(lambda: summed.give(b))
        pl.when(k == 2)(summed.take_far)
        pl.when(k == 3)(summed.take_near)
        return carry

    lax.fori_loop(0, 4, attend_one, 0)
    down_a.second()
    gate_a.second()
    summed.middle()
    down_a.third()
    summed.finish()
    tok_load.wait()
    mid = m["tok_v"][...].astype(F32) + summed.out[...]
    m["mid"][...] = mid
    m["low"][...] = (mid * inverse_rms(mid) * m["g_two"][...]).astype(BF16)
    n2_all, cot_all = m["n2_v"], m["cot_v"]
    n2 = Gather(m["low"], n2_all, m["gc_s"], m["gc_r"], keep.at[20])
    n2.start()
    cot.finish()
    gate_a.third()
    down_b.pass_ends()
    gate_b.pass_ends()
    down_b.start_inner()
    gate_b.start_inner()
    n2.forward()
    down_a.finish()
    wda, wdb = wd_v.at[pl.ds(0, half_a)], wd_v.at[pl.ds(half_a, part - half_a)]
    for zk in range(4):
        hand(13, zk, m["za"], wda, a_sems, rows_a)
    n2.finish()
    gate_a.finish()
    handed(m["za"], wda, a_sems, rows_a)
    cross_a.wait_send()
    cross_b.wait_send()

    down_b.third()
    gate_b.third()

    def feed_first(s, carry):
        at = pl.ds(pl.multiple_of(s * span, span), span)
        gu = jnp.dot(n2_all[pl.ds(2 * s, 2)].reshape(span, width), wgu[:, :cols_a],
                     preferred_element_type=F32)
        dh = last_dims(cot_all[pl.ds(2 * s, 2)].reshape(span, width), wd_v[0:half_a])
        hidden[at, 0:half_a], dgu[at, 0:half_a], dgu[at, half_a:cols_a] = swiglu(
            gu[:, :half_a], gu[:, half_a:], dh)
        out = last_dims(dgu[at, 0:cols_a], wgu[:, :cols_a]).astype(BF16)
        m["part"][pl.ds(2 * s, 2)] = out.reshape(2, rows, width)
        return carry

    summed.given()
    lax.fori_loop(0, 4, feed_first, 0)
    down_b.pass_inner()
    gate_b.pass_inner()
    block_rows = 2 * own_rows
    gga, gdo, got_a = m["gga"], m["gdo"], m["got_a"]
    gate_sum = ChainSum(lambda zk: gga.at[zk], lambda at: m["gga_slot"].at[at], m["ys_s"],
                        m["ys_r"])
    down_sum = ChainSum(lambda zk: got_a.at[zk], lambda at: m["gda_slot"].at[at], m["yd_s"],
                        m["yd_r"])

    def grad_gate(zk, carry):
        cols = pl.ds(pl.multiple_of(zk * block_rows, 128), block_rows)
        left = n2_all[:, :, cols].reshape(8 * rows, block_rows)
        gga[zk] = first_dims(left, dgu[:, :cols_a]).astype(BF16)
        return carry

    lax.fori_loop(0, 4, grad_gate, 0)
    gate_sum.start()
    for j in range(0, half_a, 128):
        grad = first_dims(hidden[:, j:j + 128], cot_all[...].reshape(8 * rows, width))
        for h in range(128 // rows_a):
            gdo[j // rows_a + h, 0:rows_a] = grad[rows_a * h:rows_a * (h + 1)].astype(BF16)

    def spread_from(i):
        return gdo.at[i, pl.ds(0, rows_a)]

    def spread(i):
        return remote(spread_from(i), got_a.at[r], m["ha_s"].at[i], m["ha_r"].at[r],
                      device(base, i // 2, i % 2, z, x))

    for i in range(4):
        pl.when(r != i)(lambda i=i: spread(i).start())
    got_a[r] = gdo[r, 0:rows_a]

    def add(block, slot):
        block[...] = (block[...].astype(F32) + slot[...].astype(F32)).astype(BF16)

    gate_sum.first_hop(add)
    for i in range(4):
        pl.when(r != i)(lambda i=i: remote(
            spread_from(i), got_a.at[i], m["ha_s"].at[i], m["ha_r"].at[i], to_c).wait_recv())
    down_sum.start()
    down_b.finish()
    for zk in range(4):
        hand(13, zk, m["zb"], wdb, b_sems, rows_b)
    gate_b.finish()
    gate_sum.second_hop(add)
    handed(m["zb"], wdb, b_sems, rows_b)
    summed.passed()

    def total_in(block):
        def total(slots):
            value = block[...].astype(F32)
            for slot in slots:
                value = value + slot[...].astype(F32)
            block[...] = value.astype(BF16)
        return total

    parts, n2, cot_v, normed = m["part"], m["n2_v"], m["cot_v"], m["tok_all"]
    wd_v[pl.ds(part, 128 - rest)] = jnp.zeros((128 - rest, width), BF16)

    def feed(k, carry):
        b, e = order(k)
        s = 2 * b + e
        at = pl.ds(pl.multiple_of(s * span, span), span)
        gu = jnp.dot(n2[pl.ds(2 * s, 2)].reshape(span, width), wgu[:, cols_a:],
                     preferred_element_type=F32)
        dh = last_dims(cot_v[pl.ds(2 * s, 2)].reshape(span, width), wd_v[half_a:])
        (hidden[at, half_a:2 * half_a], dgu[at, cols_a:cols_a + half_a],
         dgu[at, cols_a + half_a:cols_a + 2 * half_a]) = swiglu(
            gu[:, :half_a], gu[:, half_a:2 * half_a], dh[:, :half_a])
        tile = gu[:, 2 * half_a:]
        gate, up, grad = low_half(tile), low_half(roll(tile, 64)), dh[:, half_a:]
        sigma = 1.0 / (1.0 + jnp.exp(-gate))
        active = gate * sigma
        hidden[at, 2 * half_a:] = (active * up).astype(BF16)
        d_gate = grad * up * sigma * (1.0 + gate * (1.0 - sigma))
        dgu[at, cols_a + 2 * half_a:] = (
            d_gate + roll(low_half(grad * active), 64)).astype(BF16)
        out = last_dims(dgu[at, cols_a:], wgu[:, cols_a:])
        out = out + parts[pl.ds(2 * s, 2)].reshape(span, width).astype(F32)
        parts[pl.ds(2 * s, 2)] = out.astype(BF16).reshape(2, rows, width)
        pl.when(k < 2)(lambda: summed.give(b))
        pl.when(k == 2)(summed.take_far)
        pl.when(k == 3)(summed.take_near)
        return carry

    lax.fori_loop(0, 4, feed, 0)
    down_sum.first_hop(add)

    ggu = m["ggu"]
    gu_sum = ChainSum(lambda zk: ggu.at[zk], lambda at: m["gu_slot"].at[at], m["zg_s"], m["zg_r"])

    def farthest(i):
        up = z // 2
        return up * i + (1 - up) * (3 - i)

    def grad_gu(i, carry):
        zk = farthest(i)
        cols = pl.ds(pl.multiple_of(zk * block_rows, 128), block_rows)
        left = n2[:, :, cols].reshape(8 * rows, block_rows)
        ggu[zk] = first_dims(left, dgu[:, cols_a:]).astype(BF16)
        pl.when(i < 2)(lambda: gu_sum.start_one(zk))
        return carry

    lax.fori_loop(0, 2, grad_gu, 0)
    summed.middle()
    lax.fori_loop(2, 4, grad_gu, 0)
    down_sum.second_hop(add)
    summed.finish()

    v = m["mid"][...]
    dv, gain_grad = norm_back(summed.out[...], v, inverse_rms(v), m["g_two"][...])
    m["row_two"][...] = gain_grad
    dmid = cot_v[t_own].astype(F32) + dv
    m["dmid"][...] = dmid
    m["low"][...] = dmid.astype(BF16)
    branch = Gather(m["low"], m["db"], m["gd_s"], m["gd_r"], keep.at[12])
    branch.start()
    gu_sum.first_hop(add, (0,))

    got = m["got"]
    quarter_d = rows_b
    for i in range(4):
        pl.when(r != i)(lambda i=i: spread(i).wait_send())
    for j in range(0, half_a + 128, 128):
        at = half_a + j
        grad = first_dims(hidden[:, at:at + 128], cot_v[...].reshape(8 * rows, width))
        grad = grad.astype(BF16)
        for i in range(4):
            lo, hi = max(j, quarter_d * i), min(j + 128, quarter_d * (i + 1))
            if lo < hi:
                gdo[i, lo - quarter_d * i:hi - quarter_d * i] = grad[lo - j:hi - j]

    summed.sent()

    def down(s, carry):
        at = pl.ds(pl.multiple_of(s * span, span), span)
        out = jnp.dot(hidden[at], wd_v[...], preferred_element_type=F32)
        parts[pl.ds(2 * s, 2)] = out.astype(BF16).reshape(2, rows, width)
        return carry

    lax.fori_loop(0, 4, down, 0)
    mixed = SeqSum(parts, [m[n] for n in SUM_NAMES], by_x=True)

    def give(i, lo, n, ss, rs):
        return remote(gdo.at[i, pl.ds(lo, n)], got.at[r, pl.ds(lo, n)], ss.at[i], rs.at[r],
                      device(base, i // 2, i % 2, z, x))

    def give_all(lo, n, ss, rs):
        for i in range(4):
            pl.when(r != i)(lambda i=i: give(i, lo, n, ss, rs).start())
        got[r, lo:lo + n] = gdo[r, lo:lo + n]

    def given(lo, n, ss, rs):
        for i in range(4):
            pl.when(r != i)(lambda i=i: remote(
                gdo.at[i, pl.ds(lo, n)], got.at[i, pl.ds(lo, n)], ss.at[i], rs.at[i],
                to_c).wait_recv())

    def give_sent(lo, n, ss, rs):
        for i in range(4):
            pl.when(r != i)(lambda i=i: give(i, lo, n, ss, rs).wait_send())

    def swap(src, out, ss, rs):
        return remote(src.at[pl.ds(own_rows * (1 - x), own_rows)], out.at[t_own], ss, rs, to_x)

    def keep_own(k, src, out):
        copy = pltpu.make_async_copy(src.at[pl.ds(own_rows * x, own_rows)], out.at[t_own],
                                     keep.at[k])
        copy.start()
        return copy

    def swapped(src, out, ss, rs):
        return remote(src.at[pl.ds(own_rows * x, own_rows)], out.at[2 * r + 1 - x], ss, rs, to_x)

    def pairs(out):
        return lambda i: out.at[pl.ds(2 * i, 2)]

    ga_out, gb_out, qkv_out = m["ga_g"], m["gb_g"], m["qkv_g"]
    ga_swap = swap(gga.at[z], ga_out, m["xs_s"], m["xs_r"])
    ga_keep = local_copy(14, gga.at[z, pl.ds(own_rows * x, own_rows)], ga_out.at[t_own])
    da_keep = local_copy(15, got_a.at[z], m["da_g"].at[r])
    ga_share = RepShare(pairs(ga_out), m["ra_s"], m["ra_r"])
    da_share = RepShare(lambda i: m["da_g"].at[i], m["rc_s"], m["rc_r"])

    def swap_first():
        gate_sum.collect(total_in(gga.at[z]))
        down_sum.collect(total_in(got_a.at[z]))
        for copy in (ga_swap, ga_keep, da_keep):
            copy.start()

    branch.forward()
    branch.arrive(2)
    branch.keep.wait()
    give_all(0, quarter_d, m["he_s"], m["he_r"])
    mixed.give(0)
    mixed.give(1)
    swap_first()
    gu_sum.first_hop(add, (1,))

    wo, qkv, dkv = m["wo_v"], qkv_all, kv
    db, dqkv, do_v = m["db"], m["dqkv"], m["do"]
    own_kv = m["own_kv"]
    m["row_head"][...] = jnp.zeros((1, 128), F32)

    down_rest = ChainSum(lambda zk: got.at[zk, pl.ds(0, quarter_d)],
                         lambda at: m["down_slot"].at[at], m["zd_s"], m["zd_r"])

    def share_first():
        ga_keep.wait()
        da_keep.wait()
        swapped(gga.at[z], ga_out, m["xs_s"], m["xs_r"]).wait_recv()
        ga_share.start()
        da_share.start()

    def order_back(k):
        return (y + k // 2) % 2, (c + 1 + k) % 2

    kv_slot = m["kv_slot"]

    def kv_down(zk, s):
        return remote(dkv.at[zk, s], kv_slot.at[zk, s], m["zk_s"].at[zk, s], m["zk_r"].at[zk, s],
                      device(base, y, c, (z + 3) % 4, x))

    def kv_merge(k):
        b, e = order_back(k)
        s = 2 * b + e

        def one(zk, inner):
            kv_down(zk, s).wait_recv()
            dkv[zk, s] = (dkv[zk, s].astype(F32) + kv_slot[zk, s].astype(F32)).astype(BF16)
            kv_down(zk, s).start()
            return inner

        @pl.when((z == 1) | (z == 2))
        def _():
            lax.fori_loop(0, z, one, 0)

    def attend_back(k, carry):
        pl.when(k == 0)(lambda: branch.arrive(4))
        pl.when(k == 1)(branch.cross)
        pl.when(k == 2)(lambda: [branch.arrive(6), branch.arrive(7)] and None)
        b, e = order_back(k)
        s = 2 * b + e
        grads = db[pl.ds(2 * s, 2)].reshape(span, width)
        d_att = last_dims(grads, wo[...])
        first = d_att[:, 0:128]
        third = jnp.concatenate([jnp.zeros((span, HEAD_DIM), F32), d_att[:, 128:192]], axis=1)
        d_out = [high_half(roll(first, 64)), high_half(first), third]
        att_a = att[s, :, 0:128].astype(F32)
        att_b = att[s, :, 128:192].astype(F32)
        att_b = jnp.concatenate([jnp.zeros((span, HEAD_DIM), F32), att_b], axis=1)
        deltas = []
        for j, o in enumerate((roll(att_a, 64), att_a, att_b)):
            inv = inv_all[s][:, 32 * j:32 * j + 1]
            part_j = (d_out[j].astype(BF16).astype(F32) * inv).astype(BF16)
            do_v[pl.ds(j * span, span)] = part_j
            deltas.append(jnp.sum(part_j.astype(F32) * o, axis=1, keepdims=True))
        delta = jnp.concatenate(deltas, axis=0)
        m["q_t"][...] = jnp.transpose(q_all[s].astype(F32)).astype(BF16)
        m["do_t"][...] = jnp.transpose(do_v[...].astype(F32)).astype(BF16)
        q_seg[...] = segment_columns(segs, z, s)
        acc[...] = jnp.zeros_like(acc)

        def block(zk, diagonal):
            tile = kv[zk, s]
            q = q_all[s]
            d_out = do_v[...]
            p = exp_scores(q, tile, q_seg[...], segment_row(segs, zk, s), diagonal)
            ds = (p * (last_dims(d_out, tile) - delta)).astype(BF16)
            acc[...] += jnp.dot(ds, tile, preferred_element_type=F32)
            both = jnp.dot(m["q_t"][...], ds, preferred_element_type=F32)
            both = both + jnp.dot(m["do_t"][...], p.astype(BF16), preferred_element_type=F32)
            return jnp.transpose(both)

        def step(zk, inner):
            dkv[zk, s] = block(zk, False).astype(BF16)
            pl.when(z == 3)(lambda: kv_down(zk, s).start())
            return inner

        lax.fori_loop(0, z, step, 0)
        own_kv[s] = block(z, True)
        tiles = split_heads(qkv[s, :, 0:128], qkv[s, :, 128:256])
        back = []
        for j in range(GROUP):
            dy = rotated(low_half(acc[pl.ds(j * span, span)]) * HEAD_DIM ** (-0.5), cos, -sin)
            raw, gain_part = head_back(dy, tiles[j], qg)
            m["row_head"][...] += gain_part
            back.append(raw)
        dqkv[s, :, 0:128] = (back[0] + roll(back[1], 64)).astype(BF16)
        dqkv[s, :, 128:256] = back[2].astype(BF16)
        pl.when(k >= 1)(lambda: kv_merge(k - 1))
        pl.when(k == 0)(lambda: gu_sum.second_hop(add))
        pl.when(k == 0)(mixed.take_far)
        pl.when(k == 0)(mixed.take_near)
        pl.when(k == 1)(share_first)
        pl.when(k == 3)(mixed.middle)
        pl.when(k == 3)(lambda: given(0, quarter_d, m["he_s"], m["he_r"]))
        return carry

    lax.fori_loop(0, 4, attend_back, 0)
    kv_merge(3)
    gu_sum.start_one(farthest(2))
    down_rest.start()
    inputs = SeqSum(parts, [m[n] for n in SUM_NAMES], by_x=True)

    def finish_one(k, carry):
        b, e = (y + (k + 1) // 2) % 2, (c + 1 + k // 2) % 2
        s = 2 * b + e
        @pl.when(z < 3)
        def _():
            kv_down(z, s).wait_recv()
            own_kv[s] += kv_slot[z, s].astype(F32)

        total = own_kv[s]
        u = split_heads(qkv[s, :, 0:128], qkv[s, :, 128:256])[GROUP]
        dy = rotated(low_half(total), cos, -sin)
        raw, gain_part = head_back(dy, u, kg)
        m["row_head"][...] += roll(gain_part, 64)
        tile = dqkv[s, :, 128:256].astype(F32)
        dqkv[s, :, 128:256] = (low_half(tile) + roll(raw, 64)).astype(BF16)
        dqkv[s, :, 256:320] = roll(total, 64)[:, 0:HEAD_DIM].astype(BF16)
        return carry

    lax.fori_loop(0, 4, finish_one, 0)
    gqkv = m["gqkv"]
    qkv_sum = Direct(lambda zk: gqkv.at[zk], lambda zk: m["qkv_slot"].at[zk], m["zq_s"],
                     m["zq_r"])

    def grad_qkv(i, carry):
        zk = farthest(i)
        cols = pl.ds(pl.multiple_of(zk * block_rows, 128), block_rows)
        left = normed[:, :, cols].reshape(8 * rows, block_rows)
        gqkv[zk] = first_dims(left, dqkv[...].reshape(8 * rows, HEAD_COLS)).astype(BF16)
        qkv_sum.start(zk)
        return carry

    lax.fori_loop(0, 4, grad_qkv, 0)

    for j in range(0, width, 512):
        cols = slice(j, j + 512)
        grad = first_dims(att[...].reshape(8 * rows, Q_COLS),
                          db[:, :, cols].reshape(8 * rows, 512)).astype(BF16)
        for i in range(4):
            gdo[i, quarter_d:quarter_d + quarter_o, cols] = grad[quarter_o * i:quarter_o * (i + 1)]
    give_all(quarter_d, quarter_o, m["hf_s"], m["hf_r"])
    mixed.given()

    def back_in(s, carry):
        out = last_dims(dqkv[s], wq[...]).astype(BF16)
        parts[pl.ds(2 * s, 2)] = out.reshape(2, rows, width)
        return carry

    lax.fori_loop(0, 4, back_in, 0)
    gu_sum.collect(total_in(ggu.at[z]))
    gb_swap = swap(ggu.at[z], gb_out, m["xg_s"], m["xg_r"])
    gb_swap.start()
    gb_keep = keep_own(14, ggu.at[z], gb_out)
    mixed.finish()
    branch.sent()
    m["low"][...] = (m["mid"][...] + mixed.out[...]).astype(BF16)
    mixed_out = loaded(17, m["low"], m["mixed"])
    mixed.passed()
    free = m["free"]
    for to in (to_c, to_x, to_y):
        pl.semaphore_signal(free, inc=1, device_id=to, device_id_type=MESH)

    pl.semaphore_wait(free, 3)
    inputs.give(0)
    inputs.give(1)
    inputs.take_far()
    inputs.take_near()
    gb_keep.wait()
    swapped(ggu.at[z], gb_out, m["xg_s"], m["xg_r"]).wait_recv()
    gb_share = RepShare(pairs(gb_out), m["rg_s"], m["rg_r"])
    gb_share.start()
    down_rest.first_hop(add)
    inputs.middle()
    down_rest.second_hop(add, (1,))
    given(quarter_d, quarter_o, m["hf_s"], m["hf_r"])
    out_sum = Direct(lambda zk: got.at[zk, pl.ds(quarter_d, quarter_o)],
                     lambda zk: m["out_slot"].at[zk], m["zo_s"], m["zo_r"])

    def start_out(i, carry):
        out_sum.start(farthest(i))
        return carry

    lax.fori_loop(0, 4, start_out, 0)
    ga_share.forward()
    da_share.forward()

    inputs.finish()
    v = m["tok_v"][...].astype(F32)
    dv, gain_grad = norm_back(inputs.out[...], v, inverse_rms(v), m["g_one"][...])
    m["dmid"][...] += dv
    grad_out = loaded(18, m["dmid"], m["input_grad"])

    def gain_rows_of(k):
        return m["mid"].at[pl.ds(8 * k, 8)]

    gains_own = gain_rows_of(0)
    gains_own[0:1] = gain_grad
    gains_own[1:2] = m["row_two"][...]
    gains_own[2:3, 0:128] = m["row_head"][...]

    def gain_sum(k):
        return remote(gains_own, gain_rows_of(k), m["gm_s"].at[k - 1], m["gm_r"].at[k - 1],
                      mates[k - 1])

    for k in range(1, 8):
        gain_sum(k).start()

    down_rest.second_hop(add, (2,))

    total = gqkv[z].astype(F32)
    for term in qkv_sum.take():
        total = total + term
    gqkv[z] = total.astype(BF16)
    qkv_swap = swap(gqkv.at[z], qkv_out, m["xq_s"], m["xq_r"])
    qkv_swap.start()
    qkv_keep = keep_own(16, gqkv.at[z], qkv_out)
    qkv_share = RepShare(pairs(qkv_out), m["rq_s"], m["rq_r"])

    down_rest.collect(total_in(got.at[z, pl.ds(0, quarter_d)]))
    db_keep = loaded(15, got.at[z, pl.ds(0, quarter_d)], m["db_g"].at[r])
    db_keep.wait()
    db_share = RepShare(lambda i: m["db_g"].at[i], m["rd_s"], m["rd_r"])
    db_share.start()
    for k in range(1, 8):
        gain_sum(k).wait_recv()
    total = gains_own[...]
    for k in range(1, 8):
        total = total + gain_rows_of(k)[...]
    z_rows = m["z_rows"]
    z_rows[0] = total

    def gain_z(k):
        return remote(z_rows.at[0], z_rows.at[k], m["gz_s"].at[k - 1], m["gz_r"].at[k - 1],
                      device(base, y, c, (z + k) % 4, x))

    for k in range(1, 4):
        gain_z(k).start()
    gb_share.forward()
    qkv_keep.wait()
    swapped(gqkv.at[z], qkv_out, m["xq_s"], m["xq_r"]).wait_recv()
    qkv_share.start()
    out_own = got.at[z, pl.ds(quarter_d, quarter_o)]
    total = out_own[...].astype(F32)
    for term in out_sum.take():
        total = total + term
    out_own[...] = total.astype(BF16)
    out_keep = loaded(0, out_own, m["out_g"].at[r])
    out_keep.wait()
    out_share = RepShare(lambda i: m["out_g"].at[i], m["re_s"], m["re_r"])
    out_share.start()
    db_share.forward()
    for k in range(1, 4):
        gain_z(k).wait_recv()
    m["gains_g"][...] = z_rows[0] + z_rows[1] + z_rows[2] + z_rows[3]
    qkv_share.forward()
    out_share.forward()
    shares = (ga_share, da_share, gb_share, db_share, out_share, qkv_share)
    for share in shares:
        share.finish()

    for share in shares:
        share.sent()
    for copy in (ga_swap, gb_swap, qkv_swap):
        copy.wait_send()
    for k in range(1, 8):
        gain_sum(k).wait_send()
    for k in range(1, 4):
        gain_z(k).wait_send()
    mixed_out.wait()
    grad_out.wait()
    for flow in (gu_sum, down_rest, qkv_sum, out_sum, inputs):
        flow.sent()
    give_sent(0, quarter_d, m["he_s"], m["he_r"])
    give_sent(quarter_d, quarter_o, m["hf_s"], m["hf_r"])

    def dkv_sent(s, carry):
        for zk in range(3):
            pl.when(z > zk)(lambda zk=zk: kv_down(zk, s).wait_send())
        return carry

    lax.fori_loop(0, 4, dkv_sent, 0)
    for flow in (near, flip, out_q, gate_a, gate_b, down_a, down_b, gate_sum, down_sum):
        flow.sent()
    over.wait_send()
    for k in range(1, 8):
        seg_copy(k).wait_send()
        gain_copy(k).wait_send()
    for k in range(1, 4):
        pl.when(z + k < 4)(lambda k=k: seg_up(k).wait_send())

    def kv_sent(s, carry):
        for d in (1, 2, 3):
            pl.when(z + d < 4)(lambda d=d: kv_copy(d, s).wait_send())
        return carry

    lax.fori_loop(0, 4, kv_sent, 0)
    hand_sent(m["zo"], m["wo_v"], out_sems, quarter_o)
    hand_sent(m["za"], wda, a_sems, rows_a)
    hand_sent(m["zb"], wdb, b_sems, rows_b)


SUM_NAMES = ("r1", "chip", "rx", "mine", "late", "sum_out", "sum_s", "sum_r")
IN = ("tok", "cot", "small", "wqkv", "wgu", "wd", "wo")
OUT = ("mixed", "input_grad", "gains_g", "ga_g", "gb_g", "da_g", "db_g", "out_g", "qkv_g",
       "zo", "za", "zb", "gains_all")


def block_call(*args):
    shape = jax.ShapeDtypeStruct
    tok, _, _, wqkv, wgu, wd, wo = args[:7]
    rows, width = tok.shape
    span = 2 * rows
    own_rows = wqkv.shape[0]
    seg, gains = shape((8, rows), jnp.int32), shape((16, 256), BF16)
    part = wgu.shape[1] // 16
    half_a = part // 256 * 128
    part_b = part - half_a
    cols_a, cols_b = 2 * half_a, 2 * half_a + 128
    quarter_a, quarter_d, quarter_o = half_a // 4, part_b // 4, own_rows // 4
    heads = GROUP * span
    outs = {
        "mixed": shape((rows, width), BF16),
        "input_grad": shape((rows, width), F32),
        "gains_g": shape((8, width), F32),
        "ga_g": shape((8, own_rows, cols_a), BF16),
        "gb_g": shape((8, own_rows, cols_b), BF16),
        "da_g": shape((4, quarter_a, width), BF16),
        "db_g": shape((4, quarter_d, width), BF16),
        "out_g": shape((4, quarter_o, width), BF16),
        "qkv_g": shape((8, own_rows, HEAD_COLS), BF16),
        "zo": shape((4, quarter_o, width), BF16),
        "za": shape((4, quarter_a, width), BF16),
        "zb": shape((4, quarter_d, width), BF16),
        "gains_all": shape((8,) + gains.shape, BF16),
    }
    buffers = {
        "tok_all": ((8, rows, width), BF16), "cot_v": ((8, rows, width), BF16),
        "n2_v": ((8, rows, width), BF16), "db": ((8, rows, width), BF16),
        "part": ((8, rows, width), BF16),
        "tok_v": (tok.shape, BF16), "rope": ((span, 128), F32), "seg": (seg.shape, seg.dtype), "gains": (gains.shape, BF16),
        "wq": ((2, own_rows, HEAD_COLS), BF16), "wq_raw": ((own_rows, 640), BF16),
        "segs_v": ((4, 8) + seg.shape, seg.dtype), "gains_v": ((8,) + gains.shape, BF16),
        "wq_v": ((width, HEAD_COLS), BF16), "wo_v": ((Q_COLS, width), BF16),
        "wgu_v": ((width, cols_a + cols_b), BF16), "wd_v": ((2 * half_a + 128, width), BF16),
        "hidden": ((8 * rows, 2 * half_a + 128), BF16),
        "dgu": ((8 * rows, cols_a + cols_b), BF16),
        "qkv_v": ((4, span, 256), F32), "q_v": ((4, heads, 128), BF16),
        "kv_v": ((4, 4, span, 128), BF16), "kv_slot": ((3, 4, span, 128), BF16),
        "own_kv": ((4, span, 128), F32), "inv_v": ((4, span, 128), F32),
        "att_v": ((4, span, Q_COLS), BF16), "acc": ((heads, 128), F32),
        "do": ((heads, 128), BF16), "q_t": ((128, heads), BF16), "do_t": ((128, heads), BF16), "q_seg": ((span, span), jnp.int32),
        "dqkv": ((4, span, HEAD_COLS), BF16),
        "mid": ((rows, width), F32), "dmid": ((rows, width), F32), "low": ((rows, width), BF16),
        "g_one": ((1, width), F32), "g_two": ((1, width), F32),
        "gga": ((4, 2 * own_rows, cols_a), BF16), "gga_slot": ((5, 2 * own_rows, cols_a), BF16),
        "ggu": ((4, 2 * own_rows, cols_b), BF16), "gu_slot": ((5, 2 * own_rows, cols_b), BF16),
        "got_a": ((4, quarter_a, width), BF16),
        "gda_slot": ((5, quarter_a, width), BF16),
        "gdo": ((4, quarter_d + quarter_o, width), BF16),
        "got": ((4, quarter_d + quarter_o, width), BF16),
        "down_slot": ((5, quarter_d, width), BF16),
        "out_slot": ((4, quarter_o, width), BF16),
        "gqkv": ((4, 2 * own_rows, HEAD_COLS), BF16),
        "qkv_slot": ((4, 2 * own_rows, HEAD_COLS), BF16),
        "row_two": ((1, width), F32), "row_head": ((1, 128), F32),
        "z_rows": ((4, 8, width), F32),
    }
    counts = {
        "ga": (8, 8), "gb": (8, 8), "gc": (8, 8), "gd": (8, 8), "sg": (7, 7), "gn": (7, 7),
        "gm": (7, 7), "gz": (3, 3), "wa": (6, 4), "wb": (6, 4), "wo": (6, 4), "wx": (1, 1),
        "xa": (1, 1), "xb": (1, 1), "xs": (1, 1), "xg": (1, 1), "ca": (5, 4), "cb": (5, 4),
        "da": (5, 4), "db": (5, 4), "ys": (4, 5), "yd": (4, 5), "zg": (4, 5), "zd": (4, 5),
        "zo": (4, 4), "zq": (4, 4), "xq": (1, 1), "zk": ((3, 4), (3, 4)), "kv": ((3, 4), (4, 4)),
        "su": (3, 4), "ha": (4, 4), "hb": (4, 4), "hd": (4, 4), "he": (4, 4), "hf": (4, 4),
        "ho": (4, 4), "ra": (3, 3), "rc": (3, 3), "rd": (3, 3), "re": (3, 3), "rg": (3, 3),
        "rq": (3, 3),
    }
    sem = pltpu.SemaphoreType.DMA
    many = lambda n: sem if n == 1 else sem(n if isinstance(n, tuple) else (n,))
    sems = {"keep": dma(21), "free": pltpu.SemaphoreType.REGULAR}
    for n, (send, recv) in counts.items():
        sems[n + "_s"], sems[n + "_r"] = many(send), many(recv)
    scratch = {n: pltpu.VMEM(*v) for n, v in buffers.items()}
    scratch.update(zip(SUM_NAMES, seq_scratch(width)))
    names = IN + OUT + tuple(scratch) + tuple(sems)
    got = pl.pallas_call(
        functools.partial(block_kernel, names),
        name="block",
        out_shape=tuple(outs[n] for n in OUT),
        in_specs=[ANY if n in ("tok", "cot", "wqkv", "wgu", "wd", "wo") else VMEM for n in IN],
        out_specs=tuple(VMEM if n == "gains_g" else ANY for n in OUT),
        scratch_shapes=list(scratch.values()) + list(sems.values()),
        compiler_params=params(0, 63),
    )(*args)
    return dict(zip(OUT, got))


def order_kernel(names, *refs):
    m = dict(zip(names, refs))
    half_a = m["ga"].shape[2] // 2
    half_b = (m["gb"].shape[2] - 128) // 2
    main = half_a + half_b
    cols = 2 * main + 128
    own_rows = m["ga"].shape[1]
    low = lanes((own_rows, 128)) < HEAD_DIM
    x = lax.axis_index("grp") % 2

    def fetch(k, src, dst):
        copy = pltpu.make_async_copy(src, dst, m["load"].at[k])
        copy.start()
        return copy

    def store(k, src, dst):
        copy = pltpu.make_async_copy(src, dst, m["save"].at[k])
        copy.start()
        return copy

    ga, gb = m["ga_v"], m["gb_v"]
    pair = lambda i: pl.ds(2 * i, 2)
    wide = [(fetch(2 * i, m["ga"].at[pair(i)], ga.at[pair(i)]),
             fetch(2 * i + 1, m["gb"].at[pair(i)], gb.at[pair(i)])) for i in range(4)]
    rest = {n: fetch(8 + k, m[n], m[n + "_v"])
            for k, n in enumerate(("db", "qkv", "da", "out", "ig", "mixed"))}
    saved = []
    for i in range(4):
        for copy in wide[i]:
            copy.wait()
        first, second = ga.at[2 * i], ga.at[2 * i + 1]
        tiles = [gb[2 * i + k, :, 2 * half_b:].astype(F32) for k in range(2)]
        for w in range(2):
            to = m["gu_v"].at[4 * w + i]
            for k in range(2):
                lo = k * (main + 128)
                to[:, lo:lo + half_a] = ga[2 * i + k, :, w * half_a:(w + 1) * half_a].astype(F32)
                to[:, lo + half_a:lo + main] = (
                    gb[2 * i + k, :, w * half_b:(w + 1) * half_b].astype(F32))
            if w == 0:
                to[:, main:main + 128] = jnp.where(low, tiles[0], roll(tiles[1], 64))
            else:
                to[:, main:main + 128] = jnp.where(low, roll(tiles[0], 64), tiles[1])
            saved.append(store(
                4 * w + i, to, m["gu_o"].at[:, pl.ds((4 * w + i) * cols, cols)]))

    rest["da"].wait()
    rest["db"].wait()
    da, db, down = m["da_v"], m["db_v"], m["down_v"]
    part = down.shape[0]
    rows_a, rows_b = da.shape[1], db.shape[1]
    shift = (part - main) * x

    def at(start, n):
        return pl.ds(pl.multiple_of(start, 16), n)

    for i in range(4):
        down[at(rows_a * i + shift, rows_a)] = da[i].astype(F32)
        start = half_a + rows_b * i + shift
        down[at(start, 16)] = db[i, 0:16].astype(F32)
        down[at(start + 16 - (i // 3) * x * part, rows_b - 16)] = db[i, 16:].astype(F32)
    saved.append(store(8, down, m["down_o"]))
    rest["qkv"].wait()
    qkv_v, qkv_f = m["qkv_v"], m["qkv_f"]
    q_cols, kv_cols = HEADS * HEAD_DIM, KV_HEADS * HEAD_DIM
    half = lambda v, w: jnp.where(low, v, w)
    for i in range(4):
        a, b = qkv_v[2 * i].astype(F32), qkv_v[2 * i + 1].astype(F32)
        a1, a2, b0, b1 = a[:, 128:256], a[:, 256:], b[:, 0:128], b[:, 128:256]
        lo = i * 2 * Q_COLS
        qkv_f[:, lo:lo + 128] = a[:, 0:128]
        qkv_f[:, lo + 128:lo + 256] = half(a1, roll(b0, 64))
        qkv_f[:, lo + 256:lo + 384] = half(roll(b0, 64), roll(b1, 64))
        lo = q_cols + i * 128
        qkv_f[:, lo:lo + 128] = half(roll(a1, 64), b1)
        lo = lo + kv_cols
        qkv_f[:, lo:lo + 128] = jnp.concatenate([a2, b[:, 256:]], axis=1)
    saved.append(store(9, qkv_f, m["qkv_o"]))
    rest["out"].wait()
    n = m["out_v"].shape[1]
    for i in range(4):
        m["out_f"][n * i:n * (i + 1)] = m["out_v"][i].astype(F32)
    saved.append(store(10, m["out_f"], m["out_o"]))
    for k, n in ((11, "ig"), (12, "mixed")):
        rest[n].wait()
        saved.append(store(k, m[n + "_v"], m[n + "_o"]))
    gains = m["gains"][...]
    width = gains.shape[1]
    turned = pltpu.roll(gains, (width - own_rows * lax.axis_index("grp")) % width, 1)
    m["one_o"][...] = turned[0:1, 0:own_rows]
    m["two_o"][...] = turned[1:2, 0:own_rows]
    m["q_o"][...] = gains[2:3, 0:HEAD_DIM]
    m["k_o"][...] = gains[2:3, HEAD_DIM:2 * HEAD_DIM]
    for copy in saved:
        copy.wait()


def order_call(g):
    shape = jax.ShapeDtypeStruct
    ga, gb, da, db, out, qkv, mixed, ig = (g[n] for n in ORDER_IN)
    _, own_rows, cols_a = ga.shape
    cols = cols_a + gb.shape[2]
    width = da.shape[2]
    part = 4 * (da.shape[1] + db.shape[1])
    qkv_cols = (HEADS + 2 * KV_HEADS) * HEAD_DIM
    outs = {
        "gu_o": shape((own_rows, 8 * cols), F32), "down_o": shape((part, width), F32),
        "out_o": shape((own_rows, width), F32), "qkv_o": shape((own_rows, qkv_cols), F32),
        "ig_o": shape(ig.shape, F32), "mixed_o": shape(mixed.shape, BF16),
        "one_o": shape((1, own_rows), F32), "two_o": shape((1, own_rows), F32),
        "q_o": shape((1, HEAD_DIM), F32), "k_o": shape((1, HEAD_DIM), F32),
    }
    ins = ("ga", "gb", "da", "db", "out", "qkv", "mixed", "ig")
    scratch = {n + "_v": pltpu.VMEM(v.shape, v.dtype)
               for n, v in zip(ins, (ga, gb, da, db, out, qkv, mixed, ig))}
    scratch["gu_v"] = pltpu.VMEM((8, own_rows, cols), F32)
    scratch["down_v"] = pltpu.VMEM((part, width), F32)
    scratch["out_f"] = pltpu.VMEM((own_rows, width), F32)
    scratch["qkv_f"] = pltpu.VMEM((own_rows, qkv_cols), F32)
    scratch["load"], scratch["save"] = dma(14), dma(13)
    names = ins + ("gains",) + tuple(outs) + tuple(scratch)
    got = pl.pallas_call(
        functools.partial(order_kernel, names),
        name="final_order",
        out_shape=tuple(outs.values()),
        in_specs=[ANY] * 8 + [VMEM],
        out_specs=(ANY,) * 6 + (VMEM,) * 4,
        scratch_shapes=list(scratch.values()),
        compiler_params=pltpu.CompilerParams(vmem_limit_bytes=62 * 2**20),
    )(ga, gb, da, db, out, qkv, mixed, ig, g["gains_g"])
    return dict(zip(outs, got))


ORDER_IN = ("ga_g", "gb_g", "da_g", "db_g", "out_g", "qkv_g", "mixed", "input_grad")


def over_quads(array):
    reps = lax.axis_size("rep")
    if reps == 4:
        return array
    rows = [[j + 4 * q for q in range(reps // 4)] for j in range(4)]
    return lax.psum(array, "rep", axis_index_groups=rows)


def local(tokens, attn_gain, w_qkv, q_gain, k_gain, w_out, ffn_gain, w_gate_up, w_down,
          cotangent, segment_ids):
    rows, width = tokens.shape
    parts = (attn_gain, q_gain, ffn_gain, k_gain, segment_ids)
    total = sum(v.shape[0] for v in parts)
    small, at = 0.0, 0
    for v in parts:
        n = v.shape[0]
        small = small + jnp.pad(v.astype(F32), (at, total - at - n))
        at += n
    g = block_call(
        tokens, cotangent, small.reshape(1, -1), w_qkv, w_gate_up, w_down, w_out)
    g = {n: over_quads(v) if n.endswith("_g") else v for n, v in g.items()}
    o = order_call(g)
    flat = lambda n: o[n].reshape(-1)
    return (o["mixed_o"], o["ig_o"], flat("one_o"), o["qkv_o"], flat("q_o"), flat("k_o"),
            o["out_o"], flat("two_o"), o["gu_o"], o["down_o"])


def solution(mesh):
    rows, split = P(("rep", "grp"), None), P("grp", None)
    return jax.shard_map(
        local,
        mesh=mesh,
        in_specs=(rows, P("grp"), split, P(), P(), split, P("grp"), split, split, rows,
                  P(("rep", "grp"))),
        out_specs=(rows, rows, P("grp"), split, P(), P(), split, P("grp"), split, split),
        check_vma=False,
    )
```

```python
import functools

import jax
import jax.numpy as jnp
from jax import lax
from jax.experimental import pallas as pl
from jax.experimental.pallas import tpu as pltpu
from jax.sharding import PartitionSpec as P

HEADS = 24
KV_HEADS = 8
HEAD_DIM = 64
GROUP = HEADS // KV_HEADS
Q_COLS = GROUP * HEAD_DIM
HEAD_COLS = Q_COLS + 2 * HEAD_DIM

EPS = 1e-05
THETA = 1000000.0
MESH = pl.DeviceIdType.MESH
F32 = jnp.float32
BF16 = jnp.bfloat16

VMEM = pl.BlockSpec(memory_space=pltpu.VMEM)
ANY = pl.BlockSpec(memory_space=pl.ANY)


def here():
    rep = lax.axis_index("rep")
    grp = lax.axis_index("grp")
    r = rep % 4
    return rep - r, r // 2, r % 2, grp // 2, grp % 2


def device(base, y, c, z, x):
    return {"rep": base + 2 * y + c, "grp": 2 * z + x}


def remote(src, dst, send, recv, to):
    return pltpu.make_async_remote_copy(
        src_ref=src, dst_ref=dst, send_sem=send, recv_sem=recv, device_id=to, device_id_type=MESH
    )


def greet(targets):
    barrier = pltpu.get_barrier_semaphore()
    for to in targets:
        pl.semaphore_signal(barrier, inc=1, device_id=to, device_id_type=MESH)
    pl.semaphore_wait(barrier, len(targets))


def neighbours():
    base, y, c, z, x = here()
    to_c = device(base, y, 1 - c, z, x)
    to_x = device(base, y, c, z, 1 - x)
    to_y = device(base, 1 - y, c, z, x)
    return to_c, to_x, to_y


class Gather:
    def __init__(self, src, out, send, recv, local):
        self.src, self.out, self.send, self.recv = src, out, send, recv
        _, y, c, _, x = here()
        self.to_c, self.to_x, self.to_y = neighbours()
        slot = lambda a, b, d: 4 * a + 2 * b + d
        self.own = slot(y, c, x)
        self.at_c, self.at_x, self.at_y = slot(y, 1 - c, x), slot(y, c, 1 - x), slot(1 - y, c, x)
        self.at_xc, self.at_yc = slot(y, 1 - c, 1 - x), slot(1 - y, 1 - c, x)
        self.at_xy, self.at_xyc = slot(1 - y, c, 1 - x), slot(1 - y, 1 - c, 1 - x)
        self.half = src.shape[0] // 2
        self.keep = pltpu.make_async_copy(src, out.at[self.own], local)

    def part(self, at, k):
        return self.out.at[at, pl.ds(k * self.half, self.half)]

    def copy(self, k):
        out, own = self.out, self.out.at[self.own]
        src, dst, to = (
            lambda: (self.src, own, self.to_x),
            lambda: (self.src, own, self.to_y),
            lambda: (self.src, own, self.to_c),
            lambda: (self.part(self.at_x, 0),) * 2 + (self.to_y,),
            lambda: (out.at[self.at_x],) * 2 + (self.to_c,),
            lambda: (self.part(self.at_y, 1),) * 2 + (self.to_x,),
            lambda: (out.at[self.at_y],) * 2 + (self.to_c,),
            lambda: (out.at[self.at_xy],) * 2 + (self.to_c,),
        )[k]()
        return remote(src, dst, self.send.at[k], self.recv.at[k], to)

    def arrive(self, k):
        out = self.out
        ref = (
            lambda: out.at[self.at_x], lambda: out.at[self.at_y], lambda: out.at[self.at_c],
            lambda: self.part(self.at_xy, 0), lambda: out.at[self.at_xc],
            lambda: self.part(self.at_xy, 1), lambda: out.at[self.at_yc],
            lambda: out.at[self.at_xyc],
        )[k]()
        remote(ref, ref, self.send.at[k], self.recv.at[k], self.to_c).wait_recv()

    def start(self):
        self.keep.start()
        for k in range(3):
            self.copy(k).start()

    def forward(self):
        self.arrive(0)
        self.copy(3).start()
        self.copy(4).start()
        self.arrive(1)
        self.copy(5).start()
        self.copy(6).start()

    def cross(self):
        self.arrive(3)
        self.arrive(5)
        self.copy(7).start()

    def finish(self):
        self.cross()
        for k in (2, 4, 6, 7):
            self.arrive(k)
        self.keep.wait()
        self.sent()

    def sent(self):
        for k in range(8):
            self.copy(k).wait_send()


def dma(n):
    return pltpu.SemaphoreType.DMA((n,))


def params(cid, limit=60):
    return pltpu.CompilerParams(
        collective_id=cid, has_side_effects=True, vmem_limit_bytes=limit * 2**20
    )


def inverse_rms(v):
    return lax.rsqrt(jnp.mean(v * v, axis=-1, keepdims=True) + EPS)


def norm_back(dy, v, inv, gain):
    scaled = dy * gain
    gain_grad = jnp.sum(dy * v * inv, axis=0, keepdims=True)
    inner = jnp.mean(scaled * v, axis=-1, keepdims=True)
    return inv * scaled - v * inv * inv * inv * inner, gain_grad


def when(cond):
    return pl.when(cond)


def lanes(shape):
    return lax.broadcasted_iota(jnp.int32, shape, len(shape) - 1)


def roll(v, by):
    return pltpu.roll(v, by % v.shape[-1], v.ndim - 1)


class Along:
    def __init__(self, src, slot, send, recv):
        self.src, self.slot, self.send, self.recv = src, slot, send, recv
        self.base, self.y, self.c, self.z, self.x = here()

    def at(self, zk, x):
        return device(self.base, self.y, self.c, zk, x)

    def copy(self, d):
        zk = (self.z + d + 4) % 4
        return remote(self.src, self.slot(self.z), self.send.at[d + 2], self.recv.at[self.z],
                      self.at(zk, self.x))

    def fits(self, d):
        return (self.z + d >= 0) & (self.z + d < 4)

    def first(self):
        for d in (2, -2):
            pl.when(self.fits(d))(lambda d=d: self.copy(d).start())
        pl.when(self.z == 2)(lambda: self.copy(1).start())
        pl.when(self.z == 1)(lambda: self.copy(-1).start())

    def second(self):
        pl.when(self.z < 2)(lambda: self.copy(1).start())
        pl.when(self.z >= 2)(lambda: self.copy(-1).start())

    def arrival(self, zk):
        ref = self.slot(zk)
        return remote(ref, ref, self.send.at[0], self.recv.at[zk], self.at(self.z, 1 - self.x))

    def passed(self, zk, to):
        ref = self.slot(zk)
        return remote(ref, ref, self.send.at[5], self.recv.at[zk], self.at(to, self.x))

    def forward(self):
        @pl.when(self.z == 2)
        def _():
            self.arrival(0).wait_recv()
            self.passed(0, 3).start()

        @pl.when(self.z == 1)
        def _():
            self.arrival(3).wait_recv()
            self.passed(3, 0).start()

    def wait(self, zk):
        early = ((self.z == 2) & (zk == 0)) | ((self.z == 1) & (zk == 3))
        due = jnp.logical_not(early) & (self.z != zk)
        pl.when(due)(lambda: self.arrival(zk).wait_recv())

    def finish(self):
        for zk in range(4):
            self.wait(zk)

    def sent(self):
        for d in (2, -2, 1, -1):
            pl.when(self.fits(d))(lambda d=d: self.copy(d).wait_send())
        pl.when(self.z == 2)(lambda: self.passed(0, 3).wait_send())
        pl.when(self.z == 1)(lambda: self.passed(3, 0).wait_send())


class Chain:
    def __init__(self, slot, send, recv):
        self.slot, self.send, self.recv = slot, send, recv
        self.base, self.y, self.c, self.z, self.x = here()

    def copy(self, k, zk, to):
        return remote(self.slot(zk), self.slot(zk), self.send.at[k], self.recv.at[zk],
                      device(self.base, self.y, self.c, to, self.x))

    def arrive(self, zk):
        self.copy(0, zk, self.z).wait_recv()

    def inner(self):
        return (self.z == 1) | (self.z == 2)

    def start_ends(self):
        pl.when(self.z == 0)(lambda: self.copy(0, 0, 1).start())
        pl.when(self.z == 3)(lambda: self.copy(1, 3, 2).start())

    def start_inner(self):
        z = self.z

        @pl.when(self.inner())
        def _():
            self.copy(0, z, z + 1).start()
            self.copy(1, z, z - 1).start()

    def pass_ends(self):
        @pl.when(self.z == 1)
        def _():
            self.arrive(0)
            self.copy(2, 0, 2).start()

        @pl.when(self.z == 2)
        def _():
            self.arrive(3)
            self.copy(3, 3, 1).start()

    def pass_inner(self):
        @pl.when(self.z == 1)
        def _():
            self.arrive(2)
            self.copy(3, 2, 0).start()

        @pl.when(self.z == 2)
        def _():
            self.arrive(1)
            self.copy(2, 1, 3).start()

    def second(self):
        self.pass_ends()
        self.pass_inner()

    def third(self):
        @pl.when(self.z == 2)
        def _():
            self.arrive(0)
            self.copy(4, 0, 3).start()

        @pl.when(self.z == 1)
        def _():
            self.arrive(3)
            self.copy(4, 3, 0).start()

    def finish(self):
        pl.when(self.z == 0)(lambda: [self.arrive(zk) for zk in (1, 2, 3)] and None)
        pl.when(self.z == 3)(lambda: [self.arrive(zk) for zk in (2, 1, 0)] and None)

    def sent(self):
        z = self.z
        pl.when(z < 3)(lambda: self.copy(0, z, z + 1).wait_send())
        pl.when(z > 0)(lambda: self.copy(1, z, z - 1).wait_send())

        @pl.when(self.inner())
        def _():
            self.copy(2, z - 1, z + 1).wait_send()
            self.copy(3, z + 1, z - 1).wait_send()
            self.copy(4, z, z + 1).wait_send()


class ChainSum:
    def __init__(self, block, slot, send, recv):
        self.block, self.slot, self.send, self.recv = block, slot, send, recv
        self.base, self.y, self.c, self.z, self.x = here()

    def copy(self, zk, to, at):
        return remote(self.block(zk), self.slot(at), self.send.at[zk], self.recv.at[at],
                      device(self.base, self.y, self.c, to, self.x))

    def arrive(self, at):
        self.copy(0, self.z, at).wait_recv()

    def start(self):
        @pl.when(self.z == 0)
        def _():
            for zk, at in ((3, 3), (2, 2), (1, 4)):
                self.copy(zk, 1, at).start()

        @pl.when(self.z == 3)
        def _():
            for zk in (0, 1, 2):
                self.copy(zk, 2, zk).start()

    def start_one(self, zk):
        for to, at in ((3, 3), (2, 2), (1, 4)):
            pl.when((self.z == 0) & (zk == to))(
                lambda to=to, at=at: self.copy(to, 1, at).start())
        for to in (0, 1, 2):
            pl.when((self.z == 3) & (zk == to))(lambda to=to: self.copy(to, 2, to).start())

    def first_hop(self, add, which=(0, 1)):
        @pl.when(self.z == 1)
        def _():
            for i in which:
                zk, at = ((3, 3), (2, 4))[i]
                self.arrive(zk)
                add(self.block(zk), self.slot(zk))
                self.copy(zk, 2, at).start()

        @pl.when(self.z == 2)
        def _():
            for zk in which:
                self.arrive(zk)
                add(self.block(zk), self.slot(zk))
                self.copy(zk, 1, zk).start()

    def second_hop(self, add, inner=(1, 2)):
        for z, zk, to, at in ((1, 0, 0, 0), (2, 3, 3, 4)):
            if z not in inner:
                continue

            @pl.when(self.z == z)
            def _():
                self.arrive(zk)
                add(self.block(zk), self.slot(zk))
                self.copy(zk, to, at).start()

    def collect(self, total):
        z = self.z

        def take(ats):
            for at in ats:
                self.arrive(at)
            total([self.slot(at) for at in ats])

        pl.when(z == 0)(lambda: take([0]))
        pl.when(z == 3)(lambda: take([4]))
        pl.when((z == 1) | (z == 2))(lambda: take([z, 4]))

    def sent(self):
        for zk in range(4):
            pl.when(self.z != zk)(lambda zk=zk: self.copy(zk, 0, 0).wait_send())


def layer_mates():
    base, y, c, z, x = here()
    return [
        device(base, (y + k // 4) % 2, (c + k // 2) % 2, z, (x + k) % 2) for k in range(1, 8)
    ]


def z_mates():
    base, y, c, z, x = here()
    return [device(base, y, c, (z + k // 2) % 4, (x + k) % 2) for k in range(2, 8)]


def rotated(u, cos, sin):
    lane = lanes(u.shape)
    return u * cos + jnp.where(lane < 32, roll(u, -32), roll(u, 32)) * sin


def low_half(v):
    return jnp.where(lanes(v.shape) < HEAD_DIM, v, 0.0)


def high_half(v):
    return jnp.where(lanes(v.shape) >= HEAD_DIM, v, 0.0)


def split_heads(tile_a, tile_b):
    return [low_half(tile_a), low_half(roll(tile_a, 64)), low_half(tile_b),
            low_half(roll(tile_b, 64))]


def head_inverse(u):
    return lax.rsqrt(jnp.sum(u * u, axis=-1, keepdims=True) * (1.0 / HEAD_DIM) + EPS)


def exp_scores(q, kv, q_seg, k_seg, diagonal):
    s = lax.dot_general(q, kv, (((1,), (1,)), ((), ())), preferred_element_type=F32)
    allowed = q_seg == k_seg
    if diagonal:
        row = lax.broadcasted_iota(jnp.int32, allowed.shape, 0)
        col = lax.broadcasted_iota(jnp.int32, allowed.shape, 1)
        allowed = allowed & (col <= row)
    n = allowed.shape[0]
    return jnp.concatenate([
        jnp.where(allowed, jnp.exp(s[n * j:n * (j + 1)]), 0.0) for j in range(GROUP)], axis=0)


def segment_row(segs, zk, s):
    return jnp.concatenate([segs[zk, 2 * s, 0:1], segs[zk, 2 * s + 1, 0:1]], axis=1)


def segment_columns(segs, zk, s):
    parts = []
    for i in range(2):
        row = jnp.broadcast_to(segs[zk, 2 * s + i, 0:1], (128, 128))
        parts.append(jnp.transpose(row))
    col = jnp.concatenate(parts, axis=0)
    return jnp.concatenate([col, col], axis=1)


class SeqSum:
    def __init__(self, part, scratch, by_x=False):
        self.part, self.by_x = part, by_x
        (self.r1, self.chip, self.rx, self.mine, self.late, self.out,
         self.send, self.recv) = scratch
        _, self.y, self.c, _, self.x = here()
        self.to_c, self.to_x, self.to_y = neighbours()
        rows = part.shape[1]
        self.top = pl.ds(0, rows if by_x else rows // 2)
        self.low = pl.ds(rows // 2, rows // 2)

    def copy(self, k, src, dst, to):
        return remote(src, dst, self.send.at[k], self.recv.at[k], to)

    def swap(self, b, a):
        at = 2 * b + a
        return self.copy(at, self.part.at[4 * b + 2 * (1 - self.c) + a], self.r1.at[at], self.to_c)

    def give(self, b):
        for a in range(2):
            self.swap(b, a).start()

    def along_x(self, b):
        at = 2 * b + 1 - self.x
        return self.copy(4 + b, self.chip.at[at, self.top], self.rx.at[b, self.top], self.to_x)

    def along_y(self, a):
        at = 2 * (1 - self.y) + a
        return self.copy(6 + a, self.chip.at[at, self.low], self.rx.at[a, self.low], self.to_y)

    def last_y(self):
        return self.copy(8, self.mine.at[self.top], self.late.at[self.top], self.to_y)

    def last_x(self):
        return self.copy(9, self.mine.at[self.low], self.late.at[self.low], self.to_x)

    def total(self, b, a):
        self.swap(b, a).wait_recv()
        at = 2 * b + a
        return self.part[4 * b + 2 * self.c + a].astype(F32) + self.r1[at].astype(F32)

    def take_far(self):
        b = 1 - self.y
        for a in (1 - self.x, self.x):
            self.chip[2 * b + a] = self.total(b, a).astype(BF16)
            if a is not self.x:
                self.along_x(b).start()
            if not self.by_x:
                self.along_y(a).start()

    def take_near(self):
        b, x = self.y, self.x
        self.chip[2 * b + 1 - x] = self.total(b, 1 - x).astype(BF16)
        self.along_x(b).start()
        self.out[...] = self.total(b, x)

    def middle(self):
        x, y, top, low = self.x, self.y, self.top, self.low
        self.along_x(1 - y).wait_recv()
        self.mine[top] = (
            self.chip[2 * (1 - y) + x, top].astype(F32) + self.rx[1 - y, top].astype(F32)
        ).astype(BF16)
        self.last_y().start()
        if self.by_x:
            return
        self.along_y(1 - x).wait_recv()
        self.mine[low] = (
            self.chip[2 * y + 1 - x, low].astype(F32) + self.rx[1 - x, low].astype(F32)
        ).astype(BF16)
        self.last_x().start()

    def finish(self):
        x, y, top, low = self.x, self.y, self.top, self.low
        self.along_x(y).wait_recv()
        self.last_y().wait_recv()
        self.out[top] += self.rx[y, top].astype(F32) + self.late[top].astype(F32)
        if self.by_x:
            return
        self.along_y(x).wait_recv()
        self.last_x().wait_recv()
        self.out[low] += self.rx[x, low].astype(F32) + self.late[low].astype(F32)

    def given(self):
        for b in range(2):
            for a in range(2):
                self.swap(b, a).wait_send()

    def passed(self):
        for b in range(2):
            self.along_x(b).wait_send()
            if not self.by_x:
                self.along_y(b).wait_send()
        self.last_y().wait_send()
        if not self.by_x:
            self.last_x().wait_send()

    def sent(self):
        self.given()
        self.passed()


def seq_scratch(width):
    return [
        pltpu.VMEM((4, 128, width), BF16),
        pltpu.VMEM((4, 128, width), BF16),
        pltpu.VMEM((2, 128, width), BF16),
        pltpu.VMEM((128, width), BF16),
        pltpu.VMEM((128, width), BF16),
        pltpu.VMEM((128, width), F32),
        dma(10),
        dma(10),
    ]


def first_dims(left, right):
    return lax.dot_general(left, right, (((0,), (0,)), ((), ())), preferred_element_type=F32)


def last_dims(left, right):
    return lax.dot_general(left, right, (((1,), (1,)), ((), ())), preferred_element_type=F32)


def swiglu(gate, up, grad):
    sigma = 1.0 / (1.0 + jnp.exp(-gate))
    active = gate * sigma
    d_gate = grad * up * sigma * (1.0 + gate * (1.0 - sigma))
    return ((active * up).astype(BF16), d_gate.astype(BF16), (grad * active).astype(BF16))


class Direct:
    def __init__(self, block, slot, send, recv):
        self.block, self.slot, self.send, self.recv = block, slot, send, recv
        self.base, self.y, self.c, self.z, self.x = here()

    def copy(self, zk):
        return remote(self.block(zk), self.slot(self.z), self.send.at[zk], self.recv.at[self.z],
                      device(self.base, self.y, self.c, zk, self.x))

    def start(self, zk):
        pl.when(zk != self.z)(lambda: self.copy(zk).start())

    def take(self):
        for k in (1, 3, 2):
            zk = (self.z + k) % 4
            ref = self.slot(zk)
            remote(ref, ref, self.send.at[0], self.recv.at[zk],
                   device(self.base, self.y, self.c, zk, self.x)).wait_recv()
            yield ref[...].astype(F32)

    def sent(self):
        for zk in range(4):
            pl.when(self.z != zk)(lambda zk=zk: self.copy(zk).wait_send())


class RepShare:
    def __init__(self, at, send, recv):
        self.at, self.send, self.recv = at, send, recv
        _, self.y, self.c, _, _ = here()
        self.to_c, _, self.to_y = neighbours()
        self.r = 2 * self.y + self.c

    def copy(self, k, r, to):
        return remote(self.at(r), self.at(r), self.send.at[k], self.recv.at[k], to)

    def start(self):
        self.copy(0, self.r, self.to_y).start()
        self.copy(1, self.r, self.to_c).start()

    def forward(self):
        other = 2 * (1 - self.y) + self.c
        self.copy(0, other, self.to_y).wait_recv()
        self.copy(2, other, self.to_c).start()

    def finish(self):
        self.copy(1, 2 * self.y + 1 - self.c, self.to_c).wait_recv()
        self.copy(2, 2 * (1 - self.y) + 1 - self.c, self.to_c).wait_recv()

    def sent(self):
        self.copy(0, self.r, self.to_y).wait_send()
        self.copy(1, self.r, self.to_c).wait_send()
        self.copy(2, self.r, self.to_c).wait_send()


def head_back(dy, u, gain):
    inv = head_inverse(u)
    scaled = dy * gain
    gain_grad = jnp.sum(dy * u * inv, axis=0, keepdims=True)
    inner = jnp.sum(scaled * u, axis=-1, keepdims=True) * (1.0 / HEAD_DIM)
    return inv * scaled - u * (inv * inv * inv * inner), gain_grad


def rope_table(start, rows):
    half = HEAD_DIM // 2
    lane = lax.broadcasted_iota(jnp.int32, (rows, 4 * half), 1)
    freq = jnp.exp(-jnp.log(THETA) * (lane % half).astype(F32) * 2.0 / HEAD_DIM)
    position = start + lax.broadcasted_iota(jnp.int32, (rows, 4 * half), 0)
    angle = position.astype(F32) * freq
    sine = jnp.sin(angle)
    return jnp.where(lane < 2 * half, jnp.cos(angle), jnp.where(lane < 3 * half, -sine, sine))


def block_kernel(names, *refs):
    m = dict(zip(names, refs))
    base, y, c, z, x = here()
    r = 2 * y + c
    to_c, to_x, to_y = neighbours()
    q_cols, kv_cols = HEADS * HEAD_DIM, KV_HEADS * HEAD_DIM
    raw_q = [
        pltpu.make_async_copy(m["wqkv"].at[:, pl.ds(first + n * r, n)],
                              m["wq_raw"].at[:, pl.ds(to, n)], m["keep"].at[k])
        for k, (first, to, n) in enumerate((
            (0, 0, 2 * Q_COLS), (q_cols, 2 * Q_COLS, 2 * HEAD_DIM),
            (q_cols + kv_cols, 2 * Q_COLS + 2 * HEAD_DIM, 2 * HEAD_DIM)))]
    for copy in raw_q:
        copy.start()
    tok_load = pltpu.make_async_copy(m["tok"], m["tok_v"], m["keep"].at[19])
    tok_load.start()
    small = m["small"][...].astype(F32)
    m["seg"][...] = jnp.broadcast_to(small[:, 512:640], (8, 128)).astype(jnp.int32)
    m["gains"][...] = jnp.concatenate(
        [small[:, 0:256], small[:, 256:512], jnp.zeros((14, 256), F32)], axis=0).astype(BF16)
    qg, kg = low_half(roll(small[:, 128:256], 64)), low_half(roll(small[:, 384:512], 64))
    greet(layer_mates() + z_mates())
    for copy in raw_q:
        copy.wait()
    tiles = [m["wq_raw"][:, 128 * i:128 * (i + 1)].astype(F32) for i in range(5)]
    low_lanes = lanes(tiles[0].shape) < HEAD_DIM
    half_of = lambda v, w: jnp.where(low_lanes, v, w).astype(BF16)
    q0, q1, q2, k_tile, v_tile = tiles
    m["wq"][0, :, 0:128] = q0.astype(BF16)
    m["wq"][0, :, 128:256] = half_of(q1, roll(k_tile, 64))
    m["wq"][0, :, 256:] = v_tile[:, 0:HEAD_DIM].astype(BF16)
    m["wq"][1, :, 0:128] = half_of(roll(q1, 64), roll(q2, 64))
    m["wq"][1, :, 128:256] = half_of(roll(q2, 64), k_tile)
    m["wq"][1, :, 256:] = roll(v_tile, 64)[:, 0:HEAD_DIM].astype(BF16)
    rows, width = m["tok"].shape
    quarter_o = m["wo"].shape[0] // 4
    own_rows = m["wqkv"].shape[0]
    half_cols = m["wgu"].shape[1] // 2
    piece = half_cols // 4
    part = piece // 2
    main = part // 128 * 128
    half_a = main // 2
    rows_a, rows_b, rest = half_a // 4, (part - half_a) // 4, part - main
    keep = m["keep"]
    own = 2 * z + x
    t_own = 2 * r + x

    def local_copy(k, src, dst):
        return pltpu.make_async_copy(src, dst, keep.at[k])

    hidden, dgu, wgu, wd_v = m["hidden"], m["dgu"], m["wgu_v"], m["wd_v"]
    cols_a = 2 * half_a
    cols_b = dgu.shape[1] - cols_a

    def raw(i):
        return dgu.at[pl.ds(i * own_rows, own_rows)]

    def pair(a, first, n):
        return dgu.at[pl.ds((2 + a) * own_rows, own_rows), pl.ds(first, n)]

    def loaded(k, src, dst):
        copy = local_copy(k, src, dst)
        copy.start()
        return copy

    tok = Gather(m["tok"], m["tok_all"], m["ga_s"], m["ga_r"], keep.at[0])
    cot = Gather(m["cot"], m["cot_v"], m["gb_s"], m["gb_r"], keep.at[1])
    segs = m["segs_v"]
    mates = layer_mates()

    def seg_copy(k):
        return remote(m["seg"], segs.at[z, t_own], m["sg_s"].at[k - 1], m["sg_r"].at[k - 1],
                      mates[k - 1])

    def gain_target(k):
        return device(base, y, c, (z + k // 2) % 4, (x + k) % 2)

    def gain_copy(k):
        return remote(m["gains"], m["gains_all"].at[own], m["gn_s"].at[k - 1],
                      m["gn_r"].at[k - 1], gain_target(k))

    wq = m["wq_v"]

    def wq_slot(zk, a):
        return wq.at[pl.ds((2 * zk + a) * own_rows, own_rows)]

    near = Along(m["wq"].at[x], lambda zk: wq_slot(zk, x), m["wa_s"], m["wa_r"])
    flip = Along(wq_slot(z, 1 - x), lambda zk: wq_slot(zk, 1 - x), m["wb_s"], m["wb_r"])
    over = remote(m["wq"].at[1 - x], wq_slot(z, x), m["wx_s"], m["wx_r"], to_x)
    over_in = remote(m["wq"].at[x], wq_slot(z, 1 - x), m["wx_s"], m["wx_r"], to_x)
    over.start()
    near.first()
    near.second()
    tok.start()
    for k in range(1, 8):
        seg_copy(k).start()
    local = [
        local_copy(2, m["wq"].at[x], wq_slot(z, x)),
        local_copy(3, m["gains"], m["gains_all"].at[own]),
        local_copy(4, m["seg"], segs.at[z, t_own]),
        local_copy(5, m["wgu"].at[:, pl.ds(piece * r, piece)], raw(0)),
        local_copy(6, m["wgu"].at[:, pl.ds(half_cols + piece * r, piece)], raw(1)),
    ]
    for copy in local:
        copy.start()
    for k in range(1, 8):
        gain_copy(k).start()
    out_q = Along(m["wo"].at[pl.ds(quarter_o * r, quarter_o)], lambda zk: m["zo"].at[zk],
                  m["wo_s"], m["wo_r"])
    last = r // 3
    tail_at = rest * x + half_a + rows_b * r + 16 - last * x * part
    quarters = [
        local_copy(7, m["wo"].at[pl.ds(quarter_o * r, quarter_o)], m["zo"].at[z]),
        local_copy(8, m["wd"].at[pl.ds(rest * x + rows_a * r, rows_a)], m["za"].at[z]),
        local_copy(13, m["wd"].at[pl.ds(rest * x + half_a + rows_b * r, 16)],
                   m["zb"].at[z, pl.ds(0, 16)]),
        local_copy(14, m["wd"].at[pl.ds(tail_at, rows_b - 16)],
                   m["zb"].at[z, pl.ds(16, rows_b - 16)]),
    ]
    for copy in quarters:
        copy.start()
    over_in.wait_recv()
    flip.first()
    flip.second()
    out_q.first()
    out_q.second()

    def seg_up(k):
        return remote(segs.at[z], segs.at[z], m["su_s"].at[k - 1], m["su_r"].at[z],
                      device(base, y, c, (z + k) % 4, x))

    for k in range(1, 8):
        seg_copy(k).wait_recv()
    local[2].wait()
    for k in range(3, 0, -1):
        pl.when(z + k < 4)(lambda k=k: seg_up(k).start())

    local[3].wait()
    local[4].wait()
    gate, up = raw(0), raw(1)
    for a in range(2):
        at = a * (piece - main)
        for i, src in enumerate((gate, up)):
            pair(a, i * half_a, half_a)[...] = src[:, at:at + half_a]
            pair(a, cols_a + i * half_a, half_a)[...] = src[:, at + half_a:at + main]
    g_tile = gate[:, main:main + 128].astype(F32)
    u_tile = up[:, main:main + 128].astype(F32)
    low = lanes(g_tile.shape) < HEAD_DIM
    pair(0, 2 * main, 128)[...] = jnp.where(low, g_tile, roll(u_tile, 64)).astype(BF16)
    pair(1, 2 * main, 128)[...] = jnp.where(low, roll(g_tile, 64), u_tile).astype(BF16)

    def unit(first, n):
        return lambda zk: wgu.at[pl.ds(2 * zk * own_rows, 2 * own_rows), pl.ds(first, n)]

    def crossing(first, n, ss, rs, k):
        cols = pl.ds(first, n)
        mine = wgu.at[pl.ds((2 * z + x) * own_rows, own_rows), cols]
        other = wgu.at[pl.ds((2 * z + 1 - x) * own_rows, own_rows), cols]
        return (remote(pair(1 - x, first, n), mine, ss, rs, to_x),
                remote(pair(x, first, n), other, ss, rs, to_x),
                local_copy(k, pair(x, first, n), mine))

    cross_a, cross_a_in, mine_a = crossing(0, cols_a, m["xa_s"], m["xa_r"], 5)
    cross_b, cross_b_in, mine_b = crossing(cols_a, cols_b, m["xb_s"], m["xb_r"], 6)
    gate_a = Chain(unit(0, cols_a), m["ca_s"], m["ca_r"])
    gate_b = Chain(unit(cols_a, cols_b), m["cb_s"], m["cb_r"])
    down_a = Chain(lambda zk: m["za"].at[zk], m["da_s"], m["da_r"])
    down_b = Chain(lambda zk: m["zb"].at[zk], m["db_s"], m["db_r"])
    m["rope"][...] = rope_table(2 * rows * z, 2 * rows)
    tok.forward()
    for copy in (cross_a, mine_a, cross_b, mine_b):
        copy.start()
    near.forward()
    flip.forward()
    out_q.forward()
    tok.finish()
    cot.start()
    near.finish()
    flip.finish()
    for k in range(1, 8):
        at = 2 * ((z + 4 - k // 2) % 4) + (x + k) % 2
        remote(m["gains"], m["gains_all"].at[at], m["gn_s"].at[k - 1], m["gn_r"].at[k - 1],
               to_c).wait_recv()
    for k in (0, 1):
        local[k].wait()
    gather_gains = pltpu.make_async_copy(m["gains_all"], m["gains_v"], keep.at[3])
    gather_gains.start()
    gather_gains.wait()
    gain_rows = []
    for i in range(2):
        gain_rows.append(jnp.concatenate(
            [m["gains_v"][k, 0:16].astype(F32)[i:i + 1, :own_rows] for k in range(8)], axis=1))
    m["g_one"][...], m["g_two"][...] = gain_rows
    kv = m["kv_v"]
    q_all, qkv_all = m["q_v"], m["qkv_v"]
    cos, sin = low_half(m["rope"][...]), low_half(roll(m["rope"][...], 64))
    span = 2 * rows

    def order(k):
        return (y + 1 + k) % 2, (c + 1 + k // 2) % 2

    def kv_copy(d, s):
        return remote(kv.at[z, s], kv.at[z, s], m["kv_s"].at[d - 1, s], m["kv_r"].at[z, s],
                      device(base, y, c, (z + d) % 4, x))

    def kv_arrival(zk, s):
        return remote(kv.at[zk, s], kv.at[zk, s], m["kv_s"].at[0, s], m["kv_r"].at[zk, s], to_x)

    def project(k, carry):
        b, e = order(k)
        s = 2 * b + e
        tokens = m["tok_all"][pl.ds(2 * s, 2)].reshape(span, width).astype(F32)
        normed = (tokens * inverse_rms(tokens) * m["g_one"][...]).astype(BF16)
        m["tok_all"][pl.ds(2 * s, 2)] = normed.reshape(2, rows, width)
        qkv = jnp.dot(normed, wq[...], preferred_element_type=F32)
        qkv_all[s] = qkv[:, 0:256]
        heads = split_heads(qkv[:, 0:128], qkv[:, 128:256])
        for j in range(GROUP):
            u = heads[j]
            u = rotated(u * head_inverse(u) * qg, cos, sin) * HEAD_DIM ** (-0.5)
            q_all[s, pl.ds(j * span, span)] = u.astype(BF16)
        u = heads[GROUP]
        u = rotated(u * head_inverse(u) * kg, cos, sin)
        v = jnp.concatenate([jnp.zeros((span, HEAD_DIM), F32), qkv[:, 256:320]], axis=1)
        kv[z, s] = (u + v).astype(BF16)
        for d in (3, 2, 1):
            pl.when(z + d < 4)(lambda d=d: kv_copy(d, s).start())
        return carry

    lax.fori_loop(0, 4, project, 0)
    for copy in quarters[1:]:
        copy.wait()
    down_a.start_ends()
    down_a.start_inner()
    for copy in (mine_a, mine_b):
        copy.wait()
    cross_a_in.wait_recv()
    gate_a.start_ends()
    gate_a.start_inner()
    cross_b_in.wait_recv()
    down_b.start_ends()
    gate_b.start_ends()
    cot.forward()

    def hand(k, zk, src, dst, sems, n):
        ss, rs = sems
        to = device(base, zk // 2, zk % 2, z, x)
        pl.when(r != zk)(lambda: remote(src.at[zk], dst.at[pl.ds(n * r, n)], ss.at[zk],
                                        rs.at[r], to).start())

        @pl.when(r == zk)
        def _():
            copy = local_copy(k, src.at[zk], dst.at[pl.ds(n * r, n)])
            copy.start()
            copy.wait()

    def handed(src, dst, sems, n):
        ss, rs = sems
        for rk in range(4):
            ref = dst.at[pl.ds(n * rk, n)]
            pl.when(r != rk)(lambda ref=ref, rk=rk: remote(
                src.at[0], ref, ss.at[0], rs.at[rk], to_x).wait_recv())

    def hand_sent(src, dst, sems, n):
        ss, rs = sems
        for zk in range(4):
            pl.when(r != zk)(lambda zk=zk: remote(
                src.at[zk], dst.at[pl.ds(0, n)], ss.at[zk], rs.at[0], to_x).wait_send())

    quarters[0].wait()
    out_q.finish()
    out_sems = (m["ho_s"], m["ho_r"])
    a_sems, b_sems = (m["hd_s"], m["hd_r"]), (m["hb_s"], m["hb_r"])
    for zk in range(4):
        hand(13, zk, m["zo"], m["wo_v"], out_sems, quarter_o)

    for k in range(1, 4):
        pl.when(z - k >= 0)(lambda k=k: remote(
            segs.at[0], segs.at[(z + 4 - k) % 4], m["su_s"].at[k - 1],
            m["su_r"].at[(z + 4 - k) % 4], to_x).wait_recv())

    summed = SeqSum(m["part"], [m[n] for n in SUM_NAMES])
    inv_all, att = m["inv_v"], m["att_v"]
    acc, q_seg = m["acc"], m["q_seg"]

    def attend_one(k, carry):
        b, e = order(k)
        s = 2 * b + e
        q_seg[...] = segment_columns(segs, z, s)

        def block(zk, diagonal):
            tile = kv[zk, s]
            p = exp_scores(q_all[s], tile, q_seg[...], segment_row(segs, zk, s), diagonal)
            ones = jnp.where(lanes(tile.shape) < HEAD_DIM, 1.0, tile.astype(F32)).astype(BF16)
            add = jnp.dot(p.astype(BF16), ones, preferred_element_type=F32)
            if diagonal:
                acc[...] = add
            else:
                acc[...] += add

        block(z, True)

        def step(i, inner):
            zk = z - 1 - i
            kv_arrival(zk, s).wait_recv()
            block(zk, False)
            return inner

        lax.fori_loop(0, z, step, 0)
        total = acc[...]
        inv = 1.0 / jnp.where(lanes(total.shape) < HEAD_DIM, total, 1.0)
        inv = jnp.where(lanes(total.shape) < HEAD_DIM, inv, roll(inv, 64))
        o = high_half(total * inv)
        lane = lanes((span, 128))
        inv_all[s] = jnp.where(lane < 32, inv[0:span], jnp.where(
            lane < 64, inv[span:2 * span], inv[2 * span:]))
        first, second, third = o[0:span], o[span:2 * span], o[2 * span:]
        att[s, :, 0:128] = (roll(first, 64) + second).astype(BF16)
        att[s, :, 128:192] = roll(third, 64)[:, 0:HEAD_DIM].astype(BF16)
        pl.when(k == 0)(lambda: handed(m["zo"], m["wo_v"], out_sems, quarter_o))
        out = jnp.dot(att[s], m["wo_v"][...], preferred_element_type=F32).astype(BF16)
        m["part"][pl.ds(2 * s, 2)] = out.reshape(2, rows, width)
        pl.when(k < 2)(lambda: summed.give(b))
        pl.when(k == 2)(summed.take_far)
        pl.when(k == 3)(summed.take_near)
        return carry

    lax.fori_loop(0, 4, attend_one, 0)
    down_a.second()
    gate_a.second()
    summed.middle()
    down_a.third()
    summed.finish()
    tok_load.wait()
    mid = m["tok_v"][...].astype(F32) + summed.out[...]
    m["mid"][...] = mid
    m["low"][...] = (mid * inverse_rms(mid) * m["g_two"][...]).astype(BF16)
    n2_all, cot_all = m["n2_v"], m["cot_v"]
    n2 = Gather(m["low"], n2_all, m["gc_s"], m["gc_r"], keep.at[20])
    n2.start()
    cot.finish()
    gate_a.third()
    down_b.pass_ends()
    gate_b.pass_ends()
    down_b.start_inner()
    gate_b.start_inner()
    n2.forward()
    down_a.finish()
    wda, wdb = wd_v.at[pl.ds(0, half_a)], wd_v.at[pl.ds(half_a, part - half_a)]
    for zk in range(4):
        hand(13, zk, m["za"], wda, a_sems, rows_a)
    n2.finish()
    gate_a.finish()
    handed(m["za"], wda, a_sems, rows_a)
    cross_a.wait_send()
    cross_b.wait_send()

    down_b.third()
    gate_b.third()

    def feed_first(s, carry):
        at = pl.ds(pl.multiple_of(s * span, span), span)
        gu = jnp.dot(n2_all[pl.ds(2 * s, 2)].reshape(span, width), wgu[:, :cols_a],
                     preferred_element_type=F32)
        dh = last_dims(cot_all[pl.ds(2 * s, 2)].reshape(span, width), wd_v[0:half_a])
        hidden[at, 0:half_a], dgu[at, 0:half_a], dgu[at, half_a:cols_a] = swiglu(
            gu[:, :half_a], gu[:, half_a:], dh)
        out = last_dims(dgu[at, 0:cols_a], wgu[:, :cols_a]).astype(BF16)
        m["part"][pl.ds(2 * s, 2)] = out.reshape(2, rows, width)
        return carry

    summed.given()
    lax.fori_loop(0, 4, feed_first, 0)
    down_b.pass_inner()
    gate_b.pass_inner()
    block_rows = 2 * own_rows
    gga, gdo, got_a = m["gga"], m["gdo"], m["got_a"]
    gate_sum = ChainSum(lambda zk: gga.at[zk], lambda at: m["gga_slot"].at[at], m["ys_s"],
                        m["ys_r"])
    down_sum = ChainSum(lambda zk: got_a.at[zk], lambda at: m["gda_slot"].at[at], m["yd_s"],
                        m["yd_r"])

    def grad_gate(zk, carry):
        cols = pl.ds(pl.multiple_of(zk * block_rows, 128), block_rows)
        left = n2_all[:, :, cols].reshape(8 * rows, block_rows)
        gga[zk] = first_dims(left, dgu[:, :cols_a]).astype(BF16)
        return carry

    lax.fori_loop(0, 4, grad_gate, 0)
    gate_sum.start()
    for j in range(0, half_a, 128):
        grad = first_dims(hidden[:, j:j + 128], cot_all[...].reshape(8 * rows, width))
        for h in range(128 // rows_a):
            gdo[j // rows_a + h, 0:rows_a] = grad[rows_a * h:rows_a * (h + 1)].astype(BF16)

    def spread_from(i):
        return gdo.at[i, pl.ds(0, rows_a)]

    def spread(i):
        return remote(spread_from(i), got_a.at[r], m["ha_s"].at[i], m["ha_r"].at[r],
                      device(base, i // 2, i % 2, z, x))

    for i in range(4):
        pl.when(r != i)(lambda i=i: spread(i).start())
    got_a[r] = gdo[r, 0:rows_a]

    def add(block, slot):
        block[...] = (block[...].astype(F32) + slot[...].astype(F32)).astype(BF16)

    gate_sum.first_hop(add)
    for i in range(4):
        pl.when(r != i)(lambda i=i: remote(
            spread_from(i), got_a.at[i], m["ha_s"].at[i], m["ha_r"].at[i], to_c).wait_recv())
    down_sum.start()
    down_b.finish()
    for zk in range(4):
        hand(13, zk, m["zb"], wdb, b_sems, rows_b)
    gate_b.finish()
    gate_sum.second_hop(add)
    handed(m["zb"], wdb, b_sems, rows_b)
    summed.passed()

    def total_in(block):
        def total(slots):
            value = block[...].astype(F32)
            for slot in slots:
                value = value + slot[...].astype(F32)
            block[...] = value.astype(BF16)
        return total

    parts, n2, cot_v, normed = m["part"], m["n2_v"], m["cot_v"], m["tok_all"]
    wd_v[pl.ds(part, 128 - rest)] = jnp.zeros((128 - rest, width), BF16)

    def feed(k, carry):
        b, e = order(k)
        s = 2 * b + e
        at = pl.ds(pl.multiple_of(s * span, span), span)
        gu = jnp.dot(n2[pl.ds(2 * s, 2)].reshape(span, width), wgu[:, cols_a:],
                     preferred_element_type=F32)
        dh = last_dims(cot_v[pl.ds(2 * s, 2)].reshape(span, width), wd_v[half_a:])
        (hidden[at, half_a:2 * half_a], dgu[at, cols_a:cols_a + half_a],
         dgu[at, cols_a + half_a:cols_a + 2 * half_a]) = swiglu(
            gu[:, :half_a], gu[:, half_a:2 * half_a], dh[:, :half_a])
        tile = gu[:, 2 * half_a:]
        gate, up, grad = low_half(tile), low_half(roll(tile, 64)), dh[:, half_a:]
        sigma = 1.0 / (1.0 + jnp.exp(-gate))
        active = gate * sigma
        hidden[at, 2 * half_a:] = (active * up).astype(BF16)
        d_gate = grad * up * sigma * (1.0 + gate * (1.0 - sigma))
        dgu[at, cols_a + 2 * half_a:] = (
            d_gate + roll(low_half(grad * active), 64)).astype(BF16)
        out = last_dims(dgu[at, cols_a:], wgu[:, cols_a:])
        out = out + parts[pl.ds(2 * s, 2)].reshape(span, width).astype(F32)
        parts[pl.ds(2 * s, 2)] = out.astype(BF16).reshape(2, rows, width)
        pl.when(k < 2)(lambda: summed.give(b))
        pl.when(k == 2)(summed.take_far)
        pl.when(k == 3)(summed.take_near)
        return carry

    lax.fori_loop(0, 4, feed, 0)
    down_sum.first_hop(add)

    ggu = m["ggu"]
    gu_sum = ChainSum(lambda zk: ggu.at[zk], lambda at: m["gu_slot"].at[at], m["zg_s"], m["zg_r"])

    def farthest(i):
        up = z // 2
        return up * i + (1 - up) * (3 - i)

    def grad_gu(i, carry):
        zk = farthest(i)
        cols = pl.ds(pl.multiple_of(zk * block_rows, 128), block_rows)
        left = n2[:, :, cols].reshape(8 * rows, block_rows)
        ggu[zk] = first_dims(left, dgu[:, cols_a:]).astype(BF16)
        pl.when(i < 2)(lambda: gu_sum.start_one(zk))
        return carry

    lax.fori_loop(0, 2, grad_gu, 0)
    summed.middle()
    lax.fori_loop(2, 4, grad_gu, 0)
    down_sum.second_hop(add)
    summed.finish()

    v = m["mid"][...]
    dv, gain_grad = norm_back(summed.out[...], v, inverse_rms(v), m["g_two"][...])
    m["row_two"][...] = gain_grad
    dmid = cot_v[t_own].astype(F32) + dv
    m["dmid"][...] = dmid
    m["low"][...] = dmid.astype(BF16)
    branch = Gather(m["low"], m["db"], m["gd_s"], m["gd_r"], keep.at[12])
    branch.start()
    gu_sum.first_hop(add, (0,))

    got = m["got"]
    quarter_d = rows_b
    for i in range(4):
        pl.when(r != i)(lambda i=i: spread(i).wait_send())
    for j in range(0, half_a + 128, 128):
        at = half_a + j
        grad = first_dims(hidden[:, at:at + 128], cot_v[...].reshape(8 * rows, width))
        grad = grad.astype(BF16)
        for i in range(4):
            lo, hi = max(j, quarter_d * i), min(j + 128, quarter_d * (i + 1))
            if lo < hi:
                gdo[i, lo - quarter_d * i:hi - quarter_d * i] = grad[lo - j:hi - j]

    summed.sent()

    def down(s, carry):
        at = pl.ds(pl.multiple_of(s * span, span), span)
        out = jnp.dot(hidden[at], wd_v[...], preferred_element_type=F32)
        parts[pl.ds(2 * s, 2)] = out.astype(BF16).reshape(2, rows, width)
        return carry

    lax.fori_loop(0, 4, down, 0)
    mixed = SeqSum(parts, [m[n] for n in SUM_NAMES], by_x=True)

    def give(i, lo, n, ss, rs):
        return remote(gdo.at[i, pl.ds(lo, n)], got.at[r, pl.ds(lo, n)], ss.at[i], rs.at[r],
                      device(base, i // 2, i % 2, z, x))

    def give_all(lo, n, ss, rs):
        for i in range(4):
            pl.when(r != i)(lambda i=i: give(i, lo, n, ss, rs).start())
        got[r, lo:lo + n] = gdo[r, lo:lo + n]

    def given(lo, n, ss, rs):
        for i in range(4):
            pl.when(r != i)(lambda i=i: remote(
                gdo.at[i, pl.ds(lo, n)], got.at[i, pl.ds(lo, n)], ss.at[i], rs.at[i],
                to_c).wait_recv())

    def give_sent(lo, n, ss, rs):
        for i in range(4):
            pl.when(r != i)(lambda i=i: give(i, lo, n, ss, rs).wait_send())

    def swap(src, out, ss, rs):
        return remote(src.at[pl.ds(own_rows * (1 - x), own_rows)], out.at[t_own], ss, rs, to_x)

    def keep_own(k, src, out):
        copy = pltpu.make_async_copy(src.at[pl.ds(own_rows * x, own_rows)], out.at[t_own],
                                     keep.at[k])
        copy.start()
        return copy

    def swapped(src, out, ss, rs):
        return remote(src.at[pl.ds(own_rows * x, own_rows)], out.at[2 * r + 1 - x], ss, rs, to_x)

    def pairs(out):
        return lambda i: out.at[pl.ds(2 * i, 2)]

    ga_out, gb_out, qkv_out = m["ga_g"], m["gb_g"], m["qkv_g"]
    ga_swap = swap(gga.at[z], ga_out, m["xs_s"], m["xs_r"])
    ga_keep = local_copy(14, gga.at[z, pl.ds(own_rows * x, own_rows)], ga_out.at[t_own])
    da_keep = local_copy(15, got_a.at[z], m["da_g"].at[r])
    ga_share = RepShare(pairs(ga_out), m["ra_s"], m["ra_r"])
    da_share = RepShare(lambda i: m["da_g"].at[i], m["rc_s"], m["rc_r"])

    def swap_first():
        gate_sum.collect(total_in(gga.at[z]))
        down_sum.collect(total_in(got_a.at[z]))
        for copy in (ga_swap, ga_keep, da_keep):
            copy.start()

    branch.forward()
    branch.arrive(2)
    branch.keep.wait()
    give_all(0, quarter_d, m["he_s"], m["he_r"])
    mixed.give(0)
    mixed.give(1)
    swap_first()
    gu_sum.first_hop(add, (1,))

    wo, qkv, dkv = m["wo_v"], qkv_all, kv
    db, dqkv, do_v = m["db"], m["dqkv"], m["do"]
    own_kv = m["own_kv"]
    m["row_head"][...] = jnp.zeros((1, 128), F32)

    down_rest = ChainSum(lambda zk: got.at[zk, pl.ds(0, quarter_d)],
                         lambda at: m["down_slot"].at[at], m["zd_s"], m["zd_r"])

    def share_first():
        ga_keep.wait()
        da_keep.wait()
        swapped(gga.at[z], ga_out, m["xs_s"], m["xs_r"]).wait_recv()
        ga_share.start()
        da_share.start()

    def order_back(k):
        return (y + k // 2) % 2, (c + 1 + k) % 2

    kv_slot = m["kv_slot"]

    def kv_down(zk, s):
        return remote(dkv.at[zk, s], kv_slot.at[zk, s], m["zk_s"].at[zk, s], m["zk_r"].at[zk, s],
                      device(base, y, c, (z + 3) % 4, x))

    def kv_merge(k):
        b, e = order_back(k)
        s = 2 * b + e

        def one(zk, inner):
            kv_down(zk, s).wait_recv()
            dkv[zk, s] = (dkv[zk, s].astype(F32) + kv_slot[zk, s].astype(F32)).astype(BF16)
            kv_down(zk, s).start()
            return inner

        @pl.when((z == 1) | (z == 2))
        def _():
            lax.fori_loop(0, z, one, 0)

    def attend_back(k, carry):
        pl.when(k == 0)(lambda: branch.arrive(4))
        pl.when(k == 1)(branch.cross)
        pl.when(k == 2)(lambda: [branch.arrive(6), branch.arrive(7)] and None)
        b, e = order_back(k)
        s = 2 * b + e
        grads = db[pl.ds(2 * s, 2)].reshape(span, width)
        d_att = last_dims(grads, wo[...])
        first = d_att[:, 0:128]
        third = jnp.concatenate([jnp.zeros((span, HEAD_DIM), F32), d_att[:, 128:192]], axis=1)
        d_out = [high_half(roll(first, 64)), high_half(first), third]
        att_a = att[s, :, 0:128].astype(F32)
        att_b = att[s, :, 128:192].astype(F32)
        att_b = jnp.concatenate([jnp.zeros((span, HEAD_DIM), F32), att_b], axis=1)
        deltas = []
        for j, o in enumerate((roll(att_a, 64), att_a, att_b)):
            inv = inv_all[s][:, 32 * j:32 * j + 1]
            part_j = (d_out[j].astype(BF16).astype(F32) * inv).astype(BF16)
            do_v[pl.ds(j * span, span)] = part_j
            deltas.append(jnp.sum(part_j.astype(F32) * o, axis=1, keepdims=True))
        delta = jnp.concatenate(deltas, axis=0)
        m["q_t"][...] = jnp.transpose(q_all[s].astype(F32)).astype(BF16)
        m["do_t"][...] = jnp.transpose(do_v[...].astype(F32)).astype(BF16)
        q_seg[...] = segment_columns(segs, z, s)
        acc[...] = jnp.zeros_like(acc)

        def block(zk, diagonal):
            tile = kv[zk, s]
            q = q_all[s]
            d_out = do_v[...]
            p = exp_scores(q, tile, q_seg[...], segment_row(segs, zk, s), diagonal)
            ds = (p * (last_dims(d_out, tile) - delta)).astype(BF16)
            acc[...] += jnp.dot(ds, tile, preferred_element_type=F32)
            both = jnp.dot(m["q_t"][...], ds, preferred_element_type=F32)
            both = both + jnp.dot(m["do_t"][...], p.astype(BF16), preferred_element_type=F32)
            return jnp.transpose(both)

        def step(zk, inner):
            dkv[zk, s] = block(zk, False).astype(BF16)
            pl.when(z == 3)(lambda: kv_down(zk, s).start())
            return inner

        lax.fori_loop(0, z, step, 0)
        own_kv[s] = block(z, True)
        tiles = split_heads(qkv[s, :, 0:128], qkv[s, :, 128:256])
        back = []
        for j in range(GROUP):
            dy = rotated(low_half(acc[pl.ds(j * span, span)]) * HEAD_DIM ** (-0.5), cos, -sin)
            raw, gain_part = head_back(dy, tiles[j], qg)
            m["row_head"][...] += gain_part
            back.append(raw)
        dqkv[s, :, 0:128] = (back[0] + roll(back[1], 64)).astype(BF16)
        dqkv[s, :, 128:256] = back[2].astype(BF16)
        pl.when(k >= 1)(lambda: kv_merge(k - 1))
        pl.when(k == 0)(lambda: gu_sum.second_hop(add))
        pl.when(k == 0)(mixed.take_far)
        pl.when(k == 0)(mixed.take_near)
        pl.when(k == 1)(share_first)
        pl.when(k == 3)(mixed.middle)
        pl.when(k == 3)(lambda: given(0, quarter_d, m["he_s"], m["he_r"]))
        return carry

    lax.fori_loop(0, 4, attend_back, 0)
    kv_merge(3)
    gu_sum.start_one(farthest(2))
    down_rest.start()
    inputs = SeqSum(parts, [m[n] for n in SUM_NAMES], by_x=True)

    def finish_one(k, carry):
        b, e = order_back(k)
        s = 2 * b + e
        @pl.when(z < 3)
        def _():
            kv_down(z, s).wait_recv()
            own_kv[s] += kv_slot[z, s].astype(F32)

        total = own_kv[s]
        u = split_heads(qkv[s, :, 0:128], qkv[s, :, 128:256])[GROUP]
        dy = rotated(low_half(total), cos, -sin)
        raw, gain_part = head_back(dy, u, kg)
        m["row_head"][...] += roll(gain_part, 64)
        tile = dqkv[s, :, 128:256].astype(F32)
        dqkv[s, :, 128:256] = (low_half(tile) + roll(raw, 64)).astype(BF16)
        dqkv[s, :, 256:320] = roll(total, 64)[:, 0:HEAD_DIM].astype(BF16)
        return carry

    lax.fori_loop(0, 4, finish_one, 0)
    gqkv = m["gqkv"]
    qkv_sum = Direct(lambda zk: gqkv.at[zk], lambda zk: m["qkv_slot"].at[zk], m["zq_s"],
                     m["zq_r"])

    def grad_qkv(i, carry):
        zk = farthest(i)
        cols = pl.ds(pl.multiple_of(zk * block_rows, 128), block_rows)
        left = normed[:, :, cols].reshape(8 * rows, block_rows)
        gqkv[zk] = first_dims(left, dqkv[...].reshape(8 * rows, HEAD_COLS)).astype(BF16)
        qkv_sum.start(zk)
        return carry

    lax.fori_loop(0, 4, grad_qkv, 0)

    for j in range(0, width, 512):
        cols = slice(j, j + 512)
        grad = first_dims(att[...].reshape(8 * rows, Q_COLS),
                          db[:, :, cols].reshape(8 * rows, 512)).astype(BF16)
        for i in range(4):
            gdo[i, quarter_d:quarter_d + quarter_o, cols] = grad[quarter_o * i:quarter_o * (i + 1)]
    give_all(quarter_d, quarter_o, m["hf_s"], m["hf_r"])
    mixed.given()

    def back_in(s, carry):
        out = last_dims(dqkv[s], wq[...]).astype(BF16)
        parts[pl.ds(2 * s, 2)] = out.reshape(2, rows, width)
        return carry

    lax.fori_loop(0, 4, back_in, 0)
    gu_sum.collect(total_in(ggu.at[z]))
    gb_swap = swap(ggu.at[z], gb_out, m["xg_s"], m["xg_r"])
    gb_swap.start()
    gb_keep = keep_own(14, ggu.at[z], gb_out)
    mixed.finish()
    branch.sent()
    m["low"][...] = (m["mid"][...] + mixed.out[...]).astype(BF16)
    mixed_out = loaded(17, m["low"], m["mixed"])
    mixed.passed()
    free = m["free"]
    for to in (to_c, to_x, to_y):
        pl.semaphore_signal(free, inc=1, device_id=to, device_id_type=MESH)

    pl.semaphore_wait(free, 3)
    inputs.give(0)
    inputs.give(1)
    inputs.take_far()
    inputs.take_near()
    gb_keep.wait()
    swapped(ggu.at[z], gb_out, m["xg_s"], m["xg_r"]).wait_recv()
    gb_share = RepShare(pairs(gb_out), m["rg_s"], m["rg_r"])
    gb_share.start()
    down_rest.first_hop(add)
    inputs.middle()
    down_rest.second_hop(add, (1,))
    given(quarter_d, quarter_o, m["hf_s"], m["hf_r"])
    out_sum = Direct(lambda zk: got.at[zk, pl.ds(quarter_d, quarter_o)],
                     lambda zk: m["out_slot"].at[zk], m["zo_s"], m["zo_r"])

    def start_out(i, carry):
        out_sum.start(farthest(i))
        return carry

    lax.fori_loop(0, 4, start_out, 0)
    ga_share.forward()
    da_share.forward()

    inputs.finish()
    v = m["tok_v"][...].astype(F32)
    dv, gain_grad = norm_back(inputs.out[...], v, inverse_rms(v), m["g_one"][...])
    m["dmid"][...] += dv
    grad_out = loaded(18, m["dmid"], m["input_grad"])

    def gain_rows_of(k):
        return m["mid"].at[pl.ds(8 * k, 8)]

    gains_own = gain_rows_of(0)
    gains_own[0:1] = gain_grad
    gains_own[1:2] = m["row_two"][...]
    gains_own[2:3, 0:128] = m["row_head"][...]

    def gain_sum(k):
        return remote(gains_own, gain_rows_of(k), m["gm_s"].at[k - 1], m["gm_r"].at[k - 1],
                      mates[k - 1])

    for k in range(1, 8):
        gain_sum(k).start()

    down_rest.second_hop(add, (2,))

    total = gqkv[z].astype(F32)
    for term in qkv_sum.take():
        total = total + term
    gqkv[z] = total.astype(BF16)
    qkv_swap = swap(gqkv.at[z], qkv_out, m["xq_s"], m["xq_r"])
    qkv_swap.start()
    qkv_keep = keep_own(16, gqkv.at[z], qkv_out)
    qkv_share = RepShare(pairs(qkv_out), m["rq_s"], m["rq_r"])

    down_rest.collect(total_in(got.at[z, pl.ds(0, quarter_d)]))
    db_keep = loaded(15, got.at[z, pl.ds(0, quarter_d)], m["db_g"].at[r])
    db_keep.wait()
    db_share = RepShare(lambda i: m["db_g"].at[i], m["rd_s"], m["rd_r"])
    db_share.start()
    for k in range(1, 8):
        gain_sum(k).wait_recv()
    total = gains_own[...]
    for k in range(1, 8):
        total = total + gain_rows_of(k)[...]
    z_rows = m["z_rows"]
    z_rows[0] = total

    def gain_z(k):
        return remote(z_rows.at[0], z_rows.at[k], m["gz_s"].at[k - 1], m["gz_r"].at[k - 1],
                      device(base, y, c, (z + k) % 4, x))

    for k in range(1, 4):
        gain_z(k).start()
    gb_share.forward()
    qkv_keep.wait()
    swapped(gqkv.at[z], qkv_out, m["xq_s"], m["xq_r"]).wait_recv()
    qkv_share.start()
    out_own = got.at[z, pl.ds(quarter_d, quarter_o)]
    total = out_own[...].astype(F32)
    for term in out_sum.take():
        total = total + term
    out_own[...] = total.astype(BF16)
    out_keep = loaded(0, out_own, m["out_g"].at[r])
    out_keep.wait()
    out_share = RepShare(lambda i: m["out_g"].at[i], m["re_s"], m["re_r"])
    out_share.start()
    db_share.forward()
    for k in range(1, 4):
        gain_z(k).wait_recv()
    m["gains_g"][...] = z_rows[0] + z_rows[1] + z_rows[2] + z_rows[3]
    qkv_share.forward()
    out_share.forward()
    shares = (ga_share, da_share, gb_share, db_share, out_share, qkv_share)
    for share in shares:
        share.finish()

    for share in shares:
        share.sent()
    for copy in (ga_swap, gb_swap, qkv_swap):
        copy.wait_send()
    for k in range(1, 8):
        gain_sum(k).wait_send()
    for k in range(1, 4):
        gain_z(k).wait_send()
    mixed_out.wait()
    grad_out.wait()
    for flow in (gu_sum, down_rest, qkv_sum, out_sum, inputs):
        flow.sent()
    give_sent(0, quarter_d, m["he_s"], m["he_r"])
    give_sent(quarter_d, quarter_o, m["hf_s"], m["hf_r"])

    def dkv_sent(s, carry):
        for zk in range(3):
            pl.when(z > zk)(lambda zk=zk: kv_down(zk, s).wait_send())
        return carry

    lax.fori_loop(0, 4, dkv_sent, 0)
    for flow in (near, flip, out_q, gate_a, gate_b, down_a, down_b, gate_sum, down_sum):
        flow.sent()
    over.wait_send()
    for k in range(1, 8):
        seg_copy(k).wait_send()
        gain_copy(k).wait_send()
    for k in range(1, 4):
        pl.when(z + k < 4)(lambda k=k: seg_up(k).wait_send())

    def kv_sent(s, carry):
        for d in (1, 2, 3):
            pl.when(z + d < 4)(lambda d=d: kv_copy(d, s).wait_send())
        return carry

    lax.fori_loop(0, 4, kv_sent, 0)
    hand_sent(m["zo"], m["wo_v"], out_sems, quarter_o)
    hand_sent(m["za"], wda, a_sems, rows_a)
    hand_sent(m["zb"], wdb, b_sems, rows_b)


SUM_NAMES = ("r1", "chip", "rx", "mine", "late", "sum_out", "sum_s", "sum_r")
IN = ("tok", "cot", "small", "wqkv", "wgu", "wd", "wo")
OUT = ("mixed", "input_grad", "gains_g", "ga_g", "gb_g", "da_g", "db_g", "out_g", "qkv_g",
       "zo", "za", "zb", "gains_all")


def block_call(*args):
    shape = jax.ShapeDtypeStruct
    tok, _, _, wqkv, wgu, wd, wo = args[:7]
    rows, width = tok.shape
    span = 2 * rows
    own_rows = wqkv.shape[0]
    seg, gains = shape((8, rows), jnp.int32), shape((16, 256), BF16)
    part = wgu.shape[1] // 16
    half_a = part // 256 * 128
    part_b = part - half_a
    cols_a, cols_b = 2 * half_a, 2 * half_a + 128
    quarter_a, quarter_d, quarter_o = half_a // 4, part_b // 4, own_rows // 4
    heads = GROUP * span
    outs = {
        "mixed": shape((rows, width), BF16),
        "input_grad": shape((rows, width), F32),
        "gains_g": shape((8, width), F32),
        "ga_g": shape((8, own_rows, cols_a), BF16),
        "gb_g": shape((8, own_rows, cols_b), BF16),
        "da_g": shape((4, quarter_a, width), BF16),
        "db_g": shape((4, quarter_d, width), BF16),
        "out_g": shape((4, quarter_o, width), BF16),
        "qkv_g": shape((8, own_rows, HEAD_COLS), BF16),
        "zo": shape((4, quarter_o, width), BF16),
        "za": shape((4, quarter_a, width), BF16),
        "zb": shape((4, quarter_d, width), BF16),
        "gains_all": shape((8,) + gains.shape, BF16),
    }
    buffers = {
        "tok_all": ((8, rows, width), BF16), "cot_v": ((8, rows, width), BF16),
        "n2_v": ((8, rows, width), BF16), "db": ((8, rows, width), BF16),
        "part": ((8, rows, width), BF16),
        "tok_v": (tok.shape, BF16), "rope": ((span, 128), F32), "seg": (seg.shape, seg.dtype), "gains": (gains.shape, BF16),
        "wq": ((2, own_rows, HEAD_COLS), BF16), "wq_raw": ((own_rows, 640), BF16),
        "segs_v": ((4, 8) + seg.shape, seg.dtype), "gains_v": ((8,) + gains.shape, BF16),
        "wq_v": ((width, HEAD_COLS), BF16), "wo_v": ((Q_COLS, width), BF16),
        "wgu_v": ((width, cols_a + cols_b), BF16), "wd_v": ((2 * half_a + 128, width), BF16),
        "hidden": ((8 * rows, 2 * half_a + 128), BF16),
        "dgu": ((8 * rows, cols_a + cols_b), BF16),
        "qkv_v": ((4, span, 256), F32), "q_v": ((4, heads, 128), BF16),
        "kv_v": ((4, 4, span, 128), BF16), "kv_slot": ((3, 4, span, 128), BF16),
        "own_kv": ((4, span, 128), F32), "inv_v": ((4, span, 128), F32),
        "att_v": ((4, span, Q_COLS), BF16), "acc": ((heads, 128), F32),
        "do": ((heads, 128), BF16), "q_t": ((128, heads), BF16), "do_t": ((128, heads), BF16), "q_seg": ((span, span), jnp.int32),
        "dqkv": ((4, span, HEAD_COLS), BF16),
        "mid": ((rows, width), F32), "dmid": ((rows, width), F32), "low": ((rows, width), BF16),
        "g_one": ((1, width), F32), "g_two": ((1, width), F32),
        "gga": ((4, 2 * own_rows, cols_a), BF16), "gga_slot": ((5, 2 * own_rows, cols_a), BF16),
        "ggu": ((4, 2 * own_rows, cols_b), BF16), "gu_slot": ((5, 2 * own_rows, cols_b), BF16),
        "got_a": ((4, quarter_a, width), BF16),
        "gda_slot": ((5, quarter_a, width), BF16),
        "gdo": ((4, quarter_d + quarter_o, width), BF16),
        "got": ((4, quarter_d + quarter_o, width), BF16),
        "down_slot": ((5, quarter_d, width), BF16),
        "out_slot": ((4, quarter_o, width), BF16),
        "gqkv": ((4, 2 * own_rows, HEAD_COLS), BF16),
        "qkv_slot": ((4, 2 * own_rows, HEAD_COLS), BF16),
        "row_two": ((1, width), F32), "row_head": ((1, 128), F32),
        "z_rows": ((4, 8, width), F32),
    }
    counts = {
        "ga": (8, 8), "gb": (8, 8), "gc": (8, 8), "gd": (8, 8), "sg": (7, 7), "gn": (7, 7),
        "gm": (7, 7), "gz": (3, 3), "wa": (6, 4), "wb": (6, 4), "wo": (6, 4), "wx": (1, 1),
        "xa": (1, 1), "xb": (1, 1), "xs": (1, 1), "xg": (1, 1), "ca": (5, 4), "cb": (5, 4),
        "da": (5, 4), "db": (5, 4), "ys": (4, 5), "yd": (4, 5), "zg": (4, 5), "zd": (4, 5),
        "zo": (4, 4), "zq": (4, 4), "xq": (1, 1), "zk": ((3, 4), (3, 4)), "kv": ((3, 4), (4, 4)),
        "su": (3, 4), "ha": (4, 4), "hb": (4, 4), "hd": (4, 4), "he": (4, 4), "hf": (4, 4),
        "ho": (4, 4), "ra": (3, 3), "rc": (3, 3), "rd": (3, 3), "re": (3, 3), "rg": (3, 3),
        "rq": (3, 3),
    }
    sem = pltpu.SemaphoreType.DMA
    many = lambda n: sem if n == 1 else sem(n if isinstance(n, tuple) else (n,))
    sems = {"keep": dma(21), "free": pltpu.SemaphoreType.REGULAR}
    for n, (send, recv) in counts.items():
        sems[n + "_s"], sems[n + "_r"] = many(send), many(recv)
    scratch = {n: pltpu.VMEM(*v) for n, v in buffers.items()}
    scratch.update(zip(SUM_NAMES, seq_scratch(width)))
    names = IN + OUT + tuple(scratch) + tuple(sems)
    got = pl.pallas_call(
        functools.partial(block_kernel, names),
        name="block",
        out_shape=tuple(outs[n] for n in OUT),
        in_specs=[ANY if n in ("tok", "cot", "wqkv", "wgu", "wd", "wo") else VMEM for n in IN],
        out_specs=tuple(VMEM if n == "gains_g" else ANY for n in OUT),
        scratch_shapes=list(scratch.values()) + list(sems.values()),
        compiler_params=params(0, 63),
    )(*args)
    return dict(zip(OUT, got))


def order_kernel(names, *refs):
    m = dict(zip(names, refs))
    half_a = m["ga"].shape[2] // 2
    half_b = (m["gb"].shape[2] - 128) // 2
    main = half_a + half_b
    cols = 2 * main + 128
    own_rows = m["ga"].shape[1]
    low = lanes((own_rows, 128)) < HEAD_DIM
    x = lax.axis_index("grp") % 2

    def fetch(k, src, dst):
        copy = pltpu.make_async_copy(src, dst, m["load"].at[k])
        copy.start()
        return copy

    def store(k, src, dst):
        copy = pltpu.make_async_copy(src, dst, m["save"].at[k])
        copy.start()
        return copy

    ga, gb = m["ga_v"], m["gb_v"]
    pair = lambda i: pl.ds(2 * i, 2)
    wide = [(fetch(2 * i, m["ga"].at[pair(i)], ga.at[pair(i)]),
             fetch(2 * i + 1, m["gb"].at[pair(i)], gb.at[pair(i)])) for i in range(4)]
    rest = {n: fetch(8 + k, m[n], m[n + "_v"])
            for k, n in enumerate(("db", "qkv", "da", "out", "ig", "mixed"))}
    saved = []
    for i in range(4):
        for copy in wide[i]:
            copy.wait()
        first, second = ga.at[2 * i], ga.at[2 * i + 1]
        tiles = [gb[2 * i + k, :, 2 * half_b:].astype(F32) for k in range(2)]
        for w in range(2):
            to = m["gu_v"].at[4 * w + i]
            for k in range(2):
                lo = k * (main + 128)
                to[:, lo:lo + half_a] = ga[2 * i + k, :, w * half_a:(w + 1) * half_a].astype(F32)
                to[:, lo + half_a:lo + main] = (
                    gb[2 * i + k, :, w * half_b:(w + 1) * half_b].astype(F32))
            if w == 0:
                to[:, main:main + 128] = jnp.where(low, tiles[0], roll(tiles[1], 64))
            else:
                to[:, main:main + 128] = jnp.where(low, roll(tiles[0], 64), tiles[1])
            saved.append(store(
                4 * w + i, to, m["gu_o"].at[:, pl.ds((4 * w + i) * cols, cols)]))

    rest["da"].wait()
    rest["db"].wait()
    da, db, down = m["da_v"], m["db_v"], m["down_v"]
    part = down.shape[0]
    rows_a, rows_b = da.shape[1], db.shape[1]
    shift = (part - main) * x

    def at(start, n):
        return pl.ds(pl.multiple_of(start, 16), n)

    for i in range(4):
        down[at(rows_a * i + shift, rows_a)] = da[i].astype(F32)
        start = half_a + rows_b * i + shift
        down[at(start, 16)] = db[i, 0:16].astype(F32)
        down[at(start + 16 - (i // 3) * x * part, rows_b - 16)] = db[i, 16:].astype(F32)
    saved.append(store(8, down, m["down_o"]))
    rest["qkv"].wait()
    qkv_v, qkv_f = m["qkv_v"], m["qkv_f"]
    q_cols, kv_cols = HEADS * HEAD_DIM, KV_HEADS * HEAD_DIM
    half = lambda v, w: jnp.where(low, v, w)
    for i in range(4):
        a, b = qkv_v[2 * i].astype(F32), qkv_v[2 * i + 1].astype(F32)
        a1, a2, b0, b1 = a[:, 128:256], a[:, 256:], b[:, 0:128], b[:, 128:256]
        lo = i * 2 * Q_COLS
        qkv_f[:, lo:lo + 128] = a[:, 0:128]
        qkv_f[:, lo + 128:lo + 256] = half(a1, roll(b0, 64))
        qkv_f[:, lo + 256:lo + 384] = half(roll(b0, 64), roll(b1, 64))
        lo = q_cols + i * 128
        qkv_f[:, lo:lo + 128] = half(roll(a1, 64), b1)
        lo = lo + kv_cols
        qkv_f[:, lo:lo + 128] = jnp.concatenate([a2, b[:, 256:]], axis=1)
    saved.append(store(9, qkv_f, m["qkv_o"]))
    rest["out"].wait()
    n = m["out_v"].shape[1]
    for i in range(4):
        m["out_f"][n * i:n * (i + 1)] = m["out_v"][i].astype(F32)
    saved.append(store(10, m["out_f"], m["out_o"]))
    for k, n in ((11, "ig"), (12, "mixed")):
        rest[n].wait()
        saved.append(store(k, m[n + "_v"], m[n + "_o"]))
    gains = m["gains"][...]
    width = gains.shape[1]
    turned = pltpu.roll(gains, (width - own_rows * lax.axis_index("grp")) % width, 1)
    m["one_o"][...] = turned[0:1, 0:own_rows]
    m["two_o"][...] = turned[1:2, 0:own_rows]
    m["q_o"][...] = gains[2:3, 0:HEAD_DIM]
    m["k_o"][...] = gains[2:3, HEAD_DIM:2 * HEAD_DIM]
    for copy in saved:
        copy.wait()


def order_call(g):
    shape = jax.ShapeDtypeStruct
    ga, gb, da, db, out, qkv, mixed, ig = (g[n] for n in ORDER_IN)
    _, own_rows, cols_a = ga.shape
    cols = cols_a + gb.shape[2]
    width = da.shape[2]
    part = 4 * (da.shape[1] + db.shape[1])
    qkv_cols = (HEADS + 2 * KV_HEADS) * HEAD_DIM
    outs = {
        "gu_o": shape((own_rows, 8 * cols), F32), "down_o": shape((part, width), F32),
        "out_o": shape((own_rows, width), F32), "qkv_o": shape((own_rows, qkv_cols), F32),
        "ig_o": shape(ig.shape, F32), "mixed_o": shape(mixed.shape, BF16),
        "one_o": shape((1, own_rows), F32), "two_o": shape((1, own_rows), F32),
        "q_o": shape((1, HEAD_DIM), F32), "k_o": shape((1, HEAD_DIM), F32),
    }
    ins = ("ga", "gb", "da", "db", "out", "qkv", "mixed", "ig")
    scratch = {n + "_v": pltpu.VMEM(v.shape, v.dtype)
               for n, v in zip(ins, (ga, gb, da, db, out, qkv, mixed, ig))}
    scratch["gu_v"] = pltpu.VMEM((8, own_rows, cols), F32)
    scratch["down_v"] = pltpu.VMEM((part, width), F32)
    scratch["out_f"] = pltpu.VMEM((own_rows, width), F32)
    scratch["qkv_f"] = pltpu.VMEM((own_rows, qkv_cols), F32)
    scratch["load"], scratch["save"] = dma(14), dma(13)
    names = ins + ("gains",) + tuple(outs) + tuple(scratch)
    got = pl.pallas_call(
        functools.partial(order_kernel, names),
        name="final_order",
        out_shape=tuple(outs.values()),
        in_specs=[ANY] * 8 + [VMEM],
        out_specs=(ANY,) * 6 + (VMEM,) * 4,
        scratch_shapes=list(scratch.values()),
        compiler_params=pltpu.CompilerParams(vmem_limit_bytes=62 * 2**20),
    )(ga, gb, da, db, out, qkv, mixed, ig, g["gains_g"])
    return dict(zip(outs, got))


ORDER_IN = ("ga_g", "gb_g", "da_g", "db_g", "out_g", "qkv_g", "mixed", "input_grad")


def over_quads(array):
    reps = lax.axis_size("rep")
    if reps == 4:
        return array
    rows = [[j + 4 * q for q in range(reps // 4)] for j in range(4)]
    return lax.psum(array, "rep", axis_index_groups=rows)


def local(tokens, attn_gain, w_qkv, q_gain, k_gain, w_out, ffn_gain, w_gate_up, w_down,
          cotangent, segment_ids):
    rows, width = tokens.shape
    parts = (attn_gain, q_gain, ffn_gain, k_gain, segment_ids)
    total = sum(v.shape[0] for v in parts)
    small, at = 0.0, 0
    for v in parts:
        n = v.shape[0]
        small = small + jnp.pad(v.astype(F32), (at, total - at - n))
        at += n
    g = block_call(
        tokens, cotangent, small.reshape(1, -1), w_qkv, w_gate_up, w_down, w_out)
    g = {n: over_quads(v) if n.endswith("_g") else v for n, v in g.items()}
    o = order_call(g)
    flat = lambda n: o[n].reshape(-1)
    return (o["mixed_o"], o["ig_o"], flat("one_o"), o["qkv_o"], flat("q_o"), flat("k_o"),
            o["out_o"], flat("two_o"), o["gu_o"], o["down_o"])


def solution(mesh):
    rows, split = P(("rep", "grp"), None), P("grp", None)
    return jax.shard_map(
        local,
        mesh=mesh,
        in_specs=(rows, P("grp"), split, P(), P(), split, P("grp"), split, split, rows,
                  P(("rep", "grp"))),
        out_specs=(rows, rows, P("grp"), split, P(), P(), split, P("grp"), split, split),
        check_vma=False,
    )
```
